32 devices in a mesh: dp: 8 (over z, x), tensor: 4 (over y, core).
Axes of the slice: x: 2, y: 2, z: 4, core: 2. Of those that a mesh axis runs over, the one named last changes fastest.
Arguments:
- rollout_states: bfloat16 [8192, 8192], P('dp', 'tensor'), may hold values from -6 to 6
- norm_gain: float32 [8192], replicated, may hold values from 0.1 to 1.9
- w_query: bfloat16 [8192, 4096], P('dp', 'tensor'), as said below
- w_key: bfloat16 [8192, 512], P('dp', 'tensor'), as said below
- w_value: bfloat16 [8192, 512], P('dp', 'tensor'), may hold values from -0.0625 to 0.0625
- b_query: float32 [4096], P('tensor'), may hold values from -3 to 3
- b_key: float32 [512], P('tensor'), may hold values from -3 to 3
- b_value: float32 [512], P('tensor'), may hold values from -3 to 3
- seq_lengths: int32 [64], replicated, may hold values from 1 to 255, as said below
- seq_dest: int32 [64], replicated, may hold values from 0 to 7, as said below
- seq_offset: int32 [64], replicated, may hold values from 0 to 1023, as said below
Outputs:
- context: bfloat16 [8192, 4096], P('dp', 'tensor')
The draws below stay inside these ranges and needn't reach their ends.
Inputs may be any that keep to these rules, and one draw needn't show every extreme that they name: `seq_lengths`: the 8 responses r * 8 to r * 8 + 7 lie in this order in rollout device r's 1024 rows and fill them; some response has exactly 255 tokens. `seq_dest`: the responses of one rollout device go to 8 different learners, so every learner receives exactly one response from every rollout device. `seq_offset`: the responses of one learner occupy disjoint runs of rows that together cover its 1024 rows. `w_query`: A weight matrix. `w_key`: A weight matrix.
All inputs are finite; a program needn't handle non-finite values.
Results may differ from the reference program's by a relative error of at most 0.012.
The reference program's roundings to bfloat16 on the way (of `gathered`, `normed` and `weights`) count: a program that leaves them out, or rounds other values in their place, can miss the bound.
Values may be sent and summed in bfloat16 or wider, within the bound.
No kernel may reach another device: no remote copies, remote signals or barrier semaphores. Data moves between devices by JAX's collectives and lax.ppermute only.
A program may use at most 128 MiB of HBM per device.

```python
import jax
import jax.numpy as jnp
from jax import lax

D = 8192
HD = 128
HQ = 32
KV = 4
TOK_DEV = 1024
TOKENS = 8192
LEARNERS = 8
MAXLEN = 255


def shared_query(key):
    return jax.random.normal(key, (D, HQ * HD), jnp.float32)


def draw_w_query(key, part):
    base = shared_query(key)
    return (base * D ** (-0.5)).astype(jnp.bfloat16)


def draw_w_key(key, part):
    key = jax.random.fold_in(key, 12)
    own = jax.random.normal(key, (D, KV, HD), jnp.float32)
    return (own * D ** (-0.5)).reshape(D, KV * HD).astype(jnp.bfloat16)


def routing_tables(key):
    key_pairs, key_order, key_shift, key_rows = jax.random.split(key, 4)
    half_count = LEARNERS // 2
    first_part = jax.random.randint(key_pairs, (half_count,), 1, MAXLEN + 1)
    first_part = first_part.at[0].set(MAXLEN)
    pattern = jnp.concatenate([first_part, MAXLEN + 1 - first_part])
    pattern = jax.random.permutation(key_order, pattern)
    shifted = jax.random.permutation(key_shift, LEARNERS)
    rollout_ids = jnp.arange(LEARNERS)
    table = pattern[(shifted[None, :] - rollout_ids[:, None]) % LEARNERS]

    def one_order(row_key):
        return jax.random.permutation(row_key, LEARNERS)
    orders = jax.vmap(one_order)(jax.random.split(key_rows, LEARNERS))
    lengths = jnp.take_along_axis(table, orders, axis=1)
    offsets_full = jnp.cumsum(table, axis=0) - table
    offsets = jnp.take_along_axis(offsets_full, orders, axis=1)
    return (lengths.reshape(-1).astype(jnp.int32), orders.reshape(-1).astype(jnp.int32), offsets.reshape(-1).astype(jnp.int32))


def draw_seq_lengths(key, part):
    tables = routing_tables(key)
    return tables[0]


def draw_seq_dest(key, part):
    tables = routing_tables(key)
    return tables[1]


def draw_seq_offset(key, part):
    tables = routing_tables(key)
    return tables[2]


def steps_of(stream_key, shape, shards, low, largest):
    gain = 1.0
    for axis_at, blocks in shards:
        draws = jax.random.uniform(jax.random.fold_in(jax.random.fold_in(stream_key, 6), axis_at), (blocks,), jnp.float32, low / len(shards), largest / len(shards))
        gain = gain * jnp.repeat(jnp.exp(draws), shape[axis_at] // blocks).reshape((-1,) + (1,) * (len(shape) - 1 - axis_at))
    return gain


def noise(own_key, shape, spread, reach, cuts=(), held_as=jnp.bfloat16):
    result = spread * jax.random.normal(own_key, shape, jnp.float32)
    if cuts:
        result = result * steps_of(own_key, shape, cuts, -0.22, 0.18)
    return jnp.clip(result, -reach, reach).astype(held_as)


def setup_inputs(seed: int = 0) -> dict:
    key_list = jax.random.split(jax.random.key(seed), 12)
    return {
        "rollout_states": noise(key_list[0], (TOKENS, D), 1.0, 6.0, ((0, 8), (1, 4))),
        "norm_gain": jnp.clip(1.0 + 0.18 * jax.random.normal(key_list[1], (D,), jnp.float32), 0.1, 1.9),
        "w_query": draw_w_query(jax.random.fold_in(key_list[11], 71), 0),
        "w_key": draw_w_key(jax.random.fold_in(key_list[11], 71), 0),
        "w_value": noise(key_list[4], (D, KV * HD), D ** -0.5, 0.0625, ((0, 8), (1, 4))),
        "b_query": noise(key_list[5], (HQ * HD,), 0.5, 3.0, ((0, 4),), jnp.float32),
        "b_key": noise(key_list[6], (KV * HD,), 0.5, 3.0, ((0, 4),), jnp.float32),
        "b_value": noise(key_list[7], (KV * HD,), 0.5, 3.0, ((0, 4),), jnp.float32),
        "seq_lengths": draw_seq_lengths(jax.random.fold_in(key_list[11], 71), 0),
        "seq_dest": draw_seq_dest(jax.random.fold_in(key_list[11], 71), 0),
        "seq_offset": draw_seq_offset(jax.random.fold_in(key_list[11], 71), 0),
    }


rope_base = 1000000.0
norm_eps = 1e-06

def rope_tables(positions):
    half_dim = HD // 2
    frequency = rope_base ** (-(jnp.arange(half_dim).astype(jnp.float32) * 2.0 / HD))
    angles = positions.astype(jnp.float32)[:, None] * frequency[None, :]
    return (jnp.cos(angles), jnp.sin(angles))

def rotate(states, cosine, sine):
    half_dim = states.shape[-1] // 2
    first_half = states[..., :half_dim]
    second_half = states[..., half_dim:]
    cos_wide = cosine[:, None, :]
    sin_wide = sine[:, None, :]
    return jnp.concatenate([first_half * cos_wide - second_half * sin_wide, second_half * cos_wide + first_half * sin_wide], axis=-1)

def learner_layout(seq_lengths, seq_dest, seq_offset, learner, row_count, learners):
    lengths = seq_lengths.reshape(learners, learners)
    dests = seq_dest.reshape(learners, learners)
    offsets = seq_offset.reshape(learners, learners)
    starts = (jnp.cumsum(lengths, axis=1) - lengths).astype(jnp.int32)
    matched = (dests == learner).astype(jnp.int32)
    run_start = lax.optimization_barrier(jnp.sum(matched * offsets, axis=1)).astype(jnp.int32)
    run_length = lax.optimization_barrier(jnp.sum(matched * lengths, axis=1)).astype(jnp.int32)
    rollout_start = lax.optimization_barrier(jnp.sum(matched * starts, axis=1)).astype(jnp.int32)
    rows = jnp.arange(row_count, dtype=jnp.int32)
    inside = ((rows[:, None] >= run_start[None, :]) & (rows[:, None] < (run_start + run_length)[None, :])).astype(jnp.int32)
    source_ids = lax.optimization_barrier(jnp.sum(inside * jnp.arange(learners, dtype=jnp.int32)[None, :], axis=1)).astype(jnp.int32)
    within_seq = (rows - lax.optimization_barrier(jnp.sum(inside * run_start[None, :], axis=1))).astype(jnp.int32)
    first_rows = lax.optimization_barrier(jnp.sum(inside * rollout_start[None, :], axis=1)).astype(jnp.int32)
    rollout_rows = (source_ids * row_count + first_rows + within_seq).astype(jnp.int32)
    return (rollout_rows, source_ids, within_seq)

def attend(rot_query, rot_key, value_bf, query_source, key_source, query_rows, key_rows):
    scores = jnp.einsum('bcgd,kcd->cgbk', rot_query.astype(jnp.float32), rot_key.astype(jnp.float32))
    scores = scores * HD ** (-0.5)
    allowed = (key_source[None, :] == query_source[:, None]) & (key_rows[None, :] <= query_rows[:, None])
    scores = jnp.where(allowed[None, None], scores, -1e+30)
    peak = lax.optimization_barrier(jnp.max(scores, axis=-1, keepdims=True))
    raised = jnp.exp(scores - peak)
    weights = (raised / lax.optimization_barrier(jnp.sum(raised, axis=-1, keepdims=True))).astype(jnp.bfloat16)
    context = jnp.einsum('cgbk,kcd->bcgd', weights.astype(jnp.float32), value_bf.astype(jnp.float32))
    return context.astype(jnp.bfloat16)

def reference(rollout_states, norm_gain, w_query, w_key, w_value, b_query, b_key, b_value, seq_lengths, seq_dest, seq_offset):
    group = HQ // KV

    def one_learner(learner):
        rollout_rows, source_ids, within_seq = learner_layout(seq_lengths, seq_dest, seq_offset, learner, TOK_DEV, LEARNERS)
        gathered = jnp.take(rollout_states, rollout_rows, axis=0)
        widened = gathered.astype(jnp.float32)
        statistic = lax.optimization_barrier(jnp.mean(widened * widened, axis=-1, keepdims=True))
        normed = (widened * lax.rsqrt(statistic + norm_eps) * norm_gain[None, :]).astype(jnp.bfloat16)
        query = jnp.dot(normed, w_query, preferred_element_type=jnp.float32) + b_query[None, :]
        key = jnp.dot(normed, w_key, preferred_element_type=jnp.float32) + b_key[None, :]
        value = jnp.dot(normed, w_value, preferred_element_type=jnp.float32) + b_value[None, :]
        cosine, sine = rope_tables(within_seq)
        rot_query = rotate(query.reshape(TOK_DEV, HQ, HD), cosine, sine).astype(jnp.bfloat16)
        rot_query = rot_query.reshape(TOK_DEV, KV, group, HD)
        rot_key = rotate(key.reshape(TOK_DEV, KV, HD), cosine, sine).astype(jnp.bfloat16)
        value_bf = value.reshape(TOK_DEV, KV, HD).astype(jnp.bfloat16)
        rows = jnp.arange(TOK_DEV, dtype=jnp.int32)
        context = attend(rot_query, rot_key, value_bf, source_ids, source_ids, rows, rows)
        return context.reshape(TOK_DEV, HQ * HD)
    blocks = lax.map(one_learner, jnp.arange(LEARNERS, dtype=jnp.int32))
    return blocks.reshape(TOKENS, HQ * HD)
```

```python
import functools

import jax
import jax.numpy as jnp
from jax import lax
from jax.experimental import pallas as pl
from jax.experimental.pallas import tpu as pltpu
from jax.sharding import PartitionSpec as P

HD = 128

rope_base = 1000000.0
norm_eps = 1e-06
mask_value = -1e30


def rope_tables(positions):
    half_dim = HD // 2
    frequency = rope_base ** (-(jnp.arange(half_dim).astype(jnp.float32) * 2.0 / HD))
    angles = positions.astype(jnp.float32)[:, None] * frequency[None, :]
    return (jnp.cos(angles), jnp.sin(angles))


def rotate(states, cosine, sine):
    half_dim = states.shape[-1] // 2
    first_half = states[..., :half_dim]
    second_half = states[..., half_dim:]
    cos_wide = cosine[:, None, :]
    sin_wide = sine[:, None, :]
    return jnp.concatenate(
        [
            first_half * cos_wide - second_half * sin_wide,
            second_half * cos_wide + first_half * sin_wide,
        ],
        axis=-1,
    )


def local_any(
    rollout_states,
    norm_gain,
    w_query,
    w_key,
    w_value,
    b_query,
    b_key,
    b_value,
    seq_lengths,
    seq_dest,
    seq_offset,
):
    learners = lax.axis_size("dp")
    own_index = lax.axis_index("dp")
    row_count, feature_count = rollout_states.shape
    capacity = 2 * row_count // learners - 1
    lengths = seq_lengths.reshape(learners, learners)
    dests = seq_dest.reshape(learners, learners)
    offsets = seq_offset.reshape(learners, learners)
    starts = jnp.cumsum(lengths, axis=1) - lengths
    peer_ids = jnp.arange(learners, dtype=jnp.int32)
    own_length = lax.dynamic_index_in_dim(lengths, own_index, 0, keepdims=False)
    own_start = lax.dynamic_index_in_dim(starts, own_index, 0, keepdims=False)
    own_dest = lax.dynamic_index_in_dim(dests, own_index, 0, keepdims=False)
    match_send = (own_dest[None, :] == peer_ids[:, None]).astype(jnp.int32)
    send_start = jnp.sum(match_send * own_start[None, :], axis=1)
    send_length = jnp.sum(match_send * own_length[None, :], axis=1)
    slot_index = jnp.arange(capacity, dtype=jnp.int32)
    pick_rows = send_start[:, None] + slot_index[None, :]
    padded = jnp.concatenate(
        [rollout_states, jnp.zeros((capacity, feature_count), rollout_states.dtype)], axis=0
    )
    live_slots = (slot_index[None, :] < send_length[:, None])[..., None]
    outgoing = jnp.where(
        live_slots, jnp.take(padded, pick_rows, axis=0), jnp.zeros((), rollout_states.dtype)
    )
    incoming = lax.all_to_all(outgoing, "dp", split_axis=0, concat_axis=0, tiled=True)
    matched = (dests == own_index).astype(jnp.int32)
    run_start = jnp.sum(matched * offsets, axis=1)
    run_length = jnp.sum(matched * lengths, axis=1)
    rows = jnp.arange(row_count, dtype=jnp.int32)
    inside = (
        (rows[:, None] >= run_start[None, :]) & (rows[:, None] < (run_start + run_length)[None, :])
    ).astype(jnp.int32)
    source_ids = jnp.sum(inside * peer_ids[None, :], axis=1)
    within_seq = rows - jnp.sum(inside * run_start[None, :], axis=1)
    arrived = jnp.take(
        incoming.reshape(learners * capacity, feature_count),
        source_ids * capacity + within_seq,
        axis=0,
    )
    gathered = lax.all_gather(arrived, "tensor", axis=1, tiled=True)
    widened = gathered.astype(jnp.float32)
    statistic = jnp.mean(widened * widened, axis=-1, keepdims=True)
    normed = (widened * lax.rsqrt(statistic + norm_eps) * norm_gain[None, :]).astype(jnp.bfloat16)
    full_query, full_key, full_value = (
        lax.all_gather(w_query, "dp", axis=0, tiled=True),
        lax.all_gather(w_key, "dp", axis=0, tiled=True),
        lax.all_gather(w_value, "dp", axis=0, tiled=True),
    )
    query = jnp.dot(normed, full_query, preferred_element_type=jnp.float32)
    key = jnp.dot(normed, full_key, preferred_element_type=jnp.float32)
    value = jnp.dot(normed, full_value, preferred_element_type=jnp.float32)
    query = query + b_query[None, :]
    key = key + b_key[None, :]
    value = value + b_value[None, :]
    heads_here = query.shape[1] // HD
    kv_here = key.shape[1] // HD
    group = heads_here // kv_here
    cosine, sine = rope_tables(within_seq)
    rot_query = rotate(query.reshape(row_count, heads_here, HD), cosine, sine).astype(jnp.bfloat16)
    rot_query = rot_query.reshape(row_count, kv_here, group, HD)
    rot_key = rotate(key.reshape(row_count, kv_here, HD), cosine, sine).astype(jnp.bfloat16)
    value_bf = value.reshape(row_count, kv_here, HD).astype(jnp.bfloat16)
    block_rows = min(512, row_count)

    def one_block(block_number):
        first_row = block_number * block_rows
        query_block = lax.dynamic_slice_in_dim(rot_query, first_row, block_rows, 0)
        query_source = lax.dynamic_slice_in_dim(source_ids, first_row, block_rows, 0)
        query_rows = first_row + jnp.arange(block_rows, dtype=jnp.int32)
        scores = jnp.einsum(
            "bcgd,kcd->cgbk", query_block, rot_key, preferred_element_type=jnp.float32
        )
        scores = scores * HD ** (-0.5)
        allowed = (source_ids[None, :] == query_source[:, None]) & (
            rows[None, :] <= query_rows[:, None]
        )
        scores = jnp.where(allowed[None, None], scores, mask_value)
        peak = jnp.max(scores, axis=-1, keepdims=True)
        raised = jnp.exp(scores - peak)
        weights = (raised / jnp.sum(raised, axis=-1, keepdims=True)).astype(jnp.bfloat16)
        context = jnp.einsum(
            "cgbk,kcd->bcgd", weights, value_bf, preferred_element_type=jnp.float32
        )
        return context.astype(jnp.bfloat16).reshape(block_rows, heads_here * HD)

    outputs = lax.map(one_block, jnp.arange(row_count // block_rows, dtype=jnp.int32))
    return outputs.reshape(row_count, heads_here * HD)


def project_kernel(chunks, off_ref, *refs):
    x_refs = refs[:4]
    w_refs = refs[4 : 4 + 7 * chunks]
    bias_ref, cos_ref, sin_ref, out_ref, w_buf, sems = refs[4 + 7 * chunks :]

    @pl.when(pl.program_id(0) == 0)
    def _():
        for i in range(4):
            for c in range(chunks):
                for place in range(7):

                    @pl.when(off_ref[i] == place - 3)
                    def _(i=i, c=c, place=place):
                        pltpu.make_async_copy(
                            w_refs[7 * c + place],
                            w_buf.at[i, :, pl.ds(c * HD, HD)],
                            sems.at[i, c],
                        ).start()

        for i in range(4):
            for c in range(chunks):
                pltpu.make_async_copy(
                    w_refs[7 * c], w_buf.at[i, :, pl.ds(c * HD, HD)], sems.at[i, c]
                ).wait()

    total = jnp.dot(x_refs[0][...], w_buf[0], preferred_element_type=jnp.float32)
    for i in range(1, 4):
        total += jnp.dot(x_refs[i][...], w_buf[i], preferred_element_type=jnp.float32)
    for c in range(chunks):
        part = total[:, c * HD : (c + 1) * HD] + bias_ref[:, c * HD : (c + 1) * HD]
        rot = part * cos_ref[c] + pltpu.roll(part, HD // 2, 1) * sin_ref[c]
        out_ref[:, c * HD : (c + 1) * HD] = rot.astype(out_ref.dtype)


def project(off, x_blocks, w_places, bias, cos, sin):
    chunks = len(w_places)
    rows, feats = x_blocks[0].shape
    tile = min(256, rows)
    flat = [w for places in w_places for w in places]
    grid_spec = pltpu.PrefetchScalarGridSpec(
        num_scalar_prefetch=1,
        grid=(rows // tile,),
        in_specs=[pl.BlockSpec((tile, feats), lambda r, off: (r, 0))] * 4
        + [pl.BlockSpec(memory_space=pl.ANY)] * len(flat)
        + [
            pl.BlockSpec((1, chunks * HD), lambda r, off: (0, 0)),
            pl.BlockSpec((chunks, tile, HD), lambda r, off: (0, r, 0)),
            pl.BlockSpec((chunks, tile, HD), lambda r, off: (0, r, 0)),
        ],
        out_specs=pl.BlockSpec((tile, chunks * HD), lambda r, off: (r, 0)),
        scratch_shapes=[
            pltpu.VMEM((4, feats, chunks * HD), jnp.bfloat16),
            pltpu.SemaphoreType.DMA((4, chunks)),
        ],
    )
    return pl.pallas_call(
        functools.partial(project_kernel, chunks),
        grid_spec=grid_spec,
        out_shape=jax.ShapeDtypeStruct((rows, chunks * HD), jnp.bfloat16),
        compiler_params=pltpu.CompilerParams(vmem_limit_bytes=40 * 2**20),
        cost_estimate=pl.CostEstimate(
            flops=2 * rows * 4 * feats * chunks * HD,
            bytes_accessed=8 * rows * feats + 8 * feats * chunks * HD,
            transcendentals=0,
        ),
    )(off, *x_blocks, *flat, bias, cos, sin)


def attend_kernel(heads, slot, window, start_ref, len_ref, q_ref, k_ref, v_ref, out_ref):
    which = pl.program_id(0)
    rows = q_ref.shape[0]
    start = start_ref[which]
    first = pl.multiple_of(jnp.minimum((start // 16) * 16, rows - window), 16)
    row_at = lax.broadcasted_iota(jnp.int32, (slot, window), 0)
    col_at = lax.broadcasted_iota(jnp.int32, (slot, window), 1)
    pick = jnp.where(
        (col_at == row_at + (start - first)) & (row_at < len_ref[which]), 1.0, 0.0
    ).astype(jnp.bfloat16)

    def picked(ref, lanes):
        rows_here = ref[pl.ds(first, window), lanes]
        return jnp.dot(pick, rows_here, preferred_element_type=jnp.float32).astype(jnp.bfloat16)

    key = picked(k_ref, pl.ds(0, HD))
    value = picked(v_ref, pl.ds(0, HD))
    causal = lax.broadcasted_iota(jnp.int32, (slot, slot), 1) <= lax.broadcasted_iota(
        jnp.int32, (slot, slot), 0
    )
    for h in range(heads):
        query = picked(q_ref, pl.ds(h * HD, HD))
        scores = lax.dot_general(
            query, key, (((1,), (1,)), ((), ())), preferred_element_type=jnp.float32
        )
        scores = jnp.where(causal, scores * HD ** (-0.5), mask_value)
        peak = jnp.max(scores, axis=-1, keepdims=True)
        raised = jnp.exp(scores - peak)
        weights = (raised / jnp.sum(raised, axis=-1, keepdims=True)).astype(jnp.bfloat16)
        context = jnp.dot(weights, value, preferred_element_type=jnp.float32)
        out_ref[0, :, h * HD : (h + 1) * HD] = context.astype(out_ref.dtype)


def attend(starts, lens, query, key, value, slot):
    rows, columns = query.shape
    count = starts.shape[0]
    window = min(rows, -(-(slot + 16) // 128) * 128)
    heads = columns // HD
    grid_spec = pltpu.PrefetchScalarGridSpec(
        num_scalar_prefetch=2,
        grid=(count,),
        in_specs=[
            pl.BlockSpec((rows, columns), lambda s, a, b: (0, 0)),
            pl.BlockSpec((rows, HD), lambda s, a, b: (0, 0)),
            pl.BlockSpec((rows, HD), lambda s, a, b: (0, 0)),
        ],
        out_specs=pl.BlockSpec((1, slot, columns), lambda s, a, b: (s, 0, 0)),
    )
    return pl.pallas_call(
        functools.partial(attend_kernel, heads, slot, window),
        grid_spec=grid_spec,
        out_shape=jax.ShapeDtypeStruct((count, slot, columns), jnp.bfloat16),
        compiler_params=pltpu.CompilerParams(vmem_limit_bytes=32 * 2**20),
        cost_estimate=pl.CostEstimate(
            flops=2 * count * slot * (2 * slot + window) * columns,
            bytes_accessed=2 * (rows * (columns + 2 * HD) + count * slot * columns),
            transcendentals=count * heads * slot * slot,
        ),
    )(starts, lens, query, key, value)


def place_kernel(count, slot, window, start_ref, len_ref, in_ref, out_ref, total):
    learner = pl.program_id(0)
    rows = total.shape[0]
    total[...] = jnp.zeros_like(total)
    row_at = lax.broadcasted_iota(jnp.int32, (window, slot), 0)
    col_at = lax.broadcasted_iota(jnp.int32, (window, slot), 1)
    for s in range(count):
        start = start_ref[learner, s]
        first = pl.multiple_of(jnp.minimum((start // 8) * 8, rows - window), 8)
        pick = jnp.where(
            (row_at == col_at + (start - first)) & (col_at < len_ref[learner, s]), 1.0, 0.0
        ).astype(jnp.bfloat16)
        total[pl.ds(first, window), :] += jnp.dot(
            pick, in_ref[s, 0], preferred_element_type=jnp.float32
        )
    out_ref[0] = total[...].astype(out_ref.dtype)


def place(starts, lens, slots, rows):
    count, learners, slot, columns = slots.shape
    window = min(rows, slot + 8)
    grid_spec = pltpu.PrefetchScalarGridSpec(
        num_scalar_prefetch=2,
        grid=(learners,),
        in_specs=[pl.BlockSpec((count, 1, slot, columns), lambda r, a, b: (0, r, 0, 0))],
        out_specs=pl.BlockSpec((1, rows, columns), lambda r, a, b: (r, 0, 0)),
        scratch_shapes=[pltpu.VMEM((rows, columns), jnp.float32)],
    )
    return pl.pallas_call(
        functools.partial(place_kernel, count, slot, window),
        grid_spec=grid_spec,
        out_shape=jax.ShapeDtypeStruct((learners, rows, columns), jnp.bfloat16),
        compiler_params=pltpu.CompilerParams(vmem_limit_bytes=32 * 2**20),
        cost_estimate=pl.CostEstimate(
            flops=2 * learners * count * slot * window * columns,
            bytes_accessed=2 * learners * columns * (count * slot + rows),
            transcendentals=0,
        ),
    )(starts, lens, slots)


def local_line(
    rollout_states,
    norm_gain,
    w_query,
    w_key,
    w_value,
    b_query,
    b_key,
    b_value,
    seq_lengths,
    seq_dest,
    seq_offset,
):
    learners = lax.axis_size("dp")
    line = learners // 2
    me = lax.axis_index("dp")
    z, x = me // 2, me % 2
    t = lax.axis_index("tensor")
    row_count, feature_count = rollout_states.shape
    slot = 2 * row_count // learners
    half = w_query.shape[1] // 2
    heads = half // HD

    def swap_x(array):
        return lax.ppermute(array, "dp", [(i, i ^ 1) for i in range(learners)])

    def swap_y(array):
        return lax.ppermute(array, "tensor", [(i, i ^ 2) for i in range(4)])

    def swap_core(array):
        return lax.ppermute(array, "tensor", [(i, i ^ 1) for i in range(4)])

    def up(array, first):
        return lax.ppermute(array, "dp", [(i, i + 2) for i in range(2 * first, learners - 2)])

    def down(array, first):
        return lax.ppermute(array, "dp", [(i, i - 2) for i in range(2, learners - 2 * first)])

    def by_x(at_zero, at_one):
        return jnp.where(x == 0, at_zero, at_one)

    lengths = seq_lengths.reshape(learners, learners)
    dests = seq_dest.reshape(learners, learners)
    offsets = seq_offset.reshape(learners, learners)
    starts = jnp.cumsum(lengths, axis=1) - lengths
    peer_ids = jnp.arange(learners, dtype=jnp.int32)
    rows = jnp.arange(row_count, dtype=jnp.int32)

    def sends(rollout):
        length = lax.dynamic_index_in_dim(lengths, rollout, 0, keepdims=False)
        start = lax.dynamic_index_in_dim(starts, rollout, 0, keepdims=False)
        dest = lax.dynamic_index_in_dim(dests, rollout, 0, keepdims=False)
        match = (dest[None, :] == peer_ids[:, None]).astype(jnp.int32)
        inside = (rows[:, None] >= start[None, :]) & (rows[:, None] < (start + length)[None, :])
        position = rows - jnp.sum(inside.astype(jnp.int32) * start[None, :], axis=1)
        cosine, sine = rope_tables(position)
        cosine = jnp.concatenate([cosine, cosine], axis=1)
        sine = jnp.concatenate([-sine, sine], axis=1)
        return (
            jnp.sum(match * start[None, :], axis=1),
            jnp.sum(match * length[None, :], axis=1),
            cosine,
            sine,
        )

    def receives(learner):
        matched = (dests == learner).astype(jnp.int32)
        return jnp.sum(matched * offsets, axis=1), jnp.sum(matched * lengths, axis=1)

    other = me ^ 1
    own_table, other_table = sends(me), sends(other)

    kv_mine, kv_give = by_x(w_key, w_value), by_x(w_value, w_key)
    q_mine = lax.dynamic_slice_in_dim(w_query, x * half, half, 1)
    q_give = lax.dynamic_slice_in_dim(w_query, (1 - x) * half, half, 1)
    places = []
    for c in range(heads + 1):
        if c == 0:
            mine, give = kv_mine, kv_give
        else:
            mine, give = (w[:, (c - 1) * HD : c * HD] for w in (q_mine, q_give))
        got = swap_x(give)
        own = by_x(jnp.concatenate([mine, got], axis=0), jnp.concatenate([got, mine], axis=0))
        ups, downs = [own], [own]
        for step in range(line - 1):
            ups.append(up(ups[-1], step))
            downs.append(down(downs[-1], step))
        places.append(ups[:0:-1] + downs)
    bias_kv = by_x(b_key, b_value)
    bias_q = lax.dynamic_slice_in_dim(b_query, x * half, half, 0)
    bias = jnp.concatenate([bias_kv, bias_q])[None, :]

    widened = rollout_states.astype(jnp.float32)
    squares = jnp.sum(widened * widened, axis=-1)
    squares = squares + swap_core(squares)
    squares = squares + swap_y(squares)
    statistic = squares[:, None] / (4 * feature_count)
    gain = lax.dynamic_slice_in_dim(norm_gain, t * feature_count, feature_count, 0)
    normed = (widened * lax.rsqrt(statistic + norm_eps) * gain[None, :]).astype(jnp.bfloat16)

    middle = row_count // 2
    own_y = swap_y(normed)
    near = swap_x(normed)
    near_y = jnp.concatenate([swap_y(near[:middle]), swap_x(own_y[middle:])], axis=0)
    own_x = [normed, swap_core(normed), own_y, swap_core(own_y)]
    near_x = [near, swap_core(near), near_y, swap_core(near_y)]
    off = jnp.stack([(t ^ i) - z for i in range(4)]).astype(jnp.int32)

    def tables(table):
        cosine, sine = table[2], table[3]
        cos_kv = by_x(cosine, jnp.ones_like(cosine))
        sin_kv = by_x(sine, jnp.zeros_like(sine))
        return cos_kv[None], sin_kv[None], cosine[None], sine[None]

    def one(x_blocks, table, c):
        cos_kv, sin_kv, cosine, sine = table
        pick = (cos_kv, sin_kv) if c == 0 else (cosine, sine)
        return project(off, x_blocks, places[c : c + 1], bias[:, c * HD : (c + 1) * HD], *pick)

    own_tables, other_tables = tables(own_table), tables(other_table)
    own_kv = one(own_x, own_tables, 0)
    other_kv = one(near_x, other_tables, 0)
    own_kv_got, other_kv_got = swap_x(other_kv), swap_x(own_kv)
    own_k, own_v = by_x(own_kv, own_kv_got), by_x(own_kv_got, own_kv)
    other_k, other_v = by_x(other_kv, other_kv_got), by_x(other_kv_got, other_kv)

    z_ids = jnp.arange(line, dtype=jnp.int32)
    order = jnp.stack([2 * z_ids + x, 2 * z_ids + 1 - x], axis=1).reshape(-1)
    at_zero, at_one = receives(2 * z), receives(2 * z + 1)
    run_start = jnp.stack([at_zero[0][order], at_one[0][order]])
    run_length = jnp.stack([at_zero[1][order], at_one[1][order]])
    groups = [[2 * i + j for i in range(line)] for j in range(2)]

    kept, got = [], []
    for c in range(1, heads + 1):
        own_q = one(own_x, own_tables, c)
        other_q = one(near_x, other_tables, c)
        own_slots = attend(own_table[0], own_table[1], own_q, own_k, own_v, slot)
        other_slots = attend(other_table[0], other_table[1], other_q, other_k, other_v, slot)
        outgoing = jnp.stack(
            [own_slots.reshape(line, 2, slot, HD), other_slots.reshape(line, 2, slot, HD)], axis=1
        )
        incoming = lax.all_to_all(
            outgoing, "dp", split_axis=0, concat_axis=0, tiled=True, axis_index_groups=groups
        )
        placed = place(run_start, run_length, incoming.reshape(2 * line, 2, slot, HD), row_count)
        kept.append(by_x(placed[0], placed[1]))
        got.append(swap_x(by_x(placed[1], placed[0])))
    kept = jnp.concatenate(kept, axis=1)
    got = jnp.concatenate(got, axis=1)
    return by_x(jnp.concatenate([kept, got], axis=1), jnp.concatenate([got, kept], axis=1))


def solution(mesh):
    placed = (
        P("dp", "tensor"),
        P(),
        P("dp", "tensor"),
        P("dp", "tensor"),
        P("dp", "tensor"),
        P("tensor"),
        P("tensor"),
        P("tensor"),
        P(),
        P(),
        P(),
    )
    fits_line = mesh.shape["dp"] == 8 and mesh.shape["tensor"] == 4
    return jax.shard_map(
        local_line if fits_line else local_any,
        mesh=mesh,
        in_specs=placed,
        out_specs=P("dp", "tensor"),
        check_vma=False,
    )
```

```python
import functools

import jax
import jax.numpy as jnp
from jax import lax
from jax.experimental import pallas as pl
from jax.experimental.pallas import tpu as pltpu
from jax.sharding import PartitionSpec as P

HD = 128

rope_base = 1000000.0
norm_eps = 1e-06
mask_value = -1e30


def rope_tables(positions):
    half_dim = HD // 2
    frequency = rope_base ** (-(jnp.arange(half_dim).astype(jnp.float32) * 2.0 / HD))
    angles = positions.astype(jnp.float32)[:, None] * frequency[None, :]
    return (jnp.cos(angles), jnp.sin(angles))


def rotate(states, cosine, sine):
    half_dim = states.shape[-1] // 2
    first_half = states[..., :half_dim]
    second_half = states[..., half_dim:]
    cos_wide = cosine[:, None, :]
    sin_wide = sine[:, None, :]
    return jnp.concatenate(
        [
            first_half * cos_wide - second_half * sin_wide,
            second_half * cos_wide + first_half * sin_wide,
        ],
        axis=-1,
    )


def local_any(
    rollout_states,
    norm_gain,
    w_query,
    w_key,
    w_value,
    b_query,
    b_key,
    b_value,
    seq_lengths,
    seq_dest,
    seq_offset,
):
    learners = lax.axis_size("dp")
    own_index = lax.axis_index("dp")
    row_count, feature_count = rollout_states.shape
    capacity = 2 * row_count // learners - 1
    lengths = seq_lengths.reshape(learners, learners)
    dests = seq_dest.reshape(learners, learners)
    offsets = seq_offset.reshape(learners, learners)
    starts = jnp.cumsum(lengths, axis=1) - lengths
    peer_ids = jnp.arange(learners, dtype=jnp.int32)
    own_length = lax.dynamic_index_in_dim(lengths, own_index, 0, keepdims=False)
    own_start = lax.dynamic_index_in_dim(starts, own_index, 0, keepdims=False)
    own_dest = lax.dynamic_index_in_dim(dests, own_index, 0, keepdims=False)
    match_send = (own_dest[None, :] == peer_ids[:, None]).astype(jnp.int32)
    send_start = jnp.sum(match_send * own_start[None, :], axis=1)
    send_length = jnp.sum(match_send * own_length[None, :], axis=1)
    slot_index = jnp.arange(capacity, dtype=jnp.int32)
    pick_rows = send_start[:, None] + slot_index[None, :]
    padded = jnp.concatenate(
        [rollout_states, jnp.zeros((capacity, feature_count), rollout_states.dtype)], axis=0
    )
    live_slots = (slot_index[None, :] < send_length[:, None])[..., None]
    outgoing = jnp.where(
        live_slots, jnp.take(padded, pick_rows, axis=0), jnp.zeros((), rollout_states.dtype)
    )
    incoming = lax.all_to_all(outgoing, "dp", split_axis=0, concat_axis=0, tiled=True)
    matched = (dests == own_index).astype(jnp.int32)
    run_start = jnp.sum(matched * offsets, axis=1)
    run_length = jnp.sum(matched * lengths, axis=1)
    rows = jnp.arange(row_count, dtype=jnp.int32)
    inside = (
        (rows[:, None] >= run_start[None, :]) & (rows[:, None] < (run_start + run_length)[None, :])
    ).astype(jnp.int32)
    source_ids = jnp.sum(inside * peer_ids[None, :], axis=1)
    within_seq = rows - jnp.sum(inside * run_start[None, :], axis=1)
    arrived = jnp.take(
        incoming.reshape(learners * capacity, feature_count),
        source_ids * capacity + within_seq,
        axis=0,
    )
    gathered = lax.all_gather(arrived, "tensor", axis=1, tiled=True)
    widened = gathered.astype(jnp.float32)
    statistic = jnp.mean(widened * widened, axis=-1, keepdims=True)
    normed = (widened * lax.rsqrt(statistic + norm_eps) * norm_gain[None, :]).astype(jnp.bfloat16)
    full_query, full_key, full_value = (
        lax.all_gather(w_query, "dp", axis=0, tiled=True),
        lax.all_gather(w_key, "dp", axis=0, tiled=True),
        lax.all_gather(w_value, "dp", axis=0, tiled=True),
    )
    query = jnp.dot(normed, full_query, preferred_element_type=jnp.float32)
    key = jnp.dot(normed, full_key, preferred_element_type=jnp.float32)
    value = jnp.dot(normed, full_value, preferred_element_type=jnp.float32)
    query = query + b_query[None, :]
    key = key + b_key[None, :]
    value = value + b_value[None, :]
    heads_here = query.shape[1] // HD
    kv_here = key.shape[1] // HD
    group = heads_here // kv_here
    cosine, sine = rope_tables(within_seq)
    rot_query = rotate(query.reshape(row_count, heads_here, HD), cosine, sine).astype(jnp.bfloat16)
    rot_query = rot_query.reshape(row_count, kv_here, group, HD)
    rot_key = rotate(key.reshape(row_count, kv_here, HD), cosine, sine).astype(jnp.bfloat16)
    value_bf = value.reshape(row_count, kv_here, HD).astype(jnp.bfloat16)
    block_rows = min(512, row_count)

    def one_block(block_number):
        first_row = block_number * block_rows
        query_block = lax.dynamic_slice_in_dim(rot_query, first_row, block_rows, 0)
        query_source = lax.dynamic_slice_in_dim(source_ids, first_row, block_rows, 0)
        query_rows = first_row + jnp.arange(block_rows, dtype=jnp.int32)
        scores = jnp.einsum(
            "bcgd,kcd->cgbk", query_block, rot_key, preferred_element_type=jnp.float32
        )
        scores = scores * HD ** (-0.5)
        allowed = (source_ids[None, :] == query_source[:, None]) & (
            rows[None, :] <= query_rows[:, None]
        )
        scores = jnp.where(allowed[None, None], scores, mask_value)
        peak = jnp.max(scores, axis=-1, keepdims=True)
        raised = jnp.exp(scores - peak)
        weights = (raised / jnp.sum(raised, axis=-1, keepdims=True)).astype(jnp.bfloat16)
        context = jnp.einsum(
            "cgbk,kcd->bcgd", weights, value_bf, preferred_element_type=jnp.float32
        )
        return context.astype(jnp.bfloat16).reshape(block_rows, heads_here * HD)

    outputs = lax.map(one_block, jnp.arange(row_count // block_rows, dtype=jnp.int32))
    return outputs.reshape(row_count, heads_here * HD)


def pick_weights(off_ref, w_refs, w_buf, sems):
    for i in range(4):
        for place in range(7):

            @pl.when(off_ref[i] == place - 3)
            def _(i=i, place=place):
                pltpu.make_async_copy(w_refs[place], w_buf.at[i], sems.at[i]).start()

    for i in range(4):
        pltpu.make_async_copy(w_refs[0], w_buf.at[i], sems.at[i]).wait()


def product(x_refs, w_buf):
    total = jnp.dot(x_refs[0][...], w_buf[0], preferred_element_type=jnp.float32)
    for i in range(1, 4):
        total += jnp.dot(x_refs[i][...], w_buf[i], preferred_element_type=jnp.float32)
    return total


def partial_kernel(off_ref, *refs):
    x_refs, w_refs, (out_ref, w_buf, sems) = refs[:4], refs[4:11], refs[11:]

    @pl.when(pl.program_id(0) == 0)
    def _():
        pick_weights(off_ref, w_refs, w_buf, sems)

    out_ref[...] = product(x_refs, w_buf)


def project_kernel(ropes, off_ref, *refs):
    x_refs, w_refs = refs[:4], refs[4:11]
    part_ref, bias_ref, cos_ref, sin_ref, out_ref, w_buf, sems = refs[11:]

    @pl.when(pl.program_id(0) == 0)
    def _():
        pick_weights(off_ref, w_refs, w_buf, sems)

    total = product(x_refs, w_buf) + part_ref[...] + bias_ref[...]
    for c, rope in enumerate(ropes):
        part = total[:, c * HD : (c + 1) * HD]
        if rope:
            part = part * cos_ref[...] + pltpu.roll(part, HD // 2, 1) * sin_ref[...]
        out_ref[:, c * HD : (c + 1) * HD] = part.astype(out_ref.dtype)


def projection(off, x_blocks, places, finish=None):
    rows, feats = x_blocks[0].shape
    columns = places[0].shape[1]
    tile = min(512, rows)
    wide = pl.BlockSpec((tile, columns), lambda r, off: (r, 0))
    in_specs = [pl.BlockSpec((tile, feats), lambda r, off: (r, 0))] * 4
    in_specs += [pl.BlockSpec(memory_space=pl.ANY)] * 7
    operands = [*x_blocks, *places]
    body, out_type = partial_kernel, jnp.float32
    if finish is not None:
        ropes, *rest = finish
        table = pl.BlockSpec((tile, HD), lambda r, off: (r, 0))
        in_specs += [wide, pl.BlockSpec((1, columns), lambda r, off: (0, 0)), table, table]
        operands += rest
        body, out_type = functools.partial(project_kernel, ropes), jnp.bfloat16
    grid_spec = pltpu.PrefetchScalarGridSpec(
        num_scalar_prefetch=1,
        grid=(rows // tile,),
        in_specs=in_specs,
        out_specs=wide,
        scratch_shapes=[
            pltpu.VMEM((4, feats, columns), jnp.bfloat16),
            pltpu.SemaphoreType.DMA((4,)),
        ],
    )
    return pl.pallas_call(
        body,
        grid_spec=grid_spec,
        out_shape=jax.ShapeDtypeStruct((rows, columns), out_type),
        compiler_params=pltpu.CompilerParams(vmem_limit_bytes=32 * 2**20),
        cost_estimate=pl.CostEstimate(
            flops=8 * rows * feats * columns,
            bytes_accessed=8 * rows * feats + 8 * feats * columns + 4 * rows * columns,
            transcendentals=0,
        ),
    )(off, *operands)


def attend_kernel(heads, slot, window, start_ref, len_ref, q_ref, k_ref, v_ref, out_ref):
    which = pl.program_id(0)
    rows = q_ref.shape[0]
    start = start_ref[which]
    first = pl.multiple_of(jnp.minimum((start // 16) * 16, rows - window), 16)
    row_at = lax.broadcasted_iota(jnp.int32, (slot, window), 0)
    col_at = lax.broadcasted_iota(jnp.int32, (slot, window), 1)
    pick = jnp.where(
        (col_at == row_at + (start - first)) & (row_at < len_ref[which]), 1.0, 0.0
    ).astype(jnp.bfloat16)

    def picked(ref, lanes):
        rows_here = ref[pl.ds(first, window), lanes]
        return jnp.dot(pick, rows_here, preferred_element_type=jnp.float32).astype(jnp.bfloat16)

    key = picked(k_ref, pl.ds(0, HD))
    value = picked(v_ref, pl.ds(0, HD))
    causal = lax.broadcasted_iota(jnp.int32, (slot, slot), 1) <= lax.broadcasted_iota(
        jnp.int32, (slot, slot), 0
    )
    for h in range(heads):
        query = picked(q_ref, pl.ds(h * HD, HD))
        scores = lax.dot_general(
            query, key, (((1,), (1,)), ((), ())), preferred_element_type=jnp.float32
        )
        scores = jnp.where(causal, scores * HD ** (-0.5), mask_value)
        peak = jnp.max(scores, axis=-1, keepdims=True)
        raised = jnp.exp(scores - peak)
        weights = (raised / jnp.sum(raised, axis=-1, keepdims=True)).astype(jnp.bfloat16)
        context = jnp.dot(weights, value, preferred_element_type=jnp.float32)
        out_ref[0, :, h * HD : (h + 1) * HD] = context.astype(out_ref.dtype)


def attend(starts, lens, query, key, value, slot):
    rows, columns = query.shape
    count = starts.shape[0]
    window = min(rows, -(-(slot + 16) // 128) * 128)
    heads = columns // HD
    grid_spec = pltpu.PrefetchScalarGridSpec(
        num_scalar_prefetch=2,
        grid=(count,),
        in_specs=[
            pl.BlockSpec((rows, columns), lambda s, a, b: (0, 0)),
            pl.BlockSpec((rows, HD), lambda s, a, b: (0, 0)),
            pl.BlockSpec((rows, HD), lambda s, a, b: (0, 0)),
        ],
        out_specs=pl.BlockSpec((1, slot, columns), lambda s, a, b: (s, 0, 0)),
    )
    return pl.pallas_call(
        functools.partial(attend_kernel, heads, slot, window),
        grid_spec=grid_spec,
        out_shape=jax.ShapeDtypeStruct((count, slot, columns), jnp.bfloat16),
        compiler_params=pltpu.CompilerParams(vmem_limit_bytes=32 * 2**20),
        cost_estimate=pl.CostEstimate(
            flops=2 * count * slot * (2 * slot + window) * columns,
            bytes_accessed=2 * (rows * (columns + 2 * HD) + count * slot * columns),
            transcendentals=count * heads * slot * slot,
        ),
    )(starts, lens, query, key, value)


def place_kernel(count, slot, window, start_ref, len_ref, in_ref, out_ref, total):
    learner = pl.program_id(0)
    rows = total.shape[0]
    total[...] = jnp.zeros_like(total)
    row_at = lax.broadcasted_iota(jnp.int32, (window, slot), 0)
    col_at = lax.broadcasted_iota(jnp.int32, (window, slot), 1)
    for s in range(count):
        start = start_ref[learner, s]
        first = pl.multiple_of(jnp.minimum((start // 8) * 8, rows - window), 8)
        pick = jnp.where(
            (row_at == col_at + (start - first)) & (col_at < len_ref[learner, s]), 1.0, 0.0
        ).astype(jnp.bfloat16)
        total[pl.ds(first, window), :] += jnp.dot(
            pick, in_ref[s, 0], preferred_element_type=jnp.float32
        )
    out_ref[0] = total[...].astype(out_ref.dtype)


def place(starts, lens, slots, rows):
    count, learners, slot, columns = slots.shape
    window = min(rows, slot + 8)
    grid_spec = pltpu.PrefetchScalarGridSpec(
        num_scalar_prefetch=2,
        grid=(learners,),
        in_specs=[pl.BlockSpec((count, 1, slot, columns), lambda r, a, b: (0, r, 0, 0))],
        out_specs=pl.BlockSpec((1, rows, columns), lambda r, a, b: (r, 0, 0)),
        scratch_shapes=[pltpu.VMEM((rows, columns), jnp.float32)],
    )
    return pl.pallas_call(
        functools.partial(place_kernel, count, slot, window),
        grid_spec=grid_spec,
        out_shape=jax.ShapeDtypeStruct((learners, rows, columns), jnp.bfloat16),
        compiler_params=pltpu.CompilerParams(vmem_limit_bytes=32 * 2**20),
        cost_estimate=pl.CostEstimate(
            flops=2 * learners * count * slot * window * columns,
            bytes_accessed=2 * learners * columns * (count * slot + rows),
            transcendentals=0,
        ),
    )(starts, lens, slots)


def local_line(
    rollout_states,
    norm_gain,
    w_query,
    w_key,
    w_value,
    b_query,
    b_key,
    b_value,
    seq_lengths,
    seq_dest,
    seq_offset,
):
    learners = lax.axis_size("dp")
    line = learners // 2
    me = lax.axis_index("dp")
    z, x = me // 2, me % 2
    t = lax.axis_index("tensor")
    row_count, feature_count = rollout_states.shape
    slot = 2 * row_count // learners
    half = feature_count // 2
    middle = row_count // 2

    def after(array, *others):
        return lax.optimization_barrier((array, *others))[0]

    def swap_x(array):
        return lax.ppermute(array, "dp", [(i, i ^ 1) for i in range(learners)])

    def swap_y(array):
        return lax.ppermute(array, "tensor", [(i, i ^ 2) for i in range(4)])

    def swap_core(array):
        return lax.ppermute(array, "tensor", [(i, i ^ 1) for i in range(4)])

    def up(array, first):
        return lax.ppermute(array, "dp", [(i, i + 2) for i in range(2 * first, learners - 2)])

    def down(array, first):
        return lax.ppermute(array, "dp", [(i, i - 2) for i in range(2, learners - 2 * first)])

    chunks = [jnp.concatenate([w_key, w_value], axis=1)]
    edges = [0, 2, 4, 6, 7, 8]
    for low, high in zip(edges, edges[1:]):
        chunks.append(w_query[:, low * HD : high * HD])
    places, marks = [], []
    for c, own in enumerate(chunks):
        if c >= 2:
            own = after(own, *marks[c - 2][-1])
        ups, downs = [own], [own]
        for step in range(line - 1):
            ups.append(up(ups[-1], step))
            downs.append(down(downs[-1], step))
        places.append(ups[:0:-1] + downs)
        marks.append(list(zip(ups[1:], downs[1:])))

    widened = rollout_states.astype(jnp.float32)
    squares = jnp.sum(widened * widened, axis=-1)
    squares = squares + swap_core(squares)
    squares = squares + swap_y(squares)
    scale = lax.rsqrt(squares[:, None] / (4 * feature_count) + norm_eps)

    def normed(first):
        part = lax.dynamic_slice_in_dim(rollout_states, first, half, 1).astype(jnp.float32)
        gain = lax.dynamic_slice_in_dim(norm_gain, t * feature_count + first, half, 0)
        return (part * scale * gain[None, :]).astype(jnp.bfloat16)

    own, give = normed(x * half), normed((1 - x) * half)

    near_a = swap_x(give[:middle])
    own_a = swap_y(own[:middle])
    near_b = swap_x(after(give[middle:], near_a, *marks[0][0]))
    diag_a = swap_y(after(near_a, own_a, *marks[0][0]))
    near = jnp.concatenate([near_a, near_b], axis=0)
    diag_b = swap_y(after(near_b, diag_a, *marks[0][1]))
    own_b = swap_y(after(own[middle:], diag_b, *marks[1][1]))
    diag = jnp.concatenate([diag_a, diag_b], axis=0)
    own_y = jnp.concatenate([own_a, own_b], axis=0)
    own_x = [own, swap_core(own), own_y, swap_core(own_y)]
    near_x = [near, swap_core(near), diag, swap_core(diag)]
    off = jnp.stack([(t ^ i) - z for i in range(4)]).astype(jnp.int32)

    lengths = seq_lengths.reshape(learners, learners)
    dests = seq_dest.reshape(learners, learners)
    offsets = seq_offset.reshape(learners, learners)
    starts = jnp.cumsum(lengths, axis=1) - lengths
    peer_ids = jnp.arange(learners, dtype=jnp.int32)
    rows = jnp.arange(row_count, dtype=jnp.int32)
    length = lax.dynamic_index_in_dim(lengths, me, 0, keepdims=False)
    start = lax.dynamic_index_in_dim(starts, me, 0, keepdims=False)
    dest = lax.dynamic_index_in_dim(dests, me, 0, keepdims=False)
    match = (dest[None, :] == peer_ids[:, None]).astype(jnp.int32)
    send_start = jnp.sum(match * start[None, :], axis=1)
    send_length = jnp.sum(match * length[None, :], axis=1)
    inside = (rows[:, None] >= start[None, :]) & (rows[:, None] < (start + length)[None, :])
    position = rows - jnp.sum(inside.astype(jnp.int32) * start[None, :], axis=1)
    cosine, sine = rope_tables(position)
    cosine = jnp.concatenate([cosine, cosine], axis=1)
    sine = jnp.concatenate([-sine, sine], axis=1)
    matched = (dests == me).astype(jnp.int32)
    run_start = jnp.sum(matched * offsets, axis=1)[None, :]
    run_length = jnp.sum(matched * lengths, axis=1)[None, :]

    biases = [jnp.concatenate([b_key, b_value])]
    for low, high in zip(edges, edges[1:]):
        biases.append(b_query[low * HD : high * HD])
    parts = []
    for c, own_places in enumerate(places):
        near_blocks = near_x
        if parts:
            near_blocks = [after(near_x[0], parts[-1])] + near_x[1:]
        parts.append(projection(off, near_blocks, own_places))
    columns = []
    for c, own_places in enumerate(places):
        ropes = (True, False) if c == 0 else (True,) * (own_places[0].shape[1] // HD)
        got = swap_x(parts[c])
        rot = projection(
            off, own_x, own_places, (ropes, got, biases[c][None, :], cosine, sine)
        )
        if c == 0:
            key, value = rot[:, :HD], rot[:, HD:]
            continue
        outgoing = attend(send_start, send_length, rot, key, value, slot)
        incoming = lax.all_to_all(outgoing, "dp", split_axis=0, concat_axis=0, tiled=True)
        placed = place(run_start, run_length, incoming[:, None], row_count)
        columns.append(placed[0])
    return jnp.concatenate(columns, axis=1)


def solution(mesh):
    placed = (
        P("dp", "tensor"),
        P(),
        P("dp", "tensor"),
        P("dp", "tensor"),
        P("dp", "tensor"),
        P("tensor"),
        P("tensor"),
        P("tensor"),
        P(),
        P(),
        P(),
    )
    fits_line = mesh.shape["dp"] == 8 and mesh.shape["tensor"] == 4
    return jax.shard_map(
        local_line if fits_line else local_any,
        mesh=mesh,
        in_specs=placed,
        out_specs=P("dp", "tensor"),
        check_vma=False,
    )
```

```python
import functools

import jax
import jax.numpy as jnp
from jax import lax
from jax.experimental import pallas as pl
from jax.experimental.pallas import tpu as pltpu
from jax.sharding import PartitionSpec as P

HD = 128

rope_base = 1000000.0
norm_eps = 1e-06
mask_value = -1e30


def rope_tables(positions):
    half_dim = HD // 2
    frequency = rope_base ** (-(jnp.arange(half_dim).astype(jnp.float32) * 2.0 / HD))
    angles = positions.astype(jnp.float32)[:, None] * frequency[None, :]
    return (jnp.cos(angles), jnp.sin(angles))


def rotate(states, cosine, sine):
    half_dim = states.shape[-1] // 2
    first_half = states[..., :half_dim]
    second_half = states[..., half_dim:]
    cos_wide = cosine[:, None, :]
    sin_wide = sine[:, None, :]
    return jnp.concatenate(
        [
            first_half * cos_wide - second_half * sin_wide,
            second_half * cos_wide + first_half * sin_wide,
        ],
        axis=-1,
    )


def local_any(
    rollout_states,
    norm_gain,
    w_query,
    w_key,
    w_value,
    b_query,
    b_key,
    b_value,
    seq_lengths,
    seq_dest,
    seq_offset,
):
    learners = lax.axis_size("dp")
    own_index = lax.axis_index("dp")
    row_count, feature_count = rollout_states.shape
    capacity = 2 * row_count // learners - 1
    lengths = seq_lengths.reshape(learners, learners)
    dests = seq_dest.reshape(learners, learners)
    offsets = seq_offset.reshape(learners, learners)
    starts = jnp.cumsum(lengths, axis=1) - lengths
    peer_ids = jnp.arange(learners, dtype=jnp.int32)
    own_length = lax.dynamic_index_in_dim(lengths, own_index, 0, keepdims=False)
    own_start = lax.dynamic_index_in_dim(starts, own_index, 0, keepdims=False)
    own_dest = lax.dynamic_index_in_dim(dests, own_index, 0, keepdims=False)
    match_send = (own_dest[None, :] == peer_ids[:, None]).astype(jnp.int32)
    send_start = jnp.sum(match_send * own_start[None, :], axis=1)
    send_length = jnp.sum(match_send * own_length[None, :], axis=1)
    slot_index = jnp.arange(capacity, dtype=jnp.int32)
    pick_rows = send_start[:, None] + slot_index[None, :]
    padded = jnp.concatenate(
        [rollout_states, jnp.zeros((capacity, feature_count), rollout_states.dtype)], axis=0
    )
    live_slots = (slot_index[None, :] < send_length[:, None])[..., None]
    outgoing = jnp.where(
        live_slots, jnp.take(padded, pick_rows, axis=0), jnp.zeros((), rollout_states.dtype)
    )
    incoming = lax.all_to_all(outgoing, "dp", split_axis=0, concat_axis=0, tiled=True)
    matched = (dests == own_index).astype(jnp.int32)
    run_start = jnp.sum(matched * offsets, axis=1)
    run_length = jnp.sum(matched * lengths, axis=1)
    rows = jnp.arange(row_count, dtype=jnp.int32)
    inside = (
        (rows[:, None] >= run_start[None, :]) & (rows[:, None] < (run_start + run_length)[None, :])
    ).astype(jnp.int32)
    source_ids = jnp.sum(inside * peer_ids[None, :], axis=1)
    within_seq = rows - jnp.sum(inside * run_start[None, :], axis=1)
    arrived = jnp.take(
        incoming.reshape(learners * capacity, feature_count),
        source_ids * capacity + within_seq,
        axis=0,
    )
    gathered = lax.all_gather(arrived, "tensor", axis=1, tiled=True)
    widened = gathered.astype(jnp.float32)
    statistic = jnp.mean(widened * widened, axis=-1, keepdims=True)
    normed = (widened * lax.rsqrt(statistic + norm_eps) * norm_gain[None, :]).astype(jnp.bfloat16)
    full_query, full_key, full_value = (
        lax.all_gather(w_query, "dp", axis=0, tiled=True),
        lax.all_gather(w_key, "dp", axis=0, tiled=True),
        lax.all_gather(w_value, "dp", axis=0, tiled=True),
    )
    query = jnp.dot(normed, full_query, preferred_element_type=jnp.float32)
    key = jnp.dot(normed, full_key, preferred_element_type=jnp.float32)
    value = jnp.dot(normed, full_value, preferred_element_type=jnp.float32)
    query = query + b_query[None, :]
    key = key + b_key[None, :]
    value = value + b_value[None, :]
    heads_here = query.shape[1] // HD
    kv_here = key.shape[1] // HD
    group = heads_here // kv_here
    cosine, sine = rope_tables(within_seq)
    rot_query = rotate(query.reshape(row_count, heads_here, HD), cosine, sine).astype(jnp.bfloat16)
    rot_query = rot_query.reshape(row_count, kv_here, group, HD)
    rot_key = rotate(key.reshape(row_count, kv_here, HD), cosine, sine).astype(jnp.bfloat16)
    value_bf = value.reshape(row_count, kv_here, HD).astype(jnp.bfloat16)
    block_rows = min(512, row_count)

    def one_block(block_number):
        first_row = block_number * block_rows
        query_block = lax.dynamic_slice_in_dim(rot_query, first_row, block_rows, 0)
        query_source = lax.dynamic_slice_in_dim(source_ids, first_row, block_rows, 0)
        query_rows = first_row + jnp.arange(block_rows, dtype=jnp.int32)
        scores = jnp.einsum(
            "bcgd,kcd->cgbk", query_block, rot_key, preferred_element_type=jnp.float32
        )
        scores = scores * HD ** (-0.5)
        allowed = (source_ids[None, :] == query_source[:, None]) & (
            rows[None, :] <= query_rows[:, None]
        )
        scores = jnp.where(allowed[None, None], scores, mask_value)
        peak = jnp.max(scores, axis=-1, keepdims=True)
        raised = jnp.exp(scores - peak)
        weights = (raised / jnp.sum(raised, axis=-1, keepdims=True)).astype(jnp.bfloat16)
        context = jnp.einsum(
            "cgbk,kcd->bcgd", weights, value_bf, preferred_element_type=jnp.float32
        )
        return context.astype(jnp.bfloat16).reshape(block_rows, heads_here * HD)

    outputs = lax.map(one_block, jnp.arange(row_count // block_rows, dtype=jnp.int32))
    return outputs.reshape(row_count, heads_here * HD)


def start_pieces(pieces, buf, sems):
    copies, first = [], 0
    for n, piece in enumerate(pieces):
        rows = piece.shape[0]
        copies.append(pltpu.make_async_copy(piece, buf.at[pl.ds(first, rows)], sems.at[n]))
        copies[-1].start()
        first += rows
    return copies


def product_kernel(counts, ropes, off_ref, *refs):
    refs = list(refs)
    x_refs = [[refs.pop(0) for _ in range(n)] for n in counts[:4]]
    w_refs = [refs.pop(0) for _ in range(7)]
    part_refs = [refs.pop(0) for _ in range(counts[4])]
    if ropes:
        bias_ref, cos_ref, sin_ref = (refs.pop(0) for _ in range(3))
        out_ref, x_buf, w_buf, x_sems, w_sems, total, part_buf, cos_buf, sin_buf, sems = refs
    else:
        out_ref, x_buf, w_buf, x_sems, w_sems = refs
        total = out_ref
    rows = x_buf.shape[1]
    tile = min(256, rows)

    copies = []
    for i in range(4):
        for spot in range(7):

            @pl.when(off_ref[i] == spot - 3)
            def _(i=i, spot=spot):
                pltpu.make_async_copy(w_refs[spot], w_buf.at[i], w_sems.at[i]).start()

        copies.append(start_pieces(x_refs[i], x_buf.at[i], x_sems.at[i]))
    if ropes:
        late = start_pieces(part_refs, part_buf, sems)
        late.append(pltpu.make_async_copy(cos_ref, cos_buf, sems.at[2]))
        late[-1].start()
        late.append(pltpu.make_async_copy(sin_ref, sin_buf, sems.at[3]))
        late[-1].start()

    for i in range(4):
        pltpu.make_async_copy(w_refs[0], w_buf.at[i], w_sems.at[i]).wait()
        for copy in copies[i]:
            copy.wait()
        if ropes and i == 3:
            for copy in late:
                copy.wait()

        @pl.loop(0, rows // tile)
        def _(r, i=i):
            here = pl.ds(pl.multiple_of(r * tile, tile), tile)
            term = jnp.dot(x_buf[i, here, :], w_buf[i], preferred_element_type=jnp.float32)
            if i > 0:
                term = total[here, :] + term
            if not ropes or i < 3:
                total[here, :] = term
                return
            term = term + part_buf[here, :] + bias_ref[...]
            for c, rope in enumerate(ropes):
                head = term[:, c * HD : (c + 1) * HD]
                if rope:
                    head = head * cos_buf[here, :] + pltpu.roll(head, HD // 2, 1) * sin_buf[here, :]
                out_ref[here, c * HD : (c + 1) * HD] = head.astype(out_ref.dtype)


def projection(off, x_blocks, places, finish=None):
    rows = sum(piece.shape[0] for piece in x_blocks[0])
    feats, columns = places[0].shape
    counts = [len(pieces) for pieces in x_blocks]
    operands = [piece for pieces in x_blocks for piece in pieces] + list(places)
    anywhere = pl.BlockSpec(memory_space=pl.ANY)
    in_specs = [anywhere] * len(operands)
    scratch = [
        pltpu.VMEM((4, rows, feats), jnp.bfloat16),
        pltpu.VMEM((4, feats, columns), jnp.bfloat16),
        pltpu.SemaphoreType.DMA((4, 2)),
        pltpu.SemaphoreType.DMA((4,)),
    ]
    ropes, out_type = None, jnp.float32
    if finish is None:
        counts.append(0)
    else:
        ropes, parts, bias, cosine, sine = finish
        counts.append(len(parts))
        operands += [*parts, bias, cosine, sine]
        in_specs += [anywhere] * len(parts)
        in_specs += [pl.BlockSpec(memory_space=pltpu.VMEM), anywhere, anywhere]
        scratch += [
            pltpu.VMEM((rows, columns), jnp.float32),
            pltpu.VMEM((rows, columns), jnp.float32),
            pltpu.VMEM((rows, HD), jnp.float32),
            pltpu.VMEM((rows, HD), jnp.float32),
            pltpu.SemaphoreType.DMA((4,)),
        ]
        out_type = jnp.bfloat16
    return pl.pallas_call(
        functools.partial(product_kernel, tuple(counts), ropes),
        in_specs=[pl.BlockSpec(memory_space=pltpu.SMEM)] + in_specs,
        out_specs=pl.BlockSpec(memory_space=pltpu.VMEM),
        scratch_shapes=scratch,
        out_shape=jax.ShapeDtypeStruct((rows, columns), out_type),
        compiler_params=pltpu.CompilerParams(vmem_limit_bytes=56 * 2**20),
        cost_estimate=pl.CostEstimate(
            flops=8 * rows * feats * columns,
            bytes_accessed=8 * rows * feats + 8 * feats * columns + 4 * rows * columns,
            transcendentals=0,
        ),
    )(off, *operands)


def pick_rows(start, length, slot, window, ref):
    first = pl.multiple_of(jnp.minimum((start // 16) * 16, ref.shape[0] - window), 16)
    row_at = lax.broadcasted_iota(jnp.int32, (slot, window), 0)
    col_at = lax.broadcasted_iota(jnp.int32, (slot, window), 1)
    pick = jnp.where((col_at == row_at + (start - first)) & (row_at < length), 1.0, 0.0)
    rows = jnp.dot(
        pick.astype(jnp.bfloat16), ref[pl.ds(first, window), :], preferred_element_type=jnp.float32
    )
    return rows.astype(jnp.bfloat16)


def slots_kernel(slot, window, start_ref, len_ref, in_ref, out_ref):
    for s in range(out_ref.shape[0]):
        out_ref[s] = pick_rows(start_ref[s], len_ref[s], slot, window, in_ref)


def to_slots(starts, lens, array, slot, window):
    count, columns = starts.shape[0], array.shape[1]
    scalars = pl.BlockSpec(memory_space=pltpu.SMEM)
    vmem = pl.BlockSpec(memory_space=pltpu.VMEM)
    return pl.pallas_call(
        functools.partial(slots_kernel, slot, window),
        in_specs=[scalars, scalars, vmem],
        out_specs=vmem,
        out_shape=jax.ShapeDtypeStruct((count, slot, columns), jnp.bfloat16),
        compiler_params=pltpu.CompilerParams(vmem_limit_bytes=56 * 2**20),
        cost_estimate=pl.CostEstimate(
            flops=2 * count * slot * window * columns,
            bytes_accessed=2 * columns * (array.shape[0] + count * slot),
            transcendentals=0,
        ),
    )(starts, lens, array)


def attend_kernel(heads, window, start_ref, len_ref, q_ref, kv_ref, out_ref):
    batch, slot = out_ref.shape[:2]
    half = slot // 2
    group = pl.program_id(0) * batch
    for s in range(batch):
        query = pick_rows(start_ref[group + s], len_ref[group + s], slot, window, q_ref)
        for block in range(2):
            width = (block + 1) * half
            stacked = jnp.concatenate(
                [
                    query[block * half : width, h * HD : (h + 1) * HD]
                    for h in range(heads)
                ],
                axis=0,
            )
            scores = lax.dot_general(
                stacked,
                kv_ref[s, :width, :HD],
                (((1,), (1,)), ((), ())),
                preferred_element_type=jnp.float32,
            )
            row_at = lax.broadcasted_iota(jnp.int32, scores.shape, 0) & (half - 1)
            col_at = lax.broadcasted_iota(jnp.int32, scores.shape, 1)
            scores = jnp.where(
                col_at <= row_at + block * half, scores * HD ** (-0.5), mask_value
            )
            peak = jnp.max(scores, axis=-1, keepdims=True)
            raised = jnp.exp(scores - peak)
            weights = raised * (1.0 / jnp.sum(raised, axis=-1, keepdims=True))
            context = jnp.dot(
                weights.astype(jnp.bfloat16), kv_ref[s, :width, HD:], preferred_element_type=jnp.float32
            ).astype(out_ref.dtype)
            for h in range(heads):
                out_ref[s, block * half : width, h * HD : (h + 1) * HD] = context[
                    h * half : (h + 1) * half
                ]


def attend(starts, lens, query, kv_slots, window):
    rows, columns = query.shape
    count, slot = kv_slots.shape[:2]
    batch = 2
    heads = columns // HD
    grid_spec = pltpu.PrefetchScalarGridSpec(
        num_scalar_prefetch=2,
        grid=(count // batch,),
        in_specs=[
            pl.BlockSpec((rows, columns), lambda s, a, b: (0, 0)),
            pl.BlockSpec((batch, slot, 2 * HD), lambda s, a, b: (s, 0, 0)),
        ],
        out_specs=pl.BlockSpec((batch, slot, columns), lambda s, a, b: (s, 0, 0)),
    )
    return pl.pallas_call(
        functools.partial(attend_kernel, heads, window),
        grid_spec=grid_spec,
        out_shape=jax.ShapeDtypeStruct((count, slot, columns), jnp.bfloat16),
        compiler_params=pltpu.CompilerParams(vmem_limit_bytes=56 * 2**20),
        cost_estimate=pl.CostEstimate(
            flops=2 * count * slot * (2 * slot + window) * columns,
            bytes_accessed=2 * (rows * columns + 2 * count * slot * columns),
            transcendentals=count * heads * slot * slot,
        ),
    )(starts, lens, query, kv_slots)


def place_kernel(count, slot, window, start_ref, len_ref, in_ref, out_ref, total):
    learner = pl.program_id(0)
    rows = total.shape[0]
    total[...] = jnp.zeros_like(total)
    row_at = lax.broadcasted_iota(jnp.int32, (window, slot), 0)
    col_at = lax.broadcasted_iota(jnp.int32, (window, slot), 1)
    for s in range(count):
        start = start_ref[learner, s]
        first = pl.multiple_of(jnp.minimum((start // 8) * 8, rows - window), 8)
        pick = jnp.where(
            (row_at == col_at + (start - first)) & (col_at < len_ref[learner, s]), 1.0, 0.0
        ).astype(jnp.bfloat16)
        total[pl.ds(first, window), :] += jnp.dot(
            pick, in_ref[s, 0], preferred_element_type=jnp.float32
        )
    out_ref[0] = total[...].astype(out_ref.dtype)


def place(starts, lens, slots, rows):
    count, learners, slot, columns = slots.shape
    window = min(rows, slot + 8)
    grid_spec = pltpu.PrefetchScalarGridSpec(
        num_scalar_prefetch=2,
        grid=(learners,),
        in_specs=[pl.BlockSpec((count, 1, slot, columns), lambda r, a, b: (0, r, 0, 0))],
        out_specs=pl.BlockSpec((1, rows, columns), lambda r, a, b: (r, 0, 0)),
        scratch_shapes=[pltpu.VMEM((rows, columns), jnp.float32)],
    )
    return pl.pallas_call(
        functools.partial(place_kernel, count, slot, window),
        grid_spec=grid_spec,
        out_shape=jax.ShapeDtypeStruct((learners, rows, columns), jnp.bfloat16),
        compiler_params=pltpu.CompilerParams(vmem_limit_bytes=56 * 2**20),
        cost_estimate=pl.CostEstimate(
            flops=2 * learners * count * slot * window * columns,
            bytes_accessed=2 * learners * columns * (count * slot + rows),
            transcendentals=0,
        ),
    )(starts, lens, slots)


def local_line(
    rollout_states,
    norm_gain,
    w_query,
    w_key,
    w_value,
    b_query,
    b_key,
    b_value,
    seq_lengths,
    seq_dest,
    seq_offset,
):
    learners = lax.axis_size("dp")
    line = learners // 2
    me = lax.axis_index("dp")
    z, x = me // 2, me % 2
    t = lax.axis_index("tensor")
    row_count, feature_count = rollout_states.shape
    slot = 2 * row_count // learners
    half = feature_count // 2
    middle = row_count // 2

    def after(array, *others):
        return lax.optimization_barrier((array, *others))[0]

    def swap_x(array):
        return lax.ppermute(array, "dp", [(i, i ^ 1) for i in range(learners)])

    def swap_y(array):
        return lax.ppermute(array, "tensor", [(i, i ^ 2) for i in range(4)])

    def swap_core(array):
        return lax.ppermute(array, "tensor", [(i, i ^ 1) for i in range(4)])

    def up(array, first):
        return lax.ppermute(array, "dp", [(i, i + 2) for i in range(2 * first, learners - 2)])

    def down(array, first):
        return lax.ppermute(array, "dp", [(i, i - 2) for i in range(2, learners - 2 * first)])

    chunks = [jnp.concatenate([w_key, w_value], axis=1)]
    edges = [0, 2, 4, 6, 7, 8]
    for low, high in zip(edges, edges[1:]):
        chunks.append(w_query[:, low * HD : high * HD])
    places, marks = [], []
    for c, own in enumerate(chunks):
        if c >= 2:
            own = after(own, *marks[c - 2][-1])
        ups, downs = [own], [own]
        for step in range(line - 1):
            ups.append(up(ups[-1], step))
            downs.append(down(downs[-1], step))
        places.append(ups[:0:-1] + downs)
        marks.append(list(zip(ups[1:], downs[1:])))

    states = after(rollout_states, *chunks[:2])
    widened = states.astype(jnp.float32)
    squares = jnp.sum(widened * widened, axis=-1)
    squares = squares + swap_core(squares)
    squares = squares + swap_y(squares)
    scale = lax.rsqrt(squares[:, None] / (4 * feature_count) + norm_eps)

    def normed(first):
        part = lax.dynamic_slice_in_dim(states, first, half, 1).astype(jnp.float32)
        gain = lax.dynamic_slice_in_dim(norm_gain, t * feature_count + first, half, 0)
        return (part * scale * gain[None, :]).astype(jnp.bfloat16)

    own, give = normed(x * half), normed((1 - x) * half)

    near_a = swap_x(give[:middle])
    own_a = swap_y(own[:middle])
    near_b = swap_x(after(give[middle:], near_a, *marks[0][0]))
    diag_a = swap_y(after(near_a, own_a, *marks[0][0]))
    own_a_core = swap_core(after(own_a, near_a))
    own_core = swap_core(own)
    diag_b = swap_y(after(near_b, diag_a, *marks[0][1]))
    near_a_core = swap_core(after(near_a, near_b, *marks[0][1]))
    near_b_core = swap_core(after(near_b, diag_a, *marks[0][1]))
    diag_a_core = swap_core(diag_a)
    diag_b_core = swap_core(diag_b)
    own_b = swap_y(after(own[middle:], diag_b, *marks[1][2]))
    own_b_core = swap_core(own_b)
    own_x = [[own], [own_core], [own_a, own_b], [own_a_core, own_b_core]]
    near_ax = [[near_a], [near_a_core], [diag_a], [diag_a_core]]
    near_bx = [[near_b], [near_b_core], [diag_b], [diag_b_core]]
    near_x = [a + b for a, b in zip(near_ax, near_bx)]
    off = jnp.stack([(t ^ i) - z for i in range(4)]).astype(jnp.int32)

    lengths = seq_lengths.reshape(learners, learners)
    dests = seq_dest.reshape(learners, learners)
    offsets = seq_offset.reshape(learners, learners)
    starts = jnp.cumsum(lengths, axis=1) - lengths
    peer_ids = jnp.arange(learners, dtype=jnp.int32)
    rows = jnp.arange(row_count, dtype=jnp.int32)
    length = lax.dynamic_index_in_dim(lengths, me, 0, keepdims=False)
    start = lax.dynamic_index_in_dim(starts, me, 0, keepdims=False)
    dest = lax.dynamic_index_in_dim(dests, me, 0, keepdims=False)
    match = (dest[None, :] == peer_ids[:, None]).astype(jnp.int32)
    send_start = jnp.sum(match * start[None, :], axis=1)
    send_length = jnp.sum(match * length[None, :], axis=1)
    inside = (rows[:, None] >= start[None, :]) & (rows[:, None] < (start + length)[None, :])
    position = rows - jnp.sum(inside.astype(jnp.int32) * start[None, :], axis=1)
    cosine, sine = rope_tables(position)
    cosine = jnp.concatenate([cosine, cosine], axis=1)
    sine = jnp.concatenate([-sine, sine], axis=1)
    matched = (dests == me).astype(jnp.int32)
    run_start = jnp.sum(matched * offsets, axis=1)[None, :]
    run_length = jnp.sum(matched * lengths, axis=1)[None, :]

    biases = [jnp.concatenate([b_key, b_value])]
    for low, high in zip(edges, edges[1:]):
        biases.append(b_query[low * HD : high * HD])
    window = min(row_count, -(-(slot + 16) // 128) * 128)

    def partial(c, blocks, *others):
        return projection(after(off, *others), blocks, places[c])

    def finish(c, got, *others):
        ropes = (True, False) if c == 0 else (True,) * (places[c][0].shape[1] // HD)
        ending = (ropes, got, biases[c][None, :], cosine, sine)
        return projection(after(off, *others), own_x, places[c], ending)

    def heads_of(c, got, *others):
        rot = finish(c, got, *others)
        return attend(send_start, send_length, rot, kv_slots, window)

    def send(outgoing):
        return lax.all_to_all(outgoing, "dp", split_axis=0, concat_axis=0, tiled=True)

    def receive(incoming, *others):
        return place(after(run_start, *others), run_length, incoming[:, None], row_count)[0]

    part_a = partial(0, near_ax)
    got_a = swap_x(part_a)
    part_b = partial(0, near_bx, part_a, *marks[2][0])
    got_b = swap_x(after(part_b, got_a))
    parts = [None, partial(1, near_x, part_b)]
    got = [None, swap_x(after(parts[1], got_b))]
    kv = finish(0, [got_a, got_b], parts[1], *marks[2][1])
    kv_slots = to_slots(send_start, send_length, kv, slot, window)
    parts.append(partial(2, near_x, kv_slots))
    out, incoming, columns = [None], [None], []
    for c in range(1, len(places)):
        if c + 1 < len(places):
            got.append(swap_x(after(parts[c + 1], got[c])))
        ties = marks[c + 2][1] if c + 2 < len(places) else ()
        out.append(heads_of(c, [got[c]], parts[-1], *ties))
        incoming.append(send(out[c]))
        if c + 2 < len(places):
            parts.append(partial(c + 2, near_x, out[c]))
        if c >= 2:
            columns.append(receive(incoming[c - 1], out[c]))
    columns.append(receive(incoming[-1]))
    return jnp.concatenate(columns, axis=1)


def solution(mesh):
    placed = (
        P("dp", "tensor"),
        P(),
        P("dp", "tensor"),
        P("dp", "tensor"),
        P("dp", "tensor"),
        P("tensor"),
        P("tensor"),
        P("tensor"),
        P(),
        P(),
        P(),
    )
    fits_line = mesh.shape["dp"] == 8 and mesh.shape["tensor"] == 4
    return jax.shard_map(
        local_line if fits_line else local_any,
        mesh=mesh,
        in_specs=placed,
        out_specs=P("dp", "tensor"),
        check_vma=False,
    )
```

```python
import functools

import jax
import jax.numpy as jnp
from jax import lax
from jax.experimental import pallas as pl
from jax.experimental.pallas import tpu as pltpu
from jax.sharding import PartitionSpec as P

HD = 128

rope_base = 1000000.0
norm_eps = 1e-06
mask_value = -1e30


def rope_tables(positions):
    half_dim = HD // 2
    frequency = rope_base ** (-(jnp.arange(half_dim).astype(jnp.float32) * 2.0 / HD))
    angles = positions.astype(jnp.float32)[:, None] * frequency[None, :]
    return (jnp.cos(angles), jnp.sin(angles))


def rotate(states, cosine, sine):
    half_dim = states.shape[-1] // 2
    first_half = states[..., :half_dim]
    second_half = states[..., half_dim:]
    cos_wide = cosine[:, None, :]
    sin_wide = sine[:, None, :]
    return jnp.concatenate(
        [
            first_half * cos_wide - second_half * sin_wide,
            second_half * cos_wide + first_half * sin_wide,
        ],
        axis=-1,
    )


def local_any(
    rollout_states,
    norm_gain,
    w_query,
    w_key,
    w_value,
    b_query,
    b_key,
    b_value,
    seq_lengths,
    seq_dest,
    seq_offset,
):
    learners = lax.axis_size("dp")
    own_index = lax.axis_index("dp")
    row_count, feature_count = rollout_states.shape
    capacity = 2 * row_count // learners - 1
    lengths = seq_lengths.reshape(learners, learners)
    dests = seq_dest.reshape(learners, learners)
    offsets = seq_offset.reshape(learners, learners)
    starts = jnp.cumsum(lengths, axis=1) - lengths
    peer_ids = jnp.arange(learners, dtype=jnp.int32)
    own_length = lax.dynamic_index_in_dim(lengths, own_index, 0, keepdims=False)
    own_start = lax.dynamic_index_in_dim(starts, own_index, 0, keepdims=False)
    own_dest = lax.dynamic_index_in_dim(dests, own_index, 0, keepdims=False)
    match_send = (own_dest[None, :] == peer_ids[:, None]).astype(jnp.int32)
    send_start = jnp.sum(match_send * own_start[None, :], axis=1)
    send_length = jnp.sum(match_send * own_length[None, :], axis=1)
    slot_index = jnp.arange(capacity, dtype=jnp.int32)
    pick_rows = send_start[:, None] + slot_index[None, :]
    padded = jnp.concatenate(
        [rollout_states, jnp.zeros((capacity, feature_count), rollout_states.dtype)], axis=0
    )
    live_slots = (slot_index[None, :] < send_length[:, None])[..., None]
    outgoing = jnp.where(
        live_slots, jnp.take(padded, pick_rows, axis=0), jnp.zeros((), rollout_states.dtype)
    )
    incoming = lax.all_to_all(outgoing, "dp", split_axis=0, concat_axis=0, tiled=True)
    matched = (dests == own_index).astype(jnp.int32)
    run_start = jnp.sum(matched * offsets, axis=1)
    run_length = jnp.sum(matched * lengths, axis=1)
    rows = jnp.arange(row_count, dtype=jnp.int32)
    inside = (
        (rows[:, None] >= run_start[None, :]) & (rows[:, None] < (run_start + run_length)[None, :])
    ).astype(jnp.int32)
    source_ids = jnp.sum(inside * peer_ids[None, :], axis=1)
    within_seq = rows - jnp.sum(inside * run_start[None, :], axis=1)
    arrived = jnp.take(
        incoming.reshape(learners * capacity, feature_count),
        source_ids * capacity + within_seq,
        axis=0,
    )
    gathered = lax.all_gather(arrived, "tensor", axis=1, tiled=True)
    widened = gathered.astype(jnp.float32)
    statistic = jnp.mean(widened * widened, axis=-1, keepdims=True)
    normed = (widened * lax.rsqrt(statistic + norm_eps) * norm_gain[None, :]).astype(jnp.bfloat16)
    full_query, full_key, full_value = (
        lax.all_gather(w_query, "dp", axis=0, tiled=True),
        lax.all_gather(w_key, "dp", axis=0, tiled=True),
        lax.all_gather(w_value, "dp", axis=0, tiled=True),
    )
    query = jnp.dot(normed, full_query, preferred_element_type=jnp.float32)
    key = jnp.dot(normed, full_key, preferred_element_type=jnp.float32)
    value = jnp.dot(normed, full_value, preferred_element_type=jnp.float32)
    query = query + b_query[None, :]
    key = key + b_key[None, :]
    value = value + b_value[None, :]
    heads_here = query.shape[1] // HD
    kv_here = key.shape[1] // HD
    group = heads_here // kv_here
    cosine, sine = rope_tables(within_seq)
    rot_query = rotate(query.reshape(row_count, heads_here, HD), cosine, sine).astype(jnp.bfloat16)
    rot_query = rot_query.reshape(row_count, kv_here, group, HD)
    rot_key = rotate(key.reshape(row_count, kv_here, HD), cosine, sine).astype(jnp.bfloat16)
    value_bf = value.reshape(row_count, kv_here, HD).astype(jnp.bfloat16)
    block_rows = min(512, row_count)

    def one_block(block_number):
        first_row = block_number * block_rows
        query_block = lax.dynamic_slice_in_dim(rot_query, first_row, block_rows, 0)
        query_source = lax.dynamic_slice_in_dim(source_ids, first_row, block_rows, 0)
        query_rows = first_row + jnp.arange(block_rows, dtype=jnp.int32)
        scores = jnp.einsum(
            "bcgd,kcd->cgbk", query_block, rot_key, preferred_element_type=jnp.float32
        )
        scores = scores * HD ** (-0.5)
        allowed = (source_ids[None, :] == query_source[:, None]) & (
            rows[None, :] <= query_rows[:, None]
        )
        scores = jnp.where(allowed[None, None], scores, mask_value)
        peak = jnp.max(scores, axis=-1, keepdims=True)
        raised = jnp.exp(scores - peak)
        weights = (raised / jnp.sum(raised, axis=-1, keepdims=True)).astype(jnp.bfloat16)
        context = jnp.einsum(
            "cgbk,kcd->bcgd", weights, value_bf, preferred_element_type=jnp.float32
        )
        return context.astype(jnp.bfloat16).reshape(block_rows, heads_here * HD)

    outputs = lax.map(one_block, jnp.arange(row_count // block_rows, dtype=jnp.int32))
    return outputs.reshape(row_count, heads_here * HD)


def product_kernel(counts, widths, ropes, off_ref, *refs):
    refs = list(refs)
    x_refs = [[refs.pop(0) for _ in range(n)] for n in counts[:4]]
    w_refs = [[refs.pop(0) for _ in range(7)] for _ in widths]
    part_refs = [refs.pop(0) for _ in range(counts[4])]
    if ropes:
        bias_ref, cos_ref, sin_ref = (refs.pop(0) for _ in range(3))
    out_ref, w_buf, sems = refs
    rows = out_ref.shape[0]
    tile = rows // max(counts)

    def lanes(p):
        return pl.ds(sum(widths[:p]), widths[p])

    for i in range(4):
        for p, spots in enumerate(w_refs):
            for spot in range(7):

                @pl.when(off_ref[i] == spot - 3)
                def _(i=i, p=p, spot=spot, spots=spots):
                    pltpu.make_async_copy(
                        spots[spot], w_buf.at[i, :, lanes(p)], sems.at[i, p]
                    ).start()

    def piece_rows(pieces, first):
        size = pieces[0].shape[0]
        return pieces[first // size], pl.ds(first % size, tile)

    for first in range(0, rows, tile):
        here = pl.ds(first, tile)
        term = None
        for i in range(4):
            if first == 0:
                for p, spots in enumerate(w_refs):
                    pltpu.make_async_copy(
                        spots[0], w_buf.at[i, :, lanes(p)], sems.at[i, p]
                    ).wait()
            ref, at = piece_rows(x_refs[i], first)
            dot = jnp.dot(ref[at, :], w_buf[i], preferred_element_type=jnp.float32)
            term = dot if term is None else term + dot
        if not ropes:
            out_ref[here, :] = term.astype(out_ref.dtype)
            continue
        ref, at = piece_rows(part_refs, first)
        term = term + ref[at, :].astype(jnp.float32) + bias_ref[...]
        for c, rope in enumerate(ropes):
            head = term[:, c * HD : (c + 1) * HD]
            if rope:
                head = head * cos_ref[here, :] + pltpu.roll(head, HD // 2, 1) * sin_ref[here, :]
            out_ref[here, c * HD : (c + 1) * HD] = head.astype(out_ref.dtype)


def keep(array):
    return pltpu.with_memory_space_constraint(array, pltpu.VMEM)


def projection(off, x_blocks, places, finish=None):
    rows = sum(piece.shape[0] for piece in x_blocks[0])
    feats = x_blocks[0][0].shape[1]
    widths = tuple(spots[0].shape[1] for spots in places)
    columns = sum(widths)
    counts = [len(pieces) for pieces in x_blocks]
    vmem = pl.BlockSpec(memory_space=pltpu.VMEM)
    operands = [keep(piece) for pieces in x_blocks for piece in pieces]
    in_specs = [vmem] * len(operands)
    operands += [spot for spots in places for spot in spots]
    in_specs += [pl.BlockSpec(memory_space=pl.ANY)] * (7 * len(places))
    ropes, out_type = None, jnp.float32
    if finish is None:
        counts.append(0)
    else:
        ropes, parts, bias, cosine, sine = finish
        counts.append(len(parts))
        operands += [keep(part) for part in parts]
        operands += [bias, keep(cosine), keep(sine)]
        in_specs += [vmem] * (len(parts) + 3)
        out_type = jnp.bfloat16
    return pl.pallas_call(
        functools.partial(product_kernel, tuple(counts), widths, ropes),
        in_specs=[pl.BlockSpec(memory_space=pltpu.SMEM)] + in_specs,
        out_specs=vmem,
        scratch_shapes=[
            pltpu.VMEM((4, feats, columns), jnp.bfloat16),
            pltpu.SemaphoreType.DMA((4, len(places))),
        ],
        out_shape=jax.ShapeDtypeStruct((rows, columns), out_type),
        compiler_params=pltpu.CompilerParams(vmem_limit_bytes=16 * 2**20),
        cost_estimate=pl.CostEstimate(
            flops=8 * rows * feats * columns,
            bytes_accessed=8 * feats * columns + 4 * rows * columns,
            transcendentals=0,
        ),
    )(off, *operands)


def pick_rows(start, length, slot, window, ref):
    first = pl.multiple_of(jnp.minimum((start // 16) * 16, ref.shape[0] - window), 16)
    row_at = lax.broadcasted_iota(jnp.int32, (slot, window), 0)
    col_at = lax.broadcasted_iota(jnp.int32, (slot, window), 1)
    pick = jnp.where((col_at == row_at + (start - first)) & (row_at < length), 1.0, 0.0)
    rows = jnp.dot(
        pick.astype(jnp.bfloat16), ref[pl.ds(first, window), :], preferred_element_type=jnp.float32
    )
    return rows.astype(jnp.bfloat16)


def slots_kernel(slot, window, start_ref, len_ref, in_ref, out_ref):
    for s in range(out_ref.shape[0]):
        out_ref[s] = pick_rows(start_ref[s], len_ref[s], slot, window, in_ref)


def to_slots(starts, lens, array, slot, window):
    count, columns = starts.shape[0], array.shape[1]
    scalars = pl.BlockSpec(memory_space=pltpu.SMEM)
    vmem = pl.BlockSpec(memory_space=pltpu.VMEM)
    return pl.pallas_call(
        functools.partial(slots_kernel, slot, window),
        in_specs=[scalars, scalars, vmem],
        out_specs=vmem,
        out_shape=jax.ShapeDtypeStruct((count, slot, columns), jnp.bfloat16),
        compiler_params=pltpu.CompilerParams(vmem_limit_bytes=16 * 2**20),
        cost_estimate=pl.CostEstimate(
            flops=2 * count * slot * window * columns,
            bytes_accessed=2 * columns * (array.shape[0] + count * slot),
            transcendentals=0,
        ),
    )(starts, lens, array)


def attend_kernel(heads, window, start_ref, len_ref, q_ref, kv_ref, out_ref):
    batch, slot = out_ref.shape[:2]
    half = slot // 2
    group = pl.program_id(0) * batch
    for s in range(batch):
        query = pick_rows(start_ref[group + s], len_ref[group + s], slot, window, q_ref)
        for block in range(2):
            width = (block + 1) * half
            stacked = jnp.concatenate(
                [
                    query[block * half : width, h * HD : (h + 1) * HD]
                    for h in range(heads)
                ],
                axis=0,
            )
            scores = lax.dot_general(
                stacked,
                kv_ref[s, :width, :HD],
                (((1,), (1,)), ((), ())),
                preferred_element_type=jnp.float32,
            )
            row_at = lax.broadcasted_iota(jnp.int32, scores.shape, 0) & (half - 1)
            col_at = lax.broadcasted_iota(jnp.int32, scores.shape, 1)
            scores = jnp.where(
                col_at <= row_at + block * half, scores * HD ** (-0.5), mask_value
            )
            peak = jnp.max(scores, axis=-1, keepdims=True)
            raised = jnp.exp(scores - peak)
            weights = raised * (1.0 / jnp.sum(raised, axis=-1, keepdims=True))
            context = jnp.dot(
                weights.astype(jnp.bfloat16), kv_ref[s, :width, HD:], preferred_element_type=jnp.float32
            ).astype(out_ref.dtype)
            for h in range(heads):
                out_ref[s, block * half : width, h * HD : (h + 1) * HD] = context[
                    h * half : (h + 1) * half
                ]


def attend(starts, lens, query, kv_slots, window):
    rows, columns = query.shape
    count, slot = kv_slots.shape[:2]
    batch = 2
    heads = columns // HD
    grid_spec = pltpu.PrefetchScalarGridSpec(
        num_scalar_prefetch=2,
        grid=(count // batch,),
        in_specs=[
            pl.BlockSpec((rows, columns), lambda s, a, b: (0, 0)),
            pl.BlockSpec((batch, slot, 2 * HD), lambda s, a, b: (s, 0, 0)),
        ],
        out_specs=pl.BlockSpec((batch, slot, columns), lambda s, a, b: (s, 0, 0)),
    )
    return pl.pallas_call(
        functools.partial(attend_kernel, heads, window),
        grid_spec=grid_spec,
        out_shape=jax.ShapeDtypeStruct((count, slot, columns), jnp.bfloat16),
        compiler_params=pltpu.CompilerParams(vmem_limit_bytes=16 * 2**20),
        cost_estimate=pl.CostEstimate(
            flops=2 * count * slot * (2 * slot + window) * columns,
            bytes_accessed=2 * (rows * columns + 2 * count * slot * columns),
            transcendentals=count * heads * slot * slot,
        ),
    )(starts, lens, query, kv_slots)


def place_kernel(count, slot, window, start_ref, len_ref, in_ref, *rest):
    out_ref, total = rest[-2:]
    rows = total.shape[0]
    total[...] = jnp.zeros_like(total)
    row_at = lax.broadcasted_iota(jnp.int32, (window, slot), 0)
    col_at = lax.broadcasted_iota(jnp.int32, (window, slot), 1)
    for s in range(count):
        start = start_ref[s]
        first = pl.multiple_of(jnp.minimum((start // 8) * 8, rows - window), 8)
        pick = jnp.where(
            (row_at == col_at + (start - first)) & (col_at < len_ref[s]), 1.0, 0.0
        ).astype(jnp.bfloat16)
        total[pl.ds(first, window), :] += jnp.dot(
            pick, in_ref[s], preferred_element_type=jnp.float32
        )
    out_ref[...] = total[...].astype(out_ref.dtype)


def place(starts, lens, slots, rows, which, all_columns, before):
    count, slot, columns = slots.shape
    window = min(rows, slot + 8)
    in_specs = [pl.BlockSpec((count, slot, columns), lambda r, a, b: (0, 0, 0))]
    operands, aliases = [slots], {}
    if before is not None:
        in_specs.append(pl.BlockSpec(memory_space=pl.ANY))
        operands.append(before)
        aliases = {3: 0}
    grid_spec = pltpu.PrefetchScalarGridSpec(
        num_scalar_prefetch=2,
        grid=(1,),
        in_specs=in_specs,
        out_specs=pl.BlockSpec((rows, columns), lambda r, a, b: (0, which)),
        scratch_shapes=[pltpu.VMEM((rows, columns), jnp.float32)],
    )
    return pl.pallas_call(
        functools.partial(place_kernel, count, slot, window),
        grid_spec=grid_spec,
        out_shape=jax.ShapeDtypeStruct((rows, all_columns), jnp.bfloat16),
        input_output_aliases=aliases,
        compiler_params=pltpu.CompilerParams(vmem_limit_bytes=16 * 2**20),
        cost_estimate=pl.CostEstimate(
            flops=2 * count * slot * window * columns,
            bytes_accessed=2 * columns * (count * slot + rows),
            transcendentals=0,
        ),
    )(starts, lens, *operands)


def local_line(
    rollout_states,
    norm_gain,
    w_query,
    w_key,
    w_value,
    b_query,
    b_key,
    b_value,
    seq_lengths,
    seq_dest,
    seq_offset,
):
    learners = lax.axis_size("dp")
    line = learners // 2
    me = lax.axis_index("dp")
    z, x = me // 2, me % 2
    t = lax.axis_index("tensor")
    row_count, feature_count = rollout_states.shape
    slot = 2 * row_count // learners
    half = feature_count // 2
    middle = row_count // 2

    def after(array, *others):
        return lax.optimization_barrier((array, *others))[0]

    def swap_x(array):
        return lax.ppermute(array, "dp", [(i, i ^ 1) for i in range(learners)])

    def swap_y(array):
        return lax.ppermute(array, "tensor", [(i, i ^ 2) for i in range(4)])

    def swap_core(array):
        return lax.ppermute(array, "tensor", [(i, i ^ 1) for i in range(4)])

    def up(array, first):
        return lax.ppermute(array, "dp", [(i, i + 2) for i in range(2 * first, learners - 2)])

    def down(array, first):
        return lax.ppermute(array, "dp", [(i, i - 2) for i in range(2, learners - 2 * first)])

    wide = 2 * HD
    chunks = [w_key, w_value]
    for low in range(0, w_query.shape[1], wide):
        chunks.append(w_query[:, low : low + wide])
    chunk_places, marks = [], []
    for c, own in enumerate(chunks):
        if c >= 2:
            own = after(own, *marks[c - 2][-1])
        ups, downs = [own], [own]
        for step in range(line - 1):
            ups.append(up(ups[-1], step))
            downs.append(down(downs[-1], step))
        chunk_places.append(ups[:0:-1] + downs)
        marks.append(list(zip(ups[1:], downs[1:])))
    places = [chunk_places[:2]] + [[spots] for spots in chunk_places[2:]]
    biases = [jnp.concatenate([b_key, b_value])[None, :]]
    for low in range(0, w_query.shape[1], wide):
        biases.append(b_query[None, low : low + wide])

    states = rollout_states
    widened = states.astype(jnp.float32)
    squares = jnp.sum(widened * widened, axis=-1)
    squares = squares + swap_core(squares)
    squares = squares + swap_y(squares)
    scale = lax.rsqrt(squares[:, None] / (4 * feature_count) + norm_eps)

    def normed(first):
        part = lax.dynamic_slice_in_dim(states, first, half, 1).astype(jnp.float32)
        gain = lax.dynamic_slice_in_dim(norm_gain, t * feature_count + first, half, 0)
        return (part * scale * gain[None, :]).astype(jnp.bfloat16)

    own, give = normed(x * half), normed((1 - x) * half)

    near_a = swap_x(give[:middle])
    own_a = swap_y(own[:middle])
    own_core = swap_core(own)
    near_b = swap_x(after(give[middle:], near_a, *marks[0][2]))
    diag_a = swap_y(after(near_a, own_a, *marks[1][2]))
    near_a_core = swap_core(near_a)
    own_a_core = swap_core(after(own_a, near_a))
    diag_b = swap_y(after(near_b, diag_a, *marks[2][0]))
    near_b_core = swap_core(after(near_b, diag_a))
    diag_a_core = swap_core(after(diag_a, near_b))
    own_b = swap_y(after(own[middle:], diag_b, *marks[2][1]))
    diag_b_core = swap_core(after(diag_b, *marks[2][1]))
    own_b_core = swap_core(own_b)
    own_x = [[own], [own_core], [own_a, own_b], [own_a_core, own_b_core]]
    near_ax = [[near_a], [near_a_core], [diag_a], [diag_a_core]]
    near_bx = [[near_b], [near_b_core], [diag_b], [diag_b_core]]
    near_x = [a + b for a, b in zip(near_ax, near_bx)]
    off = jnp.stack([(t ^ i) - z for i in range(4)]).astype(jnp.int32)

    lengths = seq_lengths.reshape(learners, learners)
    dests = seq_dest.reshape(learners, learners)
    offsets = seq_offset.reshape(learners, learners)
    starts = jnp.cumsum(lengths, axis=1) - lengths
    peer_ids = jnp.arange(learners, dtype=jnp.int32)
    rows = jnp.arange(row_count, dtype=jnp.int32)
    length = lax.dynamic_index_in_dim(lengths, me, 0, keepdims=False)
    start = lax.dynamic_index_in_dim(starts, me, 0, keepdims=False)
    dest = lax.dynamic_index_in_dim(dests, me, 0, keepdims=False)
    match = (dest[None, :] == peer_ids[:, None]).astype(jnp.int32)
    send_start = jnp.sum(match * start[None, :], axis=1)
    send_length = jnp.sum(match * length[None, :], axis=1)
    inside = (rows[:, None] >= start[None, :]) & (rows[:, None] < (start + length)[None, :])
    position = rows - jnp.sum(inside.astype(jnp.int32) * start[None, :], axis=1)
    cosine, sine = rope_tables(position)
    cosine = jnp.concatenate([cosine, cosine], axis=1)
    sine = jnp.concatenate([-sine, sine], axis=1)
    matched = (dests == me).astype(jnp.int32)
    run_start = jnp.sum(matched * offsets, axis=1)
    run_length = jnp.sum(matched * lengths, axis=1)

    window = min(row_count, -(-(slot + 16) // 128) * 128)

    def partial(c, blocks, *others):
        return projection(after(off, *others), blocks, places[c])

    def finish(c, got, *others):
        ropes = (True, False) if c == 0 else (True, True)
        return projection(
            after(off, *others), own_x, places[c], (ropes, got, biases[c], cosine, sine)
        )

    def send(outgoing):
        return lax.all_to_all(outgoing, "dp", split_axis=0, concat_axis=0, tiled=True)

    def receive(c, incoming, before, *others):
        start_at = after(run_start, *others)
        return place(
            start_at, run_length, incoming, row_count, c - 1, w_query.shape[1], before
        )

    part_a = partial(0, near_ax, *marks[2][0])
    got_a = swap_x(part_a)
    part_b = partial(0, near_bx, part_a, *marks[2][1])
    got_b = swap_x(after(part_b, got_a))
    parts = [None, partial(1, near_x, part_b)]
    got = [None, swap_x(after(parts[1], got_b))]
    kv = finish(0, [got_a, got_b], parts[1])
    kv_slots = to_slots(send_start, send_length, kv, slot, window)
    parts.append(partial(2, near_x, kv_slots))
    out, incoming, result = [None], [None], None
    for c in range(1, len(places)):
        if c + 1 < len(places):
            got.append(swap_x(after(parts[c + 1], got[c])))
        ties = marks[4][c - 1] if c <= 2 else ()
        rot = finish(c, [got[c]], parts[-1], *ties)
        out.append(attend(send_start, send_length, rot, kv_slots, window))
        incoming.append(send(out[c]))
        if c + 2 < len(places):
            parts.append(partial(c + 2, near_x, out[c]))
        if c >= 2:
            result = receive(c - 1, incoming[c - 1], result, out[c])
    return receive(len(places) - 1, incoming[-1], result)


def solution(mesh):
    placed = (
        P("dp", "tensor"),
        P(),
        P("dp", "tensor"),
        P("dp", "tensor"),
        P("dp", "tensor"),
        P("tensor"),
        P("tensor"),
        P("tensor"),
        P(),
        P(),
        P(),
    )
    fits_line = mesh.shape["dp"] == 8 and mesh.shape["tensor"] == 4
    return jax.shard_map(
        local_line if fits_line else local_any,
        mesh=mesh,
        in_specs=placed,
        out_specs=P("dp", "tensor"),
        check_vma=False,
    )
```

```python
import functools

import jax
import jax.numpy as jnp
from jax import lax
from jax.experimental import pallas as pl
from jax.experimental.pallas import tpu as pltpu
from jax.sharding import PartitionSpec as P

HD = 128

rope_base = 1000000.0
norm_eps = 1e-06
mask_value = -1e30


def rope_tables(positions):
    half_dim = HD // 2
    frequency = rope_base ** (-(jnp.arange(half_dim).astype(jnp.float32) * 2.0 / HD))
    angles = positions.astype(jnp.float32)[:, None] * frequency[None, :]
    return (jnp.cos(angles), jnp.sin(angles))


def rotate(states, cosine, sine):
    half_dim = states.shape[-1] // 2
    first_half = states[..., :half_dim]
    second_half = states[..., half_dim:]
    cos_wide = cosine[:, None, :]
    sin_wide = sine[:, None, :]
    return jnp.concatenate(
        [
            first_half * cos_wide - second_half * sin_wide,
            second_half * cos_wide + first_half * sin_wide,
        ],
        axis=-1,
    )


def local_any(
    rollout_states,
    norm_gain,
    w_query,
    w_key,
    w_value,
    b_query,
    b_key,
    b_value,
    seq_lengths,
    seq_dest,
    seq_offset,
):
    learners = lax.axis_size("dp")
    own_index = lax.axis_index("dp")
    row_count, feature_count = rollout_states.shape
    capacity = 2 * row_count // learners - 1
    lengths = seq_lengths.reshape(learners, learners)
    dests = seq_dest.reshape(learners, learners)
    offsets = seq_offset.reshape(learners, learners)
    starts = jnp.cumsum(lengths, axis=1) - lengths
    peer_ids = jnp.arange(learners, dtype=jnp.int32)
    own_length = lax.dynamic_index_in_dim(lengths, own_index, 0, keepdims=False)
    own_start = lax.dynamic_index_in_dim(starts, own_index, 0, keepdims=False)
    own_dest = lax.dynamic_index_in_dim(dests, own_index, 0, keepdims=False)
    match_send = (own_dest[None, :] == peer_ids[:, None]).astype(jnp.int32)
    send_start = jnp.sum(match_send * own_start[None, :], axis=1)
    send_length = jnp.sum(match_send * own_length[None, :], axis=1)
    slot_index = jnp.arange(capacity, dtype=jnp.int32)
    pick_rows = send_start[:, None] + slot_index[None, :]
    padded = jnp.concatenate(
        [rollout_states, jnp.zeros((capacity, feature_count), rollout_states.dtype)], axis=0
    )
    live_slots = (slot_index[None, :] < send_length[:, None])[..., None]
    outgoing = jnp.where(
        live_slots, jnp.take(padded, pick_rows, axis=0), jnp.zeros((), rollout_states.dtype)
    )
    incoming = lax.all_to_all(outgoing, "dp", split_axis=0, concat_axis=0, tiled=True)
    matched = (dests == own_index).astype(jnp.int32)
    run_start = jnp.sum(matched * offsets, axis=1)
    run_length = jnp.sum(matched * lengths, axis=1)
    rows = jnp.arange(row_count, dtype=jnp.int32)
    inside = (
        (rows[:, None] >= run_start[None, :]) & (rows[:, None] < (run_start + run_length)[None, :])
    ).astype(jnp.int32)
    source_ids = jnp.sum(inside * peer_ids[None, :], axis=1)
    within_seq = rows - jnp.sum(inside * run_start[None, :], axis=1)
    arrived = jnp.take(
        incoming.reshape(learners * capacity, feature_count),
        source_ids * capacity + within_seq,
        axis=0,
    )
    gathered = lax.all_gather(arrived, "tensor", axis=1, tiled=True)
    widened = gathered.astype(jnp.float32)
    statistic = jnp.mean(widened * widened, axis=-1, keepdims=True)
    normed = (widened * lax.rsqrt(statistic + norm_eps) * norm_gain[None, :]).astype(jnp.bfloat16)
    full_query, full_key, full_value = (
        lax.all_gather(w_query, "dp", axis=0, tiled=True),
        lax.all_gather(w_key, "dp", axis=0, tiled=True),
        lax.all_gather(w_value, "dp", axis=0, tiled=True),
    )
    query = jnp.dot(normed, full_query, preferred_element_type=jnp.float32)
    key = jnp.dot(normed, full_key, preferred_element_type=jnp.float32)
    value = jnp.dot(normed, full_value, preferred_element_type=jnp.float32)
    query = query + b_query[None, :]
    key = key + b_key[None, :]
    value = value + b_value[None, :]
    heads_here = query.shape[1] // HD
    kv_here = key.shape[1] // HD
    group = heads_here // kv_here
    cosine, sine = rope_tables(within_seq)
    rot_query = rotate(query.reshape(row_count, heads_here, HD), cosine, sine).astype(jnp.bfloat16)
    rot_query = rot_query.reshape(row_count, kv_here, group, HD)
    rot_key = rotate(key.reshape(row_count, kv_here, HD), cosine, sine).astype(jnp.bfloat16)
    value_bf = value.reshape(row_count, kv_here, HD).astype(jnp.bfloat16)
    block_rows = min(512, row_count)

    def one_block(block_number):
        first_row = block_number * block_rows
        query_block = lax.dynamic_slice_in_dim(rot_query, first_row, block_rows, 0)
        query_source = lax.dynamic_slice_in_dim(source_ids, first_row, block_rows, 0)
        query_rows = first_row + jnp.arange(block_rows, dtype=jnp.int32)
        scores = jnp.einsum(
            "bcgd,kcd->cgbk", query_block, rot_key, preferred_element_type=jnp.float32
        )
        scores = scores * HD ** (-0.5)
        allowed = (source_ids[None, :] == query_source[:, None]) & (
            rows[None, :] <= query_rows[:, None]
        )
        scores = jnp.where(allowed[None, None], scores, mask_value)
        peak = jnp.max(scores, axis=-1, keepdims=True)
        raised = jnp.exp(scores - peak)
        weights = (raised / jnp.sum(raised, axis=-1, keepdims=True)).astype(jnp.bfloat16)
        context = jnp.einsum(
            "cgbk,kcd->bcgd", weights, value_bf, preferred_element_type=jnp.float32
        )
        return context.astype(jnp.bfloat16).reshape(block_rows, heads_here * HD)

    outputs = lax.map(one_block, jnp.arange(row_count // block_rows, dtype=jnp.int32))
    return outputs.reshape(row_count, heads_here * HD)


def choose_kernel(widths, off_ref, *refs):
    out_ref = refs[-1]
    feats = out_ref.shape[1]
    step = feats // 4
    first_lane = 0
    for p, width in enumerate(widths):
        lanes = pl.ds(first_lane, width)
        first_lane += width
        for i in range(4):
            for spot in range(7):

                @pl.when(off_ref[i] == spot - 3)
                def _(i=i, lanes=lanes, ref=refs[7 * p + spot]):
                    @pl.loop(0, feats, step=step)
                    def _(first):
                        here = pl.ds(pl.multiple_of(first, step), step)
                        out_ref[i, here, lanes] = ref[here, :]


def choose(off, places):
    feats = places[0][0].shape[0]
    widths = tuple(spots[0].shape[1] for spots in places)
    vmem = pl.BlockSpec(memory_space=pltpu.VMEM)
    return pl.pallas_call(
        functools.partial(choose_kernel, widths),
        in_specs=[pl.BlockSpec(memory_space=pltpu.SMEM)] + [vmem] * (7 * len(places)),
        out_specs=vmem,
        out_shape=jax.ShapeDtypeStruct((4, feats, sum(widths)), jnp.bfloat16),
        compiler_params=pltpu.CompilerParams(vmem_limit_bytes=8 * 2**20),
        cost_estimate=pl.CostEstimate(
            flops=0, bytes_accessed=16 * feats * sum(widths), transcendentals=0
        ),
    )(off, *[keep(spot) for spots in places for spot in spots])


def product_kernel(counts, ropes, *refs):
    refs = list(refs)
    x_refs = [[refs.pop(0) for _ in range(n)] for n in counts[:4]]
    w_ref = refs.pop(0)
    part_refs = [refs.pop(0) for _ in range(counts[4])]
    if ropes:
        bias_ref, cos_ref, sin_ref = (refs.pop(0) for _ in range(3))
    out_ref = refs[-1]
    rows = out_ref.shape[0]
    tile = rows // max(counts)

    def piece_rows(pieces, first):
        size = pieces[0].shape[0]
        return pieces[first // size], pl.ds(first % size, tile)

    for first in range(0, rows, tile):
        here = pl.ds(first, tile)
        term = None
        for i in range(4):
            ref, at = piece_rows(x_refs[i], first)
            dot = jnp.dot(ref[at, :], w_ref[i], preferred_element_type=jnp.float32)
            term = dot if term is None else term + dot
        if not ropes:
            out_ref[here, :] = term.astype(out_ref.dtype)
            continue
        ref, at = piece_rows(part_refs, first)
        term = term + ref[at, :].astype(jnp.float32) + bias_ref[...]
        for c, rope in enumerate(ropes):
            head = term[:, c * HD : (c + 1) * HD]
            if rope:
                head = head * cos_ref[here, :] + pltpu.roll(head, HD // 2, 1) * sin_ref[here, :]
            out_ref[here, c * HD : (c + 1) * HD] = head.astype(out_ref.dtype)


def keep(array):
    return pltpu.with_memory_space_constraint(array, pltpu.VMEM)


def projection(x_blocks, weights, finish=None):
    rows = sum(piece.shape[0] for piece in x_blocks[0])
    _, feats, columns = weights.shape
    counts = [len(pieces) for pieces in x_blocks]
    operands = [keep(piece) for pieces in x_blocks for piece in pieces] + [keep(weights)]
    ropes, out_type = None, jnp.float32
    if finish is None:
        counts.append(0)
    else:
        ropes, parts, bias, cosine, sine = finish
        counts.append(len(parts))
        operands += [keep(part) for part in parts]
        operands += [bias, keep(cosine), keep(sine)]
        out_type = jnp.bfloat16
    vmem = pl.BlockSpec(memory_space=pltpu.VMEM)
    return pl.pallas_call(
        functools.partial(product_kernel, tuple(counts), ropes),
        in_specs=[vmem] * len(operands),
        out_specs=vmem,
        out_shape=jax.ShapeDtypeStruct((rows, columns), out_type),
        compiler_params=pltpu.CompilerParams(vmem_limit_bytes=8 * 2**20),
        cost_estimate=pl.CostEstimate(
            flops=8 * rows * feats * columns,
            bytes_accessed=8 * feats * columns + 4 * rows * columns,
            transcendentals=0,
        ),
    )(*operands)


def pick_rows(start, length, slot, window, ref):
    first = pl.multiple_of(jnp.minimum((start // 16) * 16, ref.shape[0] - window), 16)
    row_at = lax.broadcasted_iota(jnp.int32, (slot, window), 0)
    col_at = lax.broadcasted_iota(jnp.int32, (slot, window), 1)
    pick = jnp.where((col_at == row_at + (start - first)) & (row_at < length), 1.0, 0.0)
    rows = jnp.dot(
        pick.astype(jnp.bfloat16), ref[pl.ds(first, window), :], preferred_element_type=jnp.float32
    )
    return rows.astype(jnp.bfloat16)


def slots_kernel(slot, window, start_ref, len_ref, in_ref, out_ref):
    for s in range(out_ref.shape[0]):
        out_ref[s] = pick_rows(start_ref[s], len_ref[s], slot, window, in_ref)


def to_slots(starts, lens, array, slot, window):
    count, columns = starts.shape[0], array.shape[1]
    scalars = pl.BlockSpec(memory_space=pltpu.SMEM)
    vmem = pl.BlockSpec(memory_space=pltpu.VMEM)
    return pl.pallas_call(
        functools.partial(slots_kernel, slot, window),
        in_specs=[scalars, scalars, vmem],
        out_specs=vmem,
        out_shape=jax.ShapeDtypeStruct((count, slot, columns), jnp.bfloat16),
        compiler_params=pltpu.CompilerParams(vmem_limit_bytes=8 * 2**20),
        cost_estimate=pl.CostEstimate(
            flops=2 * count * slot * window * columns,
            bytes_accessed=2 * columns * (array.shape[0] + count * slot),
            transcendentals=0,
        ),
    )(starts, lens, array)


def attend_kernel(heads, window, start_ref, len_ref, q_ref, kv_ref, out_ref):
    batch, slot = out_ref.shape[:2]
    half = slot // 2
    group = pl.program_id(0) * batch
    for s in range(batch):
        query = pick_rows(start_ref[group + s], len_ref[group + s], slot, window, q_ref)
        for block in range(2):
            width = (block + 1) * half
            stacked = jnp.concatenate(
                [
                    query[block * half : width, h * HD : (h + 1) * HD]
                    for h in range(heads)
                ],
                axis=0,
            )
            scores = lax.dot_general(
                stacked,
                kv_ref[s, :width, :HD],
                (((1,), (1,)), ((), ())),
                preferred_element_type=jnp.float32,
            )
            row_at = lax.broadcasted_iota(jnp.int32, scores.shape, 0) & (half - 1)
            col_at = lax.broadcasted_iota(jnp.int32, scores.shape, 1)
            scores = jnp.where(
                col_at <= row_at + block * half, scores * HD ** (-0.5), mask_value
            )
            peak = jnp.max(scores, axis=-1, keepdims=True)
            raised = jnp.exp(scores - peak)
            weights = raised * (1.0 / jnp.sum(raised, axis=-1, keepdims=True))
            context = jnp.dot(
                weights.astype(jnp.bfloat16), kv_ref[s, :width, HD:], preferred_element_type=jnp.float32
            ).astype(out_ref.dtype)
            for h in range(heads):
                out_ref[s, block * half : width, h * HD : (h + 1) * HD] = context[
                    h * half : (h + 1) * half
                ]


def attend(starts, lens, query, kv_slots, window):
    rows, columns = query.shape
    count, slot = kv_slots.shape[:2]
    batch = 2
    heads = columns // HD
    grid_spec = pltpu.PrefetchScalarGridSpec(
        num_scalar_prefetch=2,
        grid=(count // batch,),
        in_specs=[
            pl.BlockSpec((rows, columns), lambda s, a, b: (0, 0)),
            pl.BlockSpec((batch, slot, 2 * HD), lambda s, a, b: (s, 0, 0)),
        ],
        out_specs=pl.BlockSpec((batch, slot, columns), lambda s, a, b: (s, 0, 0)),
    )
    return pl.pallas_call(
        functools.partial(attend_kernel, heads, window),
        grid_spec=grid_spec,
        out_shape=jax.ShapeDtypeStruct((count, slot, columns), jnp.bfloat16),
        compiler_params=pltpu.CompilerParams(vmem_limit_bytes=8 * 2**20),
        cost_estimate=pl.CostEstimate(
            flops=2 * count * slot * (2 * slot + window) * columns,
            bytes_accessed=2 * (rows * columns + 2 * count * slot * columns),
            transcendentals=count * heads * slot * slot,
        ),
    )(starts, lens, query, kv_slots)


def place_kernel(count, slot, window, start_ref, len_ref, in_ref, *rest):
    out_ref, total = rest[-2:]
    rows = total.shape[0]
    total[...] = jnp.zeros_like(total)
    row_at = lax.broadcasted_iota(jnp.int32, (window, slot), 0)
    col_at = lax.broadcasted_iota(jnp.int32, (window, slot), 1)
    for s in range(count):
        start = start_ref[s]
        first = pl.multiple_of(jnp.minimum((start // 8) * 8, rows - window), 8)
        pick = jnp.where(
            (row_at == col_at + (start - first)) & (col_at < len_ref[s]), 1.0, 0.0
        ).astype(jnp.bfloat16)
        total[pl.ds(first, window), :] += jnp.dot(
            pick, in_ref[s], preferred_element_type=jnp.float32
        )
    out_ref[...] = total[...].astype(out_ref.dtype)


def place(starts, lens, slots, rows, which, all_columns, before):
    count, slot, columns = slots.shape
    window = min(rows, slot + 8)
    in_specs = [pl.BlockSpec((count, slot, columns), lambda r, a, b: (0, 0, 0))]
    operands, aliases = [slots], {}
    if before is not None:
        in_specs.append(pl.BlockSpec(memory_space=pl.ANY))
        operands.append(before)
        aliases = {3: 0}
    grid_spec = pltpu.PrefetchScalarGridSpec(
        num_scalar_prefetch=2,
        grid=(1,),
        in_specs=in_specs,
        out_specs=pl.BlockSpec((rows, columns), lambda r, a, b: (0, which)),
        scratch_shapes=[pltpu.VMEM((rows, columns), jnp.float32)],
    )
    return pl.pallas_call(
        functools.partial(place_kernel, count, slot, window),
        grid_spec=grid_spec,
        out_shape=jax.ShapeDtypeStruct((rows, all_columns), jnp.bfloat16),
        input_output_aliases=aliases,
        compiler_params=pltpu.CompilerParams(vmem_limit_bytes=8 * 2**20),
        cost_estimate=pl.CostEstimate(
            flops=2 * count * slot * window * columns,
            bytes_accessed=2 * columns * (count * slot + rows),
            transcendentals=0,
        ),
    )(starts, lens, *operands)


def local_line(
    rollout_states,
    norm_gain,
    w_query,
    w_key,
    w_value,
    b_query,
    b_key,
    b_value,
    seq_lengths,
    seq_dest,
    seq_offset,
):
    learners = lax.axis_size("dp")
    line = learners // 2
    me = lax.axis_index("dp")
    z, x = me // 2, me % 2
    t = lax.axis_index("tensor")
    row_count, feature_count = rollout_states.shape
    slot = 2 * row_count // learners
    half = feature_count // 2
    middle = row_count // 2

    def after(array, *others):
        return lax.optimization_barrier((array, *others))[0]

    def swap_x(array):
        return lax.ppermute(array, "dp", [(i, i ^ 1) for i in range(learners)])

    def swap_y(array):
        return lax.ppermute(array, "tensor", [(i, i ^ 2) for i in range(4)])

    def swap_core(array):
        return lax.ppermute(array, "tensor", [(i, i ^ 1) for i in range(4)])

    def up(array, first):
        return lax.ppermute(array, "dp", [(i, i + 2) for i in range(2 * first, learners - 2)])

    def down(array, first):
        return lax.ppermute(array, "dp", [(i, i - 2) for i in range(2, learners - 2 * first)])

    wide = 2 * HD
    chunks = [w_key, w_value]
    for low in range(0, w_query.shape[1], wide):
        chunks.append(w_query[:, low : low + wide])
    chunk_places, marks = [], []
    for c, own in enumerate(chunks):
        if c >= 2:
            own = after(own, *marks[c - 2][-1])
        ups, downs = [own], [own]
        for step in range(line - 1):
            ups.append(up(ups[-1], step))
            downs.append(down(downs[-1], step))
        chunk_places.append(ups[:0:-1] + downs)
        marks.append(list(zip(ups[1:], downs[1:])))
    places = [chunk_places[:2]] + [[spots] for spots in chunk_places[2:]]
    biases = [jnp.concatenate([b_key, b_value])[None, :]]
    for low in range(0, w_query.shape[1], wide):
        biases.append(b_query[None, low : low + wide])

    states = rollout_states
    widened = states.astype(jnp.float32)
    squares = jnp.sum(widened * widened, axis=-1)
    squares = squares + swap_core(squares)
    squares = squares + swap_y(squares)
    scale = lax.rsqrt(squares[:, None] / (4 * feature_count) + norm_eps)

    def normed(first):
        part = lax.dynamic_slice_in_dim(states, first, half, 1).astype(jnp.float32)
        gain = lax.dynamic_slice_in_dim(norm_gain, t * feature_count + first, half, 0)
        return (part * scale * gain[None, :]).astype(jnp.bfloat16)

    own, give = normed(x * half), normed((1 - x) * half)

    near_a = swap_x(after(give[:middle], *marks[0][0], *marks[1][0]))
    own_a = swap_y(after(own[:middle], *marks[0][0], *marks[1][0]))
    own_core = swap_core(own)
    near_b = swap_x(after(give[middle:], near_a, *marks[0][2]))
    diag_a = swap_y(after(near_a, own_a, *marks[1][2]))
    near_a_core = swap_core(near_a)
    own_a_core = swap_core(after(own_a, near_a))
    diag_b = swap_y(after(near_b, diag_a, *marks[2][0]))
    near_b_core = swap_core(after(near_b, diag_a))
    diag_a_core = swap_core(after(diag_a, near_b))
    own_b = swap_y(after(own[middle:], diag_b, *marks[2][1]))
    diag_b_core = swap_core(after(diag_b, *marks[2][1]))
    own_b_core = swap_core(own_b)
    own_x = [[own], [own_core], [own_a, own_b], [own_a_core, own_b_core]]
    near_ax = [[near_a], [near_a_core], [diag_a], [diag_a_core]]
    near_bx = [[near_b], [near_b_core], [diag_b], [diag_b_core]]
    near_x = [a + b for a, b in zip(near_ax, near_bx)]
    off = jnp.stack([(t ^ i) - z for i in range(4)]).astype(jnp.int32)

    lengths = seq_lengths.reshape(learners, learners)
    dests = seq_dest.reshape(learners, learners)
    offsets = seq_offset.reshape(learners, learners)
    starts = jnp.cumsum(lengths, axis=1) - lengths
    peer_ids = jnp.arange(learners, dtype=jnp.int32)
    rows = jnp.arange(row_count, dtype=jnp.int32)
    length = lax.dynamic_index_in_dim(lengths, me, 0, keepdims=False)
    start = lax.dynamic_index_in_dim(starts, me, 0, keepdims=False)
    dest = lax.dynamic_index_in_dim(dests, me, 0, keepdims=False)
    match = (dest[None, :] == peer_ids[:, None]).astype(jnp.int32)
    send_start = jnp.sum(match * start[None, :], axis=1)
    send_length = jnp.sum(match * length[None, :], axis=1)
    inside = (rows[:, None] >= start[None, :]) & (rows[:, None] < (start + length)[None, :])
    position = rows - jnp.sum(inside.astype(jnp.int32) * start[None, :], axis=1)
    cosine, sine = rope_tables(position)
    cosine = jnp.concatenate([cosine, cosine], axis=1)
    sine = jnp.concatenate([-sine, sine], axis=1)
    matched = (dests == me).astype(jnp.int32)
    run_start = jnp.sum(matched * offsets, axis=1)
    run_length = jnp.sum(matched * lengths, axis=1)

    window = min(row_count, -(-(slot + 16) // 128) * 128)

    weights = []

    def partial(c, blocks, *others):
        if c == len(weights):
            weights.append(choose(after(off, *others), places[c]))
        return projection(blocks, weights[c])

    def finish(c, got, *others):
        ropes = (True, False) if c == 0 else (True, True)
        ending = (ropes, got, biases[c], cosine, sine)
        return projection(own_x, after(weights[c], *others), ending)

    def send(outgoing):
        return lax.all_to_all(outgoing, "dp", split_axis=0, concat_axis=0, tiled=True)

    def receive(c, incoming, before, *others):
        start_at = after(run_start, *others)
        return place(
            start_at, run_length, incoming, row_count, c - 1, w_query.shape[1], before
        )

    part_a = partial(0, near_ax, *marks[2][0])
    got_a = swap_x(part_a)
    part_b = projection(near_bx, after(weights[0], part_a, *marks[2][1]))
    got_b = swap_x(after(part_b, got_a))
    parts = [None, partial(1, near_x, part_b)]
    got = [None, swap_x(after(parts[1], got_b))]
    kv = finish(0, [got_a, got_b], parts[1])
    kv_slots = to_slots(send_start, send_length, kv, slot, window)
    parts.append(partial(2, near_x, kv_slots))
    out, incoming, result = [None], [None], None
    for c in range(1, len(places)):
        if c + 1 < len(places):
            got.append(swap_x(after(parts[c + 1], got[c])))
        ties = marks[4][c - 1] if c <= 2 else ()
        rot = finish(c, [got[c]], parts[-1], *ties)
        out.append(attend(send_start, send_length, rot, kv_slots, window))
        incoming.append(send(out[c]))
        if c + 2 < len(places):
            parts.append(partial(c + 2, near_x, out[c]))
        if c >= 2:
            result = receive(c - 1, incoming[c - 1], result, out[c])
    return receive(len(places) - 1, incoming[-1], result)


def solution(mesh):
    placed = (
        P("dp", "tensor"),
        P(),
        P("dp", "tensor"),
        P("dp", "tensor"),
        P("dp", "tensor"),
        P("tensor"),
        P("tensor"),
        P("tensor"),
        P(),
        P(),
        P(),
    )
    fits_line = mesh.shape["dp"] == 8 and mesh.shape["tensor"] == 4
    return jax.shard_map(
        local_line if fits_line else local_any,
        mesh=mesh,
        in_specs=placed,
        out_specs=P("dp", "tensor"),
        check_vma=False,
    )
```

```python
import functools

import jax
import jax.numpy as jnp
from jax import lax
from jax.experimental import pallas as pl
from jax.experimental.pallas import tpu as pltpu
from jax.sharding import PartitionSpec as P

HD = 128

rope_base = 1000000.0
norm_eps = 1e-06
mask_value = -1e30


def rope_tables(positions):
    half_dim = HD // 2
    frequency = rope_base ** (-(jnp.arange(half_dim).astype(jnp.float32) * 2.0 / HD))
    angles = positions.astype(jnp.float32)[:, None] * frequency[None, :]
    return (jnp.cos(angles), jnp.sin(angles))


def rotate(states, cosine, sine):
    half_dim = states.shape[-1] // 2
    first_half = states[..., :half_dim]
    second_half = states[..., half_dim:]
    cos_wide = cosine[:, None, :]
    sin_wide = sine[:, None, :]
    return jnp.concatenate(
        [
            first_half * cos_wide - second_half * sin_wide,
            second_half * cos_wide + first_half * sin_wide,
        ],
        axis=-1,
    )


def local_any(
    rollout_states,
    norm_gain,
    w_query,
    w_key,
    w_value,
    b_query,
    b_key,
    b_value,
    seq_lengths,
    seq_dest,
    seq_offset,
):
    learners = lax.axis_size("dp")
    own_index = lax.axis_index("dp")
    row_count, feature_count = rollout_states.shape
    capacity = 2 * row_count // learners - 1
    lengths = seq_lengths.reshape(learners, learners)
    dests = seq_dest.reshape(learners, learners)
    offsets = seq_offset.reshape(learners, learners)
    starts = jnp.cumsum(lengths, axis=1) - lengths
    peer_ids = jnp.arange(learners, dtype=jnp.int32)
    own_length = lax.dynamic_index_in_dim(lengths, own_index, 0, keepdims=False)
    own_start = lax.dynamic_index_in_dim(starts, own_index, 0, keepdims=False)
    own_dest = lax.dynamic_index_in_dim(dests, own_index, 0, keepdims=False)
    match_send = (own_dest[None, :] == peer_ids[:, None]).astype(jnp.int32)
    send_start = jnp.sum(match_send * own_start[None, :], axis=1)
    send_length = jnp.sum(match_send * own_length[None, :], axis=1)
    slot_index = jnp.arange(capacity, dtype=jnp.int32)
    pick_rows = send_start[:, None] + slot_index[None, :]
    padded = jnp.concatenate(
        [rollout_states, jnp.zeros((capacity, feature_count), rollout_states.dtype)], axis=0
    )
    live_slots = (slot_index[None, :] < send_length[:, None])[..., None]
    outgoing = jnp.where(
        live_slots, jnp.take(padded, pick_rows, axis=0), jnp.zeros((), rollout_states.dtype)
    )
    incoming = lax.all_to_all(outgoing, "dp", split_axis=0, concat_axis=0, tiled=True)
    matched = (dests == own_index).astype(jnp.int32)
    run_start = jnp.sum(matched * offsets, axis=1)
    run_length = jnp.sum(matched * lengths, axis=1)
    rows = jnp.arange(row_count, dtype=jnp.int32)
    inside = (
        (rows[:, None] >= run_start[None, :]) & (rows[:, None] < (run_start + run_length)[None, :])
    ).astype(jnp.int32)
    source_ids = jnp.sum(inside * peer_ids[None, :], axis=1)
    within_seq = rows - jnp.sum(inside * run_start[None, :], axis=1)
    arrived = jnp.take(
        incoming.reshape(learners * capacity, feature_count),
        source_ids * capacity + within_seq,
        axis=0,
    )
    gathered = lax.all_gather(arrived, "tensor", axis=1, tiled=True)
    widened = gathered.astype(jnp.float32)
    statistic = jnp.mean(widened * widened, axis=-1, keepdims=True)
    normed = (widened * lax.rsqrt(statistic + norm_eps) * norm_gain[None, :]).astype(jnp.bfloat16)
    full_query, full_key, full_value = (
        lax.all_gather(w_query, "dp", axis=0, tiled=True),
        lax.all_gather(w_key, "dp", axis=0, tiled=True),
        lax.all_gather(w_value, "dp", axis=0, tiled=True),
    )
    query = jnp.dot(normed, full_query, preferred_element_type=jnp.float32)
    key = jnp.dot(normed, full_key, preferred_element_type=jnp.float32)
    value = jnp.dot(normed, full_value, preferred_element_type=jnp.float32)
    query = query + b_query[None, :]
    key = key + b_key[None, :]
    value = value + b_value[None, :]
    heads_here = query.shape[1] // HD
    kv_here = key.shape[1] // HD
    group = heads_here // kv_here
    cosine, sine = rope_tables(within_seq)
    rot_query = rotate(query.reshape(row_count, heads_here, HD), cosine, sine).astype(jnp.bfloat16)
    rot_query = rot_query.reshape(row_count, kv_here, group, HD)
    rot_key = rotate(key.reshape(row_count, kv_here, HD), cosine, sine).astype(jnp.bfloat16)
    value_bf = value.reshape(row_count, kv_here, HD).astype(jnp.bfloat16)
    block_rows = min(512, row_count)

    def one_block(block_number):
        first_row = block_number * block_rows
        query_block = lax.dynamic_slice_in_dim(rot_query, first_row, block_rows, 0)
        query_source = lax.dynamic_slice_in_dim(source_ids, first_row, block_rows, 0)
        query_rows = first_row + jnp.arange(block_rows, dtype=jnp.int32)
        scores = jnp.einsum(
            "bcgd,kcd->cgbk", query_block, rot_key, preferred_element_type=jnp.float32
        )
        scores = scores * HD ** (-0.5)
        allowed = (source_ids[None, :] == query_source[:, None]) & (
            rows[None, :] <= query_rows[:, None]
        )
        scores = jnp.where(allowed[None, None], scores, mask_value)
        peak = jnp.max(scores, axis=-1, keepdims=True)
        raised = jnp.exp(scores - peak)
        weights = (raised / jnp.sum(raised, axis=-1, keepdims=True)).astype(jnp.bfloat16)
        context = jnp.einsum(
            "cgbk,kcd->bcgd", weights, value_bf, preferred_element_type=jnp.float32
        )
        return context.astype(jnp.bfloat16).reshape(block_rows, heads_here * HD)

    outputs = lax.map(one_block, jnp.arange(row_count // block_rows, dtype=jnp.int32))
    return outputs.reshape(row_count, heads_here * HD)


def product_kernel(counts, ropes, which_ref, *refs):
    refs = list(refs)
    x_refs = [[refs.pop(0) for _ in range(n)] for n in counts[:4]]
    w_ref = refs.pop(0)
    part_refs = [refs.pop(0) for _ in range(counts[4])]
    if ropes:
        bias_ref, cos_ref, sin_ref, out_ref, total = refs
    else:
        (out_ref,) = refs
        total = out_ref
    rows = out_ref.shape[0]
    tile = rows // max(counts)

    def piece_rows(pieces, first):
        size = pieces[0].shape[0]
        return pieces[first // size], pl.ds(first % size, tile)

    for i in range(4):

        @pl.when(pl.program_id(0) == i)
        def _(i=i):
            for first in range(0, rows, tile):
                here = pl.ds(first, tile)
                ref, at = piece_rows(x_refs[i], first)
                term = jnp.dot(ref[at, :], w_ref[0], preferred_element_type=jnp.float32)
                if i > 0:
                    term = total[here, :] + term
                if not ropes or i < 3:
                    total[here, :] = term
                    continue
                ref, at = piece_rows(part_refs, first)
                term = term + ref[at, :].astype(jnp.float32) + bias_ref[...]
                for c, rope in enumerate(ropes):
                    head = term[:, c * HD : (c + 1) * HD]
                    if rope:
                        turned = pltpu.roll(head, HD // 2, 1)
                        head = head * cos_ref[here, :] + turned * sin_ref[here, :]
                    out_ref[here, c * HD : (c + 1) * HD] = head.astype(out_ref.dtype)


def keep(array):
    return pltpu.with_memory_space_constraint(array, pltpu.VMEM)


def projection(which, x_blocks, weights, finish=None):
    weights, first_column = weights
    columns = 2 * HD
    rows = sum(piece.shape[0] for piece in x_blocks[0])
    feats = weights.shape[1]
    counts = [len(pieces) for pieces in x_blocks]
    vmem = pl.BlockSpec(memory_space=pltpu.VMEM)
    operands = [keep(piece) for pieces in x_blocks for piece in pieces]
    in_specs = [vmem] * len(operands)
    block = first_column // columns
    operands.append(weights)
    in_specs.append(pl.BlockSpec((1, feats, columns), lambda i, which: (which[i], 0, block)))
    ropes, out_type, scratch = None, jnp.float32, []
    if finish is None:
        counts.append(0)
    else:
        ropes, parts, bias, cosine, sine = finish
        counts.append(len(parts))
        operands += [keep(part) for part in parts]
        operands += [bias, keep(cosine), keep(sine)]
        in_specs += [vmem] * (len(parts) + 3)
        out_type = jnp.bfloat16
        scratch = [pltpu.VMEM((rows, columns), jnp.float32)]
    grid_spec = pltpu.PrefetchScalarGridSpec(
        num_scalar_prefetch=1,
        grid=(4,),
        in_specs=in_specs,
        out_specs=pl.BlockSpec((rows, columns), lambda i, which: (0, 0)),
        scratch_shapes=scratch,
    )
    return pl.pallas_call(
        functools.partial(product_kernel, tuple(counts), ropes),
        grid_spec=grid_spec,
        out_shape=jax.ShapeDtypeStruct((rows, columns), out_type),
        compiler_params=pltpu.CompilerParams(vmem_limit_bytes=20 * 2**20),
        cost_estimate=pl.CostEstimate(
            flops=8 * rows * feats * columns,
            bytes_accessed=8 * feats * columns + 4 * rows * columns,
            transcendentals=0,
        ),
    )(which, *operands)


def pick_rows(start, length, slot, window, ref):
    first = pl.multiple_of(jnp.minimum((start // 16) * 16, ref.shape[0] - window), 16)
    row_at = lax.broadcasted_iota(jnp.int32, (slot, window), 0)
    col_at = lax.broadcasted_iota(jnp.int32, (slot, window), 1)
    pick = jnp.where((col_at == row_at + (start - first)) & (row_at < length), 1.0, 0.0)
    rows = jnp.dot(
        pick.astype(jnp.bfloat16), ref[pl.ds(first, window), :], preferred_element_type=jnp.float32
    )
    return rows.astype(jnp.bfloat16)


def slots_kernel(slot, window, start_ref, len_ref, in_ref, out_ref):
    for s in range(out_ref.shape[0]):
        out_ref[s] = pick_rows(start_ref[s], len_ref[s], slot, window, in_ref)


def to_slots(starts, lens, array, slot, window):
    count, columns = starts.shape[0], array.shape[1]
    scalars = pl.BlockSpec(memory_space=pltpu.SMEM)
    vmem = pl.BlockSpec(memory_space=pltpu.VMEM)
    return pl.pallas_call(
        functools.partial(slots_kernel, slot, window),
        in_specs=[scalars, scalars, vmem],
        out_specs=vmem,
        out_shape=jax.ShapeDtypeStruct((count, slot, columns), jnp.bfloat16),
        compiler_params=pltpu.CompilerParams(vmem_limit_bytes=8 * 2**20),
        cost_estimate=pl.CostEstimate(
            flops=2 * count * slot * window * columns,
            bytes_accessed=2 * columns * (array.shape[0] + count * slot),
            transcendentals=0,
        ),
    )(starts, lens, array)


def attend_kernel(heads, window, start_ref, len_ref, q_ref, kv_ref, out_ref):
    batch, slot = out_ref.shape[:2]
    half = slot // 2
    group = pl.program_id(0) * batch
    for s in range(batch):
        query = pick_rows(start_ref[group + s], len_ref[group + s], slot, window, q_ref)
        for block in range(2):
            width = (block + 1) * half
            stacked = jnp.concatenate(
                [
                    query[block * half : width, h * HD : (h + 1) * HD]
                    for h in range(heads)
                ],
                axis=0,
            )
            scores = lax.dot_general(
                stacked,
                kv_ref[s, :width, :HD],
                (((1,), (1,)), ((), ())),
                preferred_element_type=jnp.float32,
            )
            row_at = lax.broadcasted_iota(jnp.int32, scores.shape, 0) & (half - 1)
            col_at = lax.broadcasted_iota(jnp.int32, scores.shape, 1)
            scores = jnp.where(
                col_at <= row_at + block * half, scores * HD ** (-0.5), mask_value
            )
            peak = jnp.max(scores, axis=-1, keepdims=True)
            raised = jnp.exp(scores - peak)
            weights = raised * (1.0 / jnp.sum(raised, axis=-1, keepdims=True))
            context = jnp.dot(
                weights.astype(jnp.bfloat16), kv_ref[s, :width, HD:], preferred_element_type=jnp.float32
            ).astype(out_ref.dtype)
            for h in range(heads):
                out_ref[s, block * half : width, h * HD : (h + 1) * HD] = context[
                    h * half : (h + 1) * half
                ]


def attend(starts, lens, query, kv_slots, window):
    rows, columns = query.shape
    count, slot = kv_slots.shape[:2]
    batch = 2
    heads = columns // HD
    grid_spec = pltpu.PrefetchScalarGridSpec(
        num_scalar_prefetch=2,
        grid=(count // batch,),
        in_specs=[
            pl.BlockSpec((rows, columns), lambda s, a, b: (0, 0)),
            pl.BlockSpec((batch, slot, 2 * HD), lambda s, a, b: (s, 0, 0)),
        ],
        out_specs=pl.BlockSpec((batch, slot, columns), lambda s, a, b: (s, 0, 0)),
    )
    return pl.pallas_call(
        functools.partial(attend_kernel, heads, window),
        grid_spec=grid_spec,
        out_shape=jax.ShapeDtypeStruct((count, slot, columns), jnp.bfloat16),
        compiler_params=pltpu.CompilerParams(vmem_limit_bytes=8 * 2**20),
        cost_estimate=pl.CostEstimate(
            flops=2 * count * slot * (2 * slot + window) * columns,
            bytes_accessed=2 * (rows * columns + 2 * count * slot * columns),
            transcendentals=count * heads * slot * slot,
        ),
    )(starts, lens, query, kv_slots)


def place_kernel(count, slot, window, start_ref, len_ref, in_ref, *rest):
    out_ref, total = rest[-2:]
    rows = total.shape[0]
    total[...] = jnp.zeros_like(total)
    row_at = lax.broadcasted_iota(jnp.int32, (window, slot), 0)
    col_at = lax.broadcasted_iota(jnp.int32, (window, slot), 1)
    for s in range(count):
        start = start_ref[s]
        first = pl.multiple_of(jnp.minimum((start // 8) * 8, rows - window), 8)
        pick = jnp.where(
            (row_at == col_at + (start - first)) & (col_at < len_ref[s]), 1.0, 0.0
        ).astype(jnp.bfloat16)
        total[pl.ds(first, window), :] += jnp.dot(
            pick, in_ref[s], preferred_element_type=jnp.float32
        )
    out_ref[...] = total[...].astype(out_ref.dtype)


def place(starts, lens, slots, rows, which, all_columns, before):
    count, slot, columns = slots.shape
    window = min(rows, slot + 8)
    in_specs = [pl.BlockSpec((count, slot, columns), lambda r, a, b: (0, 0, 0))]
    operands, aliases = [slots], {}
    if before is not None:
        in_specs.append(pl.BlockSpec(memory_space=pl.ANY))
        operands.append(before)
        aliases = {3: 0}
    grid_spec = pltpu.PrefetchScalarGridSpec(
        num_scalar_prefetch=2,
        grid=(1,),
        in_specs=in_specs,
        out_specs=pl.BlockSpec((rows, columns), lambda r, a, b: (0, which)),
        scratch_shapes=[pltpu.VMEM((rows, columns), jnp.float32)],
    )
    return pl.pallas_call(
        functools.partial(place_kernel, count, slot, window),
        grid_spec=grid_spec,
        out_shape=jax.ShapeDtypeStruct((rows, all_columns), jnp.bfloat16),
        input_output_aliases=aliases,
        compiler_params=pltpu.CompilerParams(vmem_limit_bytes=8 * 2**20),
        cost_estimate=pl.CostEstimate(
            flops=2 * count * slot * window * columns,
            bytes_accessed=2 * columns * (count * slot + rows),
            transcendentals=0,
        ),
    )(starts, lens, *operands)


def local_line(
    rollout_states,
    norm_gain,
    w_query,
    w_key,
    w_value,
    b_query,
    b_key,
    b_value,
    seq_lengths,
    seq_dest,
    seq_offset,
):
    learners = lax.axis_size("dp")
    line = learners // 2
    me = lax.axis_index("dp")
    z, x = me // 2, me % 2
    t = lax.axis_index("tensor")
    row_count, feature_count = rollout_states.shape
    slot = 2 * row_count // learners
    half = feature_count // 2
    middle = row_count // 2

    def after(array, *others):
        return lax.optimization_barrier((array, *others))[0]

    def swap_x(array):
        return lax.ppermute(array, "dp", [(i, i ^ 1) for i in range(learners)])

    def swap_y(array):
        return lax.ppermute(array, "tensor", [(i, i ^ 2) for i in range(4)])

    def swap_core(array):
        return lax.ppermute(array, "tensor", [(i, i ^ 1) for i in range(4)])

    wide = 2 * HD
    along_z = [[2 * i + j for i in range(line)] for j in range(2)]
    groups = [
        jnp.concatenate([w_key, w_value, w_query[:, :wide]], axis=1),
        w_query[:, wide : 3 * wide],
        w_query[:, 3 * wide :],
    ]
    weights = []
    for group in groups:
        gathered = lax.all_gather(group, "dp", axis_index_groups=along_z)
        for low in range(0, group.shape[1], wide):
            weights.append((gathered, low))
    biases = [jnp.concatenate([b_key, b_value])[None, :]]
    for low in range(0, w_query.shape[1], wide):
        biases.append(b_query[None, low : low + wide])

    states = rollout_states
    widened = states.astype(jnp.float32)
    squares = jnp.sum(widened * widened, axis=-1)
    squares = squares + swap_core(squares)
    squares = squares + swap_y(squares)
    scale = lax.rsqrt(squares[:, None] / (4 * feature_count) + norm_eps)

    def normed(first):
        part = lax.dynamic_slice_in_dim(states, first, half, 1).astype(jnp.float32)
        gain = lax.dynamic_slice_in_dim(norm_gain, t * feature_count + first, half, 0)
        return (part * scale * gain[None, :]).astype(jnp.bfloat16)

    own, give = normed(x * half), normed((1 - x) * half)

    near_a = swap_x(give[:middle])
    own_a = swap_y(own[:middle])
    own_core = swap_core(own)
    near_b = swap_x(after(give[middle:], near_a))
    diag_a = swap_y(after(near_a, own_a))
    near_a_core = swap_core(near_a)
    own_a_core = swap_core(after(own_a, near_a))
    diag_b = swap_y(after(near_b, diag_a))
    near_b_core = swap_core(after(near_b, diag_a))
    diag_a_core = swap_core(after(diag_a, near_b))
    own_b = swap_y(after(own[middle:], diag_b))
    diag_b_core = swap_core(diag_b)
    own_b_core = swap_core(own_b)
    own_x = [[own], [own_core], [own_a, own_b], [own_a_core, own_b_core]]
    near_ax = [[near_a], [near_a_core], [diag_a], [diag_a_core]]
    near_bx = [[near_b], [near_b_core], [diag_b], [diag_b_core]]
    near_x = [a + b for a, b in zip(near_ax, near_bx)]
    which = jnp.stack([t ^ i for i in range(4)]).astype(jnp.int32)

    lengths = seq_lengths.reshape(learners, learners)
    dests = seq_dest.reshape(learners, learners)
    offsets = seq_offset.reshape(learners, learners)
    starts = jnp.cumsum(lengths, axis=1) - lengths
    peer_ids = jnp.arange(learners, dtype=jnp.int32)
    rows = jnp.arange(row_count, dtype=jnp.int32)
    length = lax.dynamic_index_in_dim(lengths, me, 0, keepdims=False)
    start = lax.dynamic_index_in_dim(starts, me, 0, keepdims=False)
    dest = lax.dynamic_index_in_dim(dests, me, 0, keepdims=False)
    match = (dest[None, :] == peer_ids[:, None]).astype(jnp.int32)
    send_start = jnp.sum(match * start[None, :], axis=1)
    send_length = jnp.sum(match * length[None, :], axis=1)
    inside = (rows[:, None] >= start[None, :]) & (rows[:, None] < (start + length)[None, :])
    position = rows - jnp.sum(inside.astype(jnp.int32) * start[None, :], axis=1)
    cosine, sine = rope_tables(position)
    cosine = jnp.concatenate([cosine, cosine], axis=1)
    sine = jnp.concatenate([-sine, sine], axis=1)
    matched = (dests == me).astype(jnp.int32)
    run_start = jnp.sum(matched * offsets, axis=1)
    run_length = jnp.sum(matched * lengths, axis=1)

    window = min(row_count, -(-(slot + 16) // 128) * 128)

    def partial(c, blocks, *others):
        return projection(after(which, *others), blocks, weights[c])

    def finish(c, got, *others):
        ropes = (True, False) if c == 0 else (True, True)
        ending = (ropes, got, biases[c], cosine, sine)
        return projection(after(which, *others), own_x, weights[c], ending)

    def send(outgoing):
        return lax.all_to_all(outgoing, "dp", split_axis=0, concat_axis=0, tiled=True)

    def receive(c, incoming, before, *others):
        start_at = after(run_start, *others)
        return place(
            start_at, run_length, incoming, row_count, c - 1, w_query.shape[1], before
        )

    part_a = partial(0, near_ax)
    got_a = swap_x(part_a)
    part_b = partial(0, near_bx, part_a)
    got_b = swap_x(after(part_b, got_a))
    parts = [None, partial(1, near_x, part_b)]
    got = [None, swap_x(after(parts[1], got_b))]
    kv = finish(0, [got_a, got_b], parts[1])
    kv_slots = to_slots(send_start, send_length, kv, slot, window)
    parts.append(partial(2, near_x, kv_slots))
    out, incoming, result = [None], [None], None
    for c in range(1, len(weights)):
        if c + 1 < len(weights):
            got.append(swap_x(after(parts[c + 1], got[c])))
        rot = finish(c, [got[c]], parts[min(c + 1, len(weights) - 1)])
        out.append(attend(send_start, send_length, rot, kv_slots, window))
        incoming.append(send(out[c]))
        if c + 2 < len(weights):
            parts.append(partial(c + 2, near_x, out[c]))
        if c >= 2:
            result = receive(c - 1, incoming[c - 1], result, out[c])
    return receive(len(weights) - 1, incoming[-1], result)


def solution(mesh):
    placed = (
        P("dp", "tensor"),
        P(),
        P("dp", "tensor"),
        P("dp", "tensor"),
        P("dp", "tensor"),
        P("tensor"),
        P("tensor"),
        P("tensor"),
        P(),
        P(),
        P(),
    )
    fits_line = mesh.shape["dp"] == 8 and mesh.shape["tensor"] == 4
    return jax.shard_map(
        local_line if fits_line else local_any,
        mesh=mesh,
        in_specs=placed,
        out_specs=P("dp", "tensor"),
        check_vma=False,
    )
```

```python
import functools

import jax
import jax.numpy as jnp
from jax import lax
from jax.experimental import pallas as pl
from jax.experimental.pallas import tpu as pltpu
from jax.sharding import PartitionSpec as P

HD = 128

rope_base = 1000000.0
norm_eps = 1e-06
mask_value = -1e30
small_cost = pl.CostEstimate(flops=1024, bytes_accessed=1024, transcendentals=0)


def rope_tables(positions):
    half_dim = HD // 2
    frequency = rope_base ** (-(jnp.arange(half_dim).astype(jnp.float32) * 2.0 / HD))
    angles = positions.astype(jnp.float32)[:, None] * frequency[None, :]
    return (jnp.cos(angles), jnp.sin(angles))


def rotate(states, cosine, sine):
    half_dim = states.shape[-1] // 2
    first_half = states[..., :half_dim]
    second_half = states[..., half_dim:]
    cos_wide = cosine[:, None, :]
    sin_wide = sine[:, None, :]
    return jnp.concatenate(
        [
            first_half * cos_wide - second_half * sin_wide,
            second_half * cos_wide + first_half * sin_wide,
        ],
        axis=-1,
    )


def local_any(
    rollout_states,
    norm_gain,
    w_query,
    w_key,
    w_value,
    b_query,
    b_key,
    b_value,
    seq_lengths,
    seq_dest,
    seq_offset,
):
    learners = lax.axis_size("dp")
    own_index = lax.axis_index("dp")
    row_count, feature_count = rollout_states.shape
    capacity = 2 * row_count // learners - 1
    lengths = seq_lengths.reshape(learners, learners)
    dests = seq_dest.reshape(learners, learners)
    offsets = seq_offset.reshape(learners, learners)
    starts = jnp.cumsum(lengths, axis=1) - lengths
    peer_ids = jnp.arange(learners, dtype=jnp.int32)
    own_length = lax.dynamic_index_in_dim(lengths, own_index, 0, keepdims=False)
    own_start = lax.dynamic_index_in_dim(starts, own_index, 0, keepdims=False)
    own_dest = lax.dynamic_index_in_dim(dests, own_index, 0, keepdims=False)
    match_send = (own_dest[None, :] == peer_ids[:, None]).astype(jnp.int32)
    send_start = jnp.sum(match_send * own_start[None, :], axis=1)
    send_length = jnp.sum(match_send * own_length[None, :], axis=1)
    slot_index = jnp.arange(capacity, dtype=jnp.int32)
    pick_rows = send_start[:, None] + slot_index[None, :]
    padded = jnp.concatenate(
        [rollout_states, jnp.zeros((capacity, feature_count), rollout_states.dtype)], axis=0
    )
    live_slots = (slot_index[None, :] < send_length[:, None])[..., None]
    outgoing = jnp.where(
        live_slots, jnp.take(padded, pick_rows, axis=0), jnp.zeros((), rollout_states.dtype)
    )
    incoming = lax.all_to_all(outgoing, "dp", split_axis=0, concat_axis=0, tiled=True)
    matched = (dests == own_index).astype(jnp.int32)
    run_start = jnp.sum(matched * offsets, axis=1)
    run_length = jnp.sum(matched * lengths, axis=1)
    rows = jnp.arange(row_count, dtype=jnp.int32)
    inside = (
        (rows[:, None] >= run_start[None, :]) & (rows[:, None] < (run_start + run_length)[None, :])
    ).astype(jnp.int32)
    source_ids = jnp.sum(inside * peer_ids[None, :], axis=1)
    within_seq = rows - jnp.sum(inside * run_start[None, :], axis=1)
    arrived = jnp.take(
        incoming.reshape(learners * capacity, feature_count),
        source_ids * capacity + within_seq,
        axis=0,
    )
    gathered = lax.all_gather(arrived, "tensor", axis=1, tiled=True)
    widened = gathered.astype(jnp.float32)
    statistic = jnp.mean(widened * widened, axis=-1, keepdims=True)
    normed = (widened * lax.rsqrt(statistic + norm_eps) * norm_gain[None, :]).astype(jnp.bfloat16)
    full_query, full_key, full_value = (
        lax.all_gather(w_query, "dp", axis=0, tiled=True),
        lax.all_gather(w_key, "dp", axis=0, tiled=True),
        lax.all_gather(w_value, "dp", axis=0, tiled=True),
    )
    query = jnp.dot(normed, full_query, preferred_element_type=jnp.float32)
    key = jnp.dot(normed, full_key, preferred_element_type=jnp.float32)
    value = jnp.dot(normed, full_value, preferred_element_type=jnp.float32)
    query = query + b_query[None, :]
    key = key + b_key[None, :]
    value = value + b_value[None, :]
    heads_here = query.shape[1] // HD
    kv_here = key.shape[1] // HD
    group = heads_here // kv_here
    cosine, sine = rope_tables(within_seq)
    rot_query = rotate(query.reshape(row_count, heads_here, HD), cosine, sine).astype(jnp.bfloat16)
    rot_query = rot_query.reshape(row_count, kv_here, group, HD)
    rot_key = rotate(key.reshape(row_count, kv_here, HD), cosine, sine).astype(jnp.bfloat16)
    value_bf = value.reshape(row_count, kv_here, HD).astype(jnp.bfloat16)
    block_rows = min(512, row_count)

    def one_block(block_number):
        first_row = block_number * block_rows
        query_block = lax.dynamic_slice_in_dim(rot_query, first_row, block_rows, 0)
        query_source = lax.dynamic_slice_in_dim(source_ids, first_row, block_rows, 0)
        query_rows = first_row + jnp.arange(block_rows, dtype=jnp.int32)
        scores = jnp.einsum(
            "bcgd,kcd->cgbk", query_block, rot_key, preferred_element_type=jnp.float32
        )
        scores = scores * HD ** (-0.5)
        allowed = (source_ids[None, :] == query_source[:, None]) & (
            rows[None, :] <= query_rows[:, None]
        )
        scores = jnp.where(allowed[None, None], scores, mask_value)
        peak = jnp.max(scores, axis=-1, keepdims=True)
        raised = jnp.exp(scores - peak)
        weights = (raised / jnp.sum(raised, axis=-1, keepdims=True)).astype(jnp.bfloat16)
        context = jnp.einsum(
            "cgbk,kcd->bcgd", weights, value_bf, preferred_element_type=jnp.float32
        )
        return context.astype(jnp.bfloat16).reshape(block_rows, heads_here * HD)

    outputs = lax.map(one_block, jnp.arange(row_count // block_rows, dtype=jnp.int32))
    return outputs.reshape(row_count, heads_here * HD)


def line_order_kernel(off_ref, *refs):
    out_ref = refs[-1]
    feats = out_ref.shape[1]
    step = feats // 4
    for at in range(4):
        for spot in range(7):

            @pl.when(off_ref[at] == spot - 3)
            def _(at=at, ref=refs[spot]):
                @pl.loop(0, feats, step=step)
                def _(first):
                    here = pl.ds(pl.multiple_of(first, step), step)
                    out_ref[at, here, :] = ref[here, :]


def line_order(off, spots):
    feats, columns = spots[0].shape
    vmem = pl.BlockSpec(memory_space=pltpu.VMEM)
    return pl.pallas_call(
        line_order_kernel,
        in_specs=[pl.BlockSpec(memory_space=pltpu.SMEM)] + [vmem] * 7,
        out_specs=vmem,
        out_shape=jax.ShapeDtypeStruct((4, feats, columns), jnp.bfloat16),
        compiler_params=pltpu.CompilerParams(vmem_limit_bytes=12 * 2**20),
        cost_estimate=small_cost,
    )(off, *[keep(spot) for spot in spots])


def product_kernel(counts, ropes, which_ref, *refs):
    refs = list(refs)
    x_refs = [[refs.pop(0) for _ in range(n)] for n in counts[:4]]
    w_ref = refs.pop(0)
    part_refs = [refs.pop(0) for _ in range(counts[4])]
    if ropes:
        bias_ref, cos_ref, sin_ref = (refs.pop(0) for _ in range(3))
    out_ref, total = refs
    rows = out_ref.shape[0]
    tile = rows // max(counts)

    def piece_rows(pieces, first):
        size = pieces[0].shape[0]
        return pieces[first // size], pl.ds(first % size, tile)

    for i in range(4):

        @pl.when(pl.program_id(0) == i)
        def _(i=i):
            for first in range(0, rows, tile):
                here = pl.ds(first, tile)
                ref, at = piece_rows(x_refs[i], first)
                term = jnp.dot(ref[at, :], w_ref[0], preferred_element_type=jnp.float32)
                if i > 0:
                    term = total[here, :] + term
                if i < 3:
                    total[here, :] = term
                    continue
                if not ropes:
                    out_ref[here, :] = term.astype(out_ref.dtype)
                    continue
                ref, at = piece_rows(part_refs, first)
                term = term + ref[at, :].astype(jnp.float32) + bias_ref[...]
                for c, rope in enumerate(ropes):
                    head = term[:, c * HD : (c + 1) * HD]
                    if rope:
                        turned = pltpu.roll(head, HD // 2, 1)
                        head = head * cos_ref[here, :] + turned * sin_ref[here, :]
                    out_ref[here, c * HD : (c + 1) * HD] = head.astype(out_ref.dtype)


def keep(array):
    return pltpu.with_memory_space_constraint(array, pltpu.VMEM)


def projection(which, x_blocks, weights, out_type, finish=None):
    weights, first_column = weights
    columns = 2 * HD
    rows = sum(piece.shape[0] for piece in x_blocks[0])
    feats = weights.shape[1]
    counts = [len(pieces) for pieces in x_blocks]
    vmem = pl.BlockSpec(memory_space=pltpu.VMEM)
    operands = [keep(piece) for pieces in x_blocks for piece in pieces]
    in_specs = [vmem] * len(operands)
    block = first_column // columns
    operands.append(weights)
    in_specs.append(pl.BlockSpec((1, feats, columns), lambda i, which: (which[i], 0, block)))
    ropes = None
    if finish is None:
        counts.append(0)
    else:
        ropes, parts, bias, cosine, sine = finish
        counts.append(len(parts))
        operands += [keep(part) for part in parts]
        operands += [bias, keep(cosine), keep(sine)]
        in_specs += [vmem] * (len(parts) + 3)
    grid_spec = pltpu.PrefetchScalarGridSpec(
        num_scalar_prefetch=1,
        grid=(4,),
        in_specs=in_specs,
        out_specs=pl.BlockSpec((rows, columns), lambda i, which: (0, 0)),
        scratch_shapes=[pltpu.VMEM((rows, columns), jnp.float32)],
    )
    return pl.pallas_call(
        functools.partial(product_kernel, tuple(counts), ropes),
        grid_spec=grid_spec,
        out_shape=jax.ShapeDtypeStruct((rows, columns), out_type),
        compiler_params=pltpu.CompilerParams(vmem_limit_bytes=20 * 2**20),
        cost_estimate=small_cost,
    )(which, *operands)


def pick_rows(start, length, slot, window, ref):
    first = pl.multiple_of(jnp.minimum((start // 16) * 16, ref.shape[0] - window), 16)
    row_at = lax.broadcasted_iota(jnp.int32, (slot, window), 0)
    col_at = lax.broadcasted_iota(jnp.int32, (slot, window), 1)
    pick = jnp.where((col_at == row_at + (start - first)) & (row_at < length), 1.0, 0.0)
    rows = jnp.dot(
        pick.astype(jnp.bfloat16), ref[pl.ds(first, window), :], preferred_element_type=jnp.float32
    )
    return rows.astype(jnp.bfloat16)


def slots_kernel(slot, window, start_ref, len_ref, in_ref, out_ref):
    for s in range(out_ref.shape[0]):
        out_ref[s] = pick_rows(start_ref[s], len_ref[s], slot, window, in_ref)


def to_slots(starts, lens, array, slot, window):
    count, columns = starts.shape[0], array.shape[1]
    scalars = pl.BlockSpec(memory_space=pltpu.SMEM)
    vmem = pl.BlockSpec(memory_space=pltpu.VMEM)
    return pl.pallas_call(
        functools.partial(slots_kernel, slot, window),
        in_specs=[scalars, scalars, vmem],
        out_specs=vmem,
        out_shape=jax.ShapeDtypeStruct((count, slot, columns), jnp.bfloat16),
        compiler_params=pltpu.CompilerParams(vmem_limit_bytes=8 * 2**20),
        cost_estimate=small_cost,
    )(starts, lens, array)


def attend_kernel(heads, window, start_ref, len_ref, q_ref, kv_ref, out_ref):
    batch, slot = out_ref.shape[:2]
    half = slot // 2
    group = pl.program_id(0) * batch
    for s in range(batch):
        query = pick_rows(start_ref[group + s], len_ref[group + s], slot, window, q_ref)
        for block in range(2):
            width = (block + 1) * half
            stacked = jnp.concatenate(
                [
                    query[block * half : width, h * HD : (h + 1) * HD]
                    for h in range(heads)
                ],
                axis=0,
            )
            scores = lax.dot_general(
                stacked,
                kv_ref[s, :width, :HD],
                (((1,), (1,)), ((), ())),
                preferred_element_type=jnp.float32,
            )
            row_at = lax.broadcasted_iota(jnp.int32, scores.shape, 0) & (half - 1)
            col_at = lax.broadcasted_iota(jnp.int32, scores.shape, 1)
            scores = jnp.where(
                col_at <= row_at + block * half, scores * HD ** (-0.5), mask_value
            )
            peak = jnp.max(scores, axis=-1, keepdims=True)
            raised = jnp.exp(scores - peak)
            weights = raised * (1.0 / jnp.sum(raised, axis=-1, keepdims=True))
            context = jnp.dot(
                weights.astype(jnp.bfloat16), kv_ref[s, :width, HD:], preferred_element_type=jnp.float32
            ).astype(out_ref.dtype)
            for h in range(heads):
                out_ref[s, block * half : width, h * HD : (h + 1) * HD] = context[
                    h * half : (h + 1) * half
                ]


def attend(starts, lens, query, kv_slots, window):
    rows, columns = query.shape
    count, slot = kv_slots.shape[:2]
    batch = 2
    heads = columns // HD
    grid_spec = pltpu.PrefetchScalarGridSpec(
        num_scalar_prefetch=2,
        grid=(count // batch,),
        in_specs=[
            pl.BlockSpec((rows, columns), lambda s, a, b: (0, 0)),
            pl.BlockSpec((batch, slot, 2 * HD), lambda s, a, b: (s, 0, 0)),
        ],
        out_specs=pl.BlockSpec((batch, slot, columns), lambda s, a, b: (s, 0, 0)),
    )
    return pl.pallas_call(
        functools.partial(attend_kernel, heads, window),
        grid_spec=grid_spec,
        out_shape=jax.ShapeDtypeStruct((count, slot, columns), jnp.bfloat16),
        compiler_params=pltpu.CompilerParams(vmem_limit_bytes=8 * 2**20),
        cost_estimate=small_cost,
    )(starts, lens, query, kv_slots)


def place_kernel(count, slot, window, start_ref, len_ref, in_ref, *rest):
    out_ref, total = rest[-2:]
    rows = total.shape[0]
    total[...] = jnp.zeros_like(total)
    row_at = lax.broadcasted_iota(jnp.int32, (window, slot), 0)
    col_at = lax.broadcasted_iota(jnp.int32, (window, slot), 1)
    for s in range(count):
        start = start_ref[s]
        first = pl.multiple_of(jnp.minimum((start // 8) * 8, rows - window), 8)
        pick = jnp.where(
            (row_at == col_at + (start - first)) & (col_at < len_ref[s]), 1.0, 0.0
        ).astype(jnp.bfloat16)
        total[pl.ds(first, window), :] += jnp.dot(
            pick, in_ref[s], preferred_element_type=jnp.float32
        )
    out_ref[...] = total[...].astype(out_ref.dtype)


def place(starts, lens, slots, rows, which, all_columns, before):
    count, slot, columns = slots.shape
    window = min(rows, slot + 8)
    in_specs = [pl.BlockSpec((count, slot, columns), lambda r, a, b: (0, 0, 0))]
    operands, aliases = [slots], {}
    if before is not None:
        in_specs.append(pl.BlockSpec(memory_space=pl.ANY))
        operands.append(before)
        aliases = {3: 0}
    grid_spec = pltpu.PrefetchScalarGridSpec(
        num_scalar_prefetch=2,
        grid=(1,),
        in_specs=in_specs,
        out_specs=pl.BlockSpec((rows, columns), lambda r, a, b: (0, which)),
        scratch_shapes=[pltpu.VMEM((rows, columns), jnp.float32)],
    )
    return pl.pallas_call(
        functools.partial(place_kernel, count, slot, window),
        grid_spec=grid_spec,
        out_shape=jax.ShapeDtypeStruct((rows, all_columns), jnp.bfloat16),
        input_output_aliases=aliases,
        compiler_params=pltpu.CompilerParams(vmem_limit_bytes=8 * 2**20),
        cost_estimate=small_cost,
    )(starts, lens, *operands)


def local_line(
    rollout_states,
    norm_gain,
    w_query,
    w_key,
    w_value,
    b_query,
    b_key,
    b_value,
    seq_lengths,
    seq_dest,
    seq_offset,
):
    learners = lax.axis_size("dp")
    line = learners // 2
    me = lax.axis_index("dp")
    z, x = me // 2, me % 2
    t = lax.axis_index("tensor")
    row_count, feature_count = rollout_states.shape
    slot = 2 * row_count // learners
    half = feature_count // 2
    middle = row_count // 2

    def after(array, *others):
        return lax.optimization_barrier((array, *others))[0]

    def swap_x(array):
        return lax.ppermute(array, "dp", [(i, i ^ 1) for i in range(learners)])

    def swap_y(array):
        return lax.ppermute(array, "tensor", [(i, i ^ 2) for i in range(4)])

    def swap_core(array):
        return lax.ppermute(array, "tensor", [(i, i ^ 1) for i in range(4)])

    def up(array, first):
        return lax.ppermute(array, "dp", [(i, i + 2) for i in range(2 * first, learners - 2)])

    def down(array, first):
        return lax.ppermute(array, "dp", [(i, i - 2) for i in range(2, learners - 2 * first)])

    wide = 2 * HD
    along_z = [[2 * i + j for i in range(line)] for j in range(2)]
    groups = [
        jnp.concatenate([w_key, w_value, w_query[:, :wide]], axis=1),
        w_query[:, wide : 3 * wide],
    ]
    weights = []
    for group in groups:
        gathered = lax.all_gather(group, "dp", axis_index_groups=along_z)
        for low in range(0, group.shape[1], wide):
            weights.append((gathered, low))
    blocks = [0, 3, 1, 2]
    biases = [jnp.concatenate([b_key, b_value])[None, :]]
    for block in blocks:
        biases.append(b_query[None, block * wide : (block + 1) * wide])

    states = rollout_states
    widened = states.astype(jnp.float32)
    squares = jnp.sum(widened * widened, axis=-1)
    squares = squares + swap_core(squares)
    squares = squares + swap_y(squares)
    scale = lax.rsqrt(squares[:, None] / (4 * feature_count) + norm_eps)

    def normed(first):
        part = lax.dynamic_slice_in_dim(states, first, half, 1).astype(jnp.float32)
        gain = lax.dynamic_slice_in_dim(norm_gain, t * feature_count + first, half, 0)
        return (part * scale * gain[None, :]).astype(jnp.bfloat16)

    own, give = normed(x * half), normed((1 - x) * half)

    near_a = swap_x(give[:middle])
    own_a = swap_y(own[:middle])
    own_core = swap_core(own)
    near_b = swap_x(after(give[middle:], near_a))
    diag_a = swap_y(after(near_a, own_a))
    near_a_core = swap_core(near_a)
    own_a_core = swap_core(after(own_a, near_a))
    diag_b = swap_y(after(near_b, diag_a))
    near_b_core = swap_core(after(near_b, diag_a))
    diag_a_core = swap_core(after(diag_a, near_b))
    own_b = swap_y(after(own[middle:], diag_b))
    diag_b_core = swap_core(diag_b)
    own_b_core = swap_core(own_b)
    last = after(w_query[:, 3 * wide :], near_a, own_a)
    ups, downs = [last], [last]
    for step, others in enumerate(((near_b, diag_a), (diag_b,), ())):
        ups.append(up(ups[-1], step))
        downs.append(down(downs[-1], step))
        if others:
            ups[-1], downs[-1] = lax.optimization_barrier((ups[-1], downs[-1], *others))[:2]
    off = (jnp.arange(line) - z).astype(jnp.int32)
    weights.insert(2, (line_order(off, ups[:0:-1] + downs), 0))
    own_x = [[own], [own_core], [own_a, own_b], [own_a_core, own_b_core]]
    near_ax = [[near_a], [near_a_core], [diag_a], [diag_a_core]]
    near_bx = [[near_b], [near_b_core], [diag_b], [diag_b_core]]
    near_x = [a + b for a, b in zip(near_ax, near_bx)]
    which = jnp.stack([t ^ i for i in range(4)]).astype(jnp.int32)

    lengths = seq_lengths.reshape(learners, learners)
    dests = seq_dest.reshape(learners, learners)
    offsets = seq_offset.reshape(learners, learners)
    starts = jnp.cumsum(lengths, axis=1) - lengths
    peer_ids = jnp.arange(learners, dtype=jnp.int32)
    rows = jnp.arange(row_count, dtype=jnp.int32)
    length = lax.dynamic_index_in_dim(lengths, me, 0, keepdims=False)
    start = lax.dynamic_index_in_dim(starts, me, 0, keepdims=False)
    dest = lax.dynamic_index_in_dim(dests, me, 0, keepdims=False)
    match = (dest[None, :] == peer_ids[:, None]).astype(jnp.int32)
    send_start = jnp.sum(match * start[None, :], axis=1)
    send_length = jnp.sum(match * length[None, :], axis=1)
    inside = (rows[:, None] >= start[None, :]) & (rows[:, None] < (start + length)[None, :])
    position = rows - jnp.sum(inside.astype(jnp.int32) * start[None, :], axis=1)
    cosine, sine = rope_tables(position)
    cosine = jnp.concatenate([cosine, cosine], axis=1)
    sine = jnp.concatenate([-sine, sine], axis=1)
    matched = (dests == me).astype(jnp.int32)
    run_start = jnp.sum(matched * offsets, axis=1)
    run_length = jnp.sum(matched * lengths, axis=1)

    window = min(row_count, -(-(slot + 16) // 128) * 128)

    def partial(c, x_blocks, *others):
        out_type = jnp.float32 if c == 0 else jnp.bfloat16
        return projection(after(which, *others), x_blocks, weights[c], out_type)

    def finish(c, got, *others):
        ropes = (True, False) if c == 0 else (True, True)
        ending = (ropes, got, biases[c], cosine, sine)
        return projection(after(which, *others), own_x, weights[c], jnp.bfloat16, ending)

    def send(outgoing):
        return lax.all_to_all(outgoing, "dp", split_axis=0, concat_axis=0, tiled=True)

    def receive(c, incoming, before, *others):
        start_at = after(run_start, *others)
        return place(
            start_at, run_length, incoming, row_count, blocks[c - 1], w_query.shape[1], before
        )

    def contexts(c, got, tie, *others):
        rot = finish(c, [got], *others)
        return attend(after(send_start, tie), send_length, rot, kv_slots, window)

    part_a = partial(0, near_ax)
    got_a = swap_x(part_a)
    part_b = partial(0, near_bx, part_a)
    got_b = swap_x(after(part_b, got_a))
    part_1 = partial(1, near_x, part_b)
    got_1 = swap_x(after(part_1, got_b))
    kv = finish(0, [got_a, got_b], part_1)
    kv_slots = to_slots(send_start, send_length, kv, slot, window)
    part_2 = partial(2, near_x, kv_slots)
    got_2 = swap_x(after(part_2, got_1))
    out_1 = contexts(1, got_1, got_2, part_2)
    in_1 = send(out_1)
    out_2 = contexts(2, got_2, out_1)
    in_2 = send(out_2)
    part_3 = partial(3, near_x, out_2)
    got_3 = swap_x(part_3)
    part_4 = partial(4, near_x, part_3)
    got_4 = swap_x(after(part_4, got_3))
    out_3 = contexts(3, got_3, got_4, part_4)
    in_3 = send(out_3)
    out_4 = contexts(4, got_4, out_3)
    in_4 = send(out_4)
    result = receive(1, in_1, None, out_3)
    result = receive(2, in_2, result, out_4)
    result = receive(3, in_3, result, out_4)
    return receive(4, in_4, result)


def solution(mesh):
    placed = (
        P("dp", "tensor"),
        P(),
        P("dp", "tensor"),
        P("dp", "tensor"),
        P("dp", "tensor"),
        P("tensor"),
        P("tensor"),
        P("tensor"),
        P(),
        P(),
        P(),
    )
    fits_line = mesh.shape["dp"] == 8 and mesh.shape["tensor"] == 4
    return jax.shard_map(
        local_line if fits_line else local_any,
        mesh=mesh,
        in_specs=placed,
        out_specs=P("dp", "tensor"),
        check_vma=False,
    )
```

```python
import functools

import jax
import jax.numpy as jnp
from jax import lax
from jax.experimental import pallas as pl
from jax.experimental.pallas import tpu as pltpu
from jax.sharding import PartitionSpec as P

HD = 128

rope_base = 1000000.0
norm_eps = 1e-06
mask_value = -1e30
small_cost = pl.CostEstimate(flops=1024, bytes_accessed=1024, transcendentals=0)


def rope_tables(positions):
    half_dim = HD // 2
    frequency = rope_base ** (-(jnp.arange(half_dim).astype(jnp.float32) * 2.0 / HD))
    angles = positions.astype(jnp.float32)[:, None] * frequency[None, :]
    return (jnp.cos(angles), jnp.sin(angles))


def rotate(states, cosine, sine):
    half_dim = states.shape[-1] // 2
    first_half = states[..., :half_dim]
    second_half = states[..., half_dim:]
    cos_wide = cosine[:, None, :]
    sin_wide = sine[:, None, :]
    return jnp.concatenate(
        [
            first_half * cos_wide - second_half * sin_wide,
            second_half * cos_wide + first_half * sin_wide,
        ],
        axis=-1,
    )


def local_any(
    rollout_states,
    norm_gain,
    w_query,
    w_key,
    w_value,
    b_query,
    b_key,
    b_value,
    seq_lengths,
    seq_dest,
    seq_offset,
):
    learners = lax.axis_size("dp")
    own_index = lax.axis_index("dp")
    row_count, feature_count = rollout_states.shape
    capacity = 2 * row_count // learners - 1
    lengths = seq_lengths.reshape(learners, learners)
    dests = seq_dest.reshape(learners, learners)
    offsets = seq_offset.reshape(learners, learners)
    starts = jnp.cumsum(lengths, axis=1) - lengths
    peer_ids = jnp.arange(learners, dtype=jnp.int32)
    own_length = lax.dynamic_index_in_dim(lengths, own_index, 0, keepdims=False)
    own_start = lax.dynamic_index_in_dim(starts, own_index, 0, keepdims=False)
    own_dest = lax.dynamic_index_in_dim(dests, own_index, 0, keepdims=False)
    match_send = (own_dest[None, :] == peer_ids[:, None]).astype(jnp.int32)
    send_start = jnp.sum(match_send * own_start[None, :], axis=1)
    send_length = jnp.sum(match_send * own_length[None, :], axis=1)
    slot_index = jnp.arange(capacity, dtype=jnp.int32)
    pick_rows = send_start[:, None] + slot_index[None, :]
    padded = jnp.concatenate(
        [rollout_states, jnp.zeros((capacity, feature_count), rollout_states.dtype)], axis=0
    )
    live_slots = (slot_index[None, :] < send_length[:, None])[..., None]
    outgoing = jnp.where(
        live_slots, jnp.take(padded, pick_rows, axis=0), jnp.zeros((), rollout_states.dtype)
    )
    incoming = lax.all_to_all(outgoing, "dp", split_axis=0, concat_axis=0, tiled=True)
    matched = (dests == own_index).astype(jnp.int32)
    run_start = jnp.sum(matched * offsets, axis=1)
    run_length = jnp.sum(matched * lengths, axis=1)
    rows = jnp.arange(row_count, dtype=jnp.int32)
    inside = (
        (rows[:, None] >= run_start[None, :]) & (rows[:, None] < (run_start + run_length)[None, :])
    ).astype(jnp.int32)
    source_ids = jnp.sum(inside * peer_ids[None, :], axis=1)
    within_seq = rows - jnp.sum(inside * run_start[None, :], axis=1)
    arrived = jnp.take(
        incoming.reshape(learners * capacity, feature_count),
        source_ids * capacity + within_seq,
        axis=0,
    )
    gathered = lax.all_gather(arrived, "tensor", axis=1, tiled=True)
    widened = gathered.astype(jnp.float32)
    statistic = jnp.mean(widened * widened, axis=-1, keepdims=True)
    normed = (widened * lax.rsqrt(statistic + norm_eps) * norm_gain[None, :]).astype(jnp.bfloat16)
    full_query, full_key, full_value = (
        lax.all_gather(w_query, "dp", axis=0, tiled=True),
        lax.all_gather(w_key, "dp", axis=0, tiled=True),
        lax.all_gather(w_value, "dp", axis=0, tiled=True),
    )
    query = jnp.dot(normed, full_query, preferred_element_type=jnp.float32)
    key = jnp.dot(normed, full_key, preferred_element_type=jnp.float32)
    value = jnp.dot(normed, full_value, preferred_element_type=jnp.float32)
    query = query + b_query[None, :]
    key = key + b_key[None, :]
    value = value + b_value[None, :]
    heads_here = query.shape[1] // HD
    kv_here = key.shape[1] // HD
    group = heads_here // kv_here
    cosine, sine = rope_tables(within_seq)
    rot_query = rotate(query.reshape(row_count, heads_here, HD), cosine, sine).astype(jnp.bfloat16)
    rot_query = rot_query.reshape(row_count, kv_here, group, HD)
    rot_key = rotate(key.reshape(row_count, kv_here, HD), cosine, sine).astype(jnp.bfloat16)
    value_bf = value.reshape(row_count, kv_here, HD).astype(jnp.bfloat16)
    block_rows = min(512, row_count)

    def one_block(block_number):
        first_row = block_number * block_rows
        query_block = lax.dynamic_slice_in_dim(rot_query, first_row, block_rows, 0)
        query_source = lax.dynamic_slice_in_dim(source_ids, first_row, block_rows, 0)
        query_rows = first_row + jnp.arange(block_rows, dtype=jnp.int32)
        scores = jnp.einsum(
            "bcgd,kcd->cgbk", query_block, rot_key, preferred_element_type=jnp.float32
        )
        scores = scores * HD ** (-0.5)
        allowed = (source_ids[None, :] == query_source[:, None]) & (
            rows[None, :] <= query_rows[:, None]
        )
        scores = jnp.where(allowed[None, None], scores, mask_value)
        peak = jnp.max(scores, axis=-1, keepdims=True)
        raised = jnp.exp(scores - peak)
        weights = (raised / jnp.sum(raised, axis=-1, keepdims=True)).astype(jnp.bfloat16)
        context = jnp.einsum(
            "cgbk,kcd->bcgd", weights, value_bf, preferred_element_type=jnp.float32
        )
        return context.astype(jnp.bfloat16).reshape(block_rows, heads_here * HD)

    outputs = lax.map(one_block, jnp.arange(row_count // block_rows, dtype=jnp.int32))
    return outputs.reshape(row_count, heads_here * HD)


def product_kernel(counts, ropes, lanes, which_ref, *refs):
    refs = list(refs)
    x_refs = [[refs.pop(0) for _ in range(n)] for n in counts[:4]]
    w_ref = refs.pop(0)
    part_refs = [refs.pop(0) for _ in range(counts[4])]
    if ropes:
        bias_ref, angle_ref = (refs.pop(0) for _ in range(2))
    out_ref, w_buf, sems = refs
    rows = out_ref.shape[0]
    tile = rows // max(counts)
    copies = [
        pltpu.make_async_copy(w_ref.at[which_ref[i], :, lanes], w_buf.at[i], sems.at[i])
        for i in range(4)
    ]
    for copy in copies:
        copy.start()

    def piece_rows(pieces, first):
        size = pieces[0].shape[0]
        return pieces[first // size], pl.ds(first % size, tile)

    for first in range(0, rows, tile):
        here = pl.ds(first, tile)
        term = None
        for i in range(4):
            ref, at = piece_rows(x_refs[i], first)
            if first == 0:
                copies[i].wait()
            dot = jnp.dot(ref[at, :], w_buf[i], preferred_element_type=jnp.float32)
            term = dot if term is None else term + dot
        if not ropes:
            out_ref[here, :] = term.astype(out_ref.dtype)
            continue
        ref, at = piece_rows(part_refs, first)
        term = term + ref[at, :].astype(jnp.float32) + bias_ref[...]
        angle = angle_ref[here, :]
        turned_angle = pltpu.roll(angle, HD // 2, 1)
        low = lax.broadcasted_iota(jnp.int32, angle.shape, 1) < HD // 2
        cosine = jnp.where(low, angle, turned_angle)
        sine = jnp.where(low, -turned_angle, angle)
        for c, rope in enumerate(ropes):
            head = term[:, c * HD : (c + 1) * HD]
            if rope:
                head = head * cosine + pltpu.roll(head, HD // 2, 1) * sine
            out_ref[here, c * HD : (c + 1) * HD] = head.astype(out_ref.dtype)


def keep(array):
    return pltpu.with_memory_space_constraint(array, pltpu.VMEM)


def projection(which, x_blocks, weights, out_type, finish=None):
    weights, first_column = weights
    columns = 2 * HD
    rows = sum(piece.shape[0] for piece in x_blocks[0])
    counts = [len(pieces) for pieces in x_blocks]
    vmem = pl.BlockSpec(memory_space=pltpu.VMEM)
    operands = [keep(piece) for pieces in x_blocks for piece in pieces]
    in_specs = [vmem] * len(operands) + [pl.BlockSpec(memory_space=pl.ANY)]
    operands.append(weights)
    ropes = None
    if finish is None:
        counts.append(0)
    else:
        ropes, parts, bias, angles = finish
        counts.append(len(parts))
        operands += [keep(part) for part in parts]
        operands += [bias, keep(angles)]
        in_specs += [vmem] * (len(parts) + 2)
    return pl.pallas_call(
        functools.partial(product_kernel, tuple(counts), ropes, pl.ds(first_column, columns)),
        in_specs=[pl.BlockSpec(memory_space=pltpu.SMEM)] + in_specs,
        out_specs=vmem,
        out_shape=pltpu.VMEM((rows, columns), out_type),
        scratch_shapes=[
            pltpu.VMEM((4, weights.shape[1], columns), jnp.bfloat16),
            pltpu.SemaphoreType.DMA((4,)),
        ],
        compiler_params=pltpu.CompilerParams(vmem_limit_bytes=12 * 2**20),
        cost_estimate=small_cost,
    )(which, *operands)


def pick_rows(start, length, slot, window, ref):
    first = pl.multiple_of(jnp.minimum((start // 16) * 16, ref.shape[0] - window), 16)
    row_at = lax.broadcasted_iota(jnp.int32, (slot, window), 0)
    col_at = lax.broadcasted_iota(jnp.int32, (slot, window), 1)
    pick = jnp.where((col_at == row_at + (start - first)) & (row_at < length), 1.0, 0.0)
    rows = jnp.dot(
        pick.astype(jnp.bfloat16), ref[pl.ds(first, window), :], preferred_element_type=jnp.float32
    )
    return rows.astype(jnp.bfloat16)


def slots_kernel(slot, window, start_ref, len_ref, in_ref, out_ref):
    for s in range(out_ref.shape[0]):
        out_ref[s] = pick_rows(start_ref[s], len_ref[s], slot, window, in_ref)


def to_slots(starts, lens, array, slot, window):
    count, columns = starts.shape[0], array.shape[1]
    scalars = pl.BlockSpec(memory_space=pltpu.SMEM)
    vmem = pl.BlockSpec(memory_space=pltpu.VMEM)
    return pl.pallas_call(
        functools.partial(slots_kernel, slot, window),
        in_specs=[scalars, scalars, vmem],
        out_specs=vmem,
        out_shape=pltpu.VMEM((count, slot, columns), jnp.bfloat16),
        compiler_params=pltpu.CompilerParams(vmem_limit_bytes=8 * 2**20),
        cost_estimate=small_cost,
    )(starts, lens, keep(array))


def attend_kernel(heads, window, batch, start_ref, len_ref, q_ref, kv_ref, out_ref):
    count, slot = out_ref.shape[:2]
    half = slot // 2

    @pl.loop(0, count, step=batch)
    def _(group):
        for s in range(batch):
            query = pick_rows(start_ref[group + s], len_ref[group + s], slot, window, q_ref)
            for block in range(2):
                width = (block + 1) * half
                stacked = jnp.concatenate(
                    [query[block * half : width, h * HD : (h + 1) * HD] for h in range(heads)],
                    axis=0,
                )
                scores = lax.dot_general(
                    stacked,
                    kv_ref[group + s, :width, :HD],
                    (((1,), (1,)), ((), ())),
                    preferred_element_type=jnp.float32,
                )
                row_at = lax.broadcasted_iota(jnp.int32, scores.shape, 0) & (half - 1)
                col_at = lax.broadcasted_iota(jnp.int32, scores.shape, 1)
                scores = jnp.where(
                    col_at <= row_at + block * half, scores * HD ** (-0.5), mask_value
                )
                peak = jnp.max(scores, axis=-1, keepdims=True)
                raised = jnp.exp(scores - peak)
                weights = raised * (1.0 / jnp.sum(raised, axis=-1, keepdims=True))
                context = jnp.dot(
                    weights.astype(jnp.bfloat16),
                    kv_ref[group + s, :width, HD:],
                    preferred_element_type=jnp.float32,
                ).astype(out_ref.dtype)
                for h in range(heads):
                    out_ref[group + s, block * half : width, h * HD : (h + 1) * HD] = context[
                        h * half : (h + 1) * half
                    ]


def attend(starts, lens, query, kv_slots, window):
    columns = query.shape[1]
    count, slot = kv_slots.shape[:2]
    scalars = pl.BlockSpec(memory_space=pltpu.SMEM)
    vmem = pl.BlockSpec(memory_space=pltpu.VMEM)
    return pl.pallas_call(
        functools.partial(attend_kernel, columns // HD, window, 2),
        in_specs=[scalars, scalars, vmem, vmem],
        out_specs=vmem,
        out_shape=pltpu.VMEM((count, slot, columns), jnp.bfloat16),
        compiler_params=pltpu.CompilerParams(vmem_limit_bytes=8 * 2**20),
        cost_estimate=small_cost,
    )(starts, lens, keep(query), keep(kv_slots))


def place_kernel(count, slot, window, start_ref, len_ref, in_ref, *rest):
    out_ref, total = rest[-2:]
    rows = total.shape[0]
    total[...] = jnp.zeros_like(total)
    row_at = lax.broadcasted_iota(jnp.int32, (window, slot), 0)
    col_at = lax.broadcasted_iota(jnp.int32, (window, slot), 1)
    for s in range(count):
        start = start_ref[s]
        first = pl.multiple_of(jnp.minimum((start // 8) * 8, rows - window), 8)
        pick = jnp.where(
            (row_at == col_at + (start - first)) & (col_at < len_ref[s]), 1.0, 0.0
        ).astype(jnp.bfloat16)
        total[pl.ds(first, window), :] += jnp.dot(
            pick, in_ref[s], preferred_element_type=jnp.float32
        )
    out_ref[...] = total[...].astype(out_ref.dtype)


def place(starts, lens, slots, rows, which, all_columns, before):
    count, slot, columns = slots.shape
    window = min(rows, slot + 8)
    in_specs = [pl.BlockSpec((count, slot, columns), lambda r, a, b: (0, 0, 0))]
    operands, aliases = [slots], {}
    if before is not None:
        in_specs.append(pl.BlockSpec(memory_space=pl.ANY))
        operands.append(before)
        aliases = {3: 0}
    grid_spec = pltpu.PrefetchScalarGridSpec(
        num_scalar_prefetch=2,
        grid=(1,),
        in_specs=in_specs,
        out_specs=pl.BlockSpec((rows, columns), lambda r, a, b: (0, which)),
        scratch_shapes=[pltpu.VMEM((rows, columns), jnp.float32)],
    )
    return pl.pallas_call(
        functools.partial(place_kernel, count, slot, window),
        grid_spec=grid_spec,
        out_shape=jax.ShapeDtypeStruct((rows, all_columns), jnp.bfloat16),
        input_output_aliases=aliases,
        compiler_params=pltpu.CompilerParams(vmem_limit_bytes=8 * 2**20),
        cost_estimate=small_cost,
    )(starts, lens, *operands)


def local_line(
    rollout_states,
    norm_gain,
    w_query,
    w_key,
    w_value,
    b_query,
    b_key,
    b_value,
    seq_lengths,
    seq_dest,
    seq_offset,
):
    learners = lax.axis_size("dp")
    line = learners // 2
    me = lax.axis_index("dp")
    z, x = me // 2, me % 2
    t = lax.axis_index("tensor")
    row_count, feature_count = rollout_states.shape
    slot = 2 * row_count // learners
    half = feature_count // 2
    middle = row_count // 2

    def after(array, *others):
        return lax.optimization_barrier((array, *others))[0]

    def swap_x(array):
        return lax.ppermute(array, "dp", [(i, i ^ 1) for i in range(learners)])

    def swap_y(array):
        return lax.ppermute(array, "tensor", [(i, i ^ 2) for i in range(4)])

    def swap_core(array):
        return lax.ppermute(array, "tensor", [(i, i ^ 1) for i in range(4)])

    wide = 2 * HD
    along_z = [[2 * i + j for i in range(line)] for j in range(2)]
    groups = [
        jnp.concatenate([w_key, w_value, w_query[:, : 2 * wide]], axis=1),
        w_query[:, 2 * wide :],
    ]
    weights = []
    for group in groups:
        gathered = lax.all_gather(group, "dp", axis_index_groups=along_z)
        gathered = pltpu.with_memory_space_constraint(gathered, pltpu.HBM)
        for low in range(0, group.shape[1], wide):
            weights.append((gathered, low))
    biases = [jnp.concatenate([b_key, b_value])[None, :]]
    for low in range(0, w_query.shape[1], wide):
        biases.append(b_query[None, low : low + wide])

    states = rollout_states
    widened = states.astype(jnp.float32)
    squares = jnp.sum(widened * widened, axis=-1)
    squares = squares + swap_core(squares)
    squares = squares + swap_y(squares)
    scale = lax.rsqrt(squares[:, None] / (4 * feature_count) + norm_eps)

    def normed(first):
        part = lax.dynamic_slice_in_dim(states, first, half, 1).astype(jnp.float32)
        gain = lax.dynamic_slice_in_dim(norm_gain, t * feature_count + first, half, 0)
        return (part * scale * gain[None, :]).astype(jnp.bfloat16)

    own, give = normed(x * half), normed((1 - x) * half)

    near_a = swap_x(give[:middle])
    own_a = swap_y(own[:middle])
    own_core = swap_core(own)
    near_b = swap_x(after(give[middle:], near_a))
    diag_a = swap_y(after(near_a, own_a))
    near_a_core = swap_core(near_a)
    own_a_core = swap_core(after(own_a, near_a))
    diag_b = swap_y(after(near_b, diag_a))
    near_b_core = swap_core(after(near_b, diag_a))
    diag_a_core = swap_core(after(diag_a, near_b))
    own_b = swap_y(after(own[middle:], diag_b))
    diag_b_core = swap_core(diag_b)
    own_b_core = swap_core(own_b)
    own_x = [[own], [own_core], [own_a, own_b], [own_a_core, own_b_core]]
    near_ax = [[near_a], [near_a_core], [diag_a], [diag_a_core]]
    near_bx = [[near_b], [near_b_core], [diag_b], [diag_b_core]]
    near_x = [a + b for a, b in zip(near_ax, near_bx)]
    which = jnp.stack([t ^ i for i in range(4)]).astype(jnp.int32)

    lengths = seq_lengths.reshape(learners, learners)
    dests = seq_dest.reshape(learners, learners)
    offsets = seq_offset.reshape(learners, learners)
    starts = jnp.cumsum(lengths, axis=1) - lengths
    peer_ids = jnp.arange(learners, dtype=jnp.int32)
    rows = jnp.arange(row_count, dtype=jnp.int32)
    length = lax.dynamic_index_in_dim(lengths, me, 0, keepdims=False)
    start = lax.dynamic_index_in_dim(starts, me, 0, keepdims=False)
    dest = lax.dynamic_index_in_dim(dests, me, 0, keepdims=False)
    match = (dest[None, :] == peer_ids[:, None]).astype(jnp.int32)
    send_start = jnp.sum(match * start[None, :], axis=1)
    send_length = jnp.sum(match * length[None, :], axis=1)
    inside = (rows[:, None] >= start[None, :]) & (rows[:, None] < (start + length)[None, :])
    position = rows - jnp.sum(inside.astype(jnp.int32) * start[None, :], axis=1)
    angles = jnp.concatenate(rope_tables(position), axis=1)
    matched = (dests == me).astype(jnp.int32)
    run_start = jnp.sum(matched * offsets, axis=1)
    run_length = jnp.sum(matched * lengths, axis=1)

    window = min(row_count, -(-(slot + 16) // 128) * 128)

    def partial(c, x_blocks, *others):
        out_type = jnp.float32 if c == 0 else jnp.bfloat16
        return projection(after(which, *others), x_blocks, weights[c], out_type)

    def finish(c, got, *others):
        ropes = (True, False) if c == 0 else (True, True)
        ending = (ropes, got, biases[c], angles)
        return projection(after(which, *others), own_x, weights[c], jnp.bfloat16, ending)

    def send(outgoing):
        return lax.all_to_all(outgoing, "dp", split_axis=0, concat_axis=0, tiled=True)

    def receive(c, incoming, before, *others):
        start_at = after(run_start, *others)
        return place(
            start_at, run_length, incoming, row_count, c - 1, w_query.shape[1], before
        )

    def contexts(c, got, tie, *others):
        rot = finish(c, [got], *others)
        return attend(after(send_start, tie), send_length, rot, kv_slots, window)

    part_a = partial(0, near_ax)
    got_a = swap_x(part_a)
    part_b = partial(0, near_bx, part_a)
    got_b = swap_x(after(part_b, got_a))
    part_1 = partial(1, near_x, part_b)
    got_1 = swap_x(after(part_1, got_b))
    kv = finish(0, [got_a, got_b], part_1)
    kv_slots = to_slots(send_start, send_length, kv, slot, window)
    part_2 = partial(2, near_x, kv_slots)
    got_2 = swap_x(after(part_2, got_1))
    out_1 = contexts(1, got_1, got_2, part_2)
    in_1 = send(out_1)
    out_2 = contexts(2, got_2, out_1)
    in_2 = send(after(out_2, in_1))
    part_3 = partial(3, near_x, out_2)
    got_3 = swap_x(part_3)
    part_4 = partial(4, near_x, part_3)
    got_4 = swap_x(after(part_4, got_3))
    out_3 = contexts(3, got_3, got_4, part_4)
    in_3 = send(after(out_3, in_2))
    out_4 = contexts(4, got_4, out_3)
    in_4 = send(after(out_4, in_3))
    result = receive(1, in_1, None, part_4)
    result = receive(2, in_2, result, out_4)
    result = receive(3, in_3, result, out_4)
    return receive(4, in_4, result)


def solution(mesh):
    placed = (
        P("dp", "tensor"),
        P(),
        P("dp", "tensor"),
        P("dp", "tensor"),
        P("dp", "tensor"),
        P("tensor"),
        P("tensor"),
        P("tensor"),
        P(),
        P(),
        P(),
    )
    fits_line = mesh.shape["dp"] == 8 and mesh.shape["tensor"] == 4
    return jax.shard_map(
        local_line if fits_line else local_any,
        mesh=mesh,
        in_specs=placed,
        out_specs=P("dp", "tensor"),
        check_vma=False,
    )
```

```python
import functools

import jax
import jax.numpy as jnp
from jax import lax
from jax.experimental import pallas as pl
from jax.experimental.pallas import tpu as pltpu
from jax.sharding import PartitionSpec as P

HD = 128

rope_base = 1000000.0
norm_eps = 1e-06
mask_value = -1e30
kernel_cost = pl.CostEstimate(flops=9 * 10**9, bytes_accessed=2**20, transcendentals=0)


def rope_tables(positions):
    half_dim = HD // 2
    frequency = rope_base ** (-(jnp.arange(half_dim).astype(jnp.float32) * 2.0 / HD))
    angles = positions.astype(jnp.float32)[:, None] * frequency[None, :]
    return (jnp.cos(angles), jnp.sin(angles))


def rotate(states, cosine, sine):
    half_dim = states.shape[-1] // 2
    first_half = states[..., :half_dim]
    second_half = states[..., half_dim:]
    cos_wide = cosine[:, None, :]
    sin_wide = sine[:, None, :]
    return jnp.concatenate(
        [
            first_half * cos_wide - second_half * sin_wide,
            second_half * cos_wide + first_half * sin_wide,
        ],
        axis=-1,
    )


def local_any(
    rollout_states,
    norm_gain,
    w_query,
    w_key,
    w_value,
    b_query,
    b_key,
    b_value,
    seq_lengths,
    seq_dest,
    seq_offset,
):
    learners = lax.axis_size("dp")
    own_index = lax.axis_index("dp")
    row_count, feature_count = rollout_states.shape
    capacity = 2 * row_count // learners - 1
    lengths = seq_lengths.reshape(learners, learners)
    dests = seq_dest.reshape(learners, learners)
    offsets = seq_offset.reshape(learners, learners)
    starts = jnp.cumsum(lengths, axis=1) - lengths
    peer_ids = jnp.arange(learners, dtype=jnp.int32)
    own_length = lax.dynamic_index_in_dim(lengths, own_index, 0, keepdims=False)
    own_start = lax.dynamic_index_in_dim(starts, own_index, 0, keepdims=False)
    own_dest = lax.dynamic_index_in_dim(dests, own_index, 0, keepdims=False)
    match_send = (own_dest[None, :] == peer_ids[:, None]).astype(jnp.int32)
    send_start = jnp.sum(match_send * own_start[None, :], axis=1)
    send_length = jnp.sum(match_send * own_length[None, :], axis=1)
    slot_index = jnp.arange(capacity, dtype=jnp.int32)
    pick_rows = send_start[:, None] + slot_index[None, :]
    padded = jnp.concatenate(
        [rollout_states, jnp.zeros((capacity, feature_count), rollout_states.dtype)], axis=0
    )
    live_slots = (slot_index[None, :] < send_length[:, None])[..., None]
    outgoing = jnp.where(
        live_slots, jnp.take(padded, pick_rows, axis=0), jnp.zeros((), rollout_states.dtype)
    )
    incoming = lax.all_to_all(outgoing, "dp", split_axis=0, concat_axis=0, tiled=True)
    matched = (dests == own_index).astype(jnp.int32)
    run_start = jnp.sum(matched * offsets, axis=1)
    run_length = jnp.sum(matched * lengths, axis=1)
    rows = jnp.arange(row_count, dtype=jnp.int32)
    inside = (
        (rows[:, None] >= run_start[None, :]) & (rows[:, None] < (run_start + run_length)[None, :])
    ).astype(jnp.int32)
    source_ids = jnp.sum(inside * peer_ids[None, :], axis=1)
    within_seq = rows - jnp.sum(inside * run_start[None, :], axis=1)
    arrived = jnp.take(
        incoming.reshape(learners * capacity, feature_count),
        source_ids * capacity + within_seq,
        axis=0,
    )
    gathered = lax.all_gather(arrived, "tensor", axis=1, tiled=True)
    widened = gathered.astype(jnp.float32)
    statistic = jnp.mean(widened * widened, axis=-1, keepdims=True)
    normed = (widened * lax.rsqrt(statistic + norm_eps) * norm_gain[None, :]).astype(jnp.bfloat16)
    full_query, full_key, full_value = (
        lax.all_gather(w_query, "dp", axis=0, tiled=True),
        lax.all_gather(w_key, "dp", axis=0, tiled=True),
        lax.all_gather(w_value, "dp", axis=0, tiled=True),
    )
    query = jnp.dot(normed, full_query, preferred_element_type=jnp.float32)
    key = jnp.dot(normed, full_key, preferred_element_type=jnp.float32)
    value = jnp.dot(normed, full_value, preferred_element_type=jnp.float32)
    query = query + b_query[None, :]
    key = key + b_key[None, :]
    value = value + b_value[None, :]
    heads_here = query.shape[1] // HD
    kv_here = key.shape[1] // HD
    group = heads_here // kv_here
    cosine, sine = rope_tables(within_seq)
    rot_query = rotate(query.reshape(row_count, heads_here, HD), cosine, sine).astype(jnp.bfloat16)
    rot_query = rot_query.reshape(row_count, kv_here, group, HD)
    rot_key = rotate(key.reshape(row_count, kv_here, HD), cosine, sine).astype(jnp.bfloat16)
    value_bf = value.reshape(row_count, kv_here, HD).astype(jnp.bfloat16)
    block_rows = min(512, row_count)

    def one_block(block_number):
        first_row = block_number * block_rows
        query_block = lax.dynamic_slice_in_dim(rot_query, first_row, block_rows, 0)
        query_source = lax.dynamic_slice_in_dim(source_ids, first_row, block_rows, 0)
        query_rows = first_row + jnp.arange(block_rows, dtype=jnp.int32)
        scores = jnp.einsum(
            "bcgd,kcd->cgbk", query_block, rot_key, preferred_element_type=jnp.float32
        )
        scores = scores * HD ** (-0.5)
        allowed = (source_ids[None, :] == query_source[:, None]) & (
            rows[None, :] <= query_rows[:, None]
        )
        scores = jnp.where(allowed[None, None], scores, mask_value)
        peak = jnp.max(scores, axis=-1, keepdims=True)
        raised = jnp.exp(scores - peak)
        weights = (raised / jnp.sum(raised, axis=-1, keepdims=True)).astype(jnp.bfloat16)
        context = jnp.einsum(
            "cgbk,kcd->bcgd", weights, value_bf, preferred_element_type=jnp.float32
        )
        return context.astype(jnp.bfloat16).reshape(block_rows, heads_here * HD)

    outputs = lax.map(one_block, jnp.arange(row_count // block_rows, dtype=jnp.int32))
    return outputs.reshape(row_count, heads_here * HD)


def product_kernel(counts, ropes, lanes, out_lanes, which_ref, *refs):
    refs = list(refs)
    x_refs = [[refs.pop(0) for _ in range(n)] for n in counts[:4]]
    w_ref = refs.pop(0)
    part_refs = [refs.pop(0) for _ in range(counts[4])]
    if ropes:
        bias_ref, angle_ref = (refs.pop(0) for _ in range(2))
    out_refs = [refs.pop(0) for _ in out_lanes]
    w_buf, sems = refs
    rows = out_refs[0].shape[0]
    tile = rows // 2
    copies = [
        pltpu.make_async_copy(w_ref.at[which_ref[i], :, lanes], w_buf.at[i], sems.at[i])
        for i in range(4)
    ]
    for copy in copies:
        copy.start()

    def piece_rows(pieces, first):
        size = pieces[0].shape[0]
        return pieces[first // size], pl.ds(first % size, tile)

    for first in range(0, rows, tile):
        here = pl.ds(first, tile)
        term = None
        for i in range(4):
            ref, at = piece_rows(x_refs[i], first)
            if first == 0:
                copies[i].wait()
            dot = jnp.dot(ref[at, :], w_buf[i], preferred_element_type=jnp.float32)
            term = dot if term is None else term + dot
        if not ropes:
            for out_ref, (low, high) in zip(out_refs, out_lanes):
                out_ref[here, :] = term[:, low:high].astype(out_ref.dtype)
            continue
        (out_ref,) = out_refs
        ref, at = piece_rows(part_refs, first)
        term = term + ref[at, :].astype(jnp.float32) + bias_ref[...]
        angle = angle_ref[here, :]
        turned_angle = pltpu.roll(angle, HD // 2, 1)
        low = lax.broadcasted_iota(jnp.int32, angle.shape, 1) < HD // 2
        cosine = jnp.where(low, angle, turned_angle)
        sine = jnp.where(low, -turned_angle, angle)
        for c, rope in enumerate(ropes):
            head = term[:, c * HD : (c + 1) * HD]
            if rope:
                head = head * cosine + pltpu.roll(head, HD // 2, 1) * sine
            out_ref[here, c * HD : (c + 1) * HD] = head.astype(out_ref.dtype)


def keep(array):
    return pltpu.with_memory_space_constraint(array, pltpu.VMEM)


def projection(which, x_blocks, weights, columns, outs, finish=None):
    rows = sum(piece.shape[0] for piece in x_blocks[0])
    counts = [len(pieces) for pieces in x_blocks]
    low, high = columns
    vmem = pl.BlockSpec(memory_space=pltpu.VMEM)
    operands = [keep(piece) for pieces in x_blocks for piece in pieces]
    in_specs = [vmem] * len(operands) + [pl.BlockSpec(memory_space=pl.ANY)]
    operands.append(weights)
    ropes = None
    if finish is None:
        counts.append(0)
    else:
        ropes, part, bias, angles = finish
        counts.append(1)
        operands += [keep(part), bias, keep(angles)]
        in_specs += [vmem] * 3
    return pl.pallas_call(
        functools.partial(
            product_kernel,
            tuple(counts),
            ropes,
            pl.ds(low, high - low),
            tuple((first, last) for first, last, _ in outs),
        ),
        in_specs=[pl.BlockSpec(memory_space=pltpu.SMEM)] + in_specs,
        out_specs=[vmem] * len(outs),
        out_shape=[pltpu.VMEM((rows, last - first), kind) for first, last, kind in outs],
        scratch_shapes=[
            pltpu.VMEM((4, weights.shape[1], high - low), jnp.bfloat16),
            pltpu.SemaphoreType.DMA((4,)),
        ],
        compiler_params=pltpu.CompilerParams(vmem_limit_bytes=(8 + (high - low) // 64) * 2**20),
        cost_estimate=kernel_cost,
    )(which, *operands)


def pick_rows(start, length, slot, window, ref, lanes=slice(None)):
    first = pl.multiple_of(jnp.minimum((start // 16) * 16, ref.shape[0] - window), 16)
    row_at = lax.broadcasted_iota(jnp.int32, (slot, window), 0)
    col_at = lax.broadcasted_iota(jnp.int32, (slot, window), 1)
    pick = jnp.where((col_at == row_at + (start - first)) & (row_at < length), 1.0, 0.0)
    rows = jnp.dot(
        pick.astype(jnp.bfloat16), ref[pl.ds(first, window), lanes], preferred_element_type=jnp.float32
    )
    return rows.astype(jnp.bfloat16)


def slots_kernel(slot, window, start_ref, len_ref, in_ref, out_ref):
    for s in range(out_ref.shape[0]):
        out_ref[s] = pick_rows(start_ref[s], len_ref[s], slot, window, in_ref)


def to_slots(starts, lens, array, slot, window):
    count, columns = starts.shape[0], array.shape[1]
    scalars = pl.BlockSpec(memory_space=pltpu.SMEM)
    vmem = pl.BlockSpec(memory_space=pltpu.VMEM)
    return pl.pallas_call(
        functools.partial(slots_kernel, slot, window),
        in_specs=[scalars, scalars, vmem],
        out_specs=vmem,
        out_shape=pltpu.VMEM((count, slot, columns), jnp.bfloat16),
        compiler_params=pltpu.CompilerParams(vmem_limit_bytes=8 * 2**20),
        cost_estimate=kernel_cost,
    )(starts, lens, keep(array))


def attend_kernel(heads, lanes, window, batch, start_ref, len_ref, q_ref, kv_ref, out_ref):
    count, slot = out_ref.shape[:2]
    half = slot // 2

    @pl.loop(0, count, step=batch)
    def _(group):
        for s in range(batch):
            query = pick_rows(
                start_ref[group + s], len_ref[group + s], slot, window, q_ref, lanes
            )
            for block in range(2):
                width = (block + 1) * half
                stacked = jnp.concatenate(
                    [query[block * half : width, h * HD : (h + 1) * HD] for h in range(heads)],
                    axis=0,
                )
                scores = lax.dot_general(
                    stacked,
                    kv_ref[group + s, :width, :HD],
                    (((1,), (1,)), ((), ())),
                    preferred_element_type=jnp.float32,
                )
                row_at = lax.broadcasted_iota(jnp.int32, scores.shape, 0) & (half - 1)
                col_at = lax.broadcasted_iota(jnp.int32, scores.shape, 1)
                scores = jnp.where(
                    col_at <= row_at + block * half, scores * HD ** (-0.5), mask_value
                )
                peak = jnp.max(scores, axis=-1, keepdims=True)
                raised = jnp.exp(scores - peak)
                weights = raised * (1.0 / jnp.sum(raised, axis=-1, keepdims=True))
                context = jnp.dot(
                    weights.astype(jnp.bfloat16),
                    kv_ref[group + s, :width, HD:],
                    preferred_element_type=jnp.float32,
                ).astype(out_ref.dtype)
                for h in range(heads):
                    out_ref[group + s, block * half : width, h * HD : (h + 1) * HD] = context[
                        h * half : (h + 1) * half
                    ]


def attend(starts, lens, query, columns, kv_slots, window):
    low, high = columns
    count, slot = kv_slots.shape[:2]
    scalars = pl.BlockSpec(memory_space=pltpu.SMEM)
    vmem = pl.BlockSpec(memory_space=pltpu.VMEM)
    return pl.pallas_call(
        functools.partial(attend_kernel, (high - low) // HD, pl.ds(low, high - low), window, 4),
        in_specs=[scalars, scalars, vmem, vmem],
        out_specs=vmem,
        out_shape=pltpu.VMEM((count, slot, high - low), jnp.bfloat16),
        compiler_params=pltpu.CompilerParams(vmem_limit_bytes=8 * 2**20),
        cost_estimate=kernel_cost,
    )(starts, lens, keep(query), keep(kv_slots))


def place_kernel(count, slot, window, start_ref, len_ref, in_ref, *rest):
    out_ref, total = rest[-2:]
    rows = total.shape[0]
    total[...] = jnp.zeros_like(total)
    row_at = lax.broadcasted_iota(jnp.int32, (window, slot), 0)
    col_at = lax.broadcasted_iota(jnp.int32, (window, slot), 1)
    for s in range(count):
        start = start_ref[s]
        first = pl.multiple_of(jnp.minimum((start // 8) * 8, rows - window), 8)
        pick = jnp.where(
            (row_at == col_at + (start - first)) & (col_at < len_ref[s]), 1.0, 0.0
        ).astype(jnp.bfloat16)
        total[pl.ds(first, window), :] += jnp.dot(
            pick, in_ref[s], preferred_element_type=jnp.float32
        )
    out_ref[...] = total[...].astype(out_ref.dtype)


def place(starts, lens, slots, rows, which, all_columns, before):
    count, slot, columns = slots.shape
    window = min(rows, slot + 8)
    in_specs = [pl.BlockSpec((count, slot, columns), lambda r, a, b: (0, 0, 0))]
    operands, aliases = [slots], {}
    if before is not None:
        in_specs.append(pl.BlockSpec(memory_space=pl.ANY))
        operands.append(before)
        aliases = {3: 0}
    grid_spec = pltpu.PrefetchScalarGridSpec(
        num_scalar_prefetch=2,
        grid=(1,),
        in_specs=in_specs,
        out_specs=pl.BlockSpec((rows, columns), lambda r, a, b: (0, which)),
        scratch_shapes=[pltpu.VMEM((rows, columns), jnp.float32)],
    )
    return pl.pallas_call(
        functools.partial(place_kernel, count, slot, window),
        grid_spec=grid_spec,
        out_shape=jax.ShapeDtypeStruct((rows, all_columns), jnp.bfloat16),
        input_output_aliases=aliases,
        compiler_params=pltpu.CompilerParams(vmem_limit_bytes=8 * 2**20),
        cost_estimate=kernel_cost,
    )(starts, lens, *operands)


def local_line(
    rollout_states,
    norm_gain,
    w_query,
    w_key,
    w_value,
    b_query,
    b_key,
    b_value,
    seq_lengths,
    seq_dest,
    seq_offset,
):
    learners = lax.axis_size("dp")
    line = learners // 2
    me = lax.axis_index("dp")
    z, x = me // 2, me % 2
    t = lax.axis_index("tensor")
    row_count, feature_count = rollout_states.shape
    slot = 2 * row_count // learners
    half = feature_count // 2
    middle = row_count // 2

    def after(array, *others):
        return lax.optimization_barrier((array, *others))[0]

    def swap_x(array):
        return lax.ppermute(array, "dp", [(i, i ^ 1) for i in range(learners)])

    def swap_y(array):
        return lax.ppermute(array, "tensor", [(i, i ^ 2) for i in range(4)])

    def swap_core(array):
        return lax.ppermute(array, "tensor", [(i, i ^ 1) for i in range(4)])

    wide = 2 * HD
    along_z = [[2 * i + j for i in range(line)] for j in range(2)]
    groups = [
        jnp.concatenate([w_key, w_value, w_query[:, : 2 * wide]], axis=1),
        w_query[:, 2 * wide :],
    ]
    weights = []
    for group in groups:
        gathered = lax.all_gather(group, "dp", axis_index_groups=along_z)
        weights.append(pltpu.with_memory_space_constraint(gathered, pltpu.HBM))
    bias_kv = jnp.concatenate([b_key, b_value])[None, :]
    bias_low, bias_high = b_query[None, : 2 * wide], b_query[None, 2 * wide :]

    states = rollout_states
    widened = states.astype(jnp.float32)
    squares = jnp.sum(widened * widened, axis=-1)
    squares = squares + swap_core(squares)
    squares = squares + swap_y(squares)
    scale = lax.rsqrt(squares[:, None] / (4 * feature_count) + norm_eps)

    def normed(first):
        part = lax.dynamic_slice_in_dim(states, first, half, 1).astype(jnp.float32)
        gain = lax.dynamic_slice_in_dim(norm_gain, t * feature_count + first, half, 0)
        return (part * scale * gain[None, :]).astype(jnp.bfloat16)

    own, give = normed(x * half), normed((1 - x) * half)

    near_a = swap_x(give[:middle])
    own_a = swap_y(own[:middle])
    own_core = swap_core(own)
    near_b = swap_x(after(give[middle:], near_a))
    diag_a = swap_y(after(near_a, own_a))
    near_a_core = swap_core(near_a)
    own_a_core = swap_core(after(own_a, near_a))
    diag_b = swap_y(after(near_b, diag_a))
    near_b_core = swap_core(after(near_b, diag_a))
    diag_a_core = swap_core(after(diag_a, near_b))
    own_b = swap_y(after(own[middle:], diag_b))
    diag_b_core = swap_core(diag_b)
    own_b_core = swap_core(own_b)
    own_x = [[own], [own_core], [own_a, own_b], [own_a_core, own_b_core]]
    near_ax = [[near_a], [near_a_core], [diag_a], [diag_a_core]]
    near_bx = [[near_b], [near_b_core], [diag_b], [diag_b_core]]
    near_x = [a + b for a, b in zip(near_ax, near_bx)]
    which = jnp.stack([t ^ i for i in range(4)]).astype(jnp.int32)

    lengths = seq_lengths.reshape(learners, learners)
    dests = seq_dest.reshape(learners, learners)
    offsets = seq_offset.reshape(learners, learners)
    starts = jnp.cumsum(lengths, axis=1) - lengths
    peer_ids = jnp.arange(learners, dtype=jnp.int32)
    rows = jnp.arange(row_count, dtype=jnp.int32)
    length = lax.dynamic_index_in_dim(lengths, me, 0, keepdims=False)
    start = lax.dynamic_index_in_dim(starts, me, 0, keepdims=False)
    dest = lax.dynamic_index_in_dim(dests, me, 0, keepdims=False)
    match = (dest[None, :] == peer_ids[:, None]).astype(jnp.int32)
    send_start = jnp.sum(match * start[None, :], axis=1)
    send_length = jnp.sum(match * length[None, :], axis=1)
    inside = (rows[:, None] >= start[None, :]) & (rows[:, None] < (start + length)[None, :])
    position = rows - jnp.sum(inside.astype(jnp.int32) * start[None, :], axis=1)
    angles = jnp.concatenate(rope_tables(position), axis=1)
    matched = (dests == me).astype(jnp.int32)
    run_start = jnp.sum(matched * offsets, axis=1)
    run_length = jnp.sum(matched * lengths, axis=1)

    window = min(row_count, -(-(slot + 16) // 128) * 128)

    def send(outgoing):
        return lax.all_to_all(outgoing, "dp", split_axis=0, concat_axis=0, tiled=True)

    def receive(c, incoming, before, *others):
        start_at = after(run_start, *others)
        return place(
            start_at, run_length, incoming, row_count, c, w_query.shape[1], before
        )

    def contexts(c, rot, *others):
        low = (c % 2) * wide
        start_at = after(send_start, *others)
        return attend(start_at, send_length, rot, (low, low + wide), kv_slots, window)

    first, second = weights
    outs = [(0, wide, jnp.float32), (wide, 3 * wide, jnp.bfloat16)]
    part_kv, part_low = projection(which, near_x, first, (0, 3 * wide), outs)
    got_low = swap_x(part_low)
    got_kv = swap_x(after(part_kv, got_low))
    whole = [(0, 2 * wide, jnp.bfloat16)]
    ropes = (True,) * (2 * wide // HD)
    (rot_low,) = projection(
        which, own_x, first, (wide, 3 * wide), whole, (ropes, got_low, bias_low, angles)
    )
    (kv,) = projection(
        after(which, rot_low),
        own_x,
        first,
        (0, wide),
        [(0, wide, jnp.bfloat16)],
        ((True, False), got_kv, bias_kv, angles),
    )
    kv_slots = to_slots(send_start, send_length, kv, slot, window)
    out_0 = contexts(0, rot_low)
    in_0 = send(out_0)

    outs = [(0, 2 * wide, jnp.bfloat16)]
    (part_high,) = projection(after(which, out_0), near_x, second, (0, 2 * wide), outs)
    got_high = swap_x(part_high)
    out_1 = contexts(1, rot_low, part_high)
    in_1 = send(after(out_1, in_0))
    (rot_high,) = projection(
        after(which, out_1), own_x, second, (0, 2 * wide), whole, (ropes, got_high, bias_high, angles)
    )
    out_2 = contexts(2, rot_high)
    in_2 = send(after(out_2, in_0))
    out_3 = contexts(3, rot_high, out_2)
    in_3 = send(after(out_3, in_1))
    result = receive(0, in_0, None, rot_high)
    result = receive(1, in_1, result, out_3)
    result = receive(2, in_2, result, out_3)
    return receive(3, in_3, result)


def solution(mesh):
    placed = (
        P("dp", "tensor"),
        P(),
        P("dp", "tensor"),
        P("dp", "tensor"),
        P("dp", "tensor"),
        P("tensor"),
        P("tensor"),
        P("tensor"),
        P(),
        P(),
        P(),
    )
    fits_line = mesh.shape["dp"] == 8 and mesh.shape["tensor"] == 4
    return jax.shard_map(
        local_line if fits_line else local_any,
        mesh=mesh,
        in_specs=placed,
        out_specs=P("dp", "tensor"),
        check_vma=False,
    )
```

```python
import functools

import jax
import jax.numpy as jnp
from jax import lax
from jax.experimental import pallas as pl
from jax.experimental.pallas import tpu as pltpu
from jax.sharding import PartitionSpec as P

HD = 128

rope_base = 1000000.0
norm_eps = 1e-06
mask_value = -1e30
kernel_cost = pl.CostEstimate(flops=4 * 10**9, bytes_accessed=2**20, transcendentals=0)


def rope_tables(positions):
    half_dim = HD // 2
    frequency = rope_base ** (-(jnp.arange(half_dim).astype(jnp.float32) * 2.0 / HD))
    angles = positions.astype(jnp.float32)[:, None] * frequency[None, :]
    return (jnp.cos(angles), jnp.sin(angles))


def rotate(states, cosine, sine):
    half_dim = states.shape[-1] // 2
    first_half = states[..., :half_dim]
    second_half = states[..., half_dim:]
    cos_wide = cosine[:, None, :]
    sin_wide = sine[:, None, :]
    return jnp.concatenate(
        [
            first_half * cos_wide - second_half * sin_wide,
            second_half * cos_wide + first_half * sin_wide,
        ],
        axis=-1,
    )


def local_any(
    rollout_states,
    norm_gain,
    w_query,
    w_key,
    w_value,
    b_query,
    b_key,
    b_value,
    seq_lengths,
    seq_dest,
    seq_offset,
):
    learners = lax.axis_size("dp")
    own_index = lax.axis_index("dp")
    row_count, feature_count = rollout_states.shape
    capacity = 2 * row_count // learners - 1
    lengths = seq_lengths.reshape(learners, learners)
    dests = seq_dest.reshape(learners, learners)
    offsets = seq_offset.reshape(learners, learners)
    starts = jnp.cumsum(lengths, axis=1) - lengths
    peer_ids = jnp.arange(learners, dtype=jnp.int32)
    own_length = lax.dynamic_index_in_dim(lengths, own_index, 0, keepdims=False)
    own_start = lax.dynamic_index_in_dim(starts, own_index, 0, keepdims=False)
    own_dest = lax.dynamic_index_in_dim(dests, own_index, 0, keepdims=False)
    match_send = (own_dest[None, :] == peer_ids[:, None]).astype(jnp.int32)
    send_start = jnp.sum(match_send * own_start[None, :], axis=1)
    send_length = jnp.sum(match_send * own_length[None, :], axis=1)
    slot_index = jnp.arange(capacity, dtype=jnp.int32)
    pick_rows = send_start[:, None] + slot_index[None, :]
    padded = jnp.concatenate(
        [rollout_states, jnp.zeros((capacity, feature_count), rollout_states.dtype)], axis=0
    )
    live_slots = (slot_index[None, :] < send_length[:, None])[..., None]
    outgoing = jnp.where(
        live_slots, jnp.take(padded, pick_rows, axis=0), jnp.zeros((), rollout_states.dtype)
    )
    incoming = lax.all_to_all(outgoing, "dp", split_axis=0, concat_axis=0, tiled=True)
    matched = (dests == own_index).astype(jnp.int32)
    run_start = jnp.sum(matched * offsets, axis=1)
    run_length = jnp.sum(matched * lengths, axis=1)
    rows = jnp.arange(row_count, dtype=jnp.int32)
    inside = (
        (rows[:, None] >= run_start[None, :]) & (rows[:, None] < (run_start + run_length)[None, :])
    ).astype(jnp.int32)
    source_ids = jnp.sum(inside * peer_ids[None, :], axis=1)
    within_seq = rows - jnp.sum(inside * run_start[None, :], axis=1)
    arrived = jnp.take(
        incoming.reshape(learners * capacity, feature_count),
        source_ids * capacity + within_seq,
        axis=0,
    )
    gathered = lax.all_gather(arrived, "tensor", axis=1, tiled=True)
    widened = gathered.astype(jnp.float32)
    statistic = jnp.mean(widened * widened, axis=-1, keepdims=True)
    normed = (widened * lax.rsqrt(statistic + norm_eps) * norm_gain[None, :]).astype(jnp.bfloat16)
    full_query, full_key, full_value = (
        lax.all_gather(w_query, "dp", axis=0, tiled=True),
        lax.all_gather(w_key, "dp", axis=0, tiled=True),
        lax.all_gather(w_value, "dp", axis=0, tiled=True),
    )
    query = jnp.dot(normed, full_query, preferred_element_type=jnp.float32)
    key = jnp.dot(normed, full_key, preferred_element_type=jnp.float32)
    value = jnp.dot(normed, full_value, preferred_element_type=jnp.float32)
    query = query + b_query[None, :]
    key = key + b_key[None, :]
    value = value + b_value[None, :]
    heads_here = query.shape[1] // HD
    kv_here = key.shape[1] // HD
    group = heads_here // kv_here
    cosine, sine = rope_tables(within_seq)
    rot_query = rotate(query.reshape(row_count, heads_here, HD), cosine, sine).astype(jnp.bfloat16)
    rot_query = rot_query.reshape(row_count, kv_here, group, HD)
    rot_key = rotate(key.reshape(row_count, kv_here, HD), cosine, sine).astype(jnp.bfloat16)
    value_bf = value.reshape(row_count, kv_here, HD).astype(jnp.bfloat16)
    block_rows = min(512, row_count)

    def one_block(block_number):
        first_row = block_number * block_rows
        query_block = lax.dynamic_slice_in_dim(rot_query, first_row, block_rows, 0)
        query_source = lax.dynamic_slice_in_dim(source_ids, first_row, block_rows, 0)
        query_rows = first_row + jnp.arange(block_rows, dtype=jnp.int32)
        scores = jnp.einsum(
            "bcgd,kcd->cgbk", query_block, rot_key, preferred_element_type=jnp.float32
        )
        scores = scores * HD ** (-0.5)
        allowed = (source_ids[None, :] == query_source[:, None]) & (
            rows[None, :] <= query_rows[:, None]
        )
        scores = jnp.where(allowed[None, None], scores, mask_value)
        peak = jnp.max(scores, axis=-1, keepdims=True)
        raised = jnp.exp(scores - peak)
        weights = (raised / jnp.sum(raised, axis=-1, keepdims=True)).astype(jnp.bfloat16)
        context = jnp.einsum(
            "cgbk,kcd->bcgd", weights, value_bf, preferred_element_type=jnp.float32
        )
        return context.astype(jnp.bfloat16).reshape(block_rows, heads_here * HD)

    outputs = lax.map(one_block, jnp.arange(row_count // block_rows, dtype=jnp.int32))
    return outputs.reshape(row_count, heads_here * HD)


def product_kernel(counts, ropes, lanes, out_lanes, which_ref, *refs):
    refs = list(refs)
    x_refs = [[refs.pop(0) for _ in range(n)] for n in counts[:4]]
    w_ref = refs.pop(0)
    part_refs = [refs.pop(0) for _ in range(counts[4])]
    if ropes:
        bias_ref, angle_ref = (refs.pop(0) for _ in range(2))
    out_refs = [refs.pop(0) for _ in out_lanes]
    w_buf, sems = refs
    rows = out_refs[0].shape[0]
    tile = rows // 2
    copies = [
        pltpu.make_async_copy(w_ref.at[which_ref[i], :, lanes], w_buf.at[i], sems.at[i])
        for i in range(4)
    ]
    for copy in copies:
        copy.start()

    def piece_rows(pieces, first):
        size = pieces[0].shape[0]
        return pieces[first // size], pl.ds(first % size, tile)

    for first in range(0, rows, tile):
        here = pl.ds(first, tile)
        term = None
        for i in range(4):
            ref, at = piece_rows(x_refs[i], first)
            if first == 0:
                copies[i].wait()
            dot = jnp.dot(ref[at, :], w_buf[i], preferred_element_type=jnp.float32)
            term = dot if term is None else term + dot
        if not ropes:
            for out_ref, (low, high) in zip(out_refs, out_lanes):
                out_ref[here, :] = term[:, low:high].astype(out_ref.dtype)
            continue
        (out_ref,) = out_refs
        ref, at = piece_rows(part_refs, first)
        term = term + ref[at, :].astype(jnp.float32) + bias_ref[...]
        angle = angle_ref[here, :]
        turned_angle = pltpu.roll(angle, HD // 2, 1)
        low = lax.broadcasted_iota(jnp.int32, angle.shape, 1) < HD // 2
        cosine = jnp.where(low, angle, turned_angle)
        sine = jnp.where(low, -turned_angle, angle)
        for c, rope in enumerate(ropes):
            head = term[:, c * HD : (c + 1) * HD]
            if rope:
                head = head * cosine + pltpu.roll(head, HD // 2, 1) * sine
            out_ref[here, c * HD : (c + 1) * HD] = head.astype(out_ref.dtype)


def keep(array):
    return pltpu.with_memory_space_constraint(array, pltpu.VMEM)


def projection(which, x_blocks, weights, columns, outs, finish=None):
    rows = sum(piece.shape[0] for piece in x_blocks[0])
    counts = [len(pieces) for pieces in x_blocks]
    low, high = columns
    vmem = pl.BlockSpec(memory_space=pltpu.VMEM)
    operands = [keep(piece) for pieces in x_blocks for piece in pieces]
    in_specs = [vmem] * len(operands) + [pl.BlockSpec(memory_space=pl.ANY)]
    operands.append(weights)
    ropes = None
    if finish is None:
        counts.append(0)
    else:
        ropes, part, bias, angles = finish
        counts.append(1)
        operands += [keep(part), bias, keep(angles)]
        in_specs += [vmem] * 3
    return pl.pallas_call(
        functools.partial(
            product_kernel,
            tuple(counts),
            ropes,
            pl.ds(low, high - low),
            tuple((first, last) for first, last, _ in outs),
        ),
        in_specs=[pl.BlockSpec(memory_space=pltpu.SMEM)] + in_specs,
        out_specs=[vmem] * len(outs),
        out_shape=[pltpu.VMEM((rows, last - first), kind) for first, last, kind in outs],
        scratch_shapes=[
            pltpu.VMEM((4, weights.shape[1], high - low), jnp.bfloat16),
            pltpu.SemaphoreType.DMA((4,)),
        ],
        compiler_params=pltpu.CompilerParams(vmem_limit_bytes=(8 + (high - low) // 64) * 2**20),
        cost_estimate=kernel_cost,
    )(which, *operands)


def pick_rows(start, length, slot, window, ref, lanes=slice(None)):
    first = pl.multiple_of(jnp.minimum((start // 16) * 16, ref.shape[0] - window), 16)
    row_at = lax.broadcasted_iota(jnp.int32, (slot, window), 0)
    col_at = lax.broadcasted_iota(jnp.int32, (slot, window), 1)
    pick = jnp.where((col_at == row_at + (start - first)) & (row_at < length), 1.0, 0.0)
    rows = jnp.dot(
        pick.astype(jnp.bfloat16), ref[pl.ds(first, window), lanes], preferred_element_type=jnp.float32
    )
    return rows.astype(jnp.bfloat16)


def slots_kernel(slot, window, start_ref, len_ref, in_ref, out_ref):
    for s in range(out_ref.shape[0]):
        out_ref[s] = pick_rows(start_ref[s], len_ref[s], slot, window, in_ref)


def to_slots(starts, lens, array, slot, window):
    count, columns = starts.shape[0], array.shape[1]
    scalars = pl.BlockSpec(memory_space=pltpu.SMEM)
    vmem = pl.BlockSpec(memory_space=pltpu.VMEM)
    return pl.pallas_call(
        functools.partial(slots_kernel, slot, window),
        in_specs=[scalars, scalars, vmem],
        out_specs=vmem,
        out_shape=pltpu.VMEM((count, slot, columns), jnp.bfloat16),
        compiler_params=pltpu.CompilerParams(vmem_limit_bytes=8 * 2**20),
        cost_estimate=kernel_cost,
    )(starts, lens, keep(array))


def attend_kernel(heads, lanes, window, batch, start_ref, len_ref, q_ref, kv_ref, out_ref):
    count, slot = out_ref.shape[:2]
    half = slot // 2

    @pl.loop(0, count, step=batch)
    def _(group):
        for s in range(batch):
            query = pick_rows(
                start_ref[group + s], len_ref[group + s], slot, window, q_ref, lanes
            )
            for block in range(2):
                width = (block + 1) * half
                stacked = jnp.concatenate(
                    [query[block * half : width, h * HD : (h + 1) * HD] for h in range(heads)],
                    axis=0,
                )
                scores = lax.dot_general(
                    stacked,
                    kv_ref[group + s, :width, :HD],
                    (((1,), (1,)), ((), ())),
                    preferred_element_type=jnp.float32,
                )
                row_at = lax.broadcasted_iota(jnp.int32, scores.shape, 0) & (half - 1)
                col_at = lax.broadcasted_iota(jnp.int32, scores.shape, 1)
                scores = jnp.where(
                    col_at <= row_at + block * half, scores * HD ** (-0.5), mask_value
                )
                peak = jnp.max(scores, axis=-1, keepdims=True)
                raised = jnp.exp(scores - peak)
                weights = raised * (1.0 / jnp.sum(raised, axis=-1, keepdims=True))
                context = jnp.dot(
                    weights.astype(jnp.bfloat16),
                    kv_ref[group + s, :width, HD:],
                    preferred_element_type=jnp.float32,
                ).astype(out_ref.dtype)
                for h in range(heads):
                    out_ref[group + s, block * half : width, h * HD : (h + 1) * HD] = context[
                        h * half : (h + 1) * half
                    ]


def attend(starts, lens, query, columns, kv_slots, window):
    low, high = columns
    count, slot = kv_slots.shape[:2]
    scalars = pl.BlockSpec(memory_space=pltpu.SMEM)
    vmem = pl.BlockSpec(memory_space=pltpu.VMEM)
    return pl.pallas_call(
        functools.partial(attend_kernel, (high - low) // HD, pl.ds(low, high - low), window, 4),
        in_specs=[scalars, scalars, vmem, vmem],
        out_specs=vmem,
        out_shape=pltpu.VMEM((count, slot, high - low), jnp.bfloat16),
        compiler_params=pltpu.CompilerParams(vmem_limit_bytes=8 * 2**20),
        cost_estimate=kernel_cost,
    )(starts, lens, keep(query), keep(kv_slots))


def place_kernel(count, slot, window, start_ref, len_ref, in_ref, *rest):
    out_ref, total = rest[-2:]
    rows = total.shape[0]
    total[...] = jnp.zeros_like(total)
    row_at = lax.broadcasted_iota(jnp.int32, (window, slot), 0)
    col_at = lax.broadcasted_iota(jnp.int32, (window, slot), 1)
    for s in range(count):
        start = start_ref[s]
        first = pl.multiple_of(jnp.minimum((start // 8) * 8, rows - window), 8)
        pick = jnp.where(
            (row_at == col_at + (start - first)) & (col_at < len_ref[s]), 1.0, 0.0
        ).astype(jnp.bfloat16)
        total[pl.ds(first, window), :] += jnp.dot(
            pick, in_ref[s], preferred_element_type=jnp.float32
        )
    out_ref[...] = total[...].astype(out_ref.dtype)


def place(starts, lens, slots, rows, which, all_columns, before):
    count, slot, columns = slots.shape
    window = min(rows, slot + 8)
    in_specs = [pl.BlockSpec((count, slot, columns), lambda r, a, b: (0, 0, 0))]
    operands, aliases = [slots], {}
    if before is not None:
        in_specs.append(pl.BlockSpec(memory_space=pl.ANY))
        operands.append(before)
        aliases = {3: 0}
    grid_spec = pltpu.PrefetchScalarGridSpec(
        num_scalar_prefetch=2,
        grid=(1,),
        in_specs=in_specs,
        out_specs=pl.BlockSpec((rows, columns), lambda r, a, b: (0, which)),
        scratch_shapes=[pltpu.VMEM((rows, columns), jnp.float32)],
    )
    return pl.pallas_call(
        functools.partial(place_kernel, count, slot, window),
        grid_spec=grid_spec,
        out_shape=jax.ShapeDtypeStruct((rows, all_columns), jnp.bfloat16),
        input_output_aliases=aliases,
        compiler_params=pltpu.CompilerParams(vmem_limit_bytes=8 * 2**20),
        cost_estimate=kernel_cost,
    )(starts, lens, *operands)


def local_line(
    rollout_states,
    norm_gain,
    w_query,
    w_key,
    w_value,
    b_query,
    b_key,
    b_value,
    seq_lengths,
    seq_dest,
    seq_offset,
):
    learners = lax.axis_size("dp")
    line = learners // 2
    me = lax.axis_index("dp")
    z, x = me // 2, me % 2
    t = lax.axis_index("tensor")
    row_count, feature_count = rollout_states.shape
    slot = 2 * row_count // learners
    half = feature_count // 2
    middle = row_count // 2

    def after(array, *others):
        return lax.optimization_barrier((array, *others))[0]

    def swap_x(array):
        return lax.ppermute(array, "dp", [(i, i ^ 1) for i in range(learners)])

    def swap_y(array):
        return lax.ppermute(array, "tensor", [(i, i ^ 2) for i in range(4)])

    def swap_core(array):
        return lax.ppermute(array, "tensor", [(i, i ^ 1) for i in range(4)])

    wide = 2 * HD
    along_z = [[2 * i + j for i in range(line)] for j in range(2)]
    groups = [
        jnp.concatenate([w_key, w_value, w_query[:, :wide]], axis=1),
        w_query[:, wide : 3 * wide],
        w_query[:, 3 * wide :],
    ]
    weights = []
    for group in groups:
        gathered = lax.all_gather(group, "dp", axis_index_groups=along_z)
        weights.append(pltpu.with_memory_space_constraint(gathered, pltpu.HBM))
    bias_kv = jnp.concatenate([b_key, b_value])[None, :]
    biases = [b_query[None, low : low + wide] for low in range(0, w_query.shape[1], wide)]

    states = rollout_states
    widened = states.astype(jnp.float32)
    squares = jnp.sum(widened * widened, axis=-1)
    squares = squares + swap_core(squares)
    squares = squares + swap_y(squares)
    scale = lax.rsqrt(squares[:, None] / (4 * feature_count) + norm_eps)

    def normed(first):
        part = lax.dynamic_slice_in_dim(states, first, half, 1).astype(jnp.float32)
        gain = lax.dynamic_slice_in_dim(norm_gain, t * feature_count + first, half, 0)
        return (part * scale * gain[None, :]).astype(jnp.bfloat16)

    own, give = normed(x * half), normed((1 - x) * half)

    near_a = swap_x(give[:middle])
    own_a = swap_y(own[:middle])
    own_core = swap_core(own)
    near_b = swap_x(after(give[middle:], near_a))
    diag_a = swap_y(after(near_a, own_a))
    near_a_core = swap_core(near_a)
    own_a_core = swap_core(after(own_a, near_a))
    diag_b = swap_y(after(near_b, diag_a))
    near_b_core = swap_core(after(near_b, diag_a))
    diag_a_core = swap_core(after(diag_a, near_b))
    own_b = swap_y(after(own[middle:], diag_b))
    diag_b_core = swap_core(diag_b)
    own_b_core = swap_core(own_b)
    own_x = [[own], [own_core], [own_a, own_b], [own_a_core, own_b_core]]
    near_ax = [[near_a], [near_a_core], [diag_a], [diag_a_core]]
    near_bx = [[near_b], [near_b_core], [diag_b], [diag_b_core]]
    near_x = [a + b for a, b in zip(near_ax, near_bx)]
    which = jnp.stack([t ^ i for i in range(4)]).astype(jnp.int32)

    lengths = seq_lengths.reshape(learners, learners)
    dests = seq_dest.reshape(learners, learners)
    offsets = seq_offset.reshape(learners, learners)
    starts = jnp.cumsum(lengths, axis=1) - lengths
    peer_ids = jnp.arange(learners, dtype=jnp.int32)
    rows = jnp.arange(row_count, dtype=jnp.int32)
    length = lax.dynamic_index_in_dim(lengths, me, 0, keepdims=False)
    start = lax.dynamic_index_in_dim(starts, me, 0, keepdims=False)
    dest = lax.dynamic_index_in_dim(dests, me, 0, keepdims=False)
    match = (dest[None, :] == peer_ids[:, None]).astype(jnp.int32)
    send_start = jnp.sum(match * start[None, :], axis=1)
    send_length = jnp.sum(match * length[None, :], axis=1)
    inside = (rows[:, None] >= start[None, :]) & (rows[:, None] < (start + length)[None, :])
    position = rows - jnp.sum(inside.astype(jnp.int32) * start[None, :], axis=1)
    angles = jnp.concatenate(rope_tables(position), axis=1)
    matched = (dests == me).astype(jnp.int32)
    run_start = jnp.sum(matched * offsets, axis=1)
    run_length = jnp.sum(matched * lengths, axis=1)

    window = min(row_count, -(-(slot + 16) // 128) * 128)

    def send(outgoing):
        return lax.all_to_all(outgoing, "dp", split_axis=0, concat_axis=0, tiled=True)

    def receive(c, incoming, before, *others):
        start_at = after(run_start, *others)
        return place(
            start_at, run_length, incoming, row_count, c, w_query.shape[1], before
        )

    first, second, third = weights
    whole = [(0, wide, jnp.bfloat16)]

    def partial(group, columns, outs, *others):
        return projection(after(which, *others), near_x, group, columns, outs)

    def contexts(c, group, low, got, others, attend_after=()):
        ending = ((True, True), got, biases[c], angles)
        (rot,) = projection(
            after(which, *others), own_x, group, (low, low + wide), whole, ending
        )
        start_at = after(send_start, *attend_after)
        return attend(start_at, send_length, rot, (0, wide), kv_slots, window)

    outs = [(0, wide, jnp.float32), (wide, 2 * wide, jnp.bfloat16)]
    part_kv, part_0 = partial(first, (0, 2 * wide), outs)
    got_kv = swap_x(part_kv)
    got_0 = swap_x(after(part_0, got_kv))
    ending = ((True, False), got_kv, bias_kv, angles)
    (kv,) = projection(which, own_x, first, (0, wide), whole, ending)
    kv_slots = to_slots(send_start, send_length, kv, slot, window)
    out_0 = contexts(0, first, wide, got_0, (kv_slots,))
    in_0 = send(out_0)
    outs = [(0, wide, jnp.bfloat16), (wide, 2 * wide, jnp.bfloat16)]
    part_1, part_2 = partial(second, (0, 2 * wide), outs, out_0)
    got_1 = swap_x(part_1)
    got_2 = swap_x(after(part_2, got_1))
    out_1 = contexts(1, second, 0, got_1, (part_2,), (got_2,))
    in_1 = send(out_1)
    out_2 = contexts(2, second, wide, got_2, (out_1,))
    in_2 = send(after(out_2, in_0))
    (part_3,) = partial(third, (0, wide), whole, out_2)
    got_3 = swap_x(part_3)
    out_3 = contexts(3, third, 0, got_3, (out_2,))
    in_3 = send(after(out_3, in_1))
    result = receive(0, in_0, None, part_3)
    result = receive(1, in_1, result, out_3)
    result = receive(2, in_2, result, out_3)
    return receive(3, in_3, result)


def solution(mesh):
    placed = (
        P("dp", "tensor"),
        P(),
        P("dp", "tensor"),
        P("dp", "tensor"),
        P("dp", "tensor"),
        P("tensor"),
        P("tensor"),
        P("tensor"),
        P(),
        P(),
        P(),
    )
    fits_line = mesh.shape["dp"] == 8 and mesh.shape["tensor"] == 4
    return jax.shard_map(
        local_line if fits_line else local_any,
        mesh=mesh,
        in_specs=placed,
        out_specs=P("dp", "tensor"),
        check_vma=False,
    )
```

```python
import functools

import jax
import jax.numpy as jnp
from jax import lax
from jax.experimental import pallas as pl
from jax.experimental.pallas import tpu as pltpu
from jax.sharding import PartitionSpec as P

HD = 128

rope_base = 1000000.0
norm_eps = 1e-06
mask_value = -1e30
kernel_cost = pl.CostEstimate(flops=4 * 10**9, bytes_accessed=2**20, transcendentals=0)


def rope_tables(positions):
    half_dim = HD // 2
    frequency = rope_base ** (-(jnp.arange(half_dim).astype(jnp.float32) * 2.0 / HD))
    angles = positions.astype(jnp.float32)[:, None] * frequency[None, :]
    return (jnp.cos(angles), jnp.sin(angles))


def rotate(states, cosine, sine):
    half_dim = states.shape[-1] // 2
    first_half = states[..., :half_dim]
    second_half = states[..., half_dim:]
    cos_wide = cosine[:, None, :]
    sin_wide = sine[:, None, :]
    return jnp.concatenate(
        [
            first_half * cos_wide - second_half * sin_wide,
            second_half * cos_wide + first_half * sin_wide,
        ],
        axis=-1,
    )


def local_any(
    rollout_states,
    norm_gain,
    w_query,
    w_key,
    w_value,
    b_query,
    b_key,
    b_value,
    seq_lengths,
    seq_dest,
    seq_offset,
):
    learners = lax.axis_size("dp")
    own_index = lax.axis_index("dp")
    row_count, feature_count = rollout_states.shape
    capacity = 2 * row_count // learners - 1
    lengths = seq_lengths.reshape(learners, learners)
    dests = seq_dest.reshape(learners, learners)
    offsets = seq_offset.reshape(learners, learners)
    starts = jnp.cumsum(lengths, axis=1) - lengths
    peer_ids = jnp.arange(learners, dtype=jnp.int32)
    own_length = lax.dynamic_index_in_dim(lengths, own_index, 0, keepdims=False)
    own_start = lax.dynamic_index_in_dim(starts, own_index, 0, keepdims=False)
    own_dest = lax.dynamic_index_in_dim(dests, own_index, 0, keepdims=False)
    match_send = (own_dest[None, :] == peer_ids[:, None]).astype(jnp.int32)
    send_start = jnp.sum(match_send * own_start[None, :], axis=1)
    send_length = jnp.sum(match_send * own_length[None, :], axis=1)
    slot_index = jnp.arange(capacity, dtype=jnp.int32)
    pick_rows = send_start[:, None] + slot_index[None, :]
    padded = jnp.concatenate(
        [rollout_states, jnp.zeros((capacity, feature_count), rollout_states.dtype)], axis=0
    )
    live_slots = (slot_index[None, :] < send_length[:, None])[..., None]
    outgoing = jnp.where(
        live_slots, jnp.take(padded, pick_rows, axis=0), jnp.zeros((), rollout_states.dtype)
    )
    incoming = lax.all_to_all(outgoing, "dp", split_axis=0, concat_axis=0, tiled=True)
    matched = (dests == own_index).astype(jnp.int32)
    run_start = jnp.sum(matched * offsets, axis=1)
    run_length = jnp.sum(matched * lengths, axis=1)
    rows = jnp.arange(row_count, dtype=jnp.int32)
    inside = (
        (rows[:, None] >= run_start[None, :]) & (rows[:, None] < (run_start + run_length)[None, :])
    ).astype(jnp.int32)
    source_ids = jnp.sum(inside * peer_ids[None, :], axis=1)
    within_seq = rows - jnp.sum(inside * run_start[None, :], axis=1)
    arrived = jnp.take(
        incoming.reshape(learners * capacity, feature_count),
        source_ids * capacity + within_seq,
        axis=0,
    )
    gathered = lax.all_gather(arrived, "tensor", axis=1, tiled=True)
    widened = gathered.astype(jnp.float32)
    statistic = jnp.mean(widened * widened, axis=-1, keepdims=True)
    normed = (widened * lax.rsqrt(statistic + norm_eps) * norm_gain[None, :]).astype(jnp.bfloat16)
    full_query, full_key, full_value = (
        lax.all_gather(w_query, "dp", axis=0, tiled=True),
        lax.all_gather(w_key, "dp", axis=0, tiled=True),
        lax.all_gather(w_value, "dp", axis=0, tiled=True),
    )
    query = jnp.dot(normed, full_query, preferred_element_type=jnp.float32)
    key = jnp.dot(normed, full_key, preferred_element_type=jnp.float32)
    value = jnp.dot(normed, full_value, preferred_element_type=jnp.float32)
    query = query + b_query[None, :]
    key = key + b_key[None, :]
    value = value + b_value[None, :]
    heads_here = query.shape[1] // HD
    kv_here = key.shape[1] // HD
    group = heads_here // kv_here
    cosine, sine = rope_tables(within_seq)
    rot_query = rotate(query.reshape(row_count, heads_here, HD), cosine, sine).astype(jnp.bfloat16)
    rot_query = rot_query.reshape(row_count, kv_here, group, HD)
    rot_key = rotate(key.reshape(row_count, kv_here, HD), cosine, sine).astype(jnp.bfloat16)
    value_bf = value.reshape(row_count, kv_here, HD).astype(jnp.bfloat16)
    block_rows = min(512, row_count)

    def one_block(block_number):
        first_row = block_number * block_rows
        query_block = lax.dynamic_slice_in_dim(rot_query, first_row, block_rows, 0)
        query_source = lax.dynamic_slice_in_dim(source_ids, first_row, block_rows, 0)
        query_rows = first_row + jnp.arange(block_rows, dtype=jnp.int32)
        scores = jnp.einsum(
            "bcgd,kcd->cgbk", query_block, rot_key, preferred_element_type=jnp.float32
        )
        scores = scores * HD ** (-0.5)
        allowed = (source_ids[None, :] == query_source[:, None]) & (
            rows[None, :] <= query_rows[:, None]
        )
        scores = jnp.where(allowed[None, None], scores, mask_value)
        peak = jnp.max(scores, axis=-1, keepdims=True)
        raised = jnp.exp(scores - peak)
        weights = (raised / jnp.sum(raised, axis=-1, keepdims=True)).astype(jnp.bfloat16)
        context = jnp.einsum(
            "cgbk,kcd->bcgd", weights, value_bf, preferred_element_type=jnp.float32
        )
        return context.astype(jnp.bfloat16).reshape(block_rows, heads_here * HD)

    outputs = lax.map(one_block, jnp.arange(row_count // block_rows, dtype=jnp.int32))
    return outputs.reshape(row_count, heads_here * HD)


def product_kernel(counts, ropes, chunks, out_lanes, which_ref, *refs):
    refs = list(refs)
    x_refs = [[refs.pop(0) for _ in range(n)] for n in counts[:4]]
    w_ref = refs.pop(0)
    part_refs = [refs.pop(0) for _ in range(counts[4])]
    if ropes:
        bias_ref, angle_ref = (refs.pop(0) for _ in range(2))
    out_refs = [refs.pop(0) for _ in out_lanes]
    w_buf, sems = refs
    rows = out_refs[0].shape[0]
    tile = rows // 2
    wide = w_ref.shape[3]
    copies = [
        [
            pltpu.make_async_copy(
                w_ref.at[which_ref[i], chunk],
                w_buf.at[i, :, pl.ds(n * wide, wide)],
                sems.at[i, n],
            )
            for n, chunk in enumerate(chunks)
        ]
        for i in range(4)
    ]
    for block in copies:
        for copy in block:
            copy.start()

    def piece_rows(pieces, first):
        size = pieces[0].shape[0]
        return pieces[first // size], pl.ds(first % size, tile)

    for first in range(0, rows, tile):
        here = pl.ds(first, tile)
        term = None
        for i in range(4):
            ref, at = piece_rows(x_refs[i], first)
            if first == 0:
                for copy in copies[i]:
                    copy.wait()
            dot = jnp.dot(ref[at, :], w_buf[i], preferred_element_type=jnp.float32)
            term = dot if term is None else term + dot
        if not ropes:
            for out_ref, (low, high) in zip(out_refs, out_lanes):
                out_ref[here, :] = term[:, low:high].astype(out_ref.dtype)
            continue
        (out_ref,) = out_refs
        ref, at = piece_rows(part_refs, first)
        term = term + ref[at, :].astype(jnp.float32) + bias_ref[...]
        angle = angle_ref[here, :]
        turned_angle = pltpu.roll(angle, HD // 2, 1)
        low = lax.broadcasted_iota(jnp.int32, angle.shape, 1) < HD // 2
        cosine = jnp.where(low, angle, turned_angle)
        sine = jnp.where(low, -turned_angle, angle)
        for c, rope in enumerate(ropes):
            head = term[:, c * HD : (c + 1) * HD]
            if rope:
                head = head * cosine + pltpu.roll(head, HD // 2, 1) * sine
            out_ref[here, c * HD : (c + 1) * HD] = head.astype(out_ref.dtype)


def keep(array):
    return pltpu.with_memory_space_constraint(array, pltpu.VMEM)


def projection(which, x_blocks, weights, chunks, outs, finish=None):
    rows = sum(piece.shape[0] for piece in x_blocks[0])
    counts = [len(pieces) for pieces in x_blocks]
    feats, columns = weights.shape[2], weights.shape[3] * len(chunks)
    vmem = pl.BlockSpec(memory_space=pltpu.VMEM)
    operands = [keep(piece) for pieces in x_blocks for piece in pieces]
    in_specs = [vmem] * len(operands) + [pl.BlockSpec(memory_space=pl.ANY)]
    operands.append(weights)
    ropes = None
    if finish is None:
        counts.append(0)
    else:
        ropes, part, bias, angles = finish
        counts.append(1)
        operands += [keep(part), bias, keep(angles)]
        in_specs += [vmem] * 3
    return pl.pallas_call(
        functools.partial(
            product_kernel,
            tuple(counts),
            ropes,
            tuple(chunks),
            tuple((first, last) for first, last, _ in outs),
        ),
        in_specs=[pl.BlockSpec(memory_space=pltpu.SMEM)] + in_specs,
        out_specs=[vmem] * len(outs),
        out_shape=[pltpu.VMEM((rows, last - first), kind) for first, last, kind in outs],
        scratch_shapes=[
            pltpu.VMEM((4, feats, columns), jnp.bfloat16),
            pltpu.SemaphoreType.DMA((4, len(chunks))),
        ],
        compiler_params=pltpu.CompilerParams(vmem_limit_bytes=(8 + columns // 64) * 2**20),
        cost_estimate=kernel_cost,
    )(which, *operands)


def pick_rows(start, length, slot, window, ref, lanes=slice(None)):
    first = pl.multiple_of(jnp.minimum((start // 16) * 16, ref.shape[0] - window), 16)
    row_at = lax.broadcasted_iota(jnp.int32, (slot, window), 0)
    col_at = lax.broadcasted_iota(jnp.int32, (slot, window), 1)
    pick = jnp.where((col_at == row_at + (start - first)) & (row_at < length), 1.0, 0.0)
    rows = jnp.dot(
        pick.astype(jnp.bfloat16), ref[pl.ds(first, window), lanes], preferred_element_type=jnp.float32
    )
    return rows.astype(jnp.bfloat16)


def slots_kernel(slot, window, start_ref, len_ref, in_ref, out_ref):
    for s in range(out_ref.shape[0]):
        out_ref[s] = pick_rows(start_ref[s], len_ref[s], slot, window, in_ref)


def to_slots(starts, lens, array, slot, window):
    count, columns = starts.shape[0], array.shape[1]
    scalars = pl.BlockSpec(memory_space=pltpu.SMEM)
    vmem = pl.BlockSpec(memory_space=pltpu.VMEM)
    return pl.pallas_call(
        functools.partial(slots_kernel, slot, window),
        in_specs=[scalars, scalars, vmem],
        out_specs=vmem,
        out_shape=pltpu.VMEM((count, slot, columns), jnp.bfloat16),
        compiler_params=pltpu.CompilerParams(vmem_limit_bytes=8 * 2**20),
        cost_estimate=kernel_cost,
    )(starts, lens, keep(array))


def attend_kernel(heads, lanes, window, batch, start_ref, len_ref, q_ref, kv_ref, out_ref):
    count, slot = out_ref.shape[:2]
    half = slot // 2

    @pl.loop(0, count, step=batch)
    def _(group):
        for s in range(batch):
            query = pick_rows(
                start_ref[group + s], len_ref[group + s], slot, window, q_ref, lanes
            )
            for block in range(2):
                width = (block + 1) * half
                stacked = jnp.concatenate(
                    [query[block * half : width, h * HD : (h + 1) * HD] for h in range(heads)],
                    axis=0,
                )
                scores = lax.dot_general(
                    stacked,
                    kv_ref[group + s, :width, :HD],
                    (((1,), (1,)), ((), ())),
                    preferred_element_type=jnp.float32,
                )
                row_at = lax.broadcasted_iota(jnp.int32, scores.shape, 0) & (half - 1)
                col_at = lax.broadcasted_iota(jnp.int32, scores.shape, 1)
                scores = jnp.where(
                    col_at <= row_at + block * half, scores * HD ** (-0.5), mask_value
                )
                peak = jnp.max(scores, axis=-1, keepdims=True)
                raised = jnp.exp(scores - peak)
                weights = raised * (1.0 / jnp.sum(raised, axis=-1, keepdims=True))
                context = jnp.dot(
                    weights.astype(jnp.bfloat16),
                    kv_ref[group + s, :width, HD:],
                    preferred_element_type=jnp.float32,
                ).astype(out_ref.dtype)
                for h in range(heads):
                    out_ref[group + s, block * half : width, h * HD : (h + 1) * HD] = context[
                        h * half : (h + 1) * half
                    ]


def attend(starts, lens, query, columns, kv_slots, window):
    low, high = columns
    count, slot = kv_slots.shape[:2]
    scalars = pl.BlockSpec(memory_space=pltpu.SMEM)
    vmem = pl.BlockSpec(memory_space=pltpu.VMEM)
    return pl.pallas_call(
        functools.partial(attend_kernel, (high - low) // HD, pl.ds(low, high - low), window, 4),
        in_specs=[scalars, scalars, vmem, vmem],
        out_specs=vmem,
        out_shape=pltpu.VMEM((count, slot, high - low), jnp.bfloat16),
        compiler_params=pltpu.CompilerParams(vmem_limit_bytes=8 * 2**20),
        cost_estimate=kernel_cost,
    )(starts, lens, keep(query), keep(kv_slots))


def place_kernel(count, slot, window, start_ref, len_ref, in_ref, *rest):
    out_ref, total = rest[-2:]
    rows = total.shape[0]
    total[...] = jnp.zeros_like(total)
    row_at = lax.broadcasted_iota(jnp.int32, (window, slot), 0)
    col_at = lax.broadcasted_iota(jnp.int32, (window, slot), 1)
    for s in range(count):
        start = start_ref[s]
        first = pl.multiple_of(jnp.minimum((start // 8) * 8, rows - window), 8)
        pick = jnp.where(
            (row_at == col_at + (start - first)) & (col_at < len_ref[s]), 1.0, 0.0
        ).astype(jnp.bfloat16)
        total[pl.ds(first, window), :] += jnp.dot(
            pick, in_ref[s], preferred_element_type=jnp.float32
        )
    out_ref[...] = total[...].astype(out_ref.dtype)


def place(starts, lens, slots, rows, which, all_columns, before):
    count, slot, columns = slots.shape
    window = min(rows, slot + 8)
    in_specs = [pl.BlockSpec((count, slot, columns), lambda r, a, b: (0, 0, 0))]
    operands, aliases = [slots], {}
    if before is not None:
        in_specs.append(pl.BlockSpec(memory_space=pl.ANY))
        operands.append(before)
        aliases = {3: 0}
    grid_spec = pltpu.PrefetchScalarGridSpec(
        num_scalar_prefetch=2,
        grid=(1,),
        in_specs=in_specs,
        out_specs=pl.BlockSpec((rows, columns), lambda r, a, b: (0, which)),
        scratch_shapes=[pltpu.VMEM((rows, columns), jnp.float32)],
    )
    return pl.pallas_call(
        functools.partial(place_kernel, count, slot, window),
        grid_spec=grid_spec,
        out_shape=jax.ShapeDtypeStruct((rows, all_columns), jnp.bfloat16),
        input_output_aliases=aliases,
        compiler_params=pltpu.CompilerParams(vmem_limit_bytes=8 * 2**20),
        cost_estimate=kernel_cost,
    )(starts, lens, *operands)


def local_line(
    rollout_states,
    norm_gain,
    w_query,
    w_key,
    w_value,
    b_query,
    b_key,
    b_value,
    seq_lengths,
    seq_dest,
    seq_offset,
):
    learners = lax.axis_size("dp")
    line = learners // 2
    me = lax.axis_index("dp")
    z, x = me // 2, me % 2
    t = lax.axis_index("tensor")
    row_count, feature_count = rollout_states.shape
    slot = 2 * row_count // learners
    half = feature_count // 2
    middle = row_count // 2

    def after(array, *others):
        return lax.optimization_barrier((array, *others))[0]

    def swap_x(array):
        return lax.ppermute(array, "dp", [(i, i ^ 1) for i in range(learners)])

    def swap_y(array):
        return lax.ppermute(array, "tensor", [(i, i ^ 2) for i in range(4)])

    def swap_core(array):
        return lax.ppermute(array, "tensor", [(i, i ^ 1) for i in range(4)])

    wide = 2 * HD
    along_z = [[2 * i + j for i in range(line)] for j in range(2)]
    groups = [
        [jnp.concatenate([w_key, w_value], axis=1), w_query[:, :wide]],
        [w_query[:, wide : 2 * wide], w_query[:, 2 * wide : 3 * wide]],
        [w_query[:, 3 * wide :]],
    ]
    weights = []
    for group in groups:
        gathered = lax.all_gather(jnp.stack(group), "dp", axis_index_groups=along_z)
        weights.append(pltpu.with_memory_space_constraint(gathered, pltpu.HBM))
    bias_kv = jnp.concatenate([b_key, b_value])[None, :]
    biases = [b_query[None, low : low + wide] for low in range(0, w_query.shape[1], wide)]

    states = rollout_states
    widened = states.astype(jnp.float32)
    squares = jnp.sum(widened * widened, axis=-1)
    squares = squares + swap_core(squares)
    squares = squares + swap_y(squares)
    scale = lax.rsqrt(squares[:, None] / (4 * feature_count) + norm_eps)

    def normed(first):
        part = lax.dynamic_slice_in_dim(states, first, half, 1).astype(jnp.float32)
        gain = lax.dynamic_slice_in_dim(norm_gain, t * feature_count + first, half, 0)
        return (part * scale * gain[None, :]).astype(jnp.bfloat16)

    own, give = normed(x * half), normed((1 - x) * half)

    near_a = swap_x(give[:middle])
    own_a = swap_y(own[:middle])
    own_core = swap_core(own)
    near_b = swap_x(after(give[middle:], near_a))
    diag_a = swap_y(after(near_a, own_a))
    near_a_core = swap_core(near_a)
    own_a_core = swap_core(after(own_a, near_a))
    diag_b = swap_y(after(near_b, diag_a))
    near_b_core = swap_core(after(near_b, diag_a))
    diag_a_core = swap_core(after(diag_a, near_b))
    own_b = swap_y(after(own[middle:], diag_b))
    diag_b_core = swap_core(diag_b)
    near_ax = [[near_a], [near_a_core], [diag_a], [diag_a_core]]
    near_bx = [[near_b], [near_b_core], [diag_b], [diag_b_core]]
    near_x = [a + b for a, b in zip(near_ax, near_bx)]
    which = jnp.stack([t ^ i for i in range(4)]).astype(jnp.int32)

    lengths = seq_lengths.reshape(learners, learners)
    dests = seq_dest.reshape(learners, learners)
    offsets = seq_offset.reshape(learners, learners)
    starts = jnp.cumsum(lengths, axis=1) - lengths
    peer_ids = jnp.arange(learners, dtype=jnp.int32)
    rows = jnp.arange(row_count, dtype=jnp.int32)
    length = lax.dynamic_index_in_dim(lengths, me, 0, keepdims=False)
    start = lax.dynamic_index_in_dim(starts, me, 0, keepdims=False)
    dest = lax.dynamic_index_in_dim(dests, me, 0, keepdims=False)
    match = (dest[None, :] == peer_ids[:, None]).astype(jnp.int32)
    send_start = jnp.sum(match * start[None, :], axis=1)
    send_length = jnp.sum(match * length[None, :], axis=1)
    inside = (rows[:, None] >= start[None, :]) & (rows[:, None] < (start + length)[None, :])
    position = rows - jnp.sum(inside.astype(jnp.int32) * start[None, :], axis=1)
    angles = jnp.concatenate(rope_tables(position), axis=1)
    matched = (dests == me).astype(jnp.int32)
    run_start = jnp.sum(matched * offsets, axis=1)
    run_length = jnp.sum(matched * lengths, axis=1)

    window = min(row_count, -(-(slot + 16) // 128) * 128)

    def send(outgoing):
        return lax.all_to_all(outgoing, "dp", split_axis=0, concat_axis=0, tiled=True)

    def receive(c, incoming, before, *others):
        start_at = after(run_start, *others)
        return place(
            start_at, run_length, incoming, row_count, c, w_query.shape[1], before
        )

    first, second, third = weights
    whole = [(0, wide, jnp.bfloat16)]

    def partial(group, chunks, outs, *others):
        return projection(after(which, *others), near_x, group, chunks, outs)

    def contexts(c, group, chunk, got, others, attend_after=()):
        ending = ((True, True), got, biases[c], angles)
        (rot,) = projection(after(which, *others), own_x, group, (chunk,), whole, ending)
        start_at = after(send_start, *attend_after)
        return attend(start_at, send_length, rot, (0, wide), kv_slots, window)

    outs = [(0, wide, jnp.float32), (wide, 2 * wide, jnp.bfloat16)]
    part_kv, part_0 = partial(first, (0, 1), outs)
    got_kv = swap_x(part_kv)
    own_b_core = swap_core(after(own_b, part_kv))
    own_x = [[own], [own_core], [own_a, own_b], [own_a_core, own_b_core]]
    got_0 = swap_x(after(part_0, got_kv))
    ending = ((True, False), got_kv, bias_kv, angles)
    (kv,) = projection(which, own_x, first, (0,), whole, ending)
    kv_slots = to_slots(send_start, send_length, kv, slot, window)
    out_0 = contexts(0, first, 1, got_0, (kv_slots,))
    in_0 = send(out_0)
    outs = [(0, wide, jnp.bfloat16), (wide, 2 * wide, jnp.bfloat16)]
    part_1, part_2 = partial(second, (0, 1), outs, out_0)
    got_1 = swap_x(part_1)
    got_2 = swap_x(after(part_2, got_1))
    out_1 = contexts(1, second, 0, got_1, (part_2,), (got_2,))
    in_1 = send(out_1)
    out_2 = contexts(2, second, 1, got_2, (out_1,))
    (part_3,) = partial(third, (0,), whole, out_2)
    got_3 = swap_x(part_3)
    in_2 = send(after(out_2, in_0, part_3))
    out_3 = contexts(3, third, 0, got_3, (out_2,))
    in_3 = send(after(out_3, in_1))
    result = receive(0, in_0, None, part_3)
    result = receive(1, in_1, result, out_3)
    result = receive(2, in_2, result, out_3)
    return receive(3, in_3, result)


def solution(mesh):
    placed = (
        P("dp", "tensor"),
        P(),
        P("dp", "tensor"),
        P("dp", "tensor"),
        P("dp", "tensor"),
        P("tensor"),
        P("tensor"),
        P("tensor"),
        P(),
        P(),
        P(),
    )
    fits_line = mesh.shape["dp"] == 8 and mesh.shape["tensor"] == 4
    return jax.shard_map(
        local_line if fits_line else local_any,
        mesh=mesh,
        in_specs=placed,
        out_specs=P("dp", "tensor"),
        check_vma=False,
    )
```

```python
import functools

import jax
import jax.numpy as jnp
from jax import lax
from jax.experimental import pallas as pl
from jax.experimental.pallas import tpu as pltpu
from jax.sharding import PartitionSpec as P

HD = 128

rope_base = 1000000.0
norm_eps = 1e-06
mask_value = -1e30
kernel_cost = pl.CostEstimate(flops=4 * 10**9, bytes_accessed=2**20, transcendentals=0)


def rope_tables(positions):
    half_dim = HD // 2
    frequency = rope_base ** (-(jnp.arange(half_dim).astype(jnp.float32) * 2.0 / HD))
    angles = positions.astype(jnp.float32)[:, None] * frequency[None, :]
    return (jnp.cos(angles), jnp.sin(angles))


def rotate(states, cosine, sine):
    half_dim = states.shape[-1] // 2
    first_half = states[..., :half_dim]
    second_half = states[..., half_dim:]
    cos_wide = cosine[:, None, :]
    sin_wide = sine[:, None, :]
    return jnp.concatenate(
        [
            first_half * cos_wide - second_half * sin_wide,
            second_half * cos_wide + first_half * sin_wide,
        ],
        axis=-1,
    )


def local_any(
    rollout_states,
    norm_gain,
    w_query,
    w_key,
    w_value,
    b_query,
    b_key,
    b_value,
    seq_lengths,
    seq_dest,
    seq_offset,
):
    learners = lax.axis_size("dp")
    own_index = lax.axis_index("dp")
    row_count, feature_count = rollout_states.shape
    capacity = 2 * row_count // learners - 1
    lengths = seq_lengths.reshape(learners, learners)
    dests = seq_dest.reshape(learners, learners)
    offsets = seq_offset.reshape(learners, learners)
    starts = jnp.cumsum(lengths, axis=1) - lengths
    peer_ids = jnp.arange(learners, dtype=jnp.int32)
    own_length = lax.dynamic_index_in_dim(lengths, own_index, 0, keepdims=False)
    own_start = lax.dynamic_index_in_dim(starts, own_index, 0, keepdims=False)
    own_dest = lax.dynamic_index_in_dim(dests, own_index, 0, keepdims=False)
    match_send = (own_dest[None, :] == peer_ids[:, None]).astype(jnp.int32)
    send_start = jnp.sum(match_send * own_start[None, :], axis=1)
    send_length = jnp.sum(match_send * own_length[None, :], axis=1)
    slot_index = jnp.arange(capacity, dtype=jnp.int32)
    pick_rows = send_start[:, None] + slot_index[None, :]
    padded = jnp.concatenate(
        [rollout_states, jnp.zeros((capacity, feature_count), rollout_states.dtype)], axis=0
    )
    live_slots = (slot_index[None, :] < send_length[:, None])[..., None]
    outgoing = jnp.where(
        live_slots, jnp.take(padded, pick_rows, axis=0), jnp.zeros((), rollout_states.dtype)
    )
    incoming = lax.all_to_all(outgoing, "dp", split_axis=0, concat_axis=0, tiled=True)
    matched = (dests == own_index).astype(jnp.int32)
    run_start = jnp.sum(matched * offsets, axis=1)
    run_length = jnp.sum(matched * lengths, axis=1)
    rows = jnp.arange(row_count, dtype=jnp.int32)
    inside = (
        (rows[:, None] >= run_start[None, :]) & (rows[:, None] < (run_start + run_length)[None, :])
    ).astype(jnp.int32)
    source_ids = jnp.sum(inside * peer_ids[None, :], axis=1)
    within_seq = rows - jnp.sum(inside * run_start[None, :], axis=1)
    arrived = jnp.take(
        incoming.reshape(learners * capacity, feature_count),
        source_ids * capacity + within_seq,
        axis=0,
    )
    gathered = lax.all_gather(arrived, "tensor", axis=1, tiled=True)
    widened = gathered.astype(jnp.float32)
    statistic = jnp.mean(widened * widened, axis=-1, keepdims=True)
    normed = (widened * lax.rsqrt(statistic + norm_eps) * norm_gain[None, :]).astype(jnp.bfloat16)
    full_query, full_key, full_value = (
        lax.all_gather(w_query, "dp", axis=0, tiled=True),
        lax.all_gather(w_key, "dp", axis=0, tiled=True),
        lax.all_gather(w_value, "dp", axis=0, tiled=True),
    )
    query = jnp.dot(normed, full_query, preferred_element_type=jnp.float32)
    key = jnp.dot(normed, full_key, preferred_element_type=jnp.float32)
    value = jnp.dot(normed, full_value, preferred_element_type=jnp.float32)
    query = query + b_query[None, :]
    key = key + b_key[None, :]
    value = value + b_value[None, :]
    heads_here = query.shape[1] // HD
    kv_here = key.shape[1] // HD
    group = heads_here // kv_here
    cosine, sine = rope_tables(within_seq)
    rot_query = rotate(query.reshape(row_count, heads_here, HD), cosine, sine).astype(jnp.bfloat16)
    rot_query = rot_query.reshape(row_count, kv_here, group, HD)
    rot_key = rotate(key.reshape(row_count, kv_here, HD), cosine, sine).astype(jnp.bfloat16)
    value_bf = value.reshape(row_count, kv_here, HD).astype(jnp.bfloat16)
    block_rows = min(512, row_count)

    def one_block(block_number):
        first_row = block_number * block_rows
        query_block = lax.dynamic_slice_in_dim(rot_query, first_row, block_rows, 0)
        query_source = lax.dynamic_slice_in_dim(source_ids, first_row, block_rows, 0)
        query_rows = first_row + jnp.arange(block_rows, dtype=jnp.int32)
        scores = jnp.einsum(
            "bcgd,kcd->cgbk", query_block, rot_key, preferred_element_type=jnp.float32
        )
        scores = scores * HD ** (-0.5)
        allowed = (source_ids[None, :] == query_source[:, None]) & (
            rows[None, :] <= query_rows[:, None]
        )
        scores = jnp.where(allowed[None, None], scores, mask_value)
        peak = jnp.max(scores, axis=-1, keepdims=True)
        raised = jnp.exp(scores - peak)
        weights = (raised / jnp.sum(raised, axis=-1, keepdims=True)).astype(jnp.bfloat16)
        context = jnp.einsum(
            "cgbk,kcd->bcgd", weights, value_bf, preferred_element_type=jnp.float32
        )
        return context.astype(jnp.bfloat16).reshape(block_rows, heads_here * HD)

    outputs = lax.map(one_block, jnp.arange(row_count // block_rows, dtype=jnp.int32))
    return outputs.reshape(row_count, heads_here * HD)


def pack_kernel(counts, *refs):
    refs = list(refs)
    pieces = [[refs.pop(0) for _ in range(n)] for n in counts]
    out_ref, sems = refs
    copies = []
    for i, block in enumerate(pieces):
        first = 0
        for n, piece in enumerate(block):
            rows = piece.shape[0]
            copies.append(
                pltpu.make_async_copy(piece, out_ref.at[i, pl.ds(first, rows)], sems.at[i, n])
            )
            first += rows
    for copy in copies:
        copy.start()
    for copy in copies:
        copy.wait()


def pack(blocks, in_vmem):
    counts = tuple(len(pieces) for pieces in blocks)
    rows = sum(piece.shape[0] for piece in blocks[0])
    feats = blocks[0][0].shape[1]
    operands = [piece for pieces in blocks for piece in pieces]
    shape = (len(blocks), rows, feats)
    if in_vmem:
        space, out_shape = pltpu.VMEM, pltpu.VMEM(shape, jnp.bfloat16)
    else:
        space, out_shape = pl.ANY, jax.ShapeDtypeStruct(shape, jnp.bfloat16)
    return pl.pallas_call(
        functools.partial(pack_kernel, counts),
        in_specs=[pl.BlockSpec(memory_space=pl.ANY)] * len(operands),
        out_specs=pl.BlockSpec(memory_space=space),
        out_shape=out_shape,
        scratch_shapes=[pltpu.SemaphoreType.DMA((len(blocks), 2))],
        compiler_params=pltpu.CompilerParams(vmem_limit_bytes=4 * 2**20),
        cost_estimate=kernel_cost,
    )(*operands)


def product_kernel(x_count, ropes, chunks, out_lanes, which_ref, *refs):
    refs = list(refs)
    x_refs = [refs.pop(0) for _ in range(x_count)]
    w_ref = refs.pop(0)
    if ropes:
        part_ref, bias_ref, angle_ref = (refs.pop(0) for _ in range(3))
    out_refs = [refs.pop(0) for _ in out_lanes]
    w_buf, sems = refs
    rows = out_refs[0].shape[0]
    part_rows = x_refs[0].shape[1]
    tile = min(512, part_rows)
    wide = w_ref.shape[3]
    copies = [
        [
            pltpu.make_async_copy(
                w_ref.at[which_ref[i], chunk],
                w_buf.at[i, :, pl.ds(n * wide, wide)],
                sems.at[i, n],
            )
            for n, chunk in enumerate(chunks)
        ]
        for i in range(4)
    ]
    for block in copies:
        for copy in block:
            copy.start()

    for first, x_ref in zip(range(0, rows, part_rows), x_refs):
        if first == 0:
            for block in copies:
                for copy in block:
                    copy.wait()

        @pl.loop(0, part_rows, step=tile)
        def _(at, first=first, x_ref=x_ref):
            here = pl.ds(pl.multiple_of(first + at, tile), tile)
            term = None
            for i in range(4):
                rows_here = x_ref[i, pl.ds(pl.multiple_of(at, tile), tile), :]
                dot = jnp.dot(rows_here, w_buf[i], preferred_element_type=jnp.float32)
                term = dot if term is None else term + dot
            if not ropes:
                for out_ref, (low, high) in zip(out_refs, out_lanes):
                    out_ref[here, :] = term[:, low:high].astype(out_ref.dtype)
                return
            (out_ref,) = out_refs
            term = term + part_ref[here, :].astype(jnp.float32) + bias_ref[...]
            angle = angle_ref[here, :]
            turned_angle = pltpu.roll(angle, HD // 2, 1)
            low = lax.broadcasted_iota(jnp.int32, angle.shape, 1) < HD // 2
            cosine = jnp.where(low, angle, turned_angle)
            sine = jnp.where(low, -turned_angle, angle)
            for c, rope in enumerate(ropes):
                head = term[:, c * HD : (c + 1) * HD]
                if rope:
                    head = head * cosine + pltpu.roll(head, HD // 2, 1) * sine
                out_ref[here, c * HD : (c + 1) * HD] = head.astype(out_ref.dtype)


def keep(array):
    return pltpu.with_memory_space_constraint(array, pltpu.VMEM)


def projection(which, x_parts, weights, chunks, outs, finish=None):
    rows = sum(part.shape[1] for part in x_parts)
    feats, columns = weights.shape[2], weights.shape[3] * len(chunks)
    vmem = pl.BlockSpec(memory_space=pltpu.VMEM)
    operands = list(x_parts)
    in_specs = [vmem] * len(operands) + [pl.BlockSpec(memory_space=pl.ANY)]
    operands.append(weights)
    ropes = None
    if finish is not None:
        ropes, part, bias, angles = finish
        operands += [keep(part), bias, angles]
        in_specs += [vmem] * 3
    return pl.pallas_call(
        functools.partial(
            product_kernel,
            len(x_parts),
            ropes,
            tuple(chunks),
            tuple((first, last) for first, last, _ in outs),
        ),
        in_specs=[pl.BlockSpec(memory_space=pltpu.SMEM)] + in_specs,
        out_specs=[vmem] * len(outs),
        out_shape=[pltpu.VMEM((rows, last - first), kind) for first, last, kind in outs],
        scratch_shapes=[
            pltpu.VMEM((4, feats, columns), jnp.bfloat16),
            pltpu.SemaphoreType.DMA((4, len(chunks))),
        ],
        compiler_params=pltpu.CompilerParams(vmem_limit_bytes=(10 + columns // 128) * 2**20),
        cost_estimate=kernel_cost,
    )(which, *operands)


def pick_rows(start, length, slot, window, ref, lanes=slice(None)):
    first = pl.multiple_of(jnp.minimum((start // 16) * 16, ref.shape[0] - window), 16)
    row_at = lax.broadcasted_iota(jnp.int32, (slot, window), 0)
    col_at = lax.broadcasted_iota(jnp.int32, (slot, window), 1)
    pick = jnp.where((col_at == row_at + (start - first)) & (row_at < length), 1.0, 0.0)
    rows = jnp.dot(
        pick.astype(jnp.bfloat16), ref[pl.ds(first, window), lanes], preferred_element_type=jnp.float32
    )
    return rows.astype(jnp.bfloat16)


def slots_kernel(slot, window, start_ref, len_ref, in_ref, out_ref):
    for s in range(out_ref.shape[0]):
        out_ref[s] = pick_rows(start_ref[s], len_ref[s], slot, window, in_ref)


def to_slots(starts, lens, array, slot, window):
    count, columns = starts.shape[0], array.shape[1]
    scalars = pl.BlockSpec(memory_space=pltpu.SMEM)
    vmem = pl.BlockSpec(memory_space=pltpu.VMEM)
    return pl.pallas_call(
        functools.partial(slots_kernel, slot, window),
        in_specs=[scalars, scalars, vmem],
        out_specs=vmem,
        out_shape=pltpu.VMEM((count, slot, columns), jnp.bfloat16),
        compiler_params=pltpu.CompilerParams(vmem_limit_bytes=5 * 2**20),
        cost_estimate=kernel_cost,
    )(starts, lens, keep(array))


def attend_kernel(heads, window, start_ref, len_ref, q_ref, kv_ref, *out_refs):
    slot = out_refs[0].shape[0]
    half = slot // 2
    for s, out_ref in enumerate(out_refs):
        query = pick_rows(start_ref[s], len_ref[s], slot, window, q_ref)
        for block in range(2):
            width = (block + 1) * half
            stacked = jnp.concatenate(
                [query[block * half : width, h * HD : (h + 1) * HD] for h in range(heads)], axis=0
            )
            scores = lax.dot_general(
                stacked,
                kv_ref[s, :width, :HD],
                (((1,), (1,)), ((), ())),
                preferred_element_type=jnp.float32,
            )
            row_at = lax.broadcasted_iota(jnp.int32, scores.shape, 0) & (half - 1)
            col_at = lax.broadcasted_iota(jnp.int32, scores.shape, 1)
            scores = jnp.where(col_at <= row_at + block * half, scores * HD ** (-0.5), mask_value)
            peak = jnp.max(scores, axis=-1, keepdims=True)
            raised = jnp.exp(scores - peak)
            weights = raised * (1.0 / jnp.sum(raised, axis=-1, keepdims=True))
            context = jnp.dot(
                weights.astype(jnp.bfloat16),
                kv_ref[s, :width, HD:],
                preferred_element_type=jnp.float32,
            ).astype(out_ref.dtype)
            for h in range(heads):
                out_ref[block * half : width, h * HD : (h + 1) * HD] = context[
                    h * half : (h + 1) * half
                ]


def attend(starts, lens, query, kv_slots, window):
    columns = query.shape[1]
    count, slot = kv_slots.shape[:2]
    scalars = pl.BlockSpec(memory_space=pltpu.SMEM)
    vmem = pl.BlockSpec(memory_space=pltpu.VMEM)
    return pl.pallas_call(
        functools.partial(attend_kernel, columns // HD, window),
        in_specs=[scalars, scalars, vmem, vmem],
        out_specs=[vmem] * count,
        out_shape=[pltpu.VMEM((slot, columns), jnp.bfloat16)] * count,
        compiler_params=pltpu.CompilerParams(vmem_limit_bytes=6 * 2**20),
        cost_estimate=kernel_cost,
    )(starts, lens, keep(query), kv_slots)


def place_kernel(count, window, start_ref, len_ref, *refs):
    in_refs, (out_ref, total) = refs[:count], refs[-2:]
    rows, slot = total.shape[0], in_refs[0].shape[0]
    total[...] = jnp.zeros_like(total)
    row_at = lax.broadcasted_iota(jnp.int32, (window, slot), 0)
    col_at = lax.broadcasted_iota(jnp.int32, (window, slot), 1)
    for s, in_ref in enumerate(in_refs):
        start = start_ref[s]
        first = pl.multiple_of(jnp.minimum((start // 8) * 8, rows - window), 8)
        pick = jnp.where(
            (row_at == col_at + (start - first)) & (col_at < len_ref[s]), 1.0, 0.0
        ).astype(jnp.bfloat16)
        total[pl.ds(first, window), :] += jnp.dot(
            pick, in_ref[...], preferred_element_type=jnp.float32
        )
    out_ref[...] = total[...].astype(out_ref.dtype)


def place(starts, lens, slots, rows, which, all_columns, before):
    count, (slot, columns) = len(slots), slots[0].shape
    window = min(rows, slot + 8)
    in_specs = [pl.BlockSpec((slot, columns), lambda r, a, b: (0, 0))] * count
    operands, aliases = list(slots), {}
    if before is not None:
        in_specs.append(pl.BlockSpec(memory_space=pl.ANY))
        operands.append(before)
        aliases = {2 + count: 0}
    grid_spec = pltpu.PrefetchScalarGridSpec(
        num_scalar_prefetch=2,
        grid=(1,),
        in_specs=in_specs,
        out_specs=pl.BlockSpec((rows, columns), lambda r, a, b: (0, which)),
        scratch_shapes=[pltpu.VMEM((rows, columns), jnp.float32)],
    )
    return pl.pallas_call(
        functools.partial(place_kernel, count, window),
        grid_spec=grid_spec,
        out_shape=jax.ShapeDtypeStruct((rows, all_columns), jnp.bfloat16),
        input_output_aliases=aliases,
        compiler_params=pltpu.CompilerParams(vmem_limit_bytes=8 * 2**20),
        cost_estimate=kernel_cost,
    )(starts, lens, *operands)


def local_line(
    rollout_states,
    norm_gain,
    w_query,
    w_key,
    w_value,
    b_query,
    b_key,
    b_value,
    seq_lengths,
    seq_dest,
    seq_offset,
):
    learners = lax.axis_size("dp")
    line = learners // 2
    me = lax.axis_index("dp")
    z, x = me // 2, me % 2
    t = lax.axis_index("tensor")
    row_count, feature_count = rollout_states.shape
    slot = 2 * row_count // learners
    half = feature_count // 2
    middle = row_count // 2

    def after(array, *others):
        return lax.optimization_barrier((array, *others))[0]

    def swap_x(array):
        return lax.ppermute(array, "dp", [(i, i ^ 1) for i in range(learners)])

    def swap_y(array):
        return lax.ppermute(array, "tensor", [(i, i ^ 2) for i in range(4)])

    def swap_core(array):
        return lax.ppermute(array, "tensor", [(i, i ^ 1) for i in range(4)])

    wide = 2 * HD
    along_z = [[2 * i + j for i in range(line)] for j in range(2)]
    groups = [
        [jnp.concatenate([w_key, w_value], axis=1), w_query[:, :wide]],
        [w_query[:, wide : 2 * wide], w_query[:, 2 * wide : 3 * wide]],
        [w_query[:, 3 * wide :]],
    ]
    weights = []
    for group in groups:
        gathered = lax.all_gather(jnp.stack(group), "dp", axis_index_groups=along_z)
        weights.append(pltpu.with_memory_space_constraint(gathered, pltpu.HBM))
    bias_kv = jnp.concatenate([b_key, b_value])[None, :]
    biases = [b_query[None, low : low + wide] for low in range(0, w_query.shape[1], wide)]

    states = rollout_states
    widened = states.astype(jnp.float32)
    squares = jnp.sum(widened * widened, axis=-1)
    squares = squares + swap_core(squares)
    squares = squares + swap_y(squares)
    scale = lax.rsqrt(squares[:, None] / (4 * feature_count) + norm_eps)

    def normed(first):
        part = lax.dynamic_slice_in_dim(states, first, half, 1).astype(jnp.float32)
        gain = lax.dynamic_slice_in_dim(norm_gain, t * feature_count + first, half, 0)
        return (part * scale * gain[None, :]).astype(jnp.bfloat16)

    own, give = normed(x * half), normed((1 - x) * half)

    near_a = swap_x(give[:middle])
    own_a = swap_y(own[:middle])
    own_core = swap_core(own)
    near_b = swap_x(after(give[middle:], near_a))
    diag_a = swap_y(after(near_a, own_a))
    near_a_core = swap_core(near_a)
    own_a_core = swap_core(after(own_a, near_a))
    diag_b = swap_y(after(near_b, diag_a))
    near_b_core = swap_core(after(near_b, diag_a))
    diag_a_core = swap_core(after(diag_a, near_b))
    own_b = swap_y(after(own[middle:], diag_b))
    diag_b_core = swap_core(diag_b)
    near_ax = [[near_a], [near_a_core], [diag_a], [diag_a_core]]
    near_bx = [[near_b], [near_b_core], [diag_b], [diag_b_core]]
    near_x = [pack(near_ax, False), pack(near_bx, False)]
    which = jnp.stack([t ^ i for i in range(4)]).astype(jnp.int32)

    lengths = seq_lengths.reshape(learners, learners)
    dests = seq_dest.reshape(learners, learners)
    offsets = seq_offset.reshape(learners, learners)
    starts = jnp.cumsum(lengths, axis=1) - lengths
    peer_ids = jnp.arange(learners, dtype=jnp.int32)
    rows = jnp.arange(row_count, dtype=jnp.int32)
    length = lax.dynamic_index_in_dim(lengths, me, 0, keepdims=False)
    start = lax.dynamic_index_in_dim(starts, me, 0, keepdims=False)
    dest = lax.dynamic_index_in_dim(dests, me, 0, keepdims=False)
    partners = me ^ peer_ids
    match = (dest[None, :] == partners[:, None]).astype(jnp.int32)
    send_start = jnp.sum(match * start[None, :], axis=1)
    send_length = jnp.sum(match * length[None, :], axis=1)
    inside = (rows[:, None] >= start[None, :]) & (rows[:, None] < (start + length)[None, :])
    position = rows - jnp.sum(inside.astype(jnp.int32) * start[None, :], axis=1)
    angles = keep(jnp.concatenate(rope_tables(position), axis=1))
    matched = (dests == me).astype(jnp.int32)
    match = (peer_ids[None, :] == partners[:, None]).astype(jnp.int32)
    run_start = jnp.sum(match * jnp.sum(matched * offsets, axis=1)[None, :], axis=1)
    run_length = jnp.sum(match * jnp.sum(matched * lengths, axis=1)[None, :], axis=1)

    window = min(row_count, -(-(slot + 16) // 128) * 128)

    def send(outgoing):
        incoming = [outgoing[0]]
        for d in range(1, learners):
            pairs = [(i, i ^ d) for i in range(learners)]
            incoming.append(lax.ppermute(outgoing[d], "dp", pairs))
        return incoming

    def receive(c, incoming, before, *others):
        start_at = after(run_start, *others)
        return place(
            start_at, run_length, incoming, row_count, c, w_query.shape[1], before
        )

    first, second, third = weights
    whole = [(0, wide, jnp.bfloat16)]

    def partial(group, chunks, outs, *others):
        return projection(after(which, *others), near_x, group, chunks, outs)

    def contexts(c, group, chunk, got, others, attend_after=()):
        ending = ((True, True), got, biases[c], angles)
        (rot,) = projection(after(which, *others), own_x, group, (chunk,), whole, ending)
        start_at = after(send_start, *attend_after)
        return attend(start_at, send_length, rot, kv_slots, window)

    outs = [(0, wide, jnp.float32), (wide, 2 * wide, jnp.bfloat16)]
    part_kv, part_0 = partial(first, (0, 1), outs)
    got_kv = swap_x(part_kv)
    own_b_core = swap_core(after(own_b, part_kv))
    own_x = [keep(pack([[own], [own_core], [own_a, own_b], [own_a_core, own_b_core]], True))]
    got_0 = swap_x(after(part_0, got_kv))
    ending = ((True, False), got_kv, bias_kv, angles)
    (kv,) = projection(which, own_x, first, (0,), whole, ending)
    kv_slots = keep(to_slots(send_start, send_length, kv, slot, window))
    out_0 = contexts(0, first, 1, got_0, (kv,))
    in_0 = send(out_0)
    outs = [(0, wide, jnp.bfloat16), (wide, 2 * wide, jnp.bfloat16)]
    part_1, part_2 = partial(second, (0, 1), outs, out_0[0])
    got_1 = swap_x(part_1)
    got_2 = swap_x(after(part_2, got_1))
    out_1 = contexts(1, second, 0, got_1, (part_2,), (got_2,))
    in_1 = send(out_1)
    (part_3,) = partial(third, (0,), whole, out_1[0])
    got_3 = swap_x(part_3)
    out_2 = contexts(2, second, 1, got_2, (part_3,), (got_3,))
    in_2 = send(out_2)
    out_3 = contexts(3, third, 0, got_3, (out_2[0],))
    in_3 = send(out_3)
    result = receive(0, in_0, None, part_3)
    result = receive(1, in_1, result, out_3[0])
    result = receive(2, in_2, result, out_3[0])
    return receive(3, in_3, result)


def solution(mesh):
    placed = (
        P("dp", "tensor"),
        P(),
        P("dp", "tensor"),
        P("dp", "tensor"),
        P("dp", "tensor"),
        P("tensor"),
        P("tensor"),
        P("tensor"),
        P(),
        P(),
        P(),
    )
    fits_line = mesh.shape["dp"] == 8 and mesh.shape["tensor"] == 4
    return jax.shard_map(
        local_line if fits_line else local_any,
        mesh=mesh,
        in_specs=placed,
        out_specs=P("dp", "tensor"),
        check_vma=False,
    )
```

```python
import functools

import jax
import jax.numpy as jnp
from jax import lax
from jax.experimental import pallas as pl
from jax.experimental.pallas import tpu as pltpu
from jax.sharding import PartitionSpec as P

HD = 128

rope_base = 1000000.0
norm_eps = 1e-06
mask_value = -1e30
kernel_cost = pl.CostEstimate(flops=2 * 10**8, bytes_accessed=2**20, transcendentals=0)


def rope_tables(positions):
    half_dim = HD // 2
    frequency = rope_base ** (-(jnp.arange(half_dim).astype(jnp.float32) * 2.0 / HD))
    angles = positions.astype(jnp.float32)[:, None] * frequency[None, :]
    return (jnp.cos(angles), jnp.sin(angles))


def rotate(states, cosine, sine):
    half_dim = states.shape[-1] // 2
    first_half = states[..., :half_dim]
    second_half = states[..., half_dim:]
    cos_wide = cosine[:, None, :]
    sin_wide = sine[:, None, :]
    return jnp.concatenate(
        [
            first_half * cos_wide - second_half * sin_wide,
            second_half * cos_wide + first_half * sin_wide,
        ],
        axis=-1,
    )


def local_any(
    rollout_states,
    norm_gain,
    w_query,
    w_key,
    w_value,
    b_query,
    b_key,
    b_value,
    seq_lengths,
    seq_dest,
    seq_offset,
):
    learners = lax.axis_size("dp")
    own_index = lax.axis_index("dp")
    row_count, feature_count = rollout_states.shape
    capacity = 2 * row_count // learners - 1
    lengths = seq_lengths.reshape(learners, learners)
    dests = seq_dest.reshape(learners, learners)
    offsets = seq_offset.reshape(learners, learners)
    starts = jnp.cumsum(lengths, axis=1) - lengths
    peer_ids = jnp.arange(learners, dtype=jnp.int32)
    own_length = lax.dynamic_index_in_dim(lengths, own_index, 0, keepdims=False)
    own_start = lax.dynamic_index_in_dim(starts, own_index, 0, keepdims=False)
    own_dest = lax.dynamic_index_in_dim(dests, own_index, 0, keepdims=False)
    match_send = (own_dest[None, :] == peer_ids[:, None]).astype(jnp.int32)
    send_start = jnp.sum(match_send * own_start[None, :], axis=1)
    send_length = jnp.sum(match_send * own_length[None, :], axis=1)
    slot_index = jnp.arange(capacity, dtype=jnp.int32)
    pick_rows = send_start[:, None] + slot_index[None, :]
    padded = jnp.concatenate(
        [rollout_states, jnp.zeros((capacity, feature_count), rollout_states.dtype)], axis=0
    )
    live_slots = (slot_index[None, :] < send_length[:, None])[..., None]
    outgoing = jnp.where(
        live_slots, jnp.take(padded, pick_rows, axis=0), jnp.zeros((), rollout_states.dtype)
    )
    incoming = lax.all_to_all(outgoing, "dp", split_axis=0, concat_axis=0, tiled=True)
    matched = (dests == own_index).astype(jnp.int32)
    run_start = jnp.sum(matched * offsets, axis=1)
    run_length = jnp.sum(matched * lengths, axis=1)
    rows = jnp.arange(row_count, dtype=jnp.int32)
    inside = (
        (rows[:, None] >= run_start[None, :]) & (rows[:, None] < (run_start + run_length)[None, :])
    ).astype(jnp.int32)
    source_ids = jnp.sum(inside * peer_ids[None, :], axis=1)
    within_seq = rows - jnp.sum(inside * run_start[None, :], axis=1)
    arrived = jnp.take(
        incoming.reshape(learners * capacity, feature_count),
        source_ids * capacity + within_seq,
        axis=0,
    )
    gathered = lax.all_gather(arrived, "tensor", axis=1, tiled=True)
    widened = gathered.astype(jnp.float32)
    statistic = jnp.mean(widened * widened, axis=-1, keepdims=True)
    normed = (widened * lax.rsqrt(statistic + norm_eps) * norm_gain[None, :]).astype(jnp.bfloat16)
    full_query, full_key, full_value = (
        lax.all_gather(w_query, "dp", axis=0, tiled=True),
        lax.all_gather(w_key, "dp", axis=0, tiled=True),
        lax.all_gather(w_value, "dp", axis=0, tiled=True),
    )
    query = jnp.dot(normed, full_query, preferred_element_type=jnp.float32)
    key = jnp.dot(normed, full_key, preferred_element_type=jnp.float32)
    value = jnp.dot(normed, full_value, preferred_element_type=jnp.float32)
    query = query + b_query[None, :]
    key = key + b_key[None, :]
    value = value + b_value[None, :]
    heads_here = query.shape[1] // HD
    kv_here = key.shape[1] // HD
    group = heads_here // kv_here
    cosine, sine = rope_tables(within_seq)
    rot_query = rotate(query.reshape(row_count, heads_here, HD), cosine, sine).astype(jnp.bfloat16)
    rot_query = rot_query.reshape(row_count, kv_here, group, HD)
    rot_key = rotate(key.reshape(row_count, kv_here, HD), cosine, sine).astype(jnp.bfloat16)
    value_bf = value.reshape(row_count, kv_here, HD).astype(jnp.bfloat16)
    block_rows = min(512, row_count)

    def one_block(block_number):
        first_row = block_number * block_rows
        query_block = lax.dynamic_slice_in_dim(rot_query, first_row, block_rows, 0)
        query_source = lax.dynamic_slice_in_dim(source_ids, first_row, block_rows, 0)
        query_rows = first_row + jnp.arange(block_rows, dtype=jnp.int32)
        scores = jnp.einsum(
            "bcgd,kcd->cgbk", query_block, rot_key, preferred_element_type=jnp.float32
        )
        scores = scores * HD ** (-0.5)
        allowed = (source_ids[None, :] == query_source[:, None]) & (
            rows[None, :] <= query_rows[:, None]
        )
        scores = jnp.where(allowed[None, None], scores, mask_value)
        peak = jnp.max(scores, axis=-1, keepdims=True)
        raised = jnp.exp(scores - peak)
        weights = (raised / jnp.sum(raised, axis=-1, keepdims=True)).astype(jnp.bfloat16)
        context = jnp.einsum(
            "cgbk,kcd->bcgd", weights, value_bf, preferred_element_type=jnp.float32
        )
        return context.astype(jnp.bfloat16).reshape(block_rows, heads_here * HD)

    outputs = lax.map(one_block, jnp.arange(row_count // block_rows, dtype=jnp.int32))
    return outputs.reshape(row_count, heads_here * HD)


def pack_kernel(counts, *refs):
    refs = list(refs)
    pieces = [[refs.pop(0) for _ in range(n)] for n in counts]
    out_ref, sems = refs
    copies = []
    for i, block in enumerate(pieces):
        first = 0
        for n, piece in enumerate(block):
            rows = piece.shape[0]
            copies.append(
                pltpu.make_async_copy(piece, out_ref.at[i, pl.ds(first, rows)], sems.at[i, n])
            )
            first += rows
    for copy in copies:
        copy.start()
    for copy in copies:
        copy.wait()


def pack(blocks, in_vmem):
    counts = tuple(len(pieces) for pieces in blocks)
    rows = sum(piece.shape[0] for piece in blocks[0])
    feats = blocks[0][0].shape[1]
    operands = [piece for pieces in blocks for piece in pieces]
    shape = (len(blocks), rows, feats)
    if in_vmem:
        space, out_shape = pltpu.VMEM, pltpu.VMEM(shape, jnp.bfloat16)
    else:
        space, out_shape = pl.ANY, jax.ShapeDtypeStruct(shape, jnp.bfloat16)
    return pl.pallas_call(
        functools.partial(pack_kernel, counts),
        in_specs=[pl.BlockSpec(memory_space=pl.ANY)] * len(operands),
        out_specs=pl.BlockSpec(memory_space=space),
        out_shape=out_shape,
        scratch_shapes=[pltpu.SemaphoreType.DMA((len(blocks), 2))],
        compiler_params=pltpu.CompilerParams(vmem_limit_bytes=4 * 2**20),
        cost_estimate=kernel_cost,
    )(*operands)


def product_kernel(x_count, ropes, chunks, out_lanes, which_ref, *refs):
    refs = list(refs)
    x_refs = [refs.pop(0) for _ in range(x_count)]
    w_ref = refs.pop(0)
    if ropes:
        part_ref, bias_ref, angle_ref = (refs.pop(0) for _ in range(3))
    out_refs = [refs.pop(0) for _ in out_lanes]
    w_buf, sems = refs
    rows = out_refs[0].shape[0]
    part_rows = x_refs[0].shape[1]
    tile = min(512, part_rows)
    wide = w_ref.shape[3]
    copies = [
        [
            pltpu.make_async_copy(
                w_ref.at[which_ref[i], chunk],
                w_buf.at[i, :, pl.ds(n * wide, wide)],
                sems.at[i, n],
            )
            for n, chunk in enumerate(chunks)
        ]
        for i in range(4)
    ]
    for block in copies:
        for copy in block:
            copy.start()

    for first, x_ref in zip(range(0, rows, part_rows), x_refs):
        if first == 0:
            for block in copies:
                for copy in block:
                    copy.wait()

        @pl.loop(0, part_rows, step=tile)
        def _(at, first=first, x_ref=x_ref):
            here = pl.ds(pl.multiple_of(first + at, tile), tile)
            term = None
            for i in range(4):
                rows_here = x_ref[i, pl.ds(pl.multiple_of(at, tile), tile), :]
                dot = jnp.dot(rows_here, w_buf[i], preferred_element_type=jnp.float32)
                term = dot if term is None else term + dot
            if not ropes:
                for out_ref, (low, high) in zip(out_refs, out_lanes):
                    out_ref[here, :] = term[:, low:high].astype(out_ref.dtype)
                return
            (out_ref,) = out_refs
            term = term + part_ref[here, :].astype(jnp.float32) + bias_ref[...]
            angle = angle_ref[here, :]
            turned_angle = pltpu.roll(angle, HD // 2, 1)
            low = lax.broadcasted_iota(jnp.int32, angle.shape, 1) < HD // 2
            cosine = jnp.where(low, angle, turned_angle)
            sine = jnp.where(low, -turned_angle, angle)
            for c, rope in enumerate(ropes):
                head = term[:, c * HD : (c + 1) * HD]
                if rope:
                    head = head * cosine + pltpu.roll(head, HD // 2, 1) * sine
                out_ref[here, c * HD : (c + 1) * HD] = head.astype(out_ref.dtype)


def keep(array):
    return pltpu.with_memory_space_constraint(array, pltpu.VMEM)


def projection(which, x_parts, weights, chunks, outs, finish=None):
    rows = sum(part.shape[1] for part in x_parts)
    feats, columns = weights.shape[2], weights.shape[3] * len(chunks)
    vmem = pl.BlockSpec(memory_space=pltpu.VMEM)
    operands = list(x_parts)
    in_specs = [vmem] * len(operands) + [pl.BlockSpec(memory_space=pl.ANY)]
    operands.append(weights)
    ropes = None
    if finish is not None:
        ropes, part, bias, angles = finish
        operands += [keep(part), bias, angles]
        in_specs += [vmem] * 3
    return pl.pallas_call(
        functools.partial(
            product_kernel,
            len(x_parts),
            ropes,
            tuple(chunks),
            tuple((first, last) for first, last, _ in outs),
        ),
        in_specs=[pl.BlockSpec(memory_space=pltpu.SMEM)] + in_specs,
        out_specs=[vmem] * len(outs),
        out_shape=[pltpu.VMEM((rows, last - first), kind) for first, last, kind in outs],
        scratch_shapes=[
            pltpu.VMEM((4, feats, columns), jnp.bfloat16),
            pltpu.SemaphoreType.DMA((4, len(chunks))),
        ],
        compiler_params=pltpu.CompilerParams(vmem_limit_bytes=(10 + columns // 128) * 2**20),
        cost_estimate=kernel_cost,
    )(which, *operands)


def pick_rows(start, length, slot, window, ref, lanes=slice(None)):
    first = pl.multiple_of(jnp.minimum((start // 16) * 16, ref.shape[0] - window), 16)
    row_at = lax.broadcasted_iota(jnp.int32, (slot, window), 0)
    col_at = lax.broadcasted_iota(jnp.int32, (slot, window), 1)
    pick = jnp.where((col_at == row_at + (start - first)) & (row_at < length), 1.0, 0.0)
    rows = jnp.dot(
        pick.astype(jnp.bfloat16), ref[pl.ds(first, window), lanes], preferred_element_type=jnp.float32
    )
    return rows.astype(jnp.bfloat16)


def slots_kernel(slot, window, start_ref, len_ref, in_ref, out_ref):
    for s in range(out_ref.shape[0]):
        out_ref[s] = pick_rows(start_ref[s], len_ref[s], slot, window, in_ref)


def to_slots(starts, lens, array, slot, window):
    count, columns = starts.shape[0], array.shape[1]
    scalars = pl.BlockSpec(memory_space=pltpu.SMEM)
    vmem = pl.BlockSpec(memory_space=pltpu.VMEM)
    return pl.pallas_call(
        functools.partial(slots_kernel, slot, window),
        in_specs=[scalars, scalars, vmem],
        out_specs=vmem,
        out_shape=pltpu.VMEM((count, slot, columns), jnp.bfloat16),
        compiler_params=pltpu.CompilerParams(vmem_limit_bytes=5 * 2**20),
        cost_estimate=kernel_cost,
    )(starts, lens, keep(array))


def attend_kernel(heads, window, start_ref, len_ref, q_ref, kv_ref, *out_refs):
    if len(out_refs) == 1:
        (whole_ref,) = out_refs
        out_refs = [whole_ref.at[s] for s in range(whole_ref.shape[0])]
    slot = out_refs[0].shape[0]
    half = slot // 2
    for s, out_ref in enumerate(out_refs):
        query = pick_rows(start_ref[s], len_ref[s], slot, window, q_ref)
        for block in range(2):
            width = (block + 1) * half
            stacked = jnp.concatenate(
                [query[block * half : width, h * HD : (h + 1) * HD] for h in range(heads)], axis=0
            )
            scores = lax.dot_general(
                stacked,
                kv_ref[s, :width, :HD],
                (((1,), (1,)), ((), ())),
                preferred_element_type=jnp.float32,
            )
            row_at = lax.broadcasted_iota(jnp.int32, scores.shape, 0) & (half - 1)
            col_at = lax.broadcasted_iota(jnp.int32, scores.shape, 1)
            scores = jnp.where(col_at <= row_at + block * half, scores * HD ** (-0.5), mask_value)
            peak = jnp.max(scores, axis=-1, keepdims=True)
            raised = jnp.exp(scores - peak)
            weights = raised * (1.0 / jnp.sum(raised, axis=-1, keepdims=True))
            context = jnp.dot(
                weights.astype(jnp.bfloat16),
                kv_ref[s, :width, HD:],
                preferred_element_type=jnp.float32,
            ).astype(out_ref.dtype)
            for h in range(heads):
                out_ref[block * half : width, h * HD : (h + 1) * HD] = context[
                    h * half : (h + 1) * half
                ]


def attend(starts, lens, query, kv_slots, window, apart):
    columns = query.shape[1]
    count, slot = kv_slots.shape[:2]
    scalars = pl.BlockSpec(memory_space=pltpu.SMEM)
    vmem = pl.BlockSpec(memory_space=pltpu.VMEM)
    return pl.pallas_call(
        functools.partial(attend_kernel, columns // HD, window),
        in_specs=[scalars, scalars, vmem, vmem],
        out_specs=[vmem] * count if apart else vmem,
        out_shape=(
            [pltpu.VMEM((slot, columns), jnp.bfloat16)] * count
            if apart
            else pltpu.VMEM((count, slot, columns), jnp.bfloat16)
        ),
        compiler_params=pltpu.CompilerParams(vmem_limit_bytes=6 * 2**20),
        cost_estimate=kernel_cost,
    )(starts, lens, keep(query), kv_slots)


def place_kernel(count, window, start_ref, len_ref, *refs):
    in_refs, (out_ref, total) = refs[:count], refs[-2:]
    rows, slot = total.shape[0], in_refs[0].shape[0]
    total[...] = jnp.zeros_like(total)
    row_at = lax.broadcasted_iota(jnp.int32, (window, slot), 0)
    col_at = lax.broadcasted_iota(jnp.int32, (window, slot), 1)
    for s, in_ref in enumerate(in_refs):
        start = start_ref[s]
        first = pl.multiple_of(jnp.minimum((start // 8) * 8, rows - window), 8)
        pick = jnp.where(
            (row_at == col_at + (start - first)) & (col_at < len_ref[s]), 1.0, 0.0
        ).astype(jnp.bfloat16)
        total[pl.ds(first, window), :] += jnp.dot(
            pick, in_ref[...], preferred_element_type=jnp.float32
        )
    out_ref[...] = total[...].astype(out_ref.dtype)


def place(starts, lens, slots, rows, which, all_columns, before):
    count, (slot, columns) = len(slots), slots[0].shape[-2:]
    window = min(rows, slot + 8)
    if isinstance(slots, list):
        in_specs = [pl.BlockSpec((slot, columns), lambda r, a, b: (0, 0))] * count
        operands = list(slots)
    else:
        in_specs = [
            pl.BlockSpec((None, slot, columns), lambda r, a, b, s=s: (s, 0, 0))
            for s in range(count)
        ]
        operands = [slots] * count
    aliases = {}
    if before is not None:
        in_specs.append(pl.BlockSpec(memory_space=pl.ANY))
        operands.append(before)
        aliases = {2 + count: 0}
    grid_spec = pltpu.PrefetchScalarGridSpec(
        num_scalar_prefetch=2,
        grid=(1,),
        in_specs=in_specs,
        out_specs=pl.BlockSpec((rows, columns), lambda r, a, b: (0, which)),
        scratch_shapes=[pltpu.VMEM((rows, columns), jnp.float32)],
    )
    return pl.pallas_call(
        functools.partial(place_kernel, count, window),
        grid_spec=grid_spec,
        out_shape=jax.ShapeDtypeStruct((rows, all_columns), jnp.bfloat16),
        input_output_aliases=aliases,
        compiler_params=pltpu.CompilerParams(vmem_limit_bytes=8 * 2**20),
        cost_estimate=kernel_cost,
    )(starts, lens, *operands)


def local_line(
    rollout_states,
    norm_gain,
    w_query,
    w_key,
    w_value,
    b_query,
    b_key,
    b_value,
    seq_lengths,
    seq_dest,
    seq_offset,
):
    learners = lax.axis_size("dp")
    line = learners // 2
    me = lax.axis_index("dp")
    z, x = me // 2, me % 2
    t = lax.axis_index("tensor")
    row_count, feature_count = rollout_states.shape
    slot = 2 * row_count // learners
    half = feature_count // 2
    middle = row_count // 2

    def after(array, *others):
        return lax.optimization_barrier((array, *others))[0]

    def swap_x(array):
        return lax.ppermute(array, "dp", [(i, i ^ 1) for i in range(learners)])

    def swap_y(array):
        return lax.ppermute(array, "tensor", [(i, i ^ 2) for i in range(4)])

    def swap_core(array):
        return lax.ppermute(array, "tensor", [(i, i ^ 1) for i in range(4)])

    wide = 2 * HD
    along_z = [[2 * i + j for i in range(line)] for j in range(2)]
    groups = [
        [jnp.concatenate([w_key, w_value], axis=1), w_query[:, :wide]],
        [w_query[:, wide : 2 * wide], w_query[:, 2 * wide : 3 * wide]],
        [w_query[:, 3 * wide :]],
    ]
    weights = []
    for group in groups:
        gathered = lax.all_gather(jnp.stack(group), "dp", axis_index_groups=along_z)
        weights.append(pltpu.with_memory_space_constraint(gathered, pltpu.HBM))
    bias_kv = jnp.concatenate([b_key, b_value])[None, :]
    biases = [b_query[None, low : low + wide] for low in range(0, w_query.shape[1], wide)]

    states = rollout_states
    widened = states.astype(jnp.float32)
    squares = jnp.sum(widened * widened, axis=-1)
    squares = squares + swap_core(squares)
    squares = squares + swap_y(squares)
    scale = lax.rsqrt(squares[:, None] / (4 * feature_count) + norm_eps)

    def normed(first):
        part = lax.dynamic_slice_in_dim(states, first, half, 1).astype(jnp.float32)
        gain = lax.dynamic_slice_in_dim(norm_gain, t * feature_count + first, half, 0)
        return (part * scale * gain[None, :]).astype(jnp.bfloat16)

    own, give = normed(x * half), normed((1 - x) * half)

    near_a = swap_x(give[:middle])
    own_a = swap_y(own[:middle])
    own_core = swap_core(own)
    near_b = swap_x(after(give[middle:], near_a))
    diag_a = swap_y(after(near_a, own_a))
    near_a_core = swap_core(near_a)
    own_a_core = swap_core(after(own_a, near_a))
    diag_b = swap_y(after(near_b, diag_a))
    near_b_core = swap_core(after(near_b, diag_a))
    diag_a_core = swap_core(after(diag_a, near_b))
    own_b = swap_y(after(own[middle:], diag_b))
    diag_b_core = swap_core(diag_b)
    near_ax = [[near_a], [near_a_core], [diag_a], [diag_a_core]]
    near_bx = [[near_b], [near_b_core], [diag_b], [diag_b_core]]
    near_x = [pack(near_ax, False), pack(near_bx, False)]
    which = jnp.stack([t ^ i for i in range(4)]).astype(jnp.int32)

    lengths = seq_lengths.reshape(learners, learners)
    dests = seq_dest.reshape(learners, learners)
    offsets = seq_offset.reshape(learners, learners)
    starts = jnp.cumsum(lengths, axis=1) - lengths
    peer_ids = jnp.arange(learners, dtype=jnp.int32)
    rows = jnp.arange(row_count, dtype=jnp.int32)
    length = lax.dynamic_index_in_dim(lengths, me, 0, keepdims=False)
    start = lax.dynamic_index_in_dim(starts, me, 0, keepdims=False)
    dest = lax.dynamic_index_in_dim(dests, me, 0, keepdims=False)
    partners = me ^ peer_ids

    def by_learner(order):
        match = (dest[None, :] == order[:, None]).astype(jnp.int32)
        return jnp.sum(match * start[None, :], axis=1), jnp.sum(match * length[None, :], axis=1)

    send_to = by_learner(partners)
    send_all = by_learner(peer_ids)
    inside = (rows[:, None] >= start[None, :]) & (rows[:, None] < (start + length)[None, :])
    position = rows - jnp.sum(inside.astype(jnp.int32) * start[None, :], axis=1)
    angles = keep(jnp.concatenate(rope_tables(position), axis=1))
    matched = (dests == me).astype(jnp.int32)
    match = (peer_ids[None, :] == partners[:, None]).astype(jnp.int32)
    runs_all = jnp.sum(matched * offsets, axis=1), jnp.sum(matched * lengths, axis=1)
    runs_from = tuple(jnp.sum(match * run[None, :], axis=1) for run in runs_all)

    window = min(row_count, -(-(slot + 16) // 128) * 128)

    def send(outgoing):
        incoming = [outgoing[0]]
        for d in range(1, learners):
            pairs = [(i, i ^ d) for i in range(learners)]
            incoming.append(lax.ppermute(outgoing[d], "dp", pairs))
        return incoming

    def receive(c, incoming, before, *others):
        run_start, run_length = runs_from if isinstance(incoming, list) else runs_all
        start_at = after(run_start, *others)
        return place(start_at, run_length, incoming, row_count, c, w_query.shape[1], before)

    first, second, third = weights
    whole = [(0, wide, jnp.bfloat16)]

    def partial(group, chunks, outs, *others):
        return projection(after(which, *others), near_x, group, chunks, outs)

    def contexts(c, group, chunk, got, others, attend_after=(), apart=True):
        ending = ((True, True), got, biases[c], angles)
        (rot,) = projection(after(which, *others), own_x, group, (chunk,), whole, ending)
        send_start, send_length = send_to if apart else send_all
        start_at = after(send_start, *attend_after)
        slots = kv_slots if apart else kv_slots_all
        return attend(start_at, send_length, rot, slots, window, apart)

    outs = [(0, wide, jnp.float32), (wide, 2 * wide, jnp.bfloat16)]
    part_kv, part_0 = partial(first, (0, 1), outs)
    got_kv = swap_x(part_kv)
    own_b_core = swap_core(after(own_b, part_kv))
    own_x = [keep(pack([[own], [own_core], [own_a, own_b], [own_a_core, own_b_core]], True))]
    got_0 = swap_x(after(part_0, got_kv))
    ending = ((True, False), got_kv, bias_kv, angles)
    (kv,) = projection(which, own_x, first, (0,), whole, ending)
    kv_slots_all = keep(to_slots(*send_all, kv, slot, window))
    kv_slots = keep(to_slots(*send_to, kv, slot, window))
    out_0 = contexts(0, first, 1, got_0, (kv,), apart=False)
    in_0 = lax.all_to_all(out_0, "dp", split_axis=0, concat_axis=0, tiled=True)
    outs = [(0, wide, jnp.bfloat16), (wide, 2 * wide, jnp.bfloat16)]
    part_1, part_2 = partial(second, (0, 1), outs, out_0)
    got_1 = swap_x(part_1)
    got_2 = swap_x(after(part_2, got_1))
    out_1 = contexts(1, second, 0, got_1, (part_2,), (got_2,))
    in_1 = send(out_1)
    (part_3,) = partial(third, (0,), whole, out_1[0])
    got_3 = swap_x(part_3)
    out_2 = contexts(2, second, 1, got_2, (part_3,))
    in_2 = send(out_2)
    out_3 = contexts(3, third, 0, got_3, (out_2[0],))
    in_3 = send(out_3)
    result = receive(0, in_0, None, out_3[0])
    result = receive(1, in_1, result, out_3[0])
    result = receive(2, in_2, result, out_3[0])
    return receive(3, in_3, result)


def solution(mesh):
    placed = (
        P("dp", "tensor"),
        P(),
        P("dp", "tensor"),
        P("dp", "tensor"),
        P("dp", "tensor"),
        P("tensor"),
        P("tensor"),
        P("tensor"),
        P(),
        P(),
        P(),
    )
    fits_line = mesh.shape["dp"] == 8 and mesh.shape["tensor"] == 4
    return jax.shard_map(
        local_line if fits_line else local_any,
        mesh=mesh,
        in_specs=placed,
        out_specs=P("dp", "tensor"),
        check_vma=False,
    )
```

```python
import functools

import jax
import jax.numpy as jnp
from jax import lax
from jax.experimental import pallas as pl
from jax.experimental.pallas import tpu as pltpu
from jax.sharding import PartitionSpec as P

HD = 128

rope_base = 1000000.0
norm_eps = 1e-06
mask_value = -1e30
kernel_cost = pl.CostEstimate(flops=4 * 10**9, bytes_accessed=2**20, transcendentals=0)


def rope_tables(positions):
    half_dim = HD // 2
    frequency = rope_base ** (-(jnp.arange(half_dim).astype(jnp.float32) * 2.0 / HD))
    angles = positions.astype(jnp.float32)[:, None] * frequency[None, :]
    return (jnp.cos(angles), jnp.sin(angles))


def rotate(states, cosine, sine):
    half_dim = states.shape[-1] // 2
    first_half = states[..., :half_dim]
    second_half = states[..., half_dim:]
    cos_wide = cosine[:, None, :]
    sin_wide = sine[:, None, :]
    return jnp.concatenate(
        [
            first_half * cos_wide - second_half * sin_wide,
            second_half * cos_wide + first_half * sin_wide,
        ],
        axis=-1,
    )


def local_any(
    rollout_states,
    norm_gain,
    w_query,
    w_key,
    w_value,
    b_query,
    b_key,
    b_value,
    seq_lengths,
    seq_dest,
    seq_offset,
):
    learners = lax.axis_size("dp")
    own_index = lax.axis_index("dp")
    row_count, feature_count = rollout_states.shape
    capacity = 2 * row_count // learners - 1
    lengths = seq_lengths.reshape(learners, learners)
    dests = seq_dest.reshape(learners, learners)
    offsets = seq_offset.reshape(learners, learners)
    starts = jnp.cumsum(lengths, axis=1) - lengths
    peer_ids = jnp.arange(learners, dtype=jnp.int32)
    own_length = lax.dynamic_index_in_dim(lengths, own_index, 0, keepdims=False)
    own_start = lax.dynamic_index_in_dim(starts, own_index, 0, keepdims=False)
    own_dest = lax.dynamic_index_in_dim(dests, own_index, 0, keepdims=False)
    match_send = (own_dest[None, :] == peer_ids[:, None]).astype(jnp.int32)
    send_start = jnp.sum(match_send * own_start[None, :], axis=1)
    send_length = jnp.sum(match_send * own_length[None, :], axis=1)
    slot_index = jnp.arange(capacity, dtype=jnp.int32)
    pick_rows = send_start[:, None] + slot_index[None, :]
    padded = jnp.concatenate(
        [rollout_states, jnp.zeros((capacity, feature_count), rollout_states.dtype)], axis=0
    )
    live_slots = (slot_index[None, :] < send_length[:, None])[..., None]
    outgoing = jnp.where(
        live_slots, jnp.take(padded, pick_rows, axis=0), jnp.zeros((), rollout_states.dtype)
    )
    incoming = lax.all_to_all(outgoing, "dp", split_axis=0, concat_axis=0, tiled=True)
    matched = (dests == own_index).astype(jnp.int32)
    run_start = jnp.sum(matched * offsets, axis=1)
    run_length = jnp.sum(matched * lengths, axis=1)
    rows = jnp.arange(row_count, dtype=jnp.int32)
    inside = (
        (rows[:, None] >= run_start[None, :]) & (rows[:, None] < (run_start + run_length)[None, :])
    ).astype(jnp.int32)
    source_ids = jnp.sum(inside * peer_ids[None, :], axis=1)
    within_seq = rows - jnp.sum(inside * run_start[None, :], axis=1)
    arrived = jnp.take(
        incoming.reshape(learners * capacity, feature_count),
        source_ids * capacity + within_seq,
        axis=0,
    )
    gathered = lax.all_gather(arrived, "tensor", axis=1, tiled=True)
    widened = gathered.astype(jnp.float32)
    statistic = jnp.mean(widened * widened, axis=-1, keepdims=True)
    normed = (widened * lax.rsqrt(statistic + norm_eps) * norm_gain[None, :]).astype(jnp.bfloat16)
    full_query, full_key, full_value = (
        lax.all_gather(w_query, "dp", axis=0, tiled=True),
        lax.all_gather(w_key, "dp", axis=0, tiled=True),
        lax.all_gather(w_value, "dp", axis=0, tiled=True),
    )
    query = jnp.dot(normed, full_query, preferred_element_type=jnp.float32)
    key = jnp.dot(normed, full_key, preferred_element_type=jnp.float32)
    value = jnp.dot(normed, full_value, preferred_element_type=jnp.float32)
    query = query + b_query[None, :]
    key = key + b_key[None, :]
    value = value + b_value[None, :]
    heads_here = query.shape[1] // HD
    kv_here = key.shape[1] // HD
    group = heads_here // kv_here
    cosine, sine = rope_tables(within_seq)
    rot_query = rotate(query.reshape(row_count, heads_here, HD), cosine, sine).astype(jnp.bfloat16)
    rot_query = rot_query.reshape(row_count, kv_here, group, HD)
    rot_key = rotate(key.reshape(row_count, kv_here, HD), cosine, sine).astype(jnp.bfloat16)
    value_bf = value.reshape(row_count, kv_here, HD).astype(jnp.bfloat16)
    block_rows = min(512, row_count)

    def one_block(block_number):
        first_row = block_number * block_rows
        query_block = lax.dynamic_slice_in_dim(rot_query, first_row, block_rows, 0)
        query_source = lax.dynamic_slice_in_dim(source_ids, first_row, block_rows, 0)
        query_rows = first_row + jnp.arange(block_rows, dtype=jnp.int32)
        scores = jnp.einsum(
            "bcgd,kcd->cgbk", query_block, rot_key, preferred_element_type=jnp.float32
        )
        scores = scores * HD ** (-0.5)
        allowed = (source_ids[None, :] == query_source[:, None]) & (
            rows[None, :] <= query_rows[:, None]
        )
        scores = jnp.where(allowed[None, None], scores, mask_value)
        peak = jnp.max(scores, axis=-1, keepdims=True)
        raised = jnp.exp(scores - peak)
        weights = (raised / jnp.sum(raised, axis=-1, keepdims=True)).astype(jnp.bfloat16)
        context = jnp.einsum(
            "cgbk,kcd->bcgd", weights, value_bf, preferred_element_type=jnp.float32
        )
        return context.astype(jnp.bfloat16).reshape(block_rows, heads_here * HD)

    outputs = lax.map(one_block, jnp.arange(row_count // block_rows, dtype=jnp.int32))
    return outputs.reshape(row_count, heads_here * HD)


def pack_kernel(counts, *refs):
    refs = list(refs)
    pieces = [[refs.pop(0) for _ in range(n)] for n in counts]
    out_ref, sems = refs
    copies = []
    for i, block in enumerate(pieces):
        first = 0
        for n, piece in enumerate(block):
            rows = piece.shape[0]
            copies.append(
                pltpu.make_async_copy(piece, out_ref.at[i, pl.ds(first, rows)], sems.at[i, n])
            )
            first += rows
    for copy in copies:
        copy.start()
    for copy in copies:
        copy.wait()


def pack(blocks, in_vmem):
    counts = tuple(len(pieces) for pieces in blocks)
    rows = sum(piece.shape[0] for piece in blocks[0])
    feats = blocks[0][0].shape[1]
    operands = [piece for pieces in blocks for piece in pieces]
    shape = (len(blocks), rows, feats)
    if in_vmem:
        space, out_shape = pltpu.VMEM, pltpu.VMEM(shape, jnp.bfloat16)
    else:
        space, out_shape = pl.ANY, jax.ShapeDtypeStruct(shape, jnp.bfloat16)
    return pl.pallas_call(
        functools.partial(pack_kernel, counts),
        in_specs=[pl.BlockSpec(memory_space=pl.ANY)] * len(operands),
        out_specs=pl.BlockSpec(memory_space=space),
        out_shape=out_shape,
        scratch_shapes=[pltpu.SemaphoreType.DMA((len(blocks), 2))],
        compiler_params=pltpu.CompilerParams(vmem_limit_bytes=4 * 2**20),
        cost_estimate=kernel_cost,
    )(*operands)


def product_kernel(x_count, ropes, chunks, out_lanes, which_ref, *refs):
    refs = list(refs)
    x_refs = [refs.pop(0) for _ in range(x_count)]
    w_ref = refs.pop(0)
    if ropes:
        part_ref, bias_ref, angle_ref = (refs.pop(0) for _ in range(3))
    out_refs = [refs.pop(0) for _ in out_lanes]
    w_buf, sems = refs
    rows = out_refs[0].shape[0]
    part_rows = x_refs[0].shape[1]
    tile = min(512, part_rows)
    wide = w_ref.shape[3]
    copies = [
        [
            pltpu.make_async_copy(
                w_ref.at[which_ref[i], chunk],
                w_buf.at[i, :, pl.ds(n * wide, wide)],
                sems.at[i, n],
            )
            for n, chunk in enumerate(chunks)
        ]
        for i in range(4)
    ]
    for block in copies:
        for copy in block:
            copy.start()

    for first, x_ref in zip(range(0, rows, part_rows), x_refs):
        if first == 0:
            for block in copies:
                for copy in block:
                    copy.wait()

        @pl.loop(0, part_rows, step=tile)
        def _(at, first=first, x_ref=x_ref):
            here = pl.ds(pl.multiple_of(first + at, tile), tile)
            term = None
            for i in range(4):
                rows_here = x_ref[i, pl.ds(pl.multiple_of(at, tile), tile), :]
                dot = jnp.dot(rows_here, w_buf[i], preferred_element_type=jnp.float32)
                term = dot if term is None else term + dot
            if not ropes:
                for out_ref, (low, high) in zip(out_refs, out_lanes):
                    out_ref[here, :] = term[:, low:high].astype(out_ref.dtype)
                return
            (out_ref,) = out_refs
            term = term + part_ref[here, :].astype(jnp.float32) + bias_ref[...]
            angle = angle_ref[here, :]
            turned_angle = pltpu.roll(angle, HD // 2, 1)
            low = lax.broadcasted_iota(jnp.int32, angle.shape, 1) < HD // 2
            cosine = jnp.where(low, angle, turned_angle)
            sine = jnp.where(low, -turned_angle, angle)
            for c, rope in enumerate(ropes):
                head = term[:, c * HD : (c + 1) * HD]
                if rope:
                    head = head * cosine + pltpu.roll(head, HD // 2, 1) * sine
                out_ref[here, c * HD : (c + 1) * HD] = head.astype(out_ref.dtype)


def keep(array):
    return pltpu.with_memory_space_constraint(array, pltpu.VMEM)


def projection(which, x_parts, weights, chunks, outs, finish=None):
    rows = sum(part.shape[1] for part in x_parts)
    feats, columns = weights.shape[2], weights.shape[3] * len(chunks)
    vmem = pl.BlockSpec(memory_space=pltpu.VMEM)
    operands = list(x_parts)
    in_specs = [vmem] * len(operands) + [pl.BlockSpec(memory_space=pl.ANY)]
    operands.append(weights)
    ropes = None
    if finish is not None:
        ropes, part, bias, angles = finish
        operands += [keep(part), bias, angles]
        in_specs += [vmem] * 3
    return pl.pallas_call(
        functools.partial(
            product_kernel,
            len(x_parts),
            ropes,
            tuple(chunks),
            tuple((first, last) for first, last, _ in outs),
        ),
        in_specs=[pl.BlockSpec(memory_space=pltpu.SMEM)] + in_specs,
        out_specs=[vmem] * len(outs),
        out_shape=[pltpu.VMEM((rows, last - first), kind) for first, last, kind in outs],
        scratch_shapes=[
            pltpu.VMEM((4, feats, columns), jnp.bfloat16),
            pltpu.SemaphoreType.DMA((4, len(chunks))),
        ],
        compiler_params=pltpu.CompilerParams(vmem_limit_bytes=(10 + columns // 128) * 2**20),
        cost_estimate=kernel_cost,
    )(which, *operands)


def pick_rows(start, length, slot, window, ref, lanes=slice(None)):
    first = pl.multiple_of(jnp.minimum((start // 16) * 16, ref.shape[0] - window), 16)
    row_at = lax.broadcasted_iota(jnp.int32, (slot, window), 0)
    col_at = lax.broadcasted_iota(jnp.int32, (slot, window), 1)
    pick = jnp.where((col_at == row_at + (start - first)) & (row_at < length), 1.0, 0.0)
    rows = jnp.dot(
        pick.astype(jnp.bfloat16), ref[pl.ds(first, window), lanes], preferred_element_type=jnp.float32
    )
    return rows.astype(jnp.bfloat16)


def slots_kernel(slot, window, start_ref, len_ref, in_ref, out_ref):
    for s in range(out_ref.shape[0]):
        out_ref[s] = pick_rows(start_ref[s], len_ref[s], slot, window, in_ref)


def to_slots(starts, lens, array, slot, window):
    count, columns = starts.shape[0], array.shape[1]
    scalars = pl.BlockSpec(memory_space=pltpu.SMEM)
    vmem = pl.BlockSpec(memory_space=pltpu.VMEM)
    return pl.pallas_call(
        functools.partial(slots_kernel, slot, window),
        in_specs=[scalars, scalars, vmem],
        out_specs=vmem,
        out_shape=pltpu.VMEM((count, slot, columns), jnp.bfloat16),
        compiler_params=pltpu.CompilerParams(vmem_limit_bytes=5 * 2**20),
        cost_estimate=kernel_cost,
    )(starts, lens, keep(array))


def attend_kernel(heads, window, start_ref, len_ref, q_ref, kv_ref, *out_refs):
    if len(out_refs) == 1:
        (whole_ref,) = out_refs
        out_refs = [whole_ref.at[s] for s in range(whole_ref.shape[0])]
    slot = out_refs[0].shape[0]
    half = slot // 2
    for s, out_ref in enumerate(out_refs):
        query = pick_rows(start_ref[s], len_ref[s], slot, window, q_ref)
        for block in range(2):
            width = (block + 1) * half
            stacked = jnp.concatenate(
                [query[block * half : width, h * HD : (h + 1) * HD] for h in range(heads)], axis=0
            )
            scores = lax.dot_general(
                stacked,
                kv_ref[s, :width, :HD],
                (((1,), (1,)), ((), ())),
                preferred_element_type=jnp.float32,
            )
            row_at = lax.broadcasted_iota(jnp.int32, scores.shape, 0) & (half - 1)
            col_at = lax.broadcasted_iota(jnp.int32, scores.shape, 1)
            scores = jnp.where(col_at <= row_at + block * half, scores * HD ** (-0.5), mask_value)
            peak = jnp.max(scores, axis=-1, keepdims=True)
            raised = jnp.exp(scores - peak)
            weights = raised * (1.0 / jnp.sum(raised, axis=-1, keepdims=True))
            context = jnp.dot(
                weights.astype(jnp.bfloat16),
                kv_ref[s, :width, HD:],
                preferred_element_type=jnp.float32,
            ).astype(out_ref.dtype)
            for h in range(heads):
                out_ref[block * half : width, h * HD : (h + 1) * HD] = context[
                    h * half : (h + 1) * half
                ]


def attend(starts, lens, query, kv_slots, window, apart):
    columns = query.shape[1]
    count, slot = kv_slots.shape[:2]
    scalars = pl.BlockSpec(memory_space=pltpu.SMEM)
    vmem = pl.BlockSpec(memory_space=pltpu.VMEM)
    return pl.pallas_call(
        functools.partial(attend_kernel, columns // HD, window),
        in_specs=[scalars, scalars, vmem, vmem],
        out_specs=[vmem] * count if apart else vmem,
        out_shape=(
            [pltpu.VMEM((slot, columns), jnp.bfloat16)] * count
            if apart
            else pltpu.VMEM((count, slot, columns), jnp.bfloat16)
        ),
        compiler_params=pltpu.CompilerParams(vmem_limit_bytes=6 * 2**20),
        cost_estimate=kernel_cost,
    )(starts, lens, keep(query), kv_slots)


def place_kernel(count, window, start_ref, len_ref, *refs):
    in_refs, (out_ref, total) = refs[:count], refs[-2:]
    rows, slot = total.shape[0], in_refs[0].shape[0]
    total[...] = jnp.zeros_like(total)
    row_at = lax.broadcasted_iota(jnp.int32, (window, slot), 0)
    col_at = lax.broadcasted_iota(jnp.int32, (window, slot), 1)
    for s, in_ref in enumerate(in_refs):
        start = start_ref[s]
        first = pl.multiple_of(jnp.minimum((start // 8) * 8, rows - window), 8)
        pick = jnp.where(
            (row_at == col_at + (start - first)) & (col_at < len_ref[s]), 1.0, 0.0
        ).astype(jnp.bfloat16)
        total[pl.ds(first, window), :] += jnp.dot(
            pick, in_ref[...], preferred_element_type=jnp.float32
        )
    out_ref[...] = total[...].astype(out_ref.dtype)


def place(starts, lens, slots, rows, which, all_columns, before):
    count, (slot, columns) = len(slots), slots[0].shape[-2:]
    window = min(rows, slot + 8)
    if isinstance(slots, list):
        in_specs = [pl.BlockSpec((slot, columns), lambda r, a, b: (0, 0))] * count
        operands = list(slots)
    else:
        in_specs = [
            pl.BlockSpec((None, slot, columns), lambda r, a, b, s=s: (s, 0, 0))
            for s in range(count)
        ]
        operands = [slots] * count
    aliases = {}
    if before is not None:
        in_specs.append(pl.BlockSpec(memory_space=pl.ANY))
        operands.append(before)
        aliases = {2 + count: 0}
    grid_spec = pltpu.PrefetchScalarGridSpec(
        num_scalar_prefetch=2,
        grid=(1,),
        in_specs=in_specs,
        out_specs=pl.BlockSpec((rows, columns), lambda r, a, b: (0, which)),
        scratch_shapes=[pltpu.VMEM((rows, columns), jnp.float32)],
    )
    return pl.pallas_call(
        functools.partial(place_kernel, count, window),
        grid_spec=grid_spec,
        out_shape=jax.ShapeDtypeStruct((rows, all_columns), jnp.bfloat16),
        input_output_aliases=aliases,
        compiler_params=pltpu.CompilerParams(vmem_limit_bytes=8 * 2**20),
        cost_estimate=kernel_cost,
    )(starts, lens, *operands)


def local_line(
    rollout_states,
    norm_gain,
    w_query,
    w_key,
    w_value,
    b_query,
    b_key,
    b_value,
    seq_lengths,
    seq_dest,
    seq_offset,
):
    learners = lax.axis_size("dp")
    line = learners // 2
    me = lax.axis_index("dp")
    z, x = me // 2, me % 2
    t = lax.axis_index("tensor")
    row_count, feature_count = rollout_states.shape
    slot = 2 * row_count // learners
    half = feature_count // 2
    middle = row_count // 2

    def after(array, *others):
        return lax.optimization_barrier((array, *others))[0]

    def swap_x(array):
        return lax.ppermute(array, "dp", [(i, i ^ 1) for i in range(learners)])

    def swap_y(array):
        return lax.ppermute(array, "tensor", [(i, i ^ 2) for i in range(4)])

    def swap_core(array):
        return lax.ppermute(array, "tensor", [(i, i ^ 1) for i in range(4)])

    wide = 2 * HD
    along_z = [[2 * i + j for i in range(line)] for j in range(2)]
    groups = [
        [jnp.concatenate([w_key, w_value], axis=1), w_query[:, :wide]],
        [w_query[:, wide : 2 * wide], w_query[:, 2 * wide : 3 * wide]],
        [w_query[:, 3 * wide :]],
    ]
    weights = []
    for group in groups:
        gathered = lax.all_gather(jnp.stack(group), "dp", axis_index_groups=along_z)
        weights.append(pltpu.with_memory_space_constraint(gathered, pltpu.HBM))
    bias_kv = jnp.concatenate([b_key, b_value])[None, :]
    biases = [b_query[None, low : low + wide] for low in range(0, w_query.shape[1], wide)]

    states = rollout_states
    widened = states.astype(jnp.float32)
    squares = jnp.sum(widened * widened, axis=-1)
    squares = squares + swap_core(squares)
    squares = squares + swap_y(squares)
    scale = lax.rsqrt(squares[:, None] / (4 * feature_count) + norm_eps)

    def normed(first):
        part = lax.dynamic_slice_in_dim(states, first, half, 1).astype(jnp.float32)
        gain = lax.dynamic_slice_in_dim(norm_gain, t * feature_count + first, half, 0)
        return (part * scale * gain[None, :]).astype(jnp.bfloat16)

    own, give = normed(x * half), normed((1 - x) * half)

    near_a = swap_x(give[:middle])
    own_a = swap_y(own[:middle])
    own_core = swap_core(own)
    near_b = swap_x(after(give[middle:], near_a))
    diag_a = swap_y(after(near_a, own_a))
    near_a_core = swap_core(near_a)
    own_a_core = swap_core(after(own_a, near_a))
    diag_b = swap_y(after(near_b, diag_a))
    near_b_core = swap_core(after(near_b, diag_a))
    diag_a_core = swap_core(after(diag_a, near_b))
    own_b = swap_y(after(own[middle:], diag_b))
    diag_b_core = swap_core(diag_b)
    near_ax = [[near_a], [near_a_core], [diag_a], [diag_a_core]]
    near_bx = [[near_b], [near_b_core], [diag_b], [diag_b_core]]
    near_x = [pack(near_ax, False), pack(near_bx, False)]
    which = jnp.stack([t ^ i for i in range(4)]).astype(jnp.int32)

    lengths = seq_lengths.reshape(learners, learners)
    dests = seq_dest.reshape(learners, learners)
    offsets = seq_offset.reshape(learners, learners)
    starts = jnp.cumsum(lengths, axis=1) - lengths
    peer_ids = jnp.arange(learners, dtype=jnp.int32)
    rows = jnp.arange(row_count, dtype=jnp.int32)
    length = lax.dynamic_index_in_dim(lengths, me, 0, keepdims=False)
    start = lax.dynamic_index_in_dim(starts, me, 0, keepdims=False)
    dest = lax.dynamic_index_in_dim(dests, me, 0, keepdims=False)
    partners = me ^ peer_ids

    def by_learner(order):
        match = (dest[None, :] == order[:, None]).astype(jnp.int32)
        return jnp.sum(match * start[None, :], axis=1), jnp.sum(match * length[None, :], axis=1)

    send_to = by_learner(partners)
    send_all = by_learner(peer_ids)
    inside = (rows[:, None] >= start[None, :]) & (rows[:, None] < (start + length)[None, :])
    position = rows - jnp.sum(inside.astype(jnp.int32) * start[None, :], axis=1)
    angles = keep(jnp.concatenate(rope_tables(position), axis=1))
    matched = (dests == me).astype(jnp.int32)
    match = (peer_ids[None, :] == partners[:, None]).astype(jnp.int32)
    runs_all = jnp.sum(matched * offsets, axis=1), jnp.sum(matched * lengths, axis=1)
    runs_from = tuple(jnp.sum(match * run[None, :], axis=1) for run in runs_all)

    window = min(row_count, -(-(slot + 16) // 128) * 128)

    def send(outgoing):
        incoming = [outgoing[0]]
        for d in range(1, learners):
            pairs = [(i, i ^ d) for i in range(learners)]
            incoming.append(lax.ppermute(outgoing[d], "dp", pairs))
        return incoming

    def exchange(outgoing):
        return lax.all_to_all(outgoing, "dp", split_axis=0, concat_axis=0, tiled=True)

    def receive(c, incoming, before, *others):
        run_start, run_length = runs_from if isinstance(incoming, list) else runs_all
        start_at = after(run_start, *others)
        return place(start_at, run_length, incoming, row_count, c, w_query.shape[1], before)

    first, second, third = weights
    whole = [(0, wide, jnp.bfloat16)]

    def partial(group, chunks, outs, *others):
        return projection(after(which, *others), near_x, group, chunks, outs)

    def contexts(c, group, chunk, got, others, attend_after=()):
        ending = ((True, True), got, biases[c], angles)
        (rot,) = projection(after(which, *others), own_x, group, (chunk,), whole, ending)
        send_start, send_length = send_all
        start_at = after(send_start, *attend_after)
        return attend(start_at, send_length, rot, kv_slots, window, False)

    outs = [(0, wide, jnp.float32), (wide, 2 * wide, jnp.bfloat16)]
    part_kv, part_0 = partial(first, (0, 1), outs)
    got_kv = swap_x(part_kv)
    own_b_core = swap_core(after(own_b, part_kv))
    own_x = [keep(pack([[own], [own_core], [own_a, own_b], [own_a_core, own_b_core]], True))]
    got_0 = swap_x(after(part_0, got_kv))
    ending = ((True, False), got_kv, bias_kv, angles)
    (kv,) = projection(which, own_x, first, (0,), whole, ending)
    kv_slots = keep(to_slots(*send_all, kv, slot, window))
    out_0 = contexts(0, first, 1, got_0, (kv,))
    in_0 = exchange(out_0)
    outs = [(0, wide, jnp.bfloat16), (wide, 2 * wide, jnp.bfloat16)]
    part_1, part_2 = partial(second, (0, 1), outs, out_0)
    got_1 = swap_x(part_1)
    got_2 = swap_x(after(part_2, got_1))
    out_1 = contexts(1, second, 0, got_1, (part_2,), (got_2,))
    in_1 = exchange(out_1)
    (part_3,) = partial(third, (0,), whole, out_1)
    got_3 = swap_x(part_3)
    result = receive(0, in_0, None, part_3)
    out_2 = contexts(2, second, 1, got_2, (part_3,))
    in_2 = exchange(after(out_2, in_0))
    out_3 = contexts(3, third, 0, got_3, (out_2,))
    in_3 = exchange(after(out_3, in_1))
    result = receive(1, in_1, result, out_3)
    result = receive(2, in_2, result, out_3)
    return receive(3, in_3, result)


def solution(mesh):
    placed = (
        P("dp", "tensor"),
        P(),
        P("dp", "tensor"),
        P("dp", "tensor"),
        P("dp", "tensor"),
        P("tensor"),
        P("tensor"),
        P("tensor"),
        P(),
        P(),
        P(),
    )
    fits_line = mesh.shape["dp"] == 8 and mesh.shape["tensor"] == 4
    return jax.shard_map(
        local_line if fits_line else local_any,
        mesh=mesh,
        in_specs=placed,
        out_specs=P("dp", "tensor"),
        check_vma=False,
    )
```

```python
import functools

import jax
import jax.numpy as jnp
from jax import lax
from jax.experimental import pallas as pl
from jax.experimental.pallas import tpu as pltpu
from jax.sharding import PartitionSpec as P

HD = 128

rope_base = 1000000.0
norm_eps = 1e-06
mask_value = -1e30
kernel_cost = pl.CostEstimate(flops=4 * 10**9, bytes_accessed=2**20, transcendentals=0)


def rope_tables(positions):
    half_dim = HD // 2
    frequency = rope_base ** (-(jnp.arange(half_dim).astype(jnp.float32) * 2.0 / HD))
    angles = positions.astype(jnp.float32)[:, None] * frequency[None, :]
    return (jnp.cos(angles), jnp.sin(angles))


def rotate(states, cosine, sine):
    half_dim = states.shape[-1] // 2
    first_half = states[..., :half_dim]
    second_half = states[..., half_dim:]
    cos_wide = cosine[:, None, :]
    sin_wide = sine[:, None, :]
    return jnp.concatenate(
        [
            first_half * cos_wide - second_half * sin_wide,
            second_half * cos_wide + first_half * sin_wide,
        ],
        axis=-1,
    )


def local_any(
    rollout_states,
    norm_gain,
    w_query,
    w_key,
    w_value,
    b_query,
    b_key,
    b_value,
    seq_lengths,
    seq_dest,
    seq_offset,
):
    learners = lax.axis_size("dp")
    own_index = lax.axis_index("dp")
    row_count, feature_count = rollout_states.shape
    capacity = 2 * row_count // learners - 1
    lengths = seq_lengths.reshape(learners, learners)
    dests = seq_dest.reshape(learners, learners)
    offsets = seq_offset.reshape(learners, learners)
    starts = jnp.cumsum(lengths, axis=1) - lengths
    peer_ids = jnp.arange(learners, dtype=jnp.int32)
    own_length = lax.dynamic_index_in_dim(lengths, own_index, 0, keepdims=False)
    own_start = lax.dynamic_index_in_dim(starts, own_index, 0, keepdims=False)
    own_dest = lax.dynamic_index_in_dim(dests, own_index, 0, keepdims=False)
    match_send = (own_dest[None, :] == peer_ids[:, None]).astype(jnp.int32)
    send_start = jnp.sum(match_send * own_start[None, :], axis=1)
    send_length = jnp.sum(match_send * own_length[None, :], axis=1)
    slot_index = jnp.arange(capacity, dtype=jnp.int32)
    pick_rows = send_start[:, None] + slot_index[None, :]
    padded = jnp.concatenate(
        [rollout_states, jnp.zeros((capacity, feature_count), rollout_states.dtype)], axis=0
    )
    live_slots = (slot_index[None, :] < send_length[:, None])[..., None]
    outgoing = jnp.where(
        live_slots, jnp.take(padded, pick_rows, axis=0), jnp.zeros((), rollout_states.dtype)
    )
    incoming = lax.all_to_all(outgoing, "dp", split_axis=0, concat_axis=0, tiled=True)
    matched = (dests == own_index).astype(jnp.int32)
    run_start = jnp.sum(matched * offsets, axis=1)
    run_length = jnp.sum(matched * lengths, axis=1)
    rows = jnp.arange(row_count, dtype=jnp.int32)
    inside = (
        (rows[:, None] >= run_start[None, :]) & (rows[:, None] < (run_start + run_length)[None, :])
    ).astype(jnp.int32)
    source_ids = jnp.sum(inside * peer_ids[None, :], axis=1)
    within_seq = rows - jnp.sum(inside * run_start[None, :], axis=1)
    arrived = jnp.take(
        incoming.reshape(learners * capacity, feature_count),
        source_ids * capacity + within_seq,
        axis=0,
    )
    gathered = lax.all_gather(arrived, "tensor", axis=1, tiled=True)
    widened = gathered.astype(jnp.float32)
    statistic = jnp.mean(widened * widened, axis=-1, keepdims=True)
    normed = (widened * lax.rsqrt(statistic + norm_eps) * norm_gain[None, :]).astype(jnp.bfloat16)
    full_query, full_key, full_value = (
        lax.all_gather(w_query, "dp", axis=0, tiled=True),
        lax.all_gather(w_key, "dp", axis=0, tiled=True),
        lax.all_gather(w_value, "dp", axis=0, tiled=True),
    )
    query = jnp.dot(normed, full_query, preferred_element_type=jnp.float32)
    key = jnp.dot(normed, full_key, preferred_element_type=jnp.float32)
    value = jnp.dot(normed, full_value, preferred_element_type=jnp.float32)
    query = query + b_query[None, :]
    key = key + b_key[None, :]
    value = value + b_value[None, :]
    heads_here = query.shape[1] // HD
    kv_here = key.shape[1] // HD
    group = heads_here // kv_here
    cosine, sine = rope_tables(within_seq)
    rot_query = rotate(query.reshape(row_count, heads_here, HD), cosine, sine).astype(jnp.bfloat16)
    rot_query = rot_query.reshape(row_count, kv_here, group, HD)
    rot_key = rotate(key.reshape(row_count, kv_here, HD), cosine, sine).astype(jnp.bfloat16)
    value_bf = value.reshape(row_count, kv_here, HD).astype(jnp.bfloat16)
    block_rows = min(512, row_count)

    def one_block(block_number):
        first_row = block_number * block_rows
        query_block = lax.dynamic_slice_in_dim(rot_query, first_row, block_rows, 0)
        query_source = lax.dynamic_slice_in_dim(source_ids, first_row, block_rows, 0)
        query_rows = first_row + jnp.arange(block_rows, dtype=jnp.int32)
        scores = jnp.einsum(
            "bcgd,kcd->cgbk", query_block, rot_key, preferred_element_type=jnp.float32
        )
        scores = scores * HD ** (-0.5)
        allowed = (source_ids[None, :] == query_source[:, None]) & (
            rows[None, :] <= query_rows[:, None]
        )
        scores = jnp.where(allowed[None, None], scores, mask_value)
        peak = jnp.max(scores, axis=-1, keepdims=True)
        raised = jnp.exp(scores - peak)
        weights = (raised / jnp.sum(raised, axis=-1, keepdims=True)).astype(jnp.bfloat16)
        context = jnp.einsum(
            "cgbk,kcd->bcgd", weights, value_bf, preferred_element_type=jnp.float32
        )
        return context.astype(jnp.bfloat16).reshape(block_rows, heads_here * HD)

    outputs = lax.map(one_block, jnp.arange(row_count // block_rows, dtype=jnp.int32))
    return outputs.reshape(row_count, heads_here * HD)


def pack_kernel(counts, *refs):
    refs = list(refs)
    pieces = [[refs.pop(0) for _ in range(n)] for n in counts]
    out_ref, sems = refs
    copies = []
    for i, block in enumerate(pieces):
        first = 0
        for n, piece in enumerate(block):
            rows = piece.shape[0]
            copies.append(
                pltpu.make_async_copy(piece, out_ref.at[i, pl.ds(first, rows)], sems.at[i, n])
            )
            first += rows
    for copy in copies:
        copy.start()
    for copy in copies:
        copy.wait()


def pack(blocks, in_vmem):
    counts = tuple(len(pieces) for pieces in blocks)
    rows = sum(piece.shape[0] for piece in blocks[0])
    feats = blocks[0][0].shape[1]
    operands = [piece for pieces in blocks for piece in pieces]
    shape = (len(blocks), rows, feats)
    if in_vmem:
        space, out_shape = pltpu.VMEM, pltpu.VMEM(shape, jnp.bfloat16)
    else:
        space, out_shape = pl.ANY, jax.ShapeDtypeStruct(shape, jnp.bfloat16)
    return pl.pallas_call(
        functools.partial(pack_kernel, counts),
        in_specs=[pl.BlockSpec(memory_space=pl.ANY)] * len(operands),
        out_specs=pl.BlockSpec(memory_space=space),
        out_shape=out_shape,
        scratch_shapes=[pltpu.SemaphoreType.DMA((len(blocks), 2))],
        compiler_params=pltpu.CompilerParams(vmem_limit_bytes=4 * 2**20),
        cost_estimate=kernel_cost,
    )(*operands)


def product_kernel(x_count, ropes, chunks, out_lanes, which_ref, *refs):
    refs = list(refs)
    x_refs = [refs.pop(0) for _ in range(x_count)]
    w_ref = refs.pop(0)
    if ropes:
        part_ref, bias_ref, angle_ref = (refs.pop(0) for _ in range(3))
    out_refs = [refs.pop(0) for _ in out_lanes]
    w_buf, sems = refs
    rows = out_refs[0].shape[0]
    part_rows = x_refs[0].shape[1]
    tile = min(512, part_rows)
    wide = w_ref.shape[3]
    copies = [
        [
            pltpu.make_async_copy(
                w_ref.at[which_ref[i], chunk],
                w_buf.at[i, :, pl.ds(n * wide, wide)],
                sems.at[i, n],
            )
            for n, chunk in enumerate(chunks)
        ]
        for i in range(4)
    ]
    for block in copies:
        for copy in block:
            copy.start()

    for first, x_ref in zip(range(0, rows, part_rows), x_refs):
        if first == 0:
            for block in copies:
                for copy in block:
                    copy.wait()

        @pl.loop(0, part_rows, step=tile)
        def _(at, first=first, x_ref=x_ref):
            here = pl.ds(pl.multiple_of(first + at, tile), tile)
            term = None
            for i in range(4):
                rows_here = x_ref[i, pl.ds(pl.multiple_of(at, tile), tile), :]
                dot = jnp.dot(rows_here, w_buf[i], preferred_element_type=jnp.float32)
                term = dot if term is None else term + dot
            if not ropes:
                for out_ref, (low, high) in zip(out_refs, out_lanes):
                    out_ref[here, :] = term[:, low:high].astype(out_ref.dtype)
                return
            (out_ref,) = out_refs
            term = term + part_ref[here, :].astype(jnp.float32) + bias_ref[...]
            angle = angle_ref[here, :]
            turned_angle = pltpu.roll(angle, HD // 2, 1)
            low = lax.broadcasted_iota(jnp.int32, angle.shape, 1) < HD // 2
            cosine = jnp.where(low, angle, turned_angle)
            sine = jnp.where(low, -turned_angle, angle)
            for c, rope in enumerate(ropes):
                head = term[:, c * HD : (c + 1) * HD]
                if rope:
                    head = head * cosine + pltpu.roll(head, HD // 2, 1) * sine
                out_ref[here, c * HD : (c + 1) * HD] = head.astype(out_ref.dtype)


def keep(array):
    return pltpu.with_memory_space_constraint(array, pltpu.VMEM)


def projection(which, x_parts, weights, chunks, outs, finish=None):
    rows = sum(part.shape[1] for part in x_parts)
    feats, columns = weights.shape[2], weights.shape[3] * len(chunks)
    vmem = pl.BlockSpec(memory_space=pltpu.VMEM)
    operands = list(x_parts)
    in_specs = [vmem] * len(operands) + [pl.BlockSpec(memory_space=pl.ANY)]
    operands.append(weights)
    ropes = None
    if finish is not None:
        ropes, part, bias, angles = finish
        operands += [keep(part), bias, angles]
        in_specs += [vmem] * 3
    return pl.pallas_call(
        functools.partial(
            product_kernel,
            len(x_parts),
            ropes,
            tuple(chunks),
            tuple((first, last) for first, last, _ in outs),
        ),
        in_specs=[pl.BlockSpec(memory_space=pltpu.SMEM)] + in_specs,
        out_specs=[vmem] * len(outs),
        out_shape=[pltpu.VMEM((rows, last - first), kind) for first, last, kind in outs],
        scratch_shapes=[
            pltpu.VMEM((4, feats, columns), jnp.bfloat16),
            pltpu.SemaphoreType.DMA((4, len(chunks))),
        ],
        compiler_params=pltpu.CompilerParams(vmem_limit_bytes=(10 + columns // 128) * 2**20),
        cost_estimate=kernel_cost,
    )(which, *operands)


def pick_rows(start, length, slot, window, ref, lanes=slice(None)):
    first = pl.multiple_of(jnp.minimum((start // 16) * 16, ref.shape[0] - window), 16)
    row_at = lax.broadcasted_iota(jnp.int32, (slot, window), 0)
    col_at = lax.broadcasted_iota(jnp.int32, (slot, window), 1)
    pick = jnp.where((col_at == row_at + (start - first)) & (row_at < length), 1.0, 0.0)
    rows = jnp.dot(
        pick.astype(jnp.bfloat16), ref[pl.ds(first, window), lanes], preferred_element_type=jnp.float32
    )
    return rows.astype(jnp.bfloat16)


def slots_kernel(slot, window, start_ref, len_ref, in_ref, out_ref):
    for s in range(out_ref.shape[0]):
        out_ref[s] = pick_rows(start_ref[s], len_ref[s], slot, window, in_ref)


def to_slots(starts, lens, array, slot, window):
    count, columns = starts.shape[0], array.shape[1]
    scalars = pl.BlockSpec(memory_space=pltpu.SMEM)
    vmem = pl.BlockSpec(memory_space=pltpu.VMEM)
    return pl.pallas_call(
        functools.partial(slots_kernel, slot, window),
        in_specs=[scalars, scalars, vmem],
        out_specs=vmem,
        out_shape=pltpu.VMEM((count, slot, columns), jnp.bfloat16),
        compiler_params=pltpu.CompilerParams(vmem_limit_bytes=5 * 2**20),
        cost_estimate=kernel_cost,
    )(starts, lens, keep(array))


def attend_kernel(heads, window, start_ref, len_ref, q_ref, kv_ref, *out_refs):
    if len(out_refs) == 1:
        (whole_ref,) = out_refs
        out_refs = [whole_ref.at[s] for s in range(whole_ref.shape[0])]
    slot = out_refs[0].shape[0]
    half = slot // 2
    for s, out_ref in enumerate(out_refs):
        query = pick_rows(start_ref[s], len_ref[s], slot, window, q_ref)
        for block in range(2):
            width = (block + 1) * half
            stacked = jnp.concatenate(
                [query[block * half : width, h * HD : (h + 1) * HD] for h in range(heads)], axis=0
            )
            scores = lax.dot_general(
                stacked,
                kv_ref[s, :width, :HD],
                (((1,), (1,)), ((), ())),
                preferred_element_type=jnp.float32,
            )
            row_at = lax.broadcasted_iota(jnp.int32, scores.shape, 0) & (half - 1)
            col_at = lax.broadcasted_iota(jnp.int32, scores.shape, 1)
            scores = jnp.where(col_at <= row_at + block * half, scores * HD ** (-0.5), mask_value)
            peak = jnp.max(scores, axis=-1, keepdims=True)
            raised = jnp.exp(scores - peak)
            weights = raised * (1.0 / jnp.sum(raised, axis=-1, keepdims=True))
            context = jnp.dot(
                weights.astype(jnp.bfloat16),
                kv_ref[s, :width, HD:],
                preferred_element_type=jnp.float32,
            ).astype(out_ref.dtype)
            for h in range(heads):
                out_ref[block * half : width, h * HD : (h + 1) * HD] = context[
                    h * half : (h + 1) * half
                ]


def attend(starts, lens, query, kv_slots, window, apart):
    columns = query.shape[1]
    count, slot = kv_slots.shape[:2]
    scalars = pl.BlockSpec(memory_space=pltpu.SMEM)
    vmem = pl.BlockSpec(memory_space=pltpu.VMEM)
    return pl.pallas_call(
        functools.partial(attend_kernel, columns // HD, window),
        in_specs=[scalars, scalars, vmem, vmem],
        out_specs=[vmem] * count if apart else vmem,
        out_shape=(
            [pltpu.VMEM((slot, columns), jnp.bfloat16)] * count
            if apart
            else pltpu.VMEM((count, slot, columns), jnp.bfloat16)
        ),
        compiler_params=pltpu.CompilerParams(vmem_limit_bytes=6 * 2**20),
        cost_estimate=kernel_cost,
    )(starts, lens, keep(query), kv_slots)


def place_kernel(count, window, start_ref, len_ref, *refs):
    in_refs, (out_ref, total) = refs[:count], refs[-2:]
    rows, slot = total.shape[0], in_refs[0].shape[0]
    total[...] = jnp.zeros_like(total)
    row_at = lax.broadcasted_iota(jnp.int32, (window, slot), 0)
    col_at = lax.broadcasted_iota(jnp.int32, (window, slot), 1)
    for s, in_ref in enumerate(in_refs):
        start = start_ref[s]
        first = pl.multiple_of(jnp.minimum((start // 8) * 8, rows - window), 8)
        pick = jnp.where(
            (row_at == col_at + (start - first)) & (col_at < len_ref[s]), 1.0, 0.0
        ).astype(jnp.bfloat16)
        total[pl.ds(first, window), :] += jnp.dot(
            pick, in_ref[...], preferred_element_type=jnp.float32
        )
    out_ref[...] = total[...].astype(out_ref.dtype)


def place(starts, lens, slots, rows, which, all_columns, before):
    count, (slot, columns) = len(slots), slots[0].shape[-2:]
    window = min(rows, slot + 8)
    if isinstance(slots, list):
        in_specs = [pl.BlockSpec((slot, columns), lambda r, a, b: (0, 0))] * count
        operands = list(slots)
    else:
        in_specs = [
            pl.BlockSpec((None, slot, columns), lambda r, a, b, s=s: (s, 0, 0))
            for s in range(count)
        ]
        operands = [slots] * count
    aliases = {}
    if before is not None:
        in_specs.append(pl.BlockSpec(memory_space=pl.ANY))
        operands.append(before)
        aliases = {2 + count: 0}
    grid_spec = pltpu.PrefetchScalarGridSpec(
        num_scalar_prefetch=2,
        grid=(1,),
        in_specs=in_specs,
        out_specs=pl.BlockSpec((rows, columns), lambda r, a, b: (0, which)),
        scratch_shapes=[pltpu.VMEM((rows, columns), jnp.float32)],
    )
    return pl.pallas_call(
        functools.partial(place_kernel, count, window),
        grid_spec=grid_spec,
        out_shape=jax.ShapeDtypeStruct((rows, all_columns), jnp.bfloat16),
        input_output_aliases=aliases,
        compiler_params=pltpu.CompilerParams(vmem_limit_bytes=8 * 2**20),
        cost_estimate=kernel_cost,
    )(starts, lens, *operands)


def local_line(
    rollout_states,
    norm_gain,
    w_query,
    w_key,
    w_value,
    b_query,
    b_key,
    b_value,
    seq_lengths,
    seq_dest,
    seq_offset,
):
    learners = lax.axis_size("dp")
    line = learners // 2
    me = lax.axis_index("dp")
    z, x = me // 2, me % 2
    t = lax.axis_index("tensor")
    row_count, feature_count = rollout_states.shape
    slot = 2 * row_count // learners
    half = feature_count // 2
    middle = row_count // 2

    def after(array, *others):
        return lax.optimization_barrier((array, *others))[0]

    def swap_x(array):
        return lax.ppermute(array, "dp", [(i, i ^ 1) for i in range(learners)])

    def swap_y(array):
        return lax.ppermute(array, "tensor", [(i, i ^ 2) for i in range(4)])

    def swap_core(array):
        return lax.ppermute(array, "tensor", [(i, i ^ 1) for i in range(4)])

    wide = 2 * HD
    along_z = [[2 * i + j for i in range(line)] for j in range(2)]
    groups = [
        [jnp.concatenate([w_key, w_value], axis=1), w_query[:, :wide]],
        [w_query[:, wide : 2 * wide], w_query[:, 2 * wide : 3 * wide]],
        [w_query[:, 3 * wide :]],
    ]
    weights = []
    for group in groups:
        gathered = lax.all_gather(jnp.stack(group), "dp", axis_index_groups=along_z)
        weights.append(pltpu.with_memory_space_constraint(gathered, pltpu.HBM))
    bias_kv = jnp.concatenate([b_key, b_value])[None, :]
    biases = [b_query[None, low : low + wide] for low in range(0, w_query.shape[1], wide)]

    states = rollout_states
    widened = states.astype(jnp.float32)
    squares = jnp.sum(widened * widened, axis=-1)
    squares = squares + swap_core(squares)
    squares = squares + swap_y(squares)
    scale = lax.rsqrt(squares[:, None] / (4 * feature_count) + norm_eps)

    def normed(first):
        part = lax.dynamic_slice_in_dim(states, first, half, 1).astype(jnp.float32)
        gain = lax.dynamic_slice_in_dim(norm_gain, t * feature_count + first, half, 0)
        return (part * scale * gain[None, :]).astype(jnp.bfloat16)

    own, give = normed(x * half), normed((1 - x) * half)

    near_a = swap_x(give[:middle])
    own_a = swap_y(own[:middle])
    own_core = swap_core(own)
    near_b = swap_x(after(give[middle:], near_a))
    diag_a = swap_y(after(near_a, own_a))
    near_a_core = swap_core(near_a)
    own_a_core = swap_core(after(own_a, near_a))
    diag_b = swap_y(after(near_b, diag_a))
    near_b_core = swap_core(after(near_b, diag_a))
    diag_a_core = swap_core(after(diag_a, near_b))
    own_b = swap_y(after(own[middle:], diag_b))
    diag_b_core = swap_core(diag_b)
    near_ax = [[near_a], [near_a_core], [diag_a], [diag_a_core]]
    near_bx = [[near_b], [near_b_core], [diag_b], [diag_b_core]]
    near_x = [pack(near_ax, False), pack(near_bx, False)]
    which = jnp.stack([t ^ i for i in range(4)]).astype(jnp.int32)

    lengths = seq_lengths.reshape(learners, learners)
    dests = seq_dest.reshape(learners, learners)
    offsets = seq_offset.reshape(learners, learners)
    starts = jnp.cumsum(lengths, axis=1) - lengths
    peer_ids = jnp.arange(learners, dtype=jnp.int32)
    rows = jnp.arange(row_count, dtype=jnp.int32)
    length = lax.dynamic_index_in_dim(lengths, me, 0, keepdims=False)
    start = lax.dynamic_index_in_dim(starts, me, 0, keepdims=False)
    dest = lax.dynamic_index_in_dim(dests, me, 0, keepdims=False)
    partners = me ^ peer_ids

    def by_learner(order):
        match = (dest[None, :] == order[:, None]).astype(jnp.int32)
        return jnp.sum(match * start[None, :], axis=1), jnp.sum(match * length[None, :], axis=1)

    send_to = by_learner(partners)
    send_all = by_learner(peer_ids)
    inside = (rows[:, None] >= start[None, :]) & (rows[:, None] < (start + length)[None, :])
    position = rows - jnp.sum(inside.astype(jnp.int32) * start[None, :], axis=1)
    angles = keep(jnp.concatenate(rope_tables(position), axis=1))
    matched = (dests == me).astype(jnp.int32)
    match = (peer_ids[None, :] == partners[:, None]).astype(jnp.int32)
    runs_all = jnp.sum(matched * offsets, axis=1), jnp.sum(matched * lengths, axis=1)
    runs_from = tuple(jnp.sum(match * run[None, :], axis=1) for run in runs_all)

    window = min(row_count, -(-(slot + 16) // 128) * 128)

    def send(outgoing):
        incoming = [outgoing[0]]
        for d in range(1, learners):
            pairs = [(i, i ^ d) for i in range(learners)]
            incoming.append(lax.ppermute(outgoing[d], "dp", pairs))
        return incoming

    def exchange(outgoing):
        return lax.all_to_all(outgoing, "dp", split_axis=0, concat_axis=0, tiled=True)

    def receive(c, incoming, before, *others):
        run_start, run_length = runs_from if isinstance(incoming, list) else runs_all
        start_at = after(run_start, *others)
        return place(start_at, run_length, incoming, row_count, c, w_query.shape[1], before)

    first, second, third = weights
    whole = [(0, wide, jnp.bfloat16)]

    def partial(group, chunks, outs, *others):
        return projection(after(which, *others), near_x, group, chunks, outs)

    def contexts(c, group, chunk, got, others, attend_after=(), apart=False):
        ending = ((True, True), got, biases[c], angles)
        (rot,) = projection(after(which, *others), own_x, group, (chunk,), whole, ending)
        send_start, send_length = send_to if apart else send_all
        start_at = after(send_start, *attend_after)
        slots = kv_slots_to if apart else kv_slots
        return attend(start_at, send_length, rot, slots, window, apart)

    outs = [(0, wide, jnp.float32), (wide, 2 * wide, jnp.bfloat16)]
    part_kv, part_0 = partial(first, (0, 1), outs)
    got_kv = swap_x(part_kv)
    own_b_core = swap_core(after(own_b, part_kv))
    own_x = [keep(pack([[own], [own_core], [own_a, own_b], [own_a_core, own_b_core]], True))]
    got_0 = swap_x(after(part_0, got_kv))
    ending = ((True, False), got_kv, bias_kv, angles)
    (kv,) = projection(which, own_x, first, (0,), whole, ending)
    kv_slots = keep(to_slots(*send_all, kv, slot, window))
    kv_slots_to = keep(to_slots(*send_to, kv, slot, window))
    out_0 = contexts(0, first, 1, got_0, (kv,))
    in_0 = exchange(out_0)
    outs = [(0, wide, jnp.bfloat16), (wide, 2 * wide, jnp.bfloat16)]
    part_1, part_2 = partial(second, (0, 1), outs, out_0)
    got_1 = swap_x(part_1)
    got_2 = swap_x(after(part_2, got_1))
    out_1 = contexts(1, second, 0, got_1, (part_2,), (got_2,))
    in_1 = exchange(out_1)
    (part_3,) = partial(third, (0,), whole, out_1)
    got_3 = swap_x(part_3)
    result = receive(0, in_0, None, part_3)
    out_2 = contexts(2, second, 1, got_2, (part_3,), (got_3,))
    in_2 = exchange(after(out_2, in_0))
    out_3 = contexts(3, third, 0, got_3, (out_2,), apart=True)
    in_3 = send(out_3)
    result = receive(1, in_1, result, out_3[0])
    result = receive(2, in_2, result, out_3[0])
    return receive(3, in_3, result)


def solution(mesh):
    placed = (
        P("dp", "tensor"),
        P(),
        P("dp", "tensor"),
        P("dp", "tensor"),
        P("dp", "tensor"),
        P("tensor"),
        P("tensor"),
        P("tensor"),
        P(),
        P(),
        P(),
    )
    fits_line = mesh.shape["dp"] == 8 and mesh.shape["tensor"] == 4
    return jax.shard_map(
        local_line if fits_line else local_any,
        mesh=mesh,
        in_specs=placed,
        out_specs=P("dp", "tensor"),
        check_vma=False,
    )
```

```python
import functools

import jax
import jax.numpy as jnp
from jax import lax
from jax.experimental import pallas as pl
from jax.experimental.pallas import tpu as pltpu
from jax.sharding import PartitionSpec as P

HD = 128

rope_base = 1000000.0
norm_eps = 1e-06
mask_value = -1e30
kernel_cost = pl.CostEstimate(flops=4 * 10**9, bytes_accessed=2**20, transcendentals=0)


def rope_tables(positions):
    half_dim = HD // 2
    frequency = rope_base ** (-(jnp.arange(half_dim).astype(jnp.float32) * 2.0 / HD))
    angles = positions.astype(jnp.float32)[:, None] * frequency[None, :]
    return (jnp.cos(angles), jnp.sin(angles))


def rotate(states, cosine, sine):
    half_dim = states.shape[-1] // 2
    first_half = states[..., :half_dim]
    second_half = states[..., half_dim:]
    cos_wide = cosine[:, None, :]
    sin_wide = sine[:, None, :]
    return jnp.concatenate(
        [
            first_half * cos_wide - second_half * sin_wide,
            second_half * cos_wide + first_half * sin_wide,
        ],
        axis=-1,
    )


def local_any(
    rollout_states,
    norm_gain,
    w_query,
    w_key,
    w_value,
    b_query,
    b_key,
    b_value,
    seq_lengths,
    seq_dest,
    seq_offset,
):
    learners = lax.axis_size("dp")
    own_index = lax.axis_index("dp")
    row_count, feature_count = rollout_states.shape
    capacity = 2 * row_count // learners - 1
    lengths = seq_lengths.reshape(learners, learners)
    dests = seq_dest.reshape(learners, learners)
    offsets = seq_offset.reshape(learners, learners)
    starts = jnp.cumsum(lengths, axis=1) - lengths
    peer_ids = jnp.arange(learners, dtype=jnp.int32)
    own_length = lax.dynamic_index_in_dim(lengths, own_index, 0, keepdims=False)
    own_start = lax.dynamic_index_in_dim(starts, own_index, 0, keepdims=False)
    own_dest = lax.dynamic_index_in_dim(dests, own_index, 0, keepdims=False)
    match_send = (own_dest[None, :] == peer_ids[:, None]).astype(jnp.int32)
    send_start = jnp.sum(match_send * own_start[None, :], axis=1)
    send_length = jnp.sum(match_send * own_length[None, :], axis=1)
    slot_index = jnp.arange(capacity, dtype=jnp.int32)
    pick_rows = send_start[:, None] + slot_index[None, :]
    padded = jnp.concatenate(
        [rollout_states, jnp.zeros((capacity, feature_count), rollout_states.dtype)], axis=0
    )
    live_slots = (slot_index[None, :] < send_length[:, None])[..., None]
    outgoing = jnp.where(
        live_slots, jnp.take(padded, pick_rows, axis=0), jnp.zeros((), rollout_states.dtype)
    )
    incoming = lax.all_to_all(outgoing, "dp", split_axis=0, concat_axis=0, tiled=True)
    matched = (dests == own_index).astype(jnp.int32)
    run_start = jnp.sum(matched * offsets, axis=1)
    run_length = jnp.sum(matched * lengths, axis=1)
    rows = jnp.arange(row_count, dtype=jnp.int32)
    inside = (
        (rows[:, None] >= run_start[None, :]) & (rows[:, None] < (run_start + run_length)[None, :])
    ).astype(jnp.int32)
    source_ids = jnp.sum(inside * peer_ids[None, :], axis=1)
    within_seq = rows - jnp.sum(inside * run_start[None, :], axis=1)
    arrived = jnp.take(
        incoming.reshape(learners * capacity, feature_count),
        source_ids * capacity + within_seq,
        axis=0,
    )
    gathered = lax.all_gather(arrived, "tensor", axis=1, tiled=True)
    widened = gathered.astype(jnp.float32)
    statistic = jnp.mean(widened * widened, axis=-1, keepdims=True)
    normed = (widened * lax.rsqrt(statistic + norm_eps) * norm_gain[None, :]).astype(jnp.bfloat16)
    full_query, full_key, full_value = (
        lax.all_gather(w_query, "dp", axis=0, tiled=True),
        lax.all_gather(w_key, "dp", axis=0, tiled=True),
        lax.all_gather(w_value, "dp", axis=0, tiled=True),
    )
    query = jnp.dot(normed, full_query, preferred_element_type=jnp.float32)
    key = jnp.dot(normed, full_key, preferred_element_type=jnp.float32)
    value = jnp.dot(normed, full_value, preferred_element_type=jnp.float32)
    query = query + b_query[None, :]
    key = key + b_key[None, :]
    value = value + b_value[None, :]
    heads_here = query.shape[1] // HD
    kv_here = key.shape[1] // HD
    group = heads_here // kv_here
    cosine, sine = rope_tables(within_seq)
    rot_query = rotate(query.reshape(row_count, heads_here, HD), cosine, sine).astype(jnp.bfloat16)
    rot_query = rot_query.reshape(row_count, kv_here, group, HD)
    rot_key = rotate(key.reshape(row_count, kv_here, HD), cosine, sine).astype(jnp.bfloat16)
    value_bf = value.reshape(row_count, kv_here, HD).astype(jnp.bfloat16)
    block_rows = min(512, row_count)

    def one_block(block_number):
        first_row = block_number * block_rows
        query_block = lax.dynamic_slice_in_dim(rot_query, first_row, block_rows, 0)
        query_source = lax.dynamic_slice_in_dim(source_ids, first_row, block_rows, 0)
        query_rows = first_row + jnp.arange(block_rows, dtype=jnp.int32)
        scores = jnp.einsum(
            "bcgd,kcd->cgbk", query_block, rot_key, preferred_element_type=jnp.float32
        )
        scores = scores * HD ** (-0.5)
        allowed = (source_ids[None, :] == query_source[:, None]) & (
            rows[None, :] <= query_rows[:, None]
        )
        scores = jnp.where(allowed[None, None], scores, mask_value)
        peak = jnp.max(scores, axis=-1, keepdims=True)
        raised = jnp.exp(scores - peak)
        weights = (raised / jnp.sum(raised, axis=-1, keepdims=True)).astype(jnp.bfloat16)
        context = jnp.einsum(
            "cgbk,kcd->bcgd", weights, value_bf, preferred_element_type=jnp.float32
        )
        return context.astype(jnp.bfloat16).reshape(block_rows, heads_here * HD)

    outputs = lax.map(one_block, jnp.arange(row_count // block_rows, dtype=jnp.int32))
    return outputs.reshape(row_count, heads_here * HD)


def pack_kernel(counts, *refs):
    refs = list(refs)
    pieces = [[refs.pop(0) for _ in range(n)] for n in counts]
    out_ref, sems = refs
    copies = []
    for i, block in enumerate(pieces):
        first = 0
        for n, piece in enumerate(block):
            rows = piece.shape[0]
            copies.append(
                pltpu.make_async_copy(piece, out_ref.at[i, pl.ds(first, rows)], sems.at[i, n])
            )
            first += rows
    for copy in copies:
        copy.start()
    for copy in copies:
        copy.wait()


def pack(blocks, in_vmem):
    counts = tuple(len(pieces) for pieces in blocks)
    rows = sum(piece.shape[0] for piece in blocks[0])
    feats = blocks[0][0].shape[1]
    operands = [piece for pieces in blocks for piece in pieces]
    shape = (len(blocks), rows, feats)
    if in_vmem:
        space, out_shape = pltpu.VMEM, pltpu.VMEM(shape, jnp.bfloat16)
    else:
        space, out_shape = pl.ANY, jax.ShapeDtypeStruct(shape, jnp.bfloat16)
    return pl.pallas_call(
        functools.partial(pack_kernel, counts),
        in_specs=[pl.BlockSpec(memory_space=pl.ANY)] * len(operands),
        out_specs=pl.BlockSpec(memory_space=space),
        out_shape=out_shape,
        scratch_shapes=[pltpu.SemaphoreType.DMA((len(blocks), 2))],
        compiler_params=pltpu.CompilerParams(vmem_limit_bytes=4 * 2**20),
        cost_estimate=kernel_cost,
    )(*operands)


def product_kernel(x_count, ropes, chunks, out_lanes, which_ref, *refs):
    refs = list(refs)
    x_refs = [refs.pop(0) for _ in range(x_count)]
    w_ref = refs.pop(0)
    if ropes:
        part_ref, bias_ref, angle_ref = (refs.pop(0) for _ in range(3))
    out_refs = [refs.pop(0) for _ in out_lanes]
    w_buf, sems = refs
    rows = out_refs[0].shape[0]
    part_rows = x_refs[0].shape[1]
    tile = min(512, part_rows)
    wide = w_ref.shape[3]
    copies = [
        [
            pltpu.make_async_copy(
                w_ref.at[which_ref[i], chunk],
                w_buf.at[i, :, pl.ds(n * wide, wide)],
                sems.at[i, n],
            )
            for n, chunk in enumerate(chunks)
        ]
        for i in range(4)
    ]
    for block in copies:
        for copy in block:
            copy.start()

    for first, x_ref in zip(range(0, rows, part_rows), x_refs):
        if first == 0:
            for block in copies:
                for copy in block:
                    copy.wait()

        @pl.loop(0, part_rows, step=tile)
        def _(at, first=first, x_ref=x_ref):
            here = pl.ds(pl.multiple_of(first + at, tile), tile)
            term = None
            for i in range(4):
                rows_here = x_ref[i, pl.ds(pl.multiple_of(at, tile), tile), :]
                dot = jnp.dot(rows_here, w_buf[i], preferred_element_type=jnp.float32)
                term = dot if term is None else term + dot
            if not ropes:
                for out_ref, (low, high) in zip(out_refs, out_lanes):
                    out_ref[here, :] = term[:, low:high].astype(out_ref.dtype)
                return
            (out_ref,) = out_refs
            term = term + part_ref[here, :].astype(jnp.float32) + bias_ref[...]
            angle = angle_ref[here, :]
            turned_angle = pltpu.roll(angle, HD // 2, 1)
            low = lax.broadcasted_iota(jnp.int32, angle.shape, 1) < HD // 2
            cosine = jnp.where(low, angle, turned_angle)
            sine = jnp.where(low, -turned_angle, angle)
            for c, rope in enumerate(ropes):
                head = term[:, c * HD : (c + 1) * HD]
                if rope:
                    head = head * cosine + pltpu.roll(head, HD // 2, 1) * sine
                out_ref[here, c * HD : (c + 1) * HD] = head.astype(out_ref.dtype)


def keep(array):
    return pltpu.with_memory_space_constraint(array, pltpu.VMEM)


def projection(which, x_parts, weights, chunks, outs, finish=None):
    rows = sum(part.shape[1] for part in x_parts)
    feats, columns = weights.shape[2], weights.shape[3] * len(chunks)
    vmem = pl.BlockSpec(memory_space=pltpu.VMEM)
    operands = list(x_parts)
    in_specs = [vmem] * len(operands) + [pl.BlockSpec(memory_space=pl.ANY)]
    operands.append(weights)
    ropes = None
    if finish is not None:
        ropes, part, bias, angles = finish
        operands += [keep(part), bias, angles]
        in_specs += [vmem] * 3
    return pl.pallas_call(
        functools.partial(
            product_kernel,
            len(x_parts),
            ropes,
            tuple(chunks),
            tuple((first, last) for first, last, _ in outs),
        ),
        in_specs=[pl.BlockSpec(memory_space=pltpu.SMEM)] + in_specs,
        out_specs=[vmem] * len(outs),
        out_shape=[pltpu.VMEM((rows, last - first), kind) for first, last, kind in outs],
        scratch_shapes=[
            pltpu.VMEM((4, feats, columns), jnp.bfloat16),
            pltpu.SemaphoreType.DMA((4, len(chunks))),
        ],
        compiler_params=pltpu.CompilerParams(vmem_limit_bytes=(10 + columns // 128) * 2**20),
        cost_estimate=kernel_cost,
    )(which, *operands)


def pick_rows(start, length, slot, window, ref, lanes=slice(None)):
    first = pl.multiple_of(jnp.minimum((start // 16) * 16, ref.shape[0] - window), 16)
    row_at = lax.broadcasted_iota(jnp.int32, (slot, window), 0)
    col_at = lax.broadcasted_iota(jnp.int32, (slot, window), 1)
    pick = jnp.where((col_at == row_at + (start - first)) & (row_at < length), 1.0, 0.0)
    rows = jnp.dot(
        pick.astype(jnp.bfloat16), ref[pl.ds(first, window), lanes], preferred_element_type=jnp.float32
    )
    return rows.astype(jnp.bfloat16)


def slots_kernel(slot, window, start_ref, len_ref, in_ref, out_ref):
    for s in range(out_ref.shape[0]):
        out_ref[s] = pick_rows(start_ref[s], len_ref[s], slot, window, in_ref)


def to_slots(starts, lens, array, slot, window):
    count, columns = starts.shape[0], array.shape[1]
    scalars = pl.BlockSpec(memory_space=pltpu.SMEM)
    vmem = pl.BlockSpec(memory_space=pltpu.VMEM)
    return pl.pallas_call(
        functools.partial(slots_kernel, slot, window),
        in_specs=[scalars, scalars, vmem],
        out_specs=vmem,
        out_shape=pltpu.VMEM((count, slot, columns), jnp.bfloat16),
        compiler_params=pltpu.CompilerParams(vmem_limit_bytes=5 * 2**20),
        cost_estimate=kernel_cost,
    )(starts, lens, keep(array))


def attend_kernel(heads, window, start_ref, len_ref, q_ref, kv_ref, *out_refs):
    if len(out_refs) == 1:
        (whole_ref,) = out_refs
        out_refs = [whole_ref.at[s] for s in range(whole_ref.shape[0])]
    slot = out_refs[0].shape[0]
    half = slot // 2
    for s, out_ref in enumerate(out_refs):
        query = pick_rows(start_ref[s], len_ref[s], slot, window, q_ref)
        for block in range(2):
            width = (block + 1) * half
            stacked = jnp.concatenate(
                [query[block * half : width, h * HD : (h + 1) * HD] for h in range(heads)], axis=0
            )
            scores = lax.dot_general(
                stacked,
                kv_ref[s, :width, :HD],
                (((1,), (1,)), ((), ())),
                preferred_element_type=jnp.float32,
            )
            row_at = lax.broadcasted_iota(jnp.int32, scores.shape, 0) & (half - 1)
            col_at = lax.broadcasted_iota(jnp.int32, scores.shape, 1)
            scores = jnp.where(col_at <= row_at + block * half, scores * HD ** (-0.5), mask_value)
            peak = jnp.max(scores, axis=-1, keepdims=True)
            raised = jnp.exp(scores - peak)
            weights = raised * (1.0 / jnp.sum(raised, axis=-1, keepdims=True))
            context = jnp.dot(
                weights.astype(jnp.bfloat16),
                kv_ref[s, :width, HD:],
                preferred_element_type=jnp.float32,
            ).astype(out_ref.dtype)
            for h in range(heads):
                out_ref[block * half : width, h * HD : (h + 1) * HD] = context[
                    h * half : (h + 1) * half
                ]


def attend(starts, lens, query, kv_slots, window, apart):
    columns = query.shape[1]
    count, slot = kv_slots.shape[:2]
    scalars = pl.BlockSpec(memory_space=pltpu.SMEM)
    vmem = pl.BlockSpec(memory_space=pltpu.VMEM)
    return pl.pallas_call(
        functools.partial(attend_kernel, columns // HD, window),
        in_specs=[scalars, scalars, vmem, vmem],
        out_specs=[vmem] * count if apart else vmem,
        out_shape=(
            [pltpu.VMEM((slot, columns), jnp.bfloat16)] * count
            if apart
            else pltpu.VMEM((count, slot, columns), jnp.bfloat16)
        ),
        compiler_params=pltpu.CompilerParams(vmem_limit_bytes=6 * 2**20),
        cost_estimate=kernel_cost,
    )(starts, lens, keep(query), kv_slots)


def place_kernel(count, window, start_ref, len_ref, *refs):
    in_refs, (out_ref, total) = refs[:count], refs[-2:]
    rows, slot = total.shape[0], in_refs[0].shape[0]
    total[...] = jnp.zeros_like(total)
    row_at = lax.broadcasted_iota(jnp.int32, (window, slot), 0)
    col_at = lax.broadcasted_iota(jnp.int32, (window, slot), 1)
    for s, in_ref in enumerate(in_refs):
        start = start_ref[s]
        first = pl.multiple_of(jnp.minimum((start // 8) * 8, rows - window), 8)
        pick = jnp.where(
            (row_at == col_at + (start - first)) & (col_at < len_ref[s]), 1.0, 0.0
        ).astype(jnp.bfloat16)
        total[pl.ds(first, window), :] += jnp.dot(
            pick, in_ref[...], preferred_element_type=jnp.float32
        )
    out_ref[...] = total[...].astype(out_ref.dtype)


def place(starts, lens, slots, rows, which, all_columns, before):
    count, (slot, columns) = len(slots), slots[0].shape[-2:]
    window = min(rows, slot + 8)
    if isinstance(slots, list):
        in_specs = [pl.BlockSpec((slot, columns), lambda r, a, b: (0, 0))] * count
        operands = list(slots)
    else:
        in_specs = [
            pl.BlockSpec((None, slot, columns), lambda r, a, b, s=s: (s, 0, 0))
            for s in range(count)
        ]
        operands = [slots] * count
    aliases = {}
    if before is not None:
        in_specs.append(pl.BlockSpec(memory_space=pl.ANY))
        operands.append(before)
        aliases = {2 + count: 0}
    grid_spec = pltpu.PrefetchScalarGridSpec(
        num_scalar_prefetch=2,
        grid=(1,),
        in_specs=in_specs,
        out_specs=pl.BlockSpec((rows, columns), lambda r, a, b: (0, which)),
        scratch_shapes=[pltpu.VMEM((rows, columns), jnp.float32)],
    )
    return pl.pallas_call(
        functools.partial(place_kernel, count, window),
        grid_spec=grid_spec,
        out_shape=jax.ShapeDtypeStruct((rows, all_columns), jnp.bfloat16),
        input_output_aliases=aliases,
        compiler_params=pltpu.CompilerParams(vmem_limit_bytes=8 * 2**20),
        cost_estimate=kernel_cost,
    )(starts, lens, *operands)


def local_line(
    rollout_states,
    norm_gain,
    w_query,
    w_key,
    w_value,
    b_query,
    b_key,
    b_value,
    seq_lengths,
    seq_dest,
    seq_offset,
):
    learners = lax.axis_size("dp")
    line = learners // 2
    me = lax.axis_index("dp")
    z, x = me // 2, me % 2
    t = lax.axis_index("tensor")
    row_count, feature_count = rollout_states.shape
    slot = 2 * row_count // learners
    half = feature_count // 2
    middle = row_count // 2

    def after(array, *others):
        return lax.optimization_barrier((array, *others))[0]

    def swap_x(array):
        return lax.ppermute(array, "dp", [(i, i ^ 1) for i in range(learners)])

    def swap_y(array):
        return lax.ppermute(array, "tensor", [(i, i ^ 2) for i in range(4)])

    def swap_core(array):
        return lax.ppermute(array, "tensor", [(i, i ^ 1) for i in range(4)])

    wide = 2 * HD
    along_z = [[2 * i + j for i in range(line)] for j in range(2)]
    groups = [
        [jnp.concatenate([w_key, w_value], axis=1), w_query[:, :wide]],
        [w_query[:, wide : 2 * wide], w_query[:, 2 * wide : 3 * wide]],
        [w_query[:, 3 * wide :]],
    ]
    weights = []
    for group in groups:
        gathered = lax.all_gather(jnp.stack(group), "dp", axis_index_groups=along_z)
        weights.append(pltpu.with_memory_space_constraint(gathered, pltpu.HBM))
    bias_kv = jnp.concatenate([b_key, b_value])[None, :]
    biases = [b_query[None, low : low + wide] for low in range(0, w_query.shape[1], wide)]

    states = rollout_states
    widened = states.astype(jnp.float32)
    squares = jnp.sum(widened * widened, axis=-1)
    squares = squares + swap_core(squares)
    squares = squares + swap_y(squares)
    scale = lax.rsqrt(squares[:, None] / (4 * feature_count) + norm_eps)

    def normed(first):
        part = lax.dynamic_slice_in_dim(states, first, half, 1).astype(jnp.float32)
        gain = lax.dynamic_slice_in_dim(norm_gain, t * feature_count + first, half, 0)
        return (part * scale * gain[None, :]).astype(jnp.bfloat16)

    own, give = normed(x * half), normed((1 - x) * half)

    near_a = swap_x(give[:middle])
    own_a = swap_y(own[:middle])
    own_core = swap_core(own)
    near_b = swap_x(after(give[middle:], near_a))
    diag_a = swap_y(after(near_a, own_a))
    near_a_core = swap_core(near_a)
    own_a_core = swap_core(after(own_a, near_a))
    diag_b = swap_y(after(near_b, diag_a))
    near_b_core = swap_core(after(near_b, diag_a))
    diag_a_core = swap_core(after(diag_a, near_b))
    own_b = swap_y(after(own[middle:], diag_b))
    diag_b_core = swap_core(diag_b)
    near_ax = [[near_a], [near_a_core], [diag_a], [diag_a_core]]
    near_bx = [[near_b], [near_b_core], [diag_b], [diag_b_core]]
    near_x = [pack(near_ax, False), pack(near_bx, False)]
    which = jnp.stack([t ^ i for i in range(4)]).astype(jnp.int32)

    lengths = seq_lengths.reshape(learners, learners)
    dests = seq_dest.reshape(learners, learners)
    offsets = seq_offset.reshape(learners, learners)
    starts = jnp.cumsum(lengths, axis=1) - lengths
    peer_ids = jnp.arange(learners, dtype=jnp.int32)
    rows = jnp.arange(row_count, dtype=jnp.int32)
    length = lax.dynamic_index_in_dim(lengths, me, 0, keepdims=False)
    start = lax.dynamic_index_in_dim(starts, me, 0, keepdims=False)
    dest = lax.dynamic_index_in_dim(dests, me, 0, keepdims=False)
    partners = me ^ peer_ids

    def by_learner(order):
        match = (dest[None, :] == order[:, None]).astype(jnp.int32)
        return jnp.sum(match * start[None, :], axis=1), jnp.sum(match * length[None, :], axis=1)

    send_to = by_learner(partners)
    send_all = by_learner(peer_ids)
    inside = (rows[:, None] >= start[None, :]) & (rows[:, None] < (start + length)[None, :])
    position = rows - jnp.sum(inside.astype(jnp.int32) * start[None, :], axis=1)
    angles = keep(jnp.concatenate(rope_tables(position), axis=1))
    matched = (dests == me).astype(jnp.int32)
    match = (peer_ids[None, :] == partners[:, None]).astype(jnp.int32)
    runs_all = jnp.sum(matched * offsets, axis=1), jnp.sum(matched * lengths, axis=1)
    runs_from = tuple(jnp.sum(match * run[None, :], axis=1) for run in runs_all)

    window = min(row_count, -(-(slot + 16) // 128) * 128)

    def send(outgoing):
        incoming = [outgoing[0]]
        for d in range(1, learners):
            pairs = [(i, i ^ d) for i in range(learners)]
            incoming.append(lax.ppermute(outgoing[d], "dp", pairs))
        return incoming

    def exchange(outgoing):
        return lax.all_to_all(outgoing, "dp", split_axis=0, concat_axis=0, tiled=True)

    def receive(c, incoming, before, *others):
        run_start, run_length = runs_from if isinstance(incoming, list) else runs_all
        start_at = after(run_start, *others)
        return place(start_at, run_length, incoming, row_count, c, w_query.shape[1], before)

    first, second, third = weights
    whole = [(0, wide, jnp.bfloat16)]

    def partial(group, chunks, outs, *others):
        return projection(after(which, *others), near_x, group, chunks, outs)

    def contexts(c, group, chunk, got, others, attend_after=(), apart=False):
        ending = ((True, True), got, biases[c], angles)
        (rot,) = projection(after(which, *others), own_x, group, (chunk,), whole, ending)
        send_start, send_length = send_to if apart else send_all
        start_at = after(send_start, *attend_after)
        slots = kv_slots_to if apart else kv_slots
        return attend(start_at, send_length, rot, slots, window, apart)

    outs = [(0, wide, jnp.float32), (wide, 2 * wide, jnp.bfloat16)]
    part_kv, part_0 = partial(first, (0, 1), outs)
    got_kv = swap_x(part_kv)
    own_b_core = swap_core(after(own_b, part_kv))
    own_x = [keep(pack([[own], [own_core], [own_a, own_b], [own_a_core, own_b_core]], True))]
    got_0 = swap_x(after(part_0, got_kv))
    ending = ((True, False), got_kv, bias_kv, angles)
    (kv,) = projection(which, own_x, first, (0,), whole, ending)
    kv_slots = keep(to_slots(*send_all, kv, slot, window))
    kv_slots_to = keep(to_slots(*send_to, kv, slot, window))
    out_0 = contexts(0, first, 1, got_0, (kv,))
    in_0 = exchange(out_0)
    outs = [(0, wide, jnp.bfloat16), (wide, 2 * wide, jnp.bfloat16)]
    part_1, part_2 = partial(second, (0, 1), outs, out_0)
    got_1 = swap_x(part_1)
    got_2 = swap_x(after(part_2, got_1))
    out_1 = contexts(1, second, 0, got_1, (part_2,), (got_2,))
    in_1 = exchange(out_1)
    out_2 = contexts(2, second, 1, got_2, (out_1,))
    (part_3,) = partial(third, (0,), whole, out_2)
    got_3 = swap_x(part_3)
    result = receive(0, in_0, None, part_3)
    in_2 = exchange(after(out_2, in_0, got_3))
    out_3 = contexts(3, third, 0, got_3, (out_2,), apart=True)
    in_3 = send(out_3)
    result = receive(1, in_1, result, out_3[0])
    result = receive(2, in_2, result, out_3[0])
    return receive(3, in_3, result)


def solution(mesh):
    placed = (
        P("dp", "tensor"),
        P(),
        P("dp", "tensor"),
        P("dp", "tensor"),
        P("dp", "tensor"),
        P("tensor"),
        P("tensor"),
        P("tensor"),
        P(),
        P(),
        P(),
    )
    fits_line = mesh.shape["dp"] == 8 and mesh.shape["tensor"] == 4
    return jax.shard_map(
        local_line if fits_line else local_any,
        mesh=mesh,
        in_specs=placed,
        out_specs=P("dp", "tensor"),
        check_vma=False,
    )
```

```python
import functools

import jax
import jax.numpy as jnp
from jax import lax
from jax.experimental import pallas as pl
from jax.experimental.pallas import tpu as pltpu
from jax.sharding import PartitionSpec as P

HD = 128

rope_base = 1000000.0
norm_eps = 1e-06
mask_value = -1e30
kernel_cost = pl.CostEstimate(flops=4 * 10**9, bytes_accessed=2**20, transcendentals=0)


def rope_tables(positions):
    half_dim = HD // 2
    frequency = rope_base ** (-(jnp.arange(half_dim).astype(jnp.float32) * 2.0 / HD))
    angles = positions.astype(jnp.float32)[:, None] * frequency[None, :]
    return (jnp.cos(angles), jnp.sin(angles))


def rotate(states, cosine, sine):
    half_dim = states.shape[-1] // 2
    first_half = states[..., :half_dim]
    second_half = states[..., half_dim:]
    cos_wide = cosine[:, None, :]
    sin_wide = sine[:, None, :]
    return jnp.concatenate(
        [
            first_half * cos_wide - second_half * sin_wide,
            second_half * cos_wide + first_half * sin_wide,
        ],
        axis=-1,
    )


def local_any(
    rollout_states,
    norm_gain,
    w_query,
    w_key,
    w_value,
    b_query,
    b_key,
    b_value,
    seq_lengths,
    seq_dest,
    seq_offset,
):
    learners = lax.axis_size("dp")
    own_index = lax.axis_index("dp")
    row_count, feature_count = rollout_states.shape
    capacity = 2 * row_count // learners - 1
    lengths = seq_lengths.reshape(learners, learners)
    dests = seq_dest.reshape(learners, learners)
    offsets = seq_offset.reshape(learners, learners)
    starts = jnp.cumsum(lengths, axis=1) - lengths
    peer_ids = jnp.arange(learners, dtype=jnp.int32)
    own_length = lax.dynamic_index_in_dim(lengths, own_index, 0, keepdims=False)
    own_start = lax.dynamic_index_in_dim(starts, own_index, 0, keepdims=False)
    own_dest = lax.dynamic_index_in_dim(dests, own_index, 0, keepdims=False)
    match_send = (own_dest[None, :] == peer_ids[:, None]).astype(jnp.int32)
    send_start = jnp.sum(match_send * own_start[None, :], axis=1)
    send_length = jnp.sum(match_send * own_length[None, :], axis=1)
    slot_index = jnp.arange(capacity, dtype=jnp.int32)
    pick_rows = send_start[:, None] + slot_index[None, :]
    padded = jnp.concatenate(
        [rollout_states, jnp.zeros((capacity, feature_count), rollout_states.dtype)], axis=0
    )
    live_slots = (slot_index[None, :] < send_length[:, None])[..., None]
    outgoing = jnp.where(
        live_slots, jnp.take(padded, pick_rows, axis=0), jnp.zeros((), rollout_states.dtype)
    )
    incoming = lax.all_to_all(outgoing, "dp", split_axis=0, concat_axis=0, tiled=True)
    matched = (dests == own_index).astype(jnp.int32)
    run_start = jnp.sum(matched * offsets, axis=1)
    run_length = jnp.sum(matched * lengths, axis=1)
    rows = jnp.arange(row_count, dtype=jnp.int32)
    inside = (
        (rows[:, None] >= run_start[None, :]) & (rows[:, None] < (run_start + run_length)[None, :])
    ).astype(jnp.int32)
    source_ids = jnp.sum(inside * peer_ids[None, :], axis=1)
    within_seq = rows - jnp.sum(inside * run_start[None, :], axis=1)
    arrived = jnp.take(
        incoming.reshape(learners * capacity, feature_count),
        source_ids * capacity + within_seq,
        axis=0,
    )
    gathered = lax.all_gather(arrived, "tensor", axis=1, tiled=True)
    widened = gathered.astype(jnp.float32)
    statistic = jnp.mean(widened * widened, axis=-1, keepdims=True)
    normed = (widened * lax.rsqrt(statistic + norm_eps) * norm_gain[None, :]).astype(jnp.bfloat16)
    full_query, full_key, full_value = (
        lax.all_gather(w_query, "dp", axis=0, tiled=True),
        lax.all_gather(w_key, "dp", axis=0, tiled=True),
        lax.all_gather(w_value, "dp", axis=0, tiled=True),
    )
    query = jnp.dot(normed, full_query, preferred_element_type=jnp.float32)
    key = jnp.dot(normed, full_key, preferred_element_type=jnp.float32)
    value = jnp.dot(normed, full_value, preferred_element_type=jnp.float32)
    query = query + b_query[None, :]
    key = key + b_key[None, :]
    value = value + b_value[None, :]
    heads_here = query.shape[1] // HD
    kv_here = key.shape[1] // HD
    group = heads_here // kv_here
    cosine, sine = rope_tables(within_seq)
    rot_query = rotate(query.reshape(row_count, heads_here, HD), cosine, sine).astype(jnp.bfloat16)
    rot_query = rot_query.reshape(row_count, kv_here, group, HD)
    rot_key = rotate(key.reshape(row_count, kv_here, HD), cosine, sine).astype(jnp.bfloat16)
    value_bf = value.reshape(row_count, kv_here, HD).astype(jnp.bfloat16)
    block_rows = min(512, row_count)

    def one_block(block_number):
        first_row = block_number * block_rows
        query_block = lax.dynamic_slice_in_dim(rot_query, first_row, block_rows, 0)
        query_source = lax.dynamic_slice_in_dim(source_ids, first_row, block_rows, 0)
        query_rows = first_row + jnp.arange(block_rows, dtype=jnp.int32)
        scores = jnp.einsum(
            "bcgd,kcd->cgbk", query_block, rot_key, preferred_element_type=jnp.float32
        )
        scores = scores * HD ** (-0.5)
        allowed = (source_ids[None, :] == query_source[:, None]) & (
            rows[None, :] <= query_rows[:, None]
        )
        scores = jnp.where(allowed[None, None], scores, mask_value)
        peak = jnp.max(scores, axis=-1, keepdims=True)
        raised = jnp.exp(scores - peak)
        weights = (raised / jnp.sum(raised, axis=-1, keepdims=True)).astype(jnp.bfloat16)
        context = jnp.einsum(
            "cgbk,kcd->bcgd", weights, value_bf, preferred_element_type=jnp.float32
        )
        return context.astype(jnp.bfloat16).reshape(block_rows, heads_here * HD)

    outputs = lax.map(one_block, jnp.arange(row_count // block_rows, dtype=jnp.int32))
    return outputs.reshape(row_count, heads_here * HD)


def pack_kernel(counts, *refs):
    refs = list(refs)
    pieces = [[refs.pop(0) for _ in range(n)] for n in counts]
    out_ref, sems = refs
    copies = []
    for i, block in enumerate(pieces):
        first = 0
        for n, piece in enumerate(block):
            rows = piece.shape[0]
            copies.append(
                pltpu.make_async_copy(piece, out_ref.at[i, pl.ds(first, rows)], sems.at[i, n])
            )
            first += rows
    for copy in copies:
        copy.start()
    for copy in copies:
        copy.wait()


def pack(blocks, in_vmem):
    counts = tuple(len(pieces) for pieces in blocks)
    rows = sum(piece.shape[0] for piece in blocks[0])
    feats = blocks[0][0].shape[1]
    operands = [piece for pieces in blocks for piece in pieces]
    shape = (len(blocks), rows, feats)
    if in_vmem:
        space, out_shape = pltpu.VMEM, pltpu.VMEM(shape, jnp.bfloat16)
    else:
        space, out_shape = pl.ANY, jax.ShapeDtypeStruct(shape, jnp.bfloat16)
    return pl.pallas_call(
        functools.partial(pack_kernel, counts),
        in_specs=[pl.BlockSpec(memory_space=pl.ANY)] * len(operands),
        out_specs=pl.BlockSpec(memory_space=space),
        out_shape=out_shape,
        scratch_shapes=[pltpu.SemaphoreType.DMA((len(blocks), 2))],
        compiler_params=pltpu.CompilerParams(vmem_limit_bytes=4 * 2**20),
        cost_estimate=kernel_cost,
    )(*operands)


def product_kernel(x_count, ropes, chunks, out_lanes, which_ref, *refs):
    refs = list(refs)
    x_refs = [refs.pop(0) for _ in range(x_count)]
    w_ref = refs.pop(0)
    if ropes:
        part_ref, bias_ref, angle_ref = (refs.pop(0) for _ in range(3))
    out_refs = [refs.pop(0) for _ in out_lanes]
    w_buf, sems = refs
    rows = out_refs[0].shape[0]
    part_rows = x_refs[0].shape[1]
    tile = min(512, part_rows)
    wide = w_ref.shape[3]
    copies = [
        [
            pltpu.make_async_copy(
                w_ref.at[which_ref[i], chunk],
                w_buf.at[i, :, pl.ds(n * wide, wide)],
                sems.at[i, n],
            )
            for n, chunk in enumerate(chunks)
        ]
        for i in range(4)
    ]
    for block in copies:
        for copy in block:
            copy.start()

    for first, x_ref in zip(range(0, rows, part_rows), x_refs):
        if first == 0:
            for block in copies:
                for copy in block:
                    copy.wait()

        @pl.loop(0, part_rows, step=tile)
        def _(at, first=first, x_ref=x_ref):
            here = pl.ds(pl.multiple_of(first + at, tile), tile)
            term = None
            for i in range(4):
                rows_here = x_ref[i, pl.ds(pl.multiple_of(at, tile), tile), :]
                dot = jnp.dot(rows_here, w_buf[i], preferred_element_type=jnp.float32)
                term = dot if term is None else term + dot
            if not ropes:
                for out_ref, (low, high) in zip(out_refs, out_lanes):
                    out_ref[here, :] = term[:, low:high].astype(out_ref.dtype)
                return
            (out_ref,) = out_refs
            term = term + part_ref[here, :].astype(jnp.float32) + bias_ref[...]
            angle = angle_ref[here, :]
            turned_angle = pltpu.roll(angle, HD // 2, 1)
            low = lax.broadcasted_iota(jnp.int32, angle.shape, 1) < HD // 2
            cosine = jnp.where(low, angle, turned_angle)
            sine = jnp.where(low, -turned_angle, angle)
            for c, rope in enumerate(ropes):
                head = term[:, c * HD : (c + 1) * HD]
                if rope:
                    head = head * cosine + pltpu.roll(head, HD // 2, 1) * sine
                out_ref[here, c * HD : (c + 1) * HD] = head.astype(out_ref.dtype)


def keep(array):
    return pltpu.with_memory_space_constraint(array, pltpu.VMEM)


def projection(which, x_parts, weights, chunks, outs, finish=None):
    rows = sum(part.shape[1] for part in x_parts)
    feats, columns = weights.shape[2], weights.shape[3] * len(chunks)
    vmem = pl.BlockSpec(memory_space=pltpu.VMEM)
    operands = list(x_parts)
    in_specs = [vmem] * len(operands) + [pl.BlockSpec(memory_space=pl.ANY)]
    operands.append(weights)
    ropes = None
    if finish is not None:
        ropes, part, bias, angles = finish
        operands += [keep(part), bias, angles]
        in_specs += [vmem] * 3
    return pl.pallas_call(
        functools.partial(
            product_kernel,
            len(x_parts),
            ropes,
            tuple(chunks),
            tuple((first, last) for first, last, _ in outs),
        ),
        in_specs=[pl.BlockSpec(memory_space=pltpu.SMEM)] + in_specs,
        out_specs=[vmem] * len(outs),
        out_shape=[pltpu.VMEM((rows, last - first), kind) for first, last, kind in outs],
        scratch_shapes=[
            pltpu.VMEM((4, feats, columns), jnp.bfloat16),
            pltpu.SemaphoreType.DMA((4, len(chunks))),
        ],
        compiler_params=pltpu.CompilerParams(vmem_limit_bytes=(10 + columns // 128) * 2**20),
        cost_estimate=kernel_cost,
    )(which, *operands)


def pick_rows(start, length, slot, window, ref, lanes=slice(None)):
    first = pl.multiple_of(jnp.minimum((start // 16) * 16, ref.shape[0] - window), 16)
    row_at = lax.broadcasted_iota(jnp.int32, (slot, window), 0)
    col_at = lax.broadcasted_iota(jnp.int32, (slot, window), 1)
    pick = jnp.where((col_at == row_at + (start - first)) & (row_at < length), 1.0, 0.0)
    rows = jnp.dot(
        pick.astype(jnp.bfloat16), ref[pl.ds(first, window), lanes], preferred_element_type=jnp.float32
    )
    return rows.astype(jnp.bfloat16)


def slots_kernel(slot, window, start_ref, len_ref, in_ref, out_ref):
    for s in range(out_ref.shape[0]):
        out_ref[s] = pick_rows(start_ref[s], len_ref[s], slot, window, in_ref)


def to_slots(starts, lens, array, slot, window):
    count, columns = starts.shape[0], array.shape[1]
    scalars = pl.BlockSpec(memory_space=pltpu.SMEM)
    vmem = pl.BlockSpec(memory_space=pltpu.VMEM)
    return pl.pallas_call(
        functools.partial(slots_kernel, slot, window),
        in_specs=[scalars, scalars, vmem],
        out_specs=vmem,
        out_shape=pltpu.VMEM((count, slot, columns), jnp.bfloat16),
        compiler_params=pltpu.CompilerParams(vmem_limit_bytes=5 * 2**20),
        cost_estimate=kernel_cost,
    )(starts, lens, keep(array))


def attend_kernel(heads, window, start_ref, len_ref, q_ref, kv_ref, *out_refs):
    if len(out_refs) == 1:
        (whole_ref,) = out_refs
        out_refs = [whole_ref.at[s] for s in range(whole_ref.shape[0])]
    slot = out_refs[0].shape[0]
    half = slot // 2
    for s, out_ref in enumerate(out_refs):
        query = pick_rows(start_ref[s], len_ref[s], slot, window, q_ref)
        for block in range(2):
            width = (block + 1) * half
            stacked = jnp.concatenate(
                [query[block * half : width, h * HD : (h + 1) * HD] for h in range(heads)], axis=0
            )
            scores = lax.dot_general(
                stacked,
                kv_ref[s, :width, :HD],
                (((1,), (1,)), ((), ())),
                preferred_element_type=jnp.float32,
            )
            row_at = lax.broadcasted_iota(jnp.int32, scores.shape, 0) & (half - 1)
            col_at = lax.broadcasted_iota(jnp.int32, scores.shape, 1)
            scores = jnp.where(col_at <= row_at + block * half, scores * HD ** (-0.5), mask_value)
            peak = jnp.max(scores, axis=-1, keepdims=True)
            raised = jnp.exp(scores - peak)
            weights = raised * (1.0 / jnp.sum(raised, axis=-1, keepdims=True))
            context = jnp.dot(
                weights.astype(jnp.bfloat16),
                kv_ref[s, :width, HD:],
                preferred_element_type=jnp.float32,
            ).astype(out_ref.dtype)
            for h in range(heads):
                out_ref[block * half : width, h * HD : (h + 1) * HD] = context[
                    h * half : (h + 1) * half
                ]


def attend(starts, lens, query, kv_slots, window, apart):
    columns = query.shape[1]
    count, slot = kv_slots.shape[:2]
    scalars = pl.BlockSpec(memory_space=pltpu.SMEM)
    vmem = pl.BlockSpec(memory_space=pltpu.VMEM)
    return pl.pallas_call(
        functools.partial(attend_kernel, columns // HD, window),
        in_specs=[scalars, scalars, vmem, vmem],
        out_specs=[vmem] * count if apart else vmem,
        out_shape=(
            [pltpu.VMEM((slot, columns), jnp.bfloat16)] * count
            if apart
            else pltpu.VMEM((count, slot, columns), jnp.bfloat16)
        ),
        compiler_params=pltpu.CompilerParams(vmem_limit_bytes=6 * 2**20),
        cost_estimate=kernel_cost,
    )(starts, lens, keep(query), kv_slots)


def place_kernel(count, window, start_ref, len_ref, *refs):
    in_refs, (out_ref, total) = refs[:count], refs[-2:]
    rows, slot = total.shape[0], in_refs[0].shape[0]
    total[...] = jnp.zeros_like(total)
    row_at = lax.broadcasted_iota(jnp.int32, (window, slot), 0)
    col_at = lax.broadcasted_iota(jnp.int32, (window, slot), 1)
    for s, in_ref in enumerate(in_refs):
        start = start_ref[s]
        first = pl.multiple_of(jnp.minimum((start // 8) * 8, rows - window), 8)
        pick = jnp.where(
            (row_at == col_at + (start - first)) & (col_at < len_ref[s]), 1.0, 0.0
        ).astype(jnp.bfloat16)
        total[pl.ds(first, window), :] += jnp.dot(
            pick, in_ref[...], preferred_element_type=jnp.float32
        )
    out_ref[...] = total[...].astype(out_ref.dtype)


def place(starts, lens, slots, rows, which, all_columns, before):
    count, (slot, columns) = len(slots), slots[0].shape[-2:]
    window = min(rows, slot + 8)
    if isinstance(slots, list):
        in_specs = [pl.BlockSpec((slot, columns), lambda r, a, b: (0, 0))] * count
        operands = list(slots)
    else:
        in_specs = [
            pl.BlockSpec((None, slot, columns), lambda r, a, b, s=s: (s, 0, 0))
            for s in range(count)
        ]
        operands = [slots] * count
    aliases = {}
    if before is not None:
        in_specs.append(pl.BlockSpec(memory_space=pl.ANY))
        operands.append(before)
        aliases = {2 + count: 0}
    grid_spec = pltpu.PrefetchScalarGridSpec(
        num_scalar_prefetch=2,
        grid=(1,),
        in_specs=in_specs,
        out_specs=pl.BlockSpec((rows, columns), lambda r, a, b: (0, which)),
        scratch_shapes=[pltpu.VMEM((rows, columns), jnp.float32)],
    )
    return pl.pallas_call(
        functools.partial(place_kernel, count, window),
        grid_spec=grid_spec,
        out_shape=jax.ShapeDtypeStruct((rows, all_columns), jnp.bfloat16),
        input_output_aliases=aliases,
        compiler_params=pltpu.CompilerParams(vmem_limit_bytes=8 * 2**20),
        cost_estimate=kernel_cost,
    )(starts, lens, *operands)


def local_line(
    rollout_states,
    norm_gain,
    w_query,
    w_key,
    w_value,
    b_query,
    b_key,
    b_value,
    seq_lengths,
    seq_dest,
    seq_offset,
):
    learners = lax.axis_size("dp")
    line = learners // 2
    me = lax.axis_index("dp")
    z, x = me // 2, me % 2
    t = lax.axis_index("tensor")
    row_count, feature_count = rollout_states.shape
    slot = 2 * row_count // learners
    half = feature_count // 2
    middle = row_count // 2

    def after(array, *others):
        return lax.optimization_barrier((array, *others))[0]

    def swap_x(array):
        return lax.ppermute(array, "dp", [(i, i ^ 1) for i in range(learners)])

    def swap_y(array):
        return lax.ppermute(array, "tensor", [(i, i ^ 2) for i in range(4)])

    def swap_core(array):
        return lax.ppermute(array, "tensor", [(i, i ^ 1) for i in range(4)])

    wide = 2 * HD
    along_z = [[2 * i + j for i in range(line)] for j in range(2)]
    groups = [
        [jnp.concatenate([w_key, w_value], axis=1), w_query[:, :wide]],
        [w_query[:, wide : 2 * wide], w_query[:, 2 * wide : 3 * wide]],
        [w_query[:, 3 * wide :]],
    ]
    weights = []
    for group in groups:
        gathered = lax.all_gather(jnp.stack(group), "dp", axis_index_groups=along_z)
        weights.append(pltpu.with_memory_space_constraint(gathered, pltpu.HBM))
    bias_kv = jnp.concatenate([b_key, b_value])[None, :]
    biases = [b_query[None, low : low + wide] for low in range(0, w_query.shape[1], wide)]

    states = rollout_states
    widened = states.astype(jnp.float32)
    squares = jnp.sum(widened * widened, axis=-1)
    squares = squares + swap_core(squares)
    squares = squares + swap_y(squares)
    scale = lax.rsqrt(squares[:, None] / (4 * feature_count) + norm_eps)

    def normed(first):
        part = lax.dynamic_slice_in_dim(states, first, half, 1).astype(jnp.float32)
        gain = lax.dynamic_slice_in_dim(norm_gain, t * feature_count + first, half, 0)
        return (part * scale * gain[None, :]).astype(jnp.bfloat16)

    own, give = normed(x * half), normed((1 - x) * half)

    near_a = swap_x(give[:middle])
    own_a = swap_y(own[:middle])
    own_core = swap_core(own)
    near_b = swap_x(after(give[middle:], near_a))
    diag_a = swap_y(after(near_a, own_a))
    near_a_core = swap_core(near_a)
    own_a_core = swap_core(after(own_a, near_a))
    diag_b = swap_y(after(near_b, diag_a))
    near_b_core = swap_core(after(near_b, diag_a))
    diag_a_core = swap_core(after(diag_a, near_b))
    own_b = swap_y(after(own[middle:], diag_b))
    diag_b_core = swap_core(diag_b)
    near_ax = [[near_a], [near_a_core], [diag_a], [diag_a_core]]
    near_bx = [[near_b], [near_b_core], [diag_b], [diag_b_core]]
    near_x = [pack(near_ax, False), pack(near_bx, False)]
    which = jnp.stack([t ^ i for i in range(4)]).astype(jnp.int32)

    lengths = seq_lengths.reshape(learners, learners)
    dests = seq_dest.reshape(learners, learners)
    offsets = seq_offset.reshape(learners, learners)
    starts = jnp.cumsum(lengths, axis=1) - lengths
    peer_ids = jnp.arange(learners, dtype=jnp.int32)
    rows = jnp.arange(row_count, dtype=jnp.int32)
    length = lax.dynamic_index_in_dim(lengths, me, 0, keepdims=False)
    start = lax.dynamic_index_in_dim(starts, me, 0, keepdims=False)
    dest = lax.dynamic_index_in_dim(dests, me, 0, keepdims=False)
    partners = me ^ peer_ids

    def by_learner(order):
        match = (dest[None, :] == order[:, None]).astype(jnp.int32)
        return jnp.sum(match * start[None, :], axis=1), jnp.sum(match * length[None, :], axis=1)

    send_to = by_learner(partners)
    send_all = by_learner(peer_ids)
    inside = (rows[:, None] >= start[None, :]) & (rows[:, None] < (start + length)[None, :])
    position = rows - jnp.sum(inside.astype(jnp.int32) * start[None, :], axis=1)
    angles = keep(jnp.concatenate(rope_tables(position), axis=1))
    matched = (dests == me).astype(jnp.int32)
    match = (peer_ids[None, :] == partners[:, None]).astype(jnp.int32)
    runs_all = jnp.sum(matched * offsets, axis=1), jnp.sum(matched * lengths, axis=1)
    runs_from = tuple(jnp.sum(match * run[None, :], axis=1) for run in runs_all)

    window = min(row_count, -(-(slot + 16) // 128) * 128)

    def send(outgoing):
        incoming = [outgoing[0]]
        for d in range(1, learners):
            pairs = [(i, i ^ d) for i in range(learners)]
            incoming.append(lax.ppermute(outgoing[d], "dp", pairs))
        return incoming

    def exchange(outgoing):
        return lax.all_to_all(outgoing, "dp", split_axis=0, concat_axis=0, tiled=True)

    def receive(c, incoming, before, *others):
        run_start, run_length = runs_from if isinstance(incoming, list) else runs_all
        start_at = after(run_start, *others)
        return place(start_at, run_length, incoming, row_count, c, w_query.shape[1], before)

    first, second, third = weights
    whole = [(0, wide, jnp.bfloat16)]

    def partial(group, chunks, outs, *others):
        return projection(after(which, *others), near_x, group, chunks, outs)

    def contexts(c, group, chunk, got, others, attend_after=()):
        ending = ((True, True), got, biases[c], angles)
        (rot,) = projection(after(which, *others), own_x, group, (chunk,), whole, ending)
        send_start, send_length = send_all
        start_at = after(send_start, *attend_after)
        return attend(start_at, send_length, rot, kv_slots, window, False)

    outs = [(0, wide, jnp.float32), (wide, 2 * wide, jnp.bfloat16)]
    part_kv, part_0 = partial(first, (0, 1), outs)
    got_kv = swap_x(part_kv)
    own_b_core = swap_core(after(own_b, part_kv))
    own_x = [keep(pack([[own], [own_core], [own_a, own_b], [own_a_core, own_b_core]], True))]
    got_0 = swap_x(after(part_0, got_kv))
    ending = ((True, False), got_kv, bias_kv, angles)
    (kv,) = projection(which, own_x, first, (0,), whole, ending)
    kv_slots = keep(to_slots(*send_all, kv, slot, window))
    kv_slots_to = keep(to_slots(*send_to, kv, slot, window))
    out_0 = contexts(0, first, 1, got_0, (kv,))
    in_0 = exchange(out_0)
    outs = [(0, wide, jnp.bfloat16), (wide, 2 * wide, jnp.bfloat16)]
    part_1, part_2 = partial(second, (0, 1), outs, out_0)
    got_1 = swap_x(part_1)
    got_2 = swap_x(after(part_2, got_1))
    out_1 = contexts(1, second, 0, got_1, (part_2,), (got_2,))
    in_1 = exchange(out_1)
    out_2 = contexts(2, second, 1, got_2, (out_1,))
    (part_3,) = partial(third, (0,), whole, out_2)
    got_3 = swap_x(part_3)
    result = receive(0, in_0, None, part_3)
    ending = ((True, True), got_3, biases[3], angles)
    (rot_3,) = projection(after(which, out_2), own_x, third, (0,), whole, ending)
    in_2 = exchange(after(out_2, in_0, rot_3))
    out_3 = attend(*send_to, rot_3, kv_slots_to, window, True)
    in_3 = send(out_3)
    result = receive(1, in_1, result, out_3[0])
    result = receive(2, in_2, result, out_3[0])
    return receive(3, in_3, result)


def solution(mesh):
    placed = (
        P("dp", "tensor"),
        P(),
        P("dp", "tensor"),
        P("dp", "tensor"),
        P("dp", "tensor"),
        P("tensor"),
        P("tensor"),
        P("tensor"),
        P(),
        P(),
        P(),
    )
    fits_line = mesh.shape["dp"] == 8 and mesh.shape["tensor"] == 4
    return jax.shard_map(
        local_line if fits_line else local_any,
        mesh=mesh,
        in_specs=placed,
        out_specs=P("dp", "tensor"),
        check_vma=False,
    )
```
